32 devices in a mesh: groups: 2 (over y), mesh: 4 (over z), feat: 2 (over x), rep: 2 (over core).
Axes of the slice: x: 2, y: 2, z: 4, core: 2. Of those that a mesh axis runs over, the one named last changes fastest.
Arguments:
- grid_feats: bfloat16 [8192, 512], P(('groups', 'mesh', 'feat', 'rep')), parts along dimension 0, may hold values from -6 to 6
- g2m_shard: int32 [8192, 2], P(('groups', 'mesh', 'feat', 'rep')), parts along dimension 0, may hold values from 0 to 3, all different within a row; in each aligned block of 256 rows (0 to 255, 256 to 511, ...) at most 256 rows name the same one
- g2m_node: int32 [8192, 2], P(('groups', 'mesh', 'feat', 'rep')), parts along dimension 0, may hold values from 0 to 511
- mesh_init: bfloat16 [4096, 512], P(('groups', 'mesh')), parts along dimension 0, may hold values from -6 to 6
- sender_slots: int32 [16384], P(('groups', 'mesh', 'feat', 'rep')), parts along dimension 0, may hold values from 0 to 639, as said below
- receivers: int32 [16384], P(('groups', 'mesh', 'feat', 'rep')), parts along dimension 0, may hold values from 0 to 511
- halo_index: int32 [8, 4, 32], P(('groups', 'mesh')), parts along dimension 0, may hold values from 0 to 512, as said below
- w_enc_grid: bfloat16 [512, 512], replicated, may hold values from -0.25 to 0.25
- w_enc_mesh: bfloat16 [512, 512], replicated, may hold values from -0.25 to 0.25
- w_enc_out: bfloat16 [512, 512], replicated, may hold values from -0.25 to 0.25
- enc_gain: float32 [512], replicated, may hold values from 0.1 to 1.9
- w_send: bfloat16 [3, 512, 512], replicated, may hold values from -0.25 to 0.25
- w_recv: bfloat16 [3, 512, 512], replicated, may hold values from -0.25 to 0.25
- w_out: bfloat16 [3, 512, 512], replicated, may hold values from -0.25 to 0.25
- layer_gain: float32 [3, 512], replicated, may hold values from 0.1 to 1.9
- out_cot: bfloat16 [4096, 512], P(('groups', 'mesh')), parts along dimension 0, may hold values from -6 to 6
Outputs:
- final_mesh: bfloat16 [4096, 512], P(('groups', 'mesh')), parts along dimension 0
- grid_grad: float32 [8192, 512], P(('groups', 'mesh', 'feat', 'rep')), parts along dimension 0
The draws below stay inside these ranges and needn't reach their ends.
There are 2 independent parts, one for each index of `groups`. The reference program is written for one: setup_inputs(seed, part) draws one part's arguments, and reference() takes and returns one part's arrays. A program takes and returns all parts, laid end to end along the dimension named above; an argument that names none is the same for every part. Nothing has to cross between parts.
Inputs may be any that keep to these rules, and one draw needn't show every extreme that they name: `g2m_shard`: in each aligned block of 256 rows (the rows of one device) no shard is named more than 256 times, a bound that some block reaches; the 2 shards of a row differ. halo_index[s, d] lists distinct nodes of shard s, numbered within the shard, followed by padding 512; it holds at least half of 32 nodes when s differs from d, the list of a shard for itself is all padding, the lists of shard 3 for every other shard are full, and for some d every list of another shard is full. `sender_slots`: A value below 512 is a node of the edge's own shard. A value 512 + s * 32 + k names entry k of halo_index[s, o] for the edge's shard o, with s other than o, and that entry is never padding.
All inputs are finite; a program needn't handle non-finite values.
Results may differ from the reference program's by a relative error of at most 0.018.
Values may be sent and summed in bfloat16 or wider, within the bound.
No kernel may reach another device: no remote copies, remote signals or barrier semaphores. Data moves between devices by JAX's collectives and lax.ppermute only.
A program may use at most 128 MiB of HBM per device.

```python
import math
import jax
import jax.numpy as jnp
import numpy as np
from jax import lax

D = 512
NODE_DEV = 512
EDGE_DEV = 512
GRID_DEV = 256
HALO = 32
TOP = 2
LAYERS = 3
CAP = 256
NODES = 2048
EDGES = 8192
GRID = 4096
N_MESH = 4
N_FEAT = 2
N_REP = 2


def halo_plan(key):
    list_key, count_key, full_key = jax.random.split(key, 3)
    pair_keys = jax.random.split(list_key, N_MESH * N_MESH)
    orders = jax.vmap(lambda one_key: jax.random.permutation(one_key, NODE_DEV)[:HALO])(pair_keys)
    orders = orders.reshape(N_MESH, N_MESH, HALO).astype(jnp.int32)
    counts = jax.random.randint(count_key, (N_MESH, N_MESH), HALO // 2, HALO + 1)
    full_shard = jax.random.randint(full_key, (), 0, N_MESH)
    source_ids = jnp.arange(N_MESH)[:, None]
    target_ids = jnp.arange(N_MESH)[None, :]
    counts = jnp.where(target_ids == full_shard, HALO, counts)
    counts = jnp.where(source_ids == N_MESH - 1, HALO, counts)
    counts = jnp.where(source_ids == target_ids, 0, counts)
    position = jnp.arange(HALO)[None, None, :]
    listed = jnp.where(position < counts[:, :, None], orders, NODE_DEV)
    return (listed.astype(jnp.int32), counts.astype(jnp.int32))


def draw_halo_index(key, part):
    listed, counts = halo_plan(key)
    return listed


def draw_sender_slots(key, part):
    listed, counts = halo_plan(key)
    key = jax.random.fold_in(key, 11)
    pick_key, node_key, shard_key, place_key = jax.random.split(key, 4)
    owner = jnp.arange(EDGES, dtype=jnp.int32) // (EDGE_DEV * N_FEAT * N_REP)
    is_local = jax.random.randint(pick_key, (EDGES,), 0, 2) == 0
    local_node = jax.random.randint(node_key, (EDGES,), 0, NODE_DEV)
    source = (owner + 1 + jax.random.randint(shard_key, (EDGES,), 0, N_MESH - 1)) % N_MESH
    available = counts[source, owner]
    place = jax.random.randint(place_key, (EDGES,), 0, 1 << 20) % jnp.maximum(available, 1)
    remote_slot = NODE_DEV + source * HALO + place
    slots = jnp.where(is_local, local_node, remote_slot).astype(jnp.int32)
    slots = slots.at[0].set(NODE_DEV + N_MESH * HALO - 1)
    slots = slots.at[1].set(0)
    return slots.astype(jnp.int32)


def set_ends(array, stream_key, low, largest):
    index_at = [jax.random.randint(jax.random.fold_in(stream_key, axis), (), 0, length) for axis, length in enumerate(array.shape)]
    widest = array.shape.index(max(array.shape))
    neighbour = index_at[:widest] + [(index_at[widest] + 1) % array.shape[widest]] + index_at[widest + 1:]
    return array.at[tuple(index_at)].set(low).at[tuple(neighbour)].set(largest)


def level_of(own_key, shape, pieces, smallest, high):
    loudness, own = 1.0, jax.random.fold_in(own_key, 6)
    for axis_at, blocks in pieces:
        draws = jnp.exp(jax.random.uniform(jax.random.fold_in(own, axis_at), (blocks,), jnp.float32, smallest / len(pieces), high / len(pieces)))
        loudness = loudness * jnp.repeat(draws, shape[axis_at] // blocks).reshape([-1 if axis == axis_at else 1 for axis in range(len(shape))])
    return loudness


def shared_out(key, own, number, rows, number_of, top, most, lean):
    sequence = jax.random.permutation(key, number_of)
    crowded, common = shares(number_of, rows * top, most, lean, True), shares(number_of, rows * top, most, lean, False)
    places = jnp.arange(number_of)

    def named(tallies, turn):
        used = int((tallies > 0).sum())
        fixed = max(1, used // 4)
        passed = fixed + (places - fixed + turn * (used - fixed)) % max(1, number_of - fixed)
        return jnp.zeros((number_of,), jnp.int32).at[sequence[jnp.where(places < fixed, places, passed)]].set(jnp.asarray(tallies, jnp.int32))

    tallies = jnp.where(number % 4 == 0, named(crowded, number // 4), named(common, number - number // 4 - 1))
    mixed = jax.random.permutation(jax.random.fold_in(own, 3), number_of)
    giver, sink = mixed[0:number_of // 2 * 2:2], mixed[1:number_of // 2 * 2:2]
    room = jnp.minimum(tallies[giver] - 1, most - tallies[sink]) // 2
    room = jnp.where((giver == sequence[0]) | (sink == sequence[0]) | (tallies[sink] == 0), 0, jnp.maximum(room, 0))
    passed = jax.random.randint(jax.random.fold_in(own, 4), (number_of // 2,), 0, 1 << 20) % (room + 1)
    tallies = tallies.at[giver].add(-passed).at[sink].add(passed)
    items = jnp.searchsorted(jnp.cumsum(tallies), jnp.arange(rows * top), side="right").astype(jnp.int32)
    table = items.reshape(top, rows).T
    table = table[jax.random.permutation(jax.random.fold_in(own, 1), rows)]
    turn = jax.random.randint(jax.random.fold_in(own, 2), (rows, 1), 0, top)
    return jnp.take_along_axis(table, (jnp.arange(top)[None, :] + turn) % top, axis=1)


def shares(number_of, total, limit, skew, full):
    loads = [(1 << 20) // math.isqrt(standing ** skew) + 1 for standing in range(1, number_of + 1)]
    largest = limit if full else min(limit, max(-(-total // number_of), total * loads[0] // sum(loads)))
    least = 1 if total - largest >= number_of - 1 else 0
    given, surplus = [largest] + [least] * (number_of - 1), total - largest - least * (number_of - 1)
    while surplus > 0:
        free = [i for i in range(1, number_of) if given[i] < largest] or [i for i in range(1, number_of) if given[i] < limit]
        mass, remaining = sum([loads[i] for i in free]), surplus
        for i in free:
            addition = min(limit - given[i], max(1, remaining * loads[i] // mass), surplus)
            given[i] = given[i] + addition
            surplus = surplus - addition
    return np.array(given)


def centred(rng, shape, scale, bound, cuts=(), held_as=jnp.bfloat16):
    result = scale * jax.random.normal(rng, shape, jnp.float32)
    if cuts:
        result = result * level_of(rng, shape, cuts, -0.22, 0.18)
    return jnp.clip(result, -bound, bound).astype(held_as)


def setup_inputs(seed: int = 0, part: int = 0) -> dict:
    splits = jax.random.split(jax.random.key(seed), 17)
    part_keys = jax.random.split(jax.random.fold_in(splits[16], part), 17)
    grid_feats = centred(part_keys[0], (GRID, D), 1.0, 6.0, ((0, 16),))
    g2m_shard_keys = jax.random.split(jax.random.fold_in(part_keys[1], 1), GRID // GRID_DEV)
    g2m_shard_turns = jax.random.permutation(jax.random.fold_in(part_keys[1], 3), GRID // GRID_DEV)
    g2m_shard = jax.vmap(lambda own, number: shared_out(jax.random.fold_in(part_keys[1], 2), own, number, GRID_DEV, N_MESH, TOP, CAP, 2))(g2m_shard_keys, g2m_shard_turns).reshape((GRID, TOP))
    g2m_node = set_ends(jax.random.randint(part_keys[2], (GRID, TOP), 0, NODE_DEV), jax.random.fold_in(part_keys[2], 1), 0, NODE_DEV - 1).astype(jnp.int32)
    mesh_init = centred(part_keys[3], (NODES, D), 1.0, 6.0, ((0, 4),))
    sender_slots = draw_sender_slots(jax.random.fold_in(jax.random.fold_in(splits[16], part), 71), part)
    receivers = set_ends(jax.random.randint(part_keys[5], (EDGES,), 0, NODE_DEV), jax.random.fold_in(part_keys[5], 1), 0, NODE_DEV - 1).astype(jnp.int32)
    halo_index = draw_halo_index(jax.random.fold_in(jax.random.fold_in(splits[16], part), 71), part)
    w_enc_grid = centred(splits[7], (D, D), D ** -0.5, 0.25)
    w_enc_mesh = centred(splits[8], (D, D), D ** -0.5, 0.25)
    w_enc_out = centred(splits[9], (D, D), D ** -0.5, 0.25)
    enc_gain = jnp.clip(1.0 + 0.18 * jax.random.normal(splits[10], (D,), jnp.float32), 0.1, 1.9)
    w_send = centred(splits[11], (LAYERS, D, D), D ** -0.5, 0.25)
    w_recv = centred(splits[12], (LAYERS, D, D), D ** -0.5, 0.25)
    w_out = centred(splits[13], (LAYERS, D, D), D ** -0.5, 0.25)
    layer_gain = jnp.clip(1.0 + 0.18 * jax.random.normal(splits[14], (LAYERS, D), jnp.float32), 0.1, 1.9)
    out_cot = centred(part_keys[15], (NODES, D), 1.0, 6.0, ((0, 4),))
    return {"grid_feats": grid_feats, "g2m_shard": g2m_shard, "g2m_node": g2m_node, "mesh_init": mesh_init, "sender_slots": sender_slots, "receivers": receivers, "halo_index": halo_index, "w_enc_grid": w_enc_grid, "w_enc_mesh": w_enc_mesh, "w_enc_out": w_enc_out, "enc_gain": enc_gain, "w_send": w_send, "w_recv": w_recv, "w_out": w_out, "layer_gain": layer_gain, "out_cot": out_cot}


eps = 1e-05

def silu_slope(values):
    sigma = jax.nn.sigmoid(values)
    return sigma * (1.0 + values * (1.0 - sigma))

def norm_scale(totals):
    return lax.rsqrt(lax.optimization_barrier(jnp.mean(totals * totals, axis=-1, keepdims=True)) + eps)

def norm_back(totals, scaled, gain_row, upstream):
    normed = totals * scaled
    slope = upstream * gain_row
    return scaled * (slope - normed * lax.optimization_barrier(jnp.mean(slope * normed, axis=-1, keepdims=True)))

def product(left, right):
    return jnp.dot(left, right, preferred_element_type=jnp.float32)

def reference(grid_feats, g2m_shard, g2m_node, mesh_init, sender_slots, receivers, halo_index, w_enc_grid, w_enc_mesh, w_enc_out, enc_gain, w_send, w_recv, w_out, layer_gain, out_cot):
    shard_edges = EDGE_DEV * N_FEAT * N_REP
    owner = (jnp.arange(EDGES, dtype=jnp.int32) // shard_edges).astype(jnp.int32)
    recv_node = owner * NODE_DEV + receivers
    remote = jnp.maximum(sender_slots - NODE_DEV, 0)
    src_shard = remote // HALO
    src_pos = remote % HALO
    listed = halo_index[src_shard, owner, src_pos]
    send_node = jnp.where(sender_slots < NODE_DEV, owner * NODE_DEV + sender_slots, src_shard * NODE_DEV + listed).astype(jnp.int32)
    pair_node = (g2m_shard * NODE_DEV + g2m_node).reshape(-1).astype(jnp.int32)
    grid_proj = jnp.repeat(product(grid_feats, w_enc_grid), TOP, axis=0)
    enc_pre = grid_proj + product(mesh_init[pair_node], w_enc_mesh)
    enc_act = jax.nn.silu(enc_pre).astype(jnp.bfloat16)
    enc_msg = product(enc_act, w_enc_out)
    enc_sum = jax.ops.segment_sum(enc_msg, pair_node, num_segments=NODES)
    enc_scale = norm_scale(enc_sum)
    hidden = (mesh_init.astype(jnp.float32) + enc_sum * enc_scale * enc_gain).astype(jnp.bfloat16)
    records = []
    for layer_index in range(LAYERS):
        edge_pre = product(hidden[send_node], w_send[layer_index]) + product(hidden[recv_node], w_recv[layer_index])
        edge_act = jax.nn.silu(edge_pre).astype(jnp.bfloat16)
        edge_msg = product(edge_act, w_out[layer_index])
        node_agg = jax.ops.segment_sum(edge_msg, recv_node, num_segments=NODES)
        scaled = norm_scale(node_agg)
        records.append((edge_pre, node_agg, scaled))
        hidden = (hidden.astype(jnp.float32) + node_agg * scaled * layer_gain[layer_index]).astype(jnp.bfloat16)
    final_mesh = hidden
    upstream = out_cot.astype(jnp.float32)
    for layer_index in reversed(range(LAYERS)):
        edge_pre, node_agg, scaled = records[layer_index]
        grad_agg = norm_back(node_agg, scaled, layer_gain[layer_index], upstream).astype(jnp.bfloat16)
        grad_act = product(grad_agg[recv_node], w_out[layer_index].T)
        grad_pre = (grad_act * silu_slope(edge_pre)).astype(jnp.bfloat16)
        grad_send = product(grad_pre, w_send[layer_index].T)
        grad_recv = product(grad_pre, w_recv[layer_index].T)
        upstream = upstream + jax.ops.segment_sum(grad_send, send_node, num_segments=NODES) + jax.ops.segment_sum(grad_recv, recv_node, num_segments=NODES)
    grad_sum = norm_back(enc_sum, enc_scale, enc_gain, upstream).astype(jnp.bfloat16)
    grad_act = product(grad_sum[pair_node], w_enc_out.T)
    grad_enc = (grad_act * silu_slope(enc_pre)).astype(jnp.bfloat16)
    pair_grad = product(grad_enc, w_enc_grid.T)
    grid_grad = lax.optimization_barrier(jnp.sum(pair_grad.reshape(GRID, TOP, D), axis=1))
    return (final_mesh, grid_grad)
```

```python
import functools

import jax
import jax.numpy as jnp
from jax import lax
from jax.experimental import pallas as pl
from jax.experimental.pallas import tpu as pltpu
from jax.sharding import PartitionSpec as P

LAYERS = 3
LANES = 128
BLOCK = 256
eps = 1e-05

f32 = jnp.float32
bf16 = jnp.bfloat16
i32 = jnp.int32


def norm_scale(totals):
    return lax.rsqrt(jnp.mean(totals * totals, axis=-1, keepdims=True) + eps)


def norm_back(totals, gain_row, upstream):
    scaled = norm_scale(totals)
    normed = totals * scaled
    slope = upstream * gain_row
    return scaled * (slope - normed * jnp.mean(slope * normed, axis=-1, keepdims=True))


def dot(left, right):
    return jnp.dot(left, right, preferred_element_type=f32)


def dot_back(left, right):
    return lax.dot_general(left, right, (((1,), (1,)), ((), ())), preferred_element_type=f32)


def gated(pre):
    sigma = 0.5 * jnp.tanh(0.5 * pre) + 0.5
    act = pre * sigma
    return act, sigma + act * (1.0 - sigma)


def as_mask(hit):
    return jnp.where(hit, 1.0, 0.0).astype(bf16)


def pick_rows(index, width):
    lane = lax.broadcasted_iota(i32, index.shape, 1)
    return jnp.concatenate([as_mask(index == lane + at) for at in range(0, width, LANES)], axis=1)


def pick_columns(index, height):
    place = lax.broadcasted_iota(i32, (height, index.shape[1]), 0)
    return as_mask(place == index)


def each_block(count, body):
    if count <= 8:
        for at in range(count):
            body(at * BLOCK)
    else:
        pl.loop(0, count)(lambda at: body(pl.multiple_of(at * BLOCK, BLOCK)))


def call(body, outs, scratch=()):
    def run(*args):
        def where(array):
            return pl.BlockSpec(memory_space=pltpu.SMEM if array.dtype == i32 and array.ndim == 1 else pltpu.VMEM)

        return pl.pallas_call(
            body,
            out_shape=tuple(jax.ShapeDtypeStruct(shape, dtype) for shape, dtype in outs),
            in_specs=[where(array) for array in args],
            out_specs=tuple(pl.BlockSpec(memory_space=pltpu.VMEM) for _ in outs),
            scratch_shapes=[pltpu.VMEM(shape, dtype) for shape, dtype in scratch],
            compiler_params=pltpu.CompilerParams(vmem_limit_bytes=40 * 1024 * 1024),
        )(*args)

    return run


def encode_kernel(count, halves, *refs):
    meta, mesh_init, w_mesh, w_grid = refs[:4]
    rows, targets = refs[4 : 4 + count], refs[4 + count : 4 + 2 * count]
    outs = refs[4 + 2 * count :]
    keep, sends, slopes, total = outs[0], outs[1 : halves], outs[halves : halves + count], outs[-1]
    nodes = mesh_init.shape[0]
    projected = dot(mesh_init[...], w_mesh[...]).astype(bf16)
    total[...] = jnp.zeros_like(total)
    for step in range(count):
        grid = rows[step].shape[0]
        target = targets[step][...]
        picked = pick_columns(target, nodes)
        column = jnp.concatenate(
            [
                jnp.broadcast_to(target[:, at : at + LANES], (LANES, LANES)).T
                for at in range(0, grid, LANES)
            ],
            axis=0,
        )
        pre = dot(rows[step][...], w_grid[...]) + dot(pick_rows(column, nodes), projected)
        act, slope = gated(pre)
        slopes[step][...] = slope.astype(bf16)
        total[...] += dot(picked, act.astype(bf16))
    part = nodes // halves
    own = meta[0]

    def half(shift):
        at = lax.rem(own + shift, halves)
        return total[pl.ds(pl.multiple_of(at * part, part), part), :]

    keep[...] = half(0)
    for shift in range(1, halves):
        sends[shift - 1][...] = half(shift).astype(bf16)


def listed_rows(projected, list_column, outs):
    nodes = projected.shape[0]
    for shift, out in enumerate(outs):
        depth = out.shape[0]
        column = list_column[shift * depth : (shift + 1) * depth, :]
        out[...] = dot(pick_rows(column, nodes), projected).astype(bf16)


def start_kernel(halves, shifts, *refs):
    meta = refs[0]
    parts = refs[1 : 1 + halves]
    mesh_init, w_enc_out, gain, w_send, w_recv, list_column = refs[1 + halves : 7 + halves]
    hidden_out, enc_sum_out, sent, received = refs[7 + halves : 11 + halves]
    outs = refs[11 + halves : 11 + halves + shifts]
    whole = refs[-1]
    part = parts[0].shape[0]
    for shift in range(halves):
        at = lax.rem(meta[0] + shift, halves)
        whole[pl.ds(pl.multiple_of(at * part, part), part), :] = parts[shift][...]
    enc_sum = dot(whole[...], w_enc_out[...])
    enc_sum_out[...] = enc_sum
    hidden = (mesh_init[...].astype(f32) + enc_sum * norm_scale(enc_sum) * gain[...]).astype(bf16)
    hidden_out[...] = hidden
    projected = dot(hidden, w_send[...]).astype(bf16)
    sent[...] = projected
    listed_rows(projected, list_column[...], outs)
    received[...] = dot(hidden, w_recv[...]).astype(bf16)


def forward_part(sent, received, halos, send_column, recv_column, recv_row, slope_out, table, total):
    nodes = sent.shape[0]
    width = table.shape[0] - nodes
    table[0:nodes, :] = sent[...]
    at = nodes
    for halo in halos:
        table[at : at + halo.shape[0], :] = halo[...]
        at += halo.shape[0]
    if at < width:
        table[at:width, :] = jnp.zeros((width - at, table.shape[1]), bf16)
    table[width:, :] = received[...]
    total[...] = jnp.zeros_like(total)

    def body(at):
        block = pl.ds(at, BLOCK)
        picked = jnp.concatenate(
            [pick_rows(send_column[block, :], width), pick_rows(recv_column[block, :], nodes)], axis=1
        )
        act, slope = gated(dot(picked, table[...]))
        slope_out[block, :] = slope.astype(bf16)
        total[...] += dot(pick_columns(recv_row[:, block], nodes), act.astype(bf16))

    each_block(send_column.shape[0] // BLOCK, body)


def layer_kernel(shifts, *refs):
    hidden, sent, received = refs[:3]
    halos = refs[3 : 3 + shifts]
    send_column, recv_column, recv_row, w_out, gain, w_send, w_recv, list_column = refs[3 + shifts : 11 + shifts]
    hidden_out, agg_out, slope_out, sent_out, received_out = refs[11 + shifts : 16 + shifts]
    outs = refs[16 + shifts : 16 + 2 * shifts]
    table, total = refs[-2:]
    forward_part(sent, received, halos, send_column, recv_column, recv_row, slope_out, table, total)
    agg = dot(total[...].astype(bf16), w_out[...])
    agg_out[...] = agg
    fresh = (hidden[...].astype(f32) + agg * norm_scale(agg) * gain[...]).astype(bf16)
    hidden_out[...] = fresh
    projected = dot(fresh, w_send[...]).astype(bf16)
    sent_out[...] = projected
    listed_rows(projected, list_column[...], outs)
    received_out[...] = dot(fresh, w_recv[...]).astype(bf16)


def backward_part(upstream, agg, slope, gain, w_out, w_recv, recv_column, recv_row, send_row, sums, rest, own_sums, outs):
    nodes = agg.shape[0]
    width = sums.shape[0] - nodes
    spread = dot_back(norm_back(agg, gain, upstream).astype(bf16), w_out).astype(bf16)
    sums[...] = jnp.zeros_like(sums)

    def body(at):
        block = pl.ds(at, BLOCK)
        grad_act = dot(pick_rows(recv_column[block, :], nodes), spread)
        grad_pre = (grad_act * slope[block, :].astype(f32)).astype(bf16)
        picked = jnp.concatenate(
            [pick_columns(send_row[:, block], width), pick_columns(recv_row[:, block], nodes)], axis=0
        )
        sums[...] += dot(picked, grad_pre)

    each_block(slope.shape[0] // BLOCK, body)
    at = nodes
    for out in outs:
        out[...] = sums[at : at + out.shape[0], :].astype(bf16)
        at += out.shape[0]
    own_sums[...] = sums[0:nodes, :]
    rest[...] = upstream + dot_back(sums[width:, :].astype(bf16), w_recv)


def turn_kernel(shifts, *refs):
    hidden, sent, received = refs[:3]
    halos = refs[3 : 3 + shifts]
    send_column, recv_column, recv_row, send_row, w_out, gain, w_recv, cot = refs[3 + shifts : 11 + shifts]
    hidden_out, rest, own_sums = refs[11 + shifts : 14 + shifts]
    outs = refs[14 + shifts : 14 + 2 * shifts]
    slope, table, total, sums = refs[-4:]
    forward_part(sent, received, halos, send_column, recv_column, recv_row, slope, table, total)
    agg = dot(total[...].astype(bf16), w_out[...])
    hidden_out[...] = (hidden[...].astype(f32) + agg * norm_scale(agg) * gain[...]).astype(bf16)
    backward_part(
        cot[...].astype(f32), agg, slope, gain[...], w_out[...], w_recv[...],
        recv_column, recv_row, send_row, sums, rest, own_sums, outs,
    )


def arrived(rest, own_sums, returned, list_row, w_send):
    nodes = own_sums.shape[0]
    totals = own_sums[...]
    at = 0
    for block in returned:
        depth = block.shape[0]
        totals = totals + dot(pick_columns(list_row[:, at : at + depth], nodes), block[...])
        at += depth
    return rest[...] + dot_back(totals.astype(bf16), w_send)


def back_kernel(shifts, *refs):
    rest_in, own_in = refs[:2]
    returned = refs[2 : 2 + shifts]
    list_row, w_send, agg, slope, gain, w_out, w_recv, recv_column, recv_row, send_row = refs[2 + shifts : 12 + shifts]
    rest, own_sums = refs[12 + shifts : 14 + shifts]
    outs = refs[14 + shifts : 14 + 2 * shifts]
    sums = refs[-1]
    upstream = arrived(rest_in, own_in, returned, list_row, w_send[...])
    backward_part(
        upstream, agg[...], slope, gain[...], w_out[...], w_recv[...],
        recv_column, recv_row, send_row, sums, rest, own_sums, outs,
    )


def finish_kernel(count, shifts, *refs):
    rest_in, own_in = refs[:2]
    returned = refs[2 : 2 + shifts]
    list_row, w_send, enc_sum, gain, w_enc_out = refs[2 + shifts : 7 + shifts]
    targets, slopes = refs[7 + shifts : 7 + shifts + count], refs[7 + shifts + count : 7 + shifts + 2 * count]
    outs = refs[7 + shifts + 2 * count :]
    nodes = enc_sum.shape[0]
    upstream = arrived(rest_in, own_in, returned, list_row, w_send[...])
    spread = dot_back(norm_back(enc_sum[...], gain[...], upstream).astype(bf16), w_enc_out[...]).astype(bf16)
    for step in range(count):
        target = targets[step][...]
        column = jnp.concatenate(
            [
                jnp.broadcast_to(target[:, at : at + LANES], (LANES, LANES)).T
                for at in range(0, target.shape[1], LANES)
            ],
            axis=0,
        )
        grad_act = dot(pick_rows(column, nodes), spread)
        outs[step][...] = (grad_act * slopes[step][...].astype(f32)).astype(bf16)


def grid_kernel(count, *refs):
    blocks, w_grid, out = refs[:count], refs[count], refs[count + 1]
    total = blocks[0][...].astype(f32)
    for block in blocks[1:]:
        total = total + block[...].astype(f32)
    out[...] = dot_back(total.astype(bf16), w_grid[...])


def shifted(value, axis, by):
    size = lax.axis_size(axis)
    return lax.ppermute(value, axis, [(at, (at + by) % size) for at in range(size)])


def lanes(index):
    return jnp.broadcast_to(index[:, None], (index.shape[0], LANES))


def on_device(
    grid_feats,
    g2m_shard,
    g2m_node,
    mesh_init,
    sender_slots,
    receivers,
    halo_index,
    w_enc_grid,
    w_enc_mesh,
    w_enc_out,
    enc_gain,
    w_send,
    w_recv,
    w_out,
    layer_gain,
    out_cot,
):
    shards = lax.axis_size("mesh")
    shard = lax.axis_index("mesh")
    members = lax.axis_size(("feat", "rep"))
    halves = lax.axis_size("rep")
    feats = lax.axis_size("feat")
    nodes, width = mesh_init.shape
    grid = grid_feats.shape[0]
    edges = sender_slots.shape[0]
    depth = halo_index.shape[2]
    shifts = shards - 1
    halo_width = -(-shifts * depth // LANES) * LANES
    all_edges = edges * members
    enc_gain = enc_gain[None, :]

    def target_for(step):
        wanted = lax.rem(shard + step, shards)
        return jnp.max(jnp.where(g2m_shard == wanted, g2m_node, -1), axis=1)[None, :]

    rows, targets = [grid_feats], [target_for(0)]
    for step in range(1, shards):
        targets.append(shifted(target_for(step), "mesh", step))
        rows.append(shifted(grid_feats, "mesh", step))

    place = sender_slots - nodes
    away = lax.rem(shard - place // depth + shards, shards)
    slots = jnp.where(sender_slots < nodes, sender_slots, nodes + (away - 1) * depth + place % depth)
    both = jnp.stack([slots, receivers])
    member = lax.axis_index(("feat", "rep"))
    ordered = jnp.stack([both] + [shifted(both, ("feat", "rep"), step) for step in range(1, members)])
    ordered = jnp.roll(ordered[::-1], member + 1, axis=0)
    all_slots, all_receivers = ordered[:, 0].reshape(-1), ordered[:, 1].reshape(-1)
    send_column, recv_column = lanes(all_slots), lanes(all_receivers)
    send_row, recv_row = all_slots[None, :], all_receivers[None, :]

    order = jnp.roll(halo_index[0], -shard, axis=0)[1:].reshape(-1)
    list_column, list_row = lanes(order), order[None, :]

    meta = lax.axis_index("rep").astype(i32).reshape(1)
    kept = call(
        functools.partial(encode_kernel, shards, halves),
        [((nodes // halves, width), f32)]
        + [((nodes // halves, width), bf16)] * (halves - 1)
        + [((grid, width), bf16)] * shards,
        [((nodes, width), f32)],
    )(meta, mesh_init, w_enc_mesh, w_enc_grid, *rows, *targets)
    part, enc_slopes = kept[0], kept[halves:]
    for step in range(1, halves):
        part = part + shifted(kept[step], "rep", step).astype(f32)
    part = part.astype(bf16)
    pieces = [part] + [shifted(part, "feat", step) for step in range(1, feats)]
    if feats > 2:
        pieces = list(jnp.roll(jnp.stack(pieces), -lax.axis_index("feat"), axis=0))
    part = sum(piece.astype(f32) for piece in pieces).astype(bf16)
    parts = [part] + [shifted(part, "rep", -step) for step in range(1, halves)]

    node_f32, node_bf16 = ((nodes, width), f32), ((nodes, width), bf16)
    listed = [((depth, width), bf16)] * shifts
    hidden, enc_sum, sent, received, *outgoing = call(
        functools.partial(start_kernel, halves, shifts),
        [node_bf16, node_f32, node_bf16, node_bf16] + listed,
        [node_bf16],
    )(meta, *parts, mesh_init, w_enc_out, enc_gain, w_send[0], w_recv[0], list_column)

    table = ((2 * nodes + halo_width, width), bf16)
    sums = ((2 * nodes + halo_width, width), f32)
    slope_shape = ((all_edges, width), bf16)
    records = []
    for layer in range(LAYERS - 1):
        halos = [shifted(block, "mesh", step + 1) for step, block in enumerate(outgoing)]
        hidden, agg, slope, sent, received, *outgoing = call(
            functools.partial(layer_kernel, shifts),
            [node_bf16, node_f32, slope_shape, node_bf16, node_bf16] + listed,
            [table, node_f32],
        )(
            hidden, sent, received, *halos, send_column, recv_column, recv_row,
            w_out[layer], layer_gain[layer][None, :], w_send[layer + 1], w_recv[layer + 1], list_column,
        )
        records.append((agg, slope))
    last = LAYERS - 1
    halos = [shifted(block, "mesh", step + 1) for step, block in enumerate(outgoing)]
    final_mesh, rest, own_sums, *outgoing = call(
        functools.partial(turn_kernel, shifts),
        [node_bf16, node_f32, node_f32] + listed,
        [slope_shape, table, node_f32, sums],
    )(
        hidden, sent, received, *halos, send_column, recv_column, recv_row, send_row,
        w_out[last], layer_gain[last][None, :], w_recv[last], out_cot,
    )
    for layer in reversed(range(LAYERS - 1)):
        returned = [shifted(block, "mesh", -step - 1) for step, block in enumerate(outgoing)]
        agg, slope = records[layer]
        rest, own_sums, *outgoing = call(
            functools.partial(back_kernel, shifts), [node_f32, node_f32] + listed, [sums]
        )(
            rest, own_sums, *returned, list_row, w_send[layer + 1], agg, slope,
            layer_gain[layer][None, :], w_out[layer], w_recv[layer], recv_column, recv_row, send_row,
        )
    returned = [shifted(block, "mesh", -step - 1) for step, block in enumerate(outgoing)]
    blocks = call(
        functools.partial(finish_kernel, shards, shifts), [((grid, width), bf16)] * shards
    )(rest, own_sums, *returned, list_row, w_send[0], enc_sum, enc_gain, w_enc_out, *targets, *enc_slopes)
    blocks = [blocks[0]] + [shifted(blocks[step], "mesh", -step) for step in range(1, shards)]
    (grid_grad,) = call(functools.partial(grid_kernel, shards), [((grid, width), f32)])(*blocks, w_enc_grid)
    return (final_mesh, grid_grad)


def solution(mesh):
    return jax.shard_map(
        on_device,
        mesh=mesh,
        in_specs=(
            P(("groups", "mesh", "feat", "rep"), None),
            P(("groups", "mesh", "feat", "rep"), None),
            P(("groups", "mesh", "feat", "rep"), None),
            P(("groups", "mesh"), None),
            P(("groups", "mesh", "feat", "rep")),
            P(("groups", "mesh", "feat", "rep")),
            P(("groups", "mesh"), None, None),
            P(),
            P(),
            P(),
            P(),
            P(),
            P(),
            P(),
            P(),
            P(("groups", "mesh"), None),
        ),
        out_specs=(P(("groups", "mesh"), None), P(("groups", "mesh", "feat", "rep"), None)),
        check_vma=False,
    )
```

```python
import functools

import jax
import jax.numpy as jnp
from jax import lax
from jax.experimental import pallas as pl
from jax.experimental.pallas import tpu as pltpu
from jax.sharding import PartitionSpec as P

LAYERS = 3
LANES = 128
BLOCK = 512
EXTRA = 16
eps = 1e-05

f32 = jnp.float32
bf16 = jnp.bfloat16
i32 = jnp.int32


def norm_scale(totals):
    return lax.rsqrt(jnp.mean(totals * totals, axis=-1, keepdims=True) + eps)


def norm_back(totals, gain_row, upstream):
    scaled = norm_scale(totals)
    normed = totals * scaled
    slope = upstream * gain_row
    return scaled * (slope - normed * jnp.mean(slope * normed, axis=-1, keepdims=True))


def dot(left, right):
    return jnp.dot(left, right, preferred_element_type=f32)


def dot_back(left, right):
    return lax.dot_general(left, right, (((1,), (1,)), ((), ())), preferred_element_type=f32)


def gated(pre):
    sigma = 0.5 * jnp.tanh(0.5 * pre) + 0.5
    act = pre * sigma
    return act, sigma + act * (1.0 - sigma)


def as_mask(hit):
    return jnp.where(hit, 1.0, 0.0).astype(bf16)


def pick_columns(index, first, height):
    place = lax.broadcasted_iota(i32, (height, index.shape[1]), 0) + first
    return as_mask(place == index)


def upright(index):
    count = index.shape[1]
    if count < LANES:
        index = jnp.concatenate([index, jnp.full((1, LANES - count), -1, i32)], axis=1)
    return jnp.broadcast_to(index, (LANES, LANES)).T[:count]


def pick_rows(column, first, width):
    lane = lax.broadcasted_iota(i32, column.shape, 1) + first
    return jnp.concatenate([as_mask(column == lane + at) for at in range(0, width, LANES)], axis=1)


def call(body, outs, scratch=()):
    def run(*args):
        def where(array):
            return pl.BlockSpec(memory_space=pltpu.SMEM if array.dtype == i32 and array.ndim == 1 else pltpu.VMEM)

        held = [(shape, dtype) for shape, dtype in scratch]
        room = sum(jnp.dtype(dtype).itemsize * shape[0] * shape[1] for shape, dtype in held)
        room += sum(array.dtype.itemsize * array.size for array in args)
        room += sum(jnp.dtype(dtype).itemsize * shape[0] * shape[1] for shape, dtype in outs)
        return pl.pallas_call(
            body,
            out_shape=tuple(jax.ShapeDtypeStruct(shape, dtype) for shape, dtype in outs),
            in_specs=[where(array) for array in args],
            out_specs=tuple(pl.BlockSpec(memory_space=pltpu.VMEM) for _ in outs),
            scratch_shapes=[pltpu.VMEM(shape, dtype) for shape, dtype in held],
            compiler_params=pltpu.CompilerParams(vmem_limit_bytes=min(room + (8 << 20), 60 << 20)),
        )(*args)

    return run


def place_kernel(slots, receivers, order, here, there, halo_here, halo_there, list_here, list_there):
    nodes = here.shape[1] // 2
    wide = halo_here.shape[1]

    def body(at):
        block = pl.ds(pl.multiple_of(at * LANES, LANES), LANES)
        slot, receiver = slots[:, block], receivers[:, block]
        slot_column, receiver_column = upright(slot), upright(receiver)
        here[block, 0:nodes] = pick_rows(slot_column, 0, nodes)
        here[block, nodes:] = pick_rows(receiver_column, 0, nodes)
        halo_here[block, :] = pick_rows(slot_column, nodes, wide)
        there[0:nodes, block] = pick_columns(slot, 0, nodes)
        there[nodes:, block] = pick_columns(receiver, 0, nodes)
        halo_there[:, block] = pick_columns(slot, nodes, wide)

    pl.loop(0, slots.shape[1] // LANES)(body)
    count = order.shape[1]
    for at in range(0, count, LANES):
        end = min(at + LANES, count)
        list_here[at:end, :] = pick_rows(upright(order[:, at:end]), 0, nodes)
    list_there[...] = pick_columns(order[...], 0, nodes)


def encode_kernel(steps, first, last, halves, *refs):
    refs = list(refs)
    meta, base, w_grid = refs[:3]
    del refs[:3]
    if first:
        w_mesh = refs.pop(0)
        projected = dot(base[...], w_mesh[...]).astype(bf16)
    else:
        total_in = refs.pop(0)
        projected = base[...]
    payloads = refs[:steps]
    del refs[:steps]
    picks, slopes = refs[:steps], refs[steps : 2 * steps]
    del refs[: 2 * steps]
    total = None if first else total_in[...]
    nodes = projected.shape[0]
    for payload, pick, slope_out in zip(payloads, picks, slopes):
        grid = pick.shape[0]
        notes = payload[grid:, 0:grid].astype(f32)
        target = jnp.full((1, grid), -1.0, f32)
        for at in range(0, notes.shape[0] // 3 * 3, 3):
            named = notes[at : at + 1] == meta[1].astype(f32)
            target = jnp.where(named, notes[at + 1 : at + 2] + 256.0 * notes[at + 2 : at + 3], target)
        target = target.astype(i32)
        column = jnp.concatenate([upright(target[:, at : at + LANES]) for at in range(0, grid, LANES)], axis=0)
        picked = pick_rows(column, 0, nodes)
        pick[...] = picked
        pre = dot(payload[0:grid, :], w_grid[...]) + dot(picked, projected)
        act, slope = gated(pre)
        slope_out[...] = slope.astype(bf16)
        added = dot(pick_columns(target, 0, nodes), act.astype(bf16))
        total = added if total is None else total + added
    if first:
        refs.pop(0)[...] = projected
    if not last:
        refs[0][...] = total
        return
    keep, sends, whole = refs[0], refs[1:halves], refs[-1]
    whole[...] = total
    part = nodes // halves

    def half(shift):
        at = lax.rem(meta[0] + shift, halves)
        return whole[pl.ds(pl.multiple_of(at * part, part), part), :]

    keep[...] = half(0)
    for shift in range(1, halves):
        sends[shift - 1][...] = half(shift).astype(bf16)


def list_rows(list_here, projected, outs):
    listed = dot(list_here[...], projected).astype(bf16)
    at = 0
    for out in outs:
        out[...] = listed[at : at + out.shape[0]]
        at += out.shape[0]


def start_kernel(halves, shifts, *refs):
    meta = refs[0]
    parts = refs[1 : 1 + halves]
    mesh_init, w_enc_out, gain, w_send, list_here = refs[1 + halves : 6 + halves]
    hidden_out, enc_sum_out, sent = refs[6 + halves : 9 + halves]
    outs = refs[9 + halves : 9 + halves + shifts]
    whole = refs[-1]
    part = parts[0].shape[0]
    for shift in range(halves):
        at = lax.rem(meta[0] + shift, halves)
        whole[pl.ds(pl.multiple_of(at * part, part), part), :] = parts[shift][...]
    enc_sum = dot(whole[...], w_enc_out[...])
    enc_sum_out[...] = enc_sum
    hidden = (mesh_init[...].astype(f32) + enc_sum * norm_scale(enc_sum) * gain[...]).astype(bf16)
    hidden_out[...] = hidden
    projected = dot(hidden, w_send[0]).astype(bf16)
    sent[...] = projected
    list_rows(list_here, projected, outs)


def local_kernel(layer, hidden, sent, here, w_recv, pre, table):
    nodes = hidden.shape[0]
    table[0:nodes, :] = sent[...]
    table[nodes:, :] = dot(hidden[...], w_recv[layer]).astype(bf16)
    for at in range(0, pre.shape[0], BLOCK):
        pre[at : at + BLOCK, :] = dot(here[at : at + BLOCK, :], table[...])


def stack_halo(halos, halo):
    at = 0
    for block in halos:
        halo[at : at + block.shape[0], :] = block[...]
        at += block.shape[0]
    if at < halo.shape[0]:
        halo[at:, :] = jnp.zeros((halo.shape[0] - at, halo.shape[1]), bf16)


def node_sum(pre, halos, halo_here, there, slope_out, halo, act_out):
    nodes = there.shape[0] // 2
    stack_halo(halos, halo)
    for at in range(0, pre.shape[0], BLOCK):
        block = slice(at, at + BLOCK)
        act, slope = gated(pre[block, :] + dot(halo_here[block, :], halo[...]))
        slope_out[block, :] = slope.astype(bf16)
        act_out[block, :] = act.astype(bf16)
    return dot(there[nodes:, :], act_out[...])


def layer_kernel(layer, shifts, *refs):
    hidden, pre = refs[:2]
    halos = refs[2 : 2 + shifts]
    halo_here, there, w_out, gain, w_send, list_here = refs[2 + shifts : 8 + shifts]
    hidden_out, agg_out, slope_out, sent_out = refs[8 + shifts : 12 + shifts]
    outs = refs[12 + shifts : 12 + 2 * shifts]
    halo, act = refs[-2:]
    total = node_sum(pre, halos, halo_here, there, slope_out, halo, act)
    agg = dot(total.astype(bf16), w_out[layer])
    agg_out[...] = agg
    fresh = (hidden[...].astype(f32) + agg * norm_scale(agg) * gain[layer : layer + 1, :]).astype(bf16)
    hidden_out[...] = fresh
    projected = dot(fresh, w_send[layer + 1]).astype(bf16)
    sent_out[...] = projected
    list_rows(list_here, projected, outs)


def edge_grads(grad_agg, w_out, here, halo_there, slope, grad_pre, outs):
    nodes = grad_agg.shape[0]
    spread = dot_back(grad_agg.astype(bf16), w_out).astype(bf16)
    for at in range(0, slope.shape[0], BLOCK):
        block = slice(at, at + BLOCK)
        grad_act = dot(here[block, nodes:], spread)
        grad_pre[block, :] = (grad_act * slope[block, :].astype(f32)).astype(bf16)
    given = dot(halo_there[...], grad_pre[...]).astype(bf16)
    at = 0
    for out in outs:
        out[...] = given[at : at + out.shape[0]]
        at += out.shape[0]


def turn_kernel(layer, shifts, *refs):
    hidden, pre = refs[:2]
    halos = refs[2 : 2 + shifts]
    halo_here, there, w_out, gain, here, halo_there, cot = refs[2 + shifts : 9 + shifts]
    hidden_out, grad_pre = refs[9 + shifts : 11 + shifts]
    outs = refs[11 + shifts : 11 + 2 * shifts]
    slope, halo = refs[-2:]
    total = node_sum(pre, halos, halo_here, there, slope, halo, grad_pre)
    agg = dot(total.astype(bf16), w_out[layer])
    gain_row = gain[layer : layer + 1, :]
    hidden_out[...] = (hidden[...].astype(f32) + agg * norm_scale(agg) * gain_row).astype(bf16)
    edge_grads(norm_back(agg, gain_row, cot[...].astype(f32)), w_out[layer], here, halo_there, slope, grad_pre, outs)


def rest_kernel(layer, upstream, grad_pre, there, w_send, w_recv, rest):
    nodes = upstream.shape[0]
    sums = dot(there[...], grad_pre[...]).astype(bf16)
    rest[...] = (
        upstream[...].astype(f32)
        + dot_back(sums[0:nodes], w_send[layer])
        + dot_back(sums[nodes:], w_recv[layer])
    )


def arrived(rest, returned, list_there, w_send, halo):
    at = 0
    for block in returned:
        halo[at : at + block.shape[0], :] = block[...]
        at += block.shape[0]
    projected = dot_back(halo[...], w_send).astype(bf16)
    return rest[...] + dot(list_there[...], projected)


def back_kernel(layer, shifts, *refs):
    rest = refs[0]
    returned = refs[1 : 1 + shifts]
    list_there, w_send, agg, slope, gain, w_out, here, halo_there = refs[1 + shifts : 9 + shifts]
    upstream_out, grad_pre = refs[9 + shifts : 11 + shifts]
    outs = refs[11 + shifts : 11 + 2 * shifts]
    halo = refs[-1]
    upstream = arrived(rest, returned, list_there, w_send[layer + 1], halo)
    upstream_out[...] = upstream
    grad_agg = norm_back(agg[...], gain[layer : layer + 1, :], upstream)
    edge_grads(grad_agg, w_out[layer], here, halo_there, slope, grad_pre, outs)


def finish_kernel(count, shifts, *refs):
    rest = refs[0]
    returned = refs[1 : 1 + shifts]
    list_there, w_send, enc_sum, gain, w_enc_out = refs[1 + shifts : 6 + shifts]
    picks, slopes = refs[6 + shifts : 6 + shifts + count], refs[6 + shifts + count : 6 + shifts + 2 * count]
    outs = refs[6 + shifts + 2 * count : -1]
    halo = refs[-1]
    upstream = arrived(rest, returned, list_there, w_send[0], halo)
    spread = dot_back(norm_back(enc_sum[...], gain[...], upstream).astype(bf16), w_enc_out[...]).astype(bf16)
    for pick, slope, out in zip(picks, slopes, outs):
        out[...] = (dot(pick[...], spread) * slope[...].astype(f32)).astype(bf16)


def grid_kernel(count, *refs):
    blocks, w_grid, out = refs[:count], refs[count], refs[count + 1]
    total = blocks[0][...].astype(f32)
    for block in blocks[1:]:
        total = total + block[...].astype(f32)
    out[...] = dot_back(total.astype(bf16), w_grid[...])


def shifted(value, axis, by):
    size = lax.axis_size(axis)
    return lax.ppermute(value, axis, [(at, (at + by) % size) for at in range(size)])


def in_order(pieces, axis):
    return jnp.roll(jnp.stack(pieces)[::-1], lax.axis_index(axis) + 1, axis=0)


def on_device(
    grid_feats,
    g2m_shard,
    g2m_node,
    mesh_init,
    sender_slots,
    receivers,
    halo_index,
    w_enc_grid,
    w_enc_mesh,
    w_enc_out,
    enc_gain,
    w_send,
    w_recv,
    w_out,
    layer_gain,
    out_cot,
):
    shards = lax.axis_size("mesh")
    shard = lax.axis_index("mesh")
    halves = lax.axis_size("rep")
    feats = lax.axis_size("feat")
    nodes, width = mesh_init.shape
    grid, tops = g2m_shard.shape
    edges = sender_slots.shape[0]
    depth = halo_index.shape[2]
    shifts = shards - 1
    listed_rows = shifts * depth
    wide = -(-listed_rows // LANES) * LANES
    all_edges = edges * halves * feats
    enc_gain = enc_gain[None, :]

    notes = jnp.stack([g2m_shard, g2m_node % 256, g2m_node // 256], axis=2).reshape(grid, 3 * tops).T.astype(bf16)
    notes = jnp.pad(notes, ((0, EXTRA - 3 * tops), (0, width - grid)), constant_values=-1)
    payload = jnp.concatenate([grid_feats, notes], axis=0)
    order = sorted(range(shards), key=lambda step: min(step, shards - step))
    payloads = [payload] + [shifted(payload, "mesh", step) for step in order[1:]]

    place = sender_slots - nodes
    away = lax.rem(shard - place // depth + shards, shards)
    slots = jnp.where(sender_slots < nodes, sender_slots, nodes + (away - 1) * depth + place % depth)
    both = jnp.stack([slots, receivers])
    both = in_order([both] + [shifted(both, "rep", step) for step in range(1, halves)], "rep")
    both = in_order([both] + [shifted(both, "feat", step) for step in range(1, feats)], "feat")
    both = both.reshape(feats * halves, 2, edges)
    lists = jnp.roll(halo_index[0], -shard, axis=0)[1:].reshape(1, -1)
    here, there, halo_here, halo_there, list_here, list_there = call(
        place_kernel,
        [
            ((all_edges, 2 * nodes), bf16),
            ((2 * nodes, all_edges), bf16),
            ((all_edges, wide), bf16),
            ((wide, all_edges), bf16),
            ((listed_rows, nodes), bf16),
            ((nodes, listed_rows), bf16),
        ],
    )(both[:, 0].reshape(1, -1), both[:, 1].reshape(1, -1), lists)

    meta = jnp.stack([lax.axis_index("rep"), shard]).astype(i32)
    node_f32, node_bf16 = ((nodes, width), f32), ((nodes, width), bf16)
    row_shape, half = ((grid, width), bf16), nodes // halves
    enc_picks, enc_slopes = [], []
    base, total = mesh_init, None
    groups = [payloads[:2]] + [payloads[at : at + 1] for at in range(2, shards)]
    for at, group in enumerate(groups):
        first, last = at == 0, at == len(groups) - 1
        count = len(group)
        outs = [((grid, nodes), bf16)] * count + [row_shape] * count
        outs += [node_bf16] if first else []
        outs += [((half, width), f32)] + [((half, width), bf16)] * (halves - 1) if last else [node_f32]
        got = list(
            call(functools.partial(encode_kernel, count, first, last, halves), outs, [node_f32] if last else [])(
                meta, base, w_enc_grid, w_enc_mesh if first else total, *group
            )
        )
        enc_picks += got[:count]
        enc_slopes += got[count : 2 * count]
        del got[: 2 * count]
        if first:
            base = got.pop(0)
        total = got[0]
    part = got[0]
    for step in range(1, halves):
        part = part + shifted(got[step], "rep", step).astype(f32)
    part = part.astype(bf16)
    pieces = [part] + [shifted(part, "feat", step) for step in range(1, feats)]
    if feats > 2:
        pieces = list(in_order(pieces, "feat"))
    part = sum(piece.astype(f32) for piece in pieces).astype(bf16)
    parts = [part] + [shifted(part, "rep", -step) for step in range(1, halves)]

    listed = [((depth, width), bf16)] * shifts
    hidden, enc_sum, sent, *outgoing = call(
        functools.partial(start_kernel, halves, shifts), [node_bf16, node_f32, node_bf16] + listed, [node_bf16]
    )(meta, *parts, mesh_init, w_enc_out, enc_gain, w_send, list_here)

    edge_f32, edge_bf16 = ((all_edges, width), f32), ((all_edges, width), bf16)
    halo, back_halo = ((wide, width), bf16), ((listed_rows, width), bf16)

    def local(layer):
        (pre,) = call(functools.partial(local_kernel, layer), [edge_f32], [((2 * nodes, width), bf16)])(
            hidden, sent, here, w_recv
        )
        return pre

    records = []
    for layer in range(LAYERS - 1):
        halos = [shifted(block, "mesh", step + 1) for step, block in enumerate(outgoing)]
        hidden, agg, slope, sent, *outgoing = call(
            functools.partial(layer_kernel, layer, shifts),
            [node_bf16, node_f32, edge_bf16, node_bf16] + listed,
            [halo, edge_bf16],
        )(hidden, local(layer), *halos, halo_here, there, w_out, layer_gain, w_send, list_here)
        records.append((agg, slope))
    last = LAYERS - 1
    halos = [shifted(block, "mesh", step + 1) for step, block in enumerate(outgoing)]
    final_mesh, grad_pre, *outgoing = call(
        functools.partial(turn_kernel, last, shifts), [node_bf16, edge_bf16] + listed, [edge_bf16, halo]
    )(hidden, local(last), *halos, halo_here, there, w_out, layer_gain, here, halo_there, out_cot)
    upstream = out_cot
    for layer in reversed(range(LAYERS)):
        returned = [shifted(block, "mesh", -step - 1) for step, block in enumerate(outgoing)]
        (rest,) = call(functools.partial(rest_kernel, layer), [node_f32])(upstream, grad_pre, there, w_send, w_recv)
        if layer:
            agg, slope = records[layer - 1]
            upstream, grad_pre, *outgoing = call(
                functools.partial(back_kernel, layer - 1, shifts), [node_f32, edge_bf16] + listed, [back_halo]
            )(rest, *returned, list_there, w_send, agg, slope, layer_gain, w_out, here, halo_there)
    blocks = call(functools.partial(finish_kernel, shards, shifts), [row_shape] * shards, [back_halo])(
        rest, *returned, list_there, w_send, enc_sum, enc_gain, w_enc_out, *enc_picks, *enc_slopes
    )
    blocks = [blocks[0]] + [shifted(block, "mesh", -step) for step, block in zip(order[1:], blocks[1:])]
    (grid_grad,) = call(functools.partial(grid_kernel, shards), [((grid, width), f32)])(*blocks, w_enc_grid)
    return (final_mesh, grid_grad)


def solution(mesh):
    return jax.shard_map(
        on_device,
        mesh=mesh,
        in_specs=(
            P(("groups", "mesh", "feat", "rep"), None),
            P(("groups", "mesh", "feat", "rep"), None),
            P(("groups", "mesh", "feat", "rep"), None),
            P(("groups", "mesh"), None),
            P(("groups", "mesh", "feat", "rep")),
            P(("groups", "mesh", "feat", "rep")),
            P(("groups", "mesh"), None, None),
            P(),
            P(),
            P(),
            P(),
            P(),
            P(),
            P(),
            P(),
            P(("groups", "mesh"), None),
        ),
        out_specs=(P(("groups", "mesh"), None), P(("groups", "mesh", "feat", "rep"), None)),
        check_vma=False,
    )
```

```python
import functools

import jax
import jax.numpy as jnp
from jax import lax
from jax.experimental import pallas as pl
from jax.experimental.pallas import tpu as pltpu
from jax.sharding import PartitionSpec as P

LAYERS = 3
LANES = 128
BLOCK = 512
EXTRA = 16
eps = 1e-05

f32 = jnp.float32
bf16 = jnp.bfloat16
i32 = jnp.int32


def norm_scale(totals):
    return lax.rsqrt(jnp.mean(totals * totals, axis=-1, keepdims=True) + eps)


def norm_back(totals, gain_row, upstream):
    scaled = norm_scale(totals)
    normed = totals * scaled
    slope = upstream * gain_row
    return scaled * (slope - normed * jnp.mean(slope * normed, axis=-1, keepdims=True))


def dot(left, right):
    return jnp.dot(left, right, preferred_element_type=f32)


def dot_back(left, right):
    return lax.dot_general(left, right, (((1,), (1,)), ((), ())), preferred_element_type=f32)


def gated(pre):
    sigma = 0.5 * jnp.tanh(0.5 * pre) + 0.5
    act = pre * sigma
    return act, sigma + act * (1.0 - sigma)


def as_mask(hit):
    return jnp.where(hit, 1.0, 0.0).astype(bf16)


def pick_columns(index, first, height):
    place = lax.broadcasted_iota(i32, (height, index.shape[1]), 0) + first
    return as_mask(place == index)


def upright(index):
    count = index.shape[1]
    if count < LANES:
        index = jnp.concatenate([index, jnp.full((1, LANES - count), -1, i32)], axis=1)
    return jnp.broadcast_to(index, (LANES, LANES)).T[:count]


def pick_rows(column, first, width):
    lane = lax.broadcasted_iota(i32, column.shape, 1) + first
    return jnp.concatenate([as_mask(column == lane + at) for at in range(0, width, LANES)], axis=1)


def call(body, outs, scratch=()):
    def run(*args):
        def where(array):
            return pl.BlockSpec(memory_space=pltpu.SMEM if array.dtype == i32 and array.ndim == 1 else pltpu.VMEM)

        held = [(shape, dtype) for shape, dtype in scratch]
        own = sum(jnp.dtype(dtype).itemsize * shape[0] * shape[1] for shape, dtype in held) + (10 << 20)
        room = own + sum(array.dtype.itemsize * array.size for array in args)
        room += sum(jnp.dtype(dtype).itemsize * shape[0] * shape[1] for shape, dtype in outs)
        limit = own if room < 40 << 20 else min(room, 60 << 20)
        return pl.pallas_call(
            body,
            out_shape=tuple(jax.ShapeDtypeStruct(shape, dtype) for shape, dtype in outs),
            in_specs=[where(array) for array in args],
            out_specs=tuple(pl.BlockSpec(memory_space=pltpu.VMEM) for _ in outs),
            scratch_shapes=[pltpu.VMEM(shape, dtype) for shape, dtype in held],
            compiler_params=pltpu.CompilerParams(vmem_limit_bytes=limit),
        )(*args)

    return run


def place_kernel(slots, receivers, order, here, there, halo_here, halo_there, list_here, list_there):
    nodes = here.shape[1] // 2
    wide = halo_here.shape[1]

    def body(at):
        block = pl.ds(pl.multiple_of(at * LANES, LANES), LANES)
        slot, receiver = slots[:, block], receivers[:, block]
        slot_column, receiver_column = upright(slot), upright(receiver)
        here[block, 0:nodes] = pick_rows(slot_column, 0, nodes)
        here[block, nodes:] = pick_rows(receiver_column, 0, nodes)
        halo_here[block, :] = pick_rows(slot_column, nodes, wide)
        there[0:nodes, block] = pick_columns(slot, 0, nodes)
        there[nodes:, block] = pick_columns(receiver, 0, nodes)
        halo_there[:, block] = pick_columns(slot, nodes, wide)

    pl.loop(0, slots.shape[1] // LANES)(body)
    count = order.shape[1]
    for at in range(0, count, LANES):
        end = min(at + LANES, count)
        list_here[at:end, :] = pick_rows(upright(order[:, at:end]), 0, nodes)
    list_there[...] = pick_columns(order[...], 0, nodes)


def note_kernel(rows, shards, nodes, payload):
    grid = rows.shape[0]
    payload[0:grid, :] = rows[...]
    row = lax.broadcasted_iota(i32, (EXTRA, grid), 0)
    notes = jnp.full((EXTRA, grid), -1, i32)
    for top in range(shards.shape[0]):
        node = nodes[top : top + 1, :]
        for at, value in enumerate((shards[top : top + 1, :], node & 255, node >> 8)):
            notes = jnp.where(row == 3 * top + at, value, notes)
    payload[grid:, 0:grid] = notes.astype(f32).astype(bf16)
    if grid < payload.shape[1]:
        payload[grid:, grid:] = jnp.zeros((EXTRA, payload.shape[1] - grid), bf16)


def encode_kernel(steps, first, last, halves, *refs):
    refs = list(refs)
    meta, base, w_grid = refs[:3]
    del refs[:3]
    if first:
        w_mesh, _ = refs.pop(0), refs.pop(0)
        projected = dot(base[...], w_mesh[...]).astype(bf16)
    else:
        total_in = refs.pop(0)
        projected = base[...]
    payloads = refs[:steps]
    del refs[:steps]
    picks, slopes = refs[:steps], refs[steps : 2 * steps]
    del refs[: 2 * steps]
    total = None if first else total_in[...]
    nodes = projected.shape[0]
    for payload, pick, slope_out in zip(payloads, picks, slopes):
        grid = pick.shape[0]
        notes = payload[grid:, 0:grid].astype(f32)
        target = jnp.full((1, grid), -1.0, f32)
        for at in range(0, notes.shape[0] // 3 * 3, 3):
            named = notes[at : at + 1] == meta[1].astype(f32)
            target = jnp.where(named, notes[at + 1 : at + 2] + 256.0 * notes[at + 2 : at + 3], target)
        target = target.astype(i32)
        column = jnp.concatenate([upright(target[:, at : at + LANES]) for at in range(0, grid, LANES)], axis=0)
        picked = pick_rows(column, 0, nodes)
        pick[...] = picked
        pre = dot(payload[0:grid, :], w_grid[...]) + dot(picked, projected)
        act, slope = gated(pre)
        slope_out[...] = slope.astype(bf16)
        added = dot(pick_columns(target, 0, nodes), act.astype(bf16))
        total = added if total is None else total + added
    if first:
        refs.pop(0)[...] = projected
    if not last:
        refs[0][...] = total
        return
    keep, sends, whole = refs[0], refs[1:halves], refs[-1]
    whole[...] = total
    part = nodes // halves

    def half(shift):
        at = lax.rem(meta[0] + shift, halves)
        return whole[pl.ds(pl.multiple_of(at * part, part), part), :]

    keep[...] = half(0)
    for shift in range(1, halves):
        sends[shift - 1][...] = half(shift).astype(bf16)


def list_rows(list_here, projected, outs):
    listed = dot(list_here[...], projected).astype(bf16)
    at = 0
    for out in outs:
        out[...] = listed[at : at + out.shape[0]]
        at += out.shape[0]


def start_kernel(halves, shifts, *refs):
    meta = refs[0]
    parts = refs[1 : 1 + halves]
    mesh_init, w_enc_out, gain, w_send, list_here = refs[1 + halves : 6 + halves]
    hidden_out, enc_sum_out, sent = refs[6 + halves : 9 + halves]
    outs = refs[9 + halves : 9 + halves + shifts]
    whole = refs[-1]
    part = parts[0].shape[0]
    for shift in range(halves):
        at = lax.rem(meta[0] + shift, halves)
        whole[pl.ds(pl.multiple_of(at * part, part), part), :] = parts[shift][...]
    enc_sum = dot(whole[...], w_enc_out[...])
    enc_sum_out[...] = enc_sum
    hidden = (mesh_init[...].astype(f32) + enc_sum * norm_scale(enc_sum) * gain[...]).astype(bf16)
    hidden_out[...] = hidden
    projected = dot(hidden, w_send[0]).astype(bf16)
    sent[...] = projected
    list_rows(list_here, projected, outs)


def local_kernel(layer, hidden, sent, here, w_recv, pre, table):
    nodes = hidden.shape[0]
    table[0:nodes, :] = sent[...]
    table[nodes:, :] = dot(hidden[...], w_recv[layer]).astype(bf16)
    for at in range(0, pre.shape[0], BLOCK):
        pre[at : at + BLOCK, :] = dot(here[at : at + BLOCK, :], table[...])


def stack_halo(halos, halo):
    at = 0
    for block in halos:
        halo[at : at + block.shape[0], :] = block[...]
        at += block.shape[0]
    if at < halo.shape[0]:
        halo[at:, :] = jnp.zeros((halo.shape[0] - at, halo.shape[1]), bf16)


def node_sum(pre, halos, halo_here, there, slope_out, halo, act_out):
    nodes = there.shape[0] // 2
    stack_halo(halos, halo)
    for at in range(0, pre.shape[0], BLOCK):
        block = slice(at, at + BLOCK)
        act, slope = gated(pre[block, :] + dot(halo_here[block, :], halo[...]))
        slope_out[block, :] = slope.astype(bf16)
        act_out[block, :] = act.astype(bf16)
    return dot(there[nodes:, :], act_out[...])


def layer_kernel(layer, shifts, *refs):
    hidden, pre = refs[:2]
    halos = refs[2 : 2 + shifts]
    halo_here, there, w_out, gain, w_send, list_here = refs[2 + shifts : 8 + shifts]
    hidden_out, agg_out, slope_out, sent_out = refs[8 + shifts : 12 + shifts]
    outs = refs[12 + shifts : 12 + 2 * shifts]
    halo, act = refs[-2:]
    total = node_sum(pre, halos, halo_here, there, slope_out, halo, act)
    agg = dot(total.astype(bf16), w_out[layer])
    agg_out[...] = agg
    fresh = (hidden[...].astype(f32) + agg * norm_scale(agg) * gain[layer : layer + 1, :]).astype(bf16)
    hidden_out[...] = fresh
    projected = dot(fresh, w_send[layer + 1]).astype(bf16)
    sent_out[...] = projected
    list_rows(list_here, projected, outs)


def edge_grads(grad_agg, w_out, here, halo_there, slope, grad_pre, outs):
    nodes = grad_agg.shape[0]
    spread = dot_back(grad_agg.astype(bf16), w_out).astype(bf16)
    for at in range(0, slope.shape[0], BLOCK):
        block = slice(at, at + BLOCK)
        grad_act = dot(here[block, nodes:], spread)
        grad_pre[block, :] = (grad_act * slope[block, :].astype(f32)).astype(bf16)
    given = dot(halo_there[...], grad_pre[...]).astype(bf16)
    at = 0
    for out in outs:
        out[...] = given[at : at + out.shape[0]]
        at += out.shape[0]


def turn_kernel(layer, shifts, *refs):
    hidden, pre = refs[:2]
    halos = refs[2 : 2 + shifts]
    halo_here, there, w_out, gain, here, halo_there, cot = refs[2 + shifts : 9 + shifts]
    hidden_out, grad_pre = refs[9 + shifts : 11 + shifts]
    outs = refs[11 + shifts : 11 + 2 * shifts]
    slope, halo = refs[-2:]
    total = node_sum(pre, halos, halo_here, there, slope, halo, grad_pre)
    agg = dot(total.astype(bf16), w_out[layer])
    gain_row = gain[layer : layer + 1, :]
    hidden_out[...] = (hidden[...].astype(f32) + agg * norm_scale(agg) * gain_row).astype(bf16)
    edge_grads(norm_back(agg, gain_row, cot[...].astype(f32)), w_out[layer], here, halo_there, slope, grad_pre, outs)


def rest_kernel(layer, upstream, grad_pre, there, w_send, w_recv, rest):
    nodes = upstream.shape[0]
    sums = dot(there[...], grad_pre[...]).astype(bf16)
    rest[...] = (
        upstream[...].astype(f32)
        + dot_back(sums[0:nodes], w_send[layer])
        + dot_back(sums[nodes:], w_recv[layer])
    )


def arrived(rest, returned, list_there, w_send, halo):
    at = 0
    for block in returned:
        halo[at : at + block.shape[0], :] = block[...]
        at += block.shape[0]
    projected = dot_back(halo[...], w_send).astype(bf16)
    return rest[...] + dot(list_there[...], projected)


def back_kernel(layer, shifts, *refs):
    rest = refs[0]
    returned = refs[1 : 1 + shifts]
    list_there, w_send, agg, slope, gain, w_out, here, halo_there = refs[1 + shifts : 9 + shifts]
    upstream_out, grad_pre = refs[9 + shifts : 11 + shifts]
    outs = refs[11 + shifts : 11 + 2 * shifts]
    halo = refs[-1]
    upstream = arrived(rest, returned, list_there, w_send[layer + 1], halo)
    upstream_out[...] = upstream
    grad_agg = norm_back(agg[...], gain[layer : layer + 1, :], upstream)
    edge_grads(grad_agg, w_out[layer], here, halo_there, slope, grad_pre, outs)


def finish_kernel(count, shifts, *refs):
    rest = refs[0]
    returned = refs[1 : 1 + shifts]
    list_there, w_send, enc_sum, gain, w_enc_out = refs[1 + shifts : 6 + shifts]
    picks, slopes = refs[6 + shifts : 6 + shifts + count], refs[6 + shifts + count : 6 + shifts + 2 * count]
    outs = refs[6 + shifts + 2 * count : -1]
    halo = refs[-1]
    upstream = arrived(rest, returned, list_there, w_send[0], halo)
    spread = dot_back(norm_back(enc_sum[...], gain[...], upstream).astype(bf16), w_enc_out[...]).astype(bf16)
    for pick, slope, out in zip(picks, slopes, outs):
        out[...] = (dot(pick[...], spread) * slope[...].astype(f32)).astype(bf16)


def grid_kernel(count, *refs):
    blocks, w_grid, out = refs[:count], refs[count], refs[count + 1]
    total = blocks[0][...].astype(f32)
    for block in blocks[1:]:
        total = total + block[...].astype(f32)
    out[...] = dot_back(total.astype(bf16), w_grid[...])


def shifted(value, axis, by):
    size = lax.axis_size(axis)
    return lax.ppermute(value, axis, [(at, (at + by) % size) for at in range(size)])


def swapped(value, by):
    return lax.ppermute(value, "mesh", [(at, at ^ by) for at in range(lax.axis_size("mesh"))])


def in_order(pieces, axis):
    return jnp.roll(jnp.stack(pieces)[::-1], lax.axis_index(axis) + 1, axis=0)


def on_device(
    grid_feats,
    g2m_shard,
    g2m_node,
    mesh_init,
    sender_slots,
    receivers,
    halo_index,
    w_enc_grid,
    w_enc_mesh,
    w_enc_out,
    enc_gain,
    w_send,
    w_recv,
    w_out,
    layer_gain,
    out_cot,
):
    shards = lax.axis_size("mesh")
    shard = lax.axis_index("mesh")
    halves = lax.axis_size("rep")
    feats = lax.axis_size("feat")
    nodes, width = mesh_init.shape
    grid, tops = g2m_shard.shape
    edges = sender_slots.shape[0]
    depth = halo_index.shape[2]
    shifts = shards - 1
    listed_rows = shifts * depth
    wide = -(-listed_rows // LANES) * LANES
    all_edges = edges * halves * feats
    enc_gain = enc_gain[None, :]

    (payload,) = call(note_kernel, [((grid + EXTRA, width), bf16)])(grid_feats, g2m_shard.T, g2m_node.T)
    if shards == 4:
        across = swapped(payload, 2)
        payloads = [payload, swapped(payload, 1), across, swapped(across, 1)]
    else:
        payloads = [payload] + [shifted(payload, "mesh", step) for step in range(1, shards)]

    place = sender_slots - nodes
    away = lax.rem(shard - place // depth + shards, shards)
    slots = jnp.where(sender_slots < nodes, sender_slots, nodes + (away - 1) * depth + place % depth)
    both = jnp.stack([slots, receivers])
    both = in_order([both] + [shifted(both, "rep", step) for step in range(1, halves)], "rep")
    both = in_order([both] + [shifted(both, "feat", step) for step in range(1, feats)], "feat")
    both = both.reshape(feats * halves, 2, edges)
    lists = jnp.roll(halo_index[0], -shard, axis=0)[1:].reshape(1, -1)
    here, there, halo_here, halo_there, list_here, list_there = call(
        place_kernel,
        [
            ((all_edges, 2 * nodes), bf16),
            ((2 * nodes, all_edges), bf16),
            ((all_edges, wide), bf16),
            ((wide, all_edges), bf16),
            ((listed_rows, nodes), bf16),
            ((nodes, listed_rows), bf16),
        ],
    )(both[:, 0].reshape(1, -1), both[:, 1].reshape(1, -1), lists)

    meta = jnp.stack([lax.axis_index("rep"), shard]).astype(i32)
    node_f32, node_bf16 = ((nodes, width), f32), ((nodes, width), bf16)
    row_shape, half = ((grid, width), bf16), nodes // halves
    enc_picks, enc_slopes = [], []
    base, total = mesh_init, None
    groups = [payloads[:2]] + [payloads[at : at + 1] for at in range(2, shards)]
    for at, group in enumerate(groups):
        first, last = at == 0, at == len(groups) - 1
        count = len(group)
        outs = [((grid, nodes), bf16)] * count + [row_shape] * count
        outs += [node_bf16] if first else []
        outs += [((half, width), f32)] + [((half, width), bf16)] * (halves - 1) if last else [node_f32]
        got = list(
            call(functools.partial(encode_kernel, count, first, last, halves), outs, [node_f32] if last else [])(
                meta, base, w_enc_grid, *((w_enc_mesh, list_here) if first else (total,)), *group
            )
        )
        enc_picks += got[:count]
        enc_slopes += got[count : 2 * count]
        del got[: 2 * count]
        if first:
            base = got.pop(0)
        total = got[0]
    part = got[0]
    for step in range(1, halves):
        part = part + shifted(got[step], "rep", step).astype(f32)
    part = part.astype(bf16)
    pieces = [part] + [shifted(part, "feat", step) for step in range(1, feats)]
    if feats > 2:
        pieces = list(in_order(pieces, "feat"))
    part = sum(piece.astype(f32) for piece in pieces).astype(bf16)
    parts = [part] + [shifted(part, "rep", -step) for step in range(1, halves)]

    listed = [((depth, width), bf16)] * shifts
    hidden, enc_sum, sent, *outgoing = call(
        functools.partial(start_kernel, halves, shifts), [node_bf16, node_f32, node_bf16] + listed, [node_bf16]
    )(meta, *parts, mesh_init, w_enc_out, enc_gain, w_send, list_here)

    edge_f32, edge_bf16 = ((all_edges, width), f32), ((all_edges, width), bf16)
    halo, back_halo = ((wide, width), bf16), ((listed_rows, width), bf16)

    def local(layer):
        (pre,) = call(functools.partial(local_kernel, layer), [edge_f32], [((2 * nodes, width), bf16)])(
            hidden, sent, here, w_recv
        )
        return pre

    records = []
    for layer in range(LAYERS - 1):
        halos = [shifted(block, "mesh", step + 1) for step, block in enumerate(outgoing)]
        hidden, agg, slope, sent, *outgoing = call(
            functools.partial(layer_kernel, layer, shifts),
            [node_bf16, node_f32, edge_bf16, node_bf16] + listed,
            [halo, edge_bf16],
        )(hidden, local(layer), *halos, halo_here, there, w_out, layer_gain, w_send, list_here)
        records.append((agg, slope))
    last = LAYERS - 1
    halos = [shifted(block, "mesh", step + 1) for step, block in enumerate(outgoing)]
    final_mesh, grad_pre, *outgoing = call(
        functools.partial(turn_kernel, last, shifts), [node_bf16, edge_bf16] + listed, [edge_bf16, halo]
    )(hidden, local(last), *halos, halo_here, there, w_out, layer_gain, here, halo_there, out_cot)
    upstream = out_cot
    for layer in reversed(range(LAYERS)):
        returned = [shifted(block, "mesh", -step - 1) for step, block in enumerate(outgoing)]
        (rest,) = call(functools.partial(rest_kernel, layer), [node_f32])(upstream, grad_pre, there, w_send, w_recv)
        if layer:
            agg, slope = records[layer - 1]
            upstream, grad_pre, *outgoing = call(
                functools.partial(back_kernel, layer - 1, shifts), [node_f32, edge_bf16] + listed, [back_halo]
            )(rest, *returned, list_there, w_send, agg, slope, layer_gain, w_out, here, halo_there)
    blocks = call(functools.partial(finish_kernel, shards, shifts), [row_shape] * shards, [back_halo])(
        rest, *returned, list_there, w_send, enc_sum, enc_gain, w_enc_out, *enc_picks, *enc_slopes
    )
    if shards == 4:
        passed = swapped(blocks[3], 1)
        near = swapped(blocks[1], 1)
        blocks = [blocks[0], near, swapped((blocks[2].astype(f32) + passed.astype(f32)).astype(bf16), 2)]
    else:
        blocks = [blocks[0]] + [shifted(block, "mesh", -step) for step, block in enumerate(blocks) if step]
    (grid_grad,) = call(functools.partial(grid_kernel, len(blocks)), [((grid, width), f32)])(*blocks, w_enc_grid)
    return (final_mesh, grid_grad)


def solution(mesh):
    return jax.shard_map(
        on_device,
        mesh=mesh,
        in_specs=(
            P(("groups", "mesh", "feat", "rep"), None),
            P(("groups", "mesh", "feat", "rep"), None),
            P(("groups", "mesh", "feat", "rep"), None),
            P(("groups", "mesh"), None),
            P(("groups", "mesh", "feat", "rep")),
            P(("groups", "mesh", "feat", "rep")),
            P(("groups", "mesh"), None, None),
            P(),
            P(),
            P(),
            P(),
            P(),
            P(),
            P(),
            P(),
            P(("groups", "mesh"), None),
        ),
        out_specs=(P(("groups", "mesh"), None), P(("groups", "mesh", "feat", "rep"), None)),
        check_vma=False,
    )
```

```python
import functools
import math

import jax
import jax.numpy as jnp
from jax import lax
from jax.experimental import pallas as pl
from jax.experimental.pallas import tpu as pltpu
from jax.sharding import PartitionSpec as P

LAYERS = 3
LANES = 128
BLOCK = 512
EXTRA = 16
eps = 1e-05

f32 = jnp.float32
bf16 = jnp.bfloat16
i32 = jnp.int32


def norm_scale(totals):
    return lax.rsqrt(jnp.mean(totals * totals, axis=-1, keepdims=True) + eps)


def norm_back(totals, gain_row, upstream):
    scaled = norm_scale(totals)
    normed = totals * scaled
    slope = upstream * gain_row
    return scaled * (slope - normed * jnp.mean(slope * normed, axis=-1, keepdims=True))


def dot(left, right):
    return jnp.dot(left, right, preferred_element_type=f32)


def dot_back(left, right):
    return lax.dot_general(left, right, (((1,), (1,)), ((), ())), preferred_element_type=f32)


def gated(pre):
    sigma = 0.5 * jnp.tanh(0.5 * pre) + 0.5
    act = pre * sigma
    return act, sigma + act * (1.0 - sigma)


def as_mask(hit):
    return jnp.where(hit, 1.0, 0.0).astype(bf16)


def pick_columns(index, first, height):
    place = lax.broadcasted_iota(i32, (height, index.shape[1]), 0) + first
    return as_mask(place == index)


def upright(index):
    count = index.shape[1]
    if count < LANES:
        index = jnp.concatenate([index, jnp.full((1, LANES - count), -1, i32)], axis=1)
    return jnp.broadcast_to(index, (LANES, LANES)).T[:count]


def pick_rows(column, first, width):
    lane = lax.broadcasted_iota(i32, column.shape, 1) + first
    return jnp.concatenate([as_mask(column == lane + at) for at in range(0, width, LANES)], axis=1)


def call(body, outs, scratch=(), products=(), copied=False):
    def run(*args):
        def where(array):
            if copied:
                return pl.BlockSpec(memory_space=pltpu.HBM)
            return pl.BlockSpec(memory_space=pltpu.SMEM if array.dtype == i32 and array.ndim == 1 else pltpu.VMEM)

        def size(shape, dtype):
            return jnp.dtype(dtype).itemsize * math.prod(shape)

        own = sum(size(*held) for held in scratch) + (10 << 20)
        moved = sum(array.dtype.itemsize * array.size for array in args) + sum(size(*out) for out in outs)
        limit = own if own + moved < 40 << 20 else min(own + moved, 60 << 20)
        semaphores = [pltpu.SemaphoreType.DMA((len(args),))] if copied else []
        return pl.pallas_call(
            body,
            out_shape=tuple(jax.ShapeDtypeStruct(shape, dtype) for shape, dtype in outs),
            in_specs=[where(array) for array in args],
            out_specs=tuple(pl.BlockSpec(memory_space=pltpu.VMEM) for _ in outs),
            scratch_shapes=[pltpu.VMEM(shape, dtype) for shape, dtype in scratch] + semaphores,
            compiler_params=pltpu.CompilerParams(vmem_limit_bytes=limit),
            cost_estimate=pl.CostEstimate(
                flops=2 * sum(math.prod(product) for product in products), bytes_accessed=moved, transcendentals=0
            ),
        )(*args)

    return run


def place_kernel(slots, receivers, order, here, there, halo_here, halo_there, list_here, list_there):
    nodes = here.shape[1] // 2
    wide = halo_here.shape[1]

    def body(at):
        block = pl.ds(pl.multiple_of(at * LANES, LANES), LANES)
        slot, receiver = slots[:, block], receivers[:, block]
        slot_column, receiver_column = upright(slot), upright(receiver)
        here[block, 0:nodes] = pick_rows(slot_column, 0, nodes)
        here[block, nodes:] = pick_rows(receiver_column, 0, nodes)
        halo_here[block, :] = pick_rows(slot_column, nodes, wide)
        there[0:nodes, block] = pick_columns(slot, 0, nodes)
        there[nodes:, block] = pick_columns(receiver, 0, nodes)
        halo_there[:, block] = pick_columns(slot, nodes, wide)

    pl.loop(0, slots.shape[1] // LANES)(body)
    count = order.shape[1]
    for at in range(0, count, LANES):
        end = min(at + LANES, count)
        list_here[at:end, :] = pick_rows(upright(order[:, at:end]), 0, nodes)
    list_there[...] = pick_columns(order[...], 0, nodes)


def note_kernel(rows, shards, nodes, payload, shard_rows, node_rows, arrived):
    grid = rows.shape[0]
    copies = [
        pltpu.make_async_copy(rows, payload.at[0:grid], arrived.at[0]),
        pltpu.make_async_copy(shards, shard_rows, arrived.at[1]),
        pltpu.make_async_copy(nodes, node_rows, arrived.at[2]),
    ]
    for copy in copies:
        copy.start()
    copies[1].wait()
    copies[2].wait()
    row = lax.broadcasted_iota(i32, (EXTRA, grid), 0)
    notes = jnp.full((EXTRA, grid), -1, i32)
    for top in range(shards.shape[0]):
        node = node_rows[top : top + 1, :]
        for at, value in enumerate((shard_rows[top : top + 1, :], node & 255, node >> 8)):
            notes = jnp.where(row == 3 * top + at, value, notes)
    payload[grid:, 0:grid] = notes.astype(f32).astype(bf16)
    if grid < payload.shape[1]:
        payload[grid:, grid:] = jnp.zeros((EXTRA, payload.shape[1] - grid), bf16)
    copies[0].wait()


def encode_kernel(steps, first, last, halves, *refs):
    refs = list(refs)
    meta, base, w_grid = refs[:3]
    del refs[:3]
    if first:
        w_mesh, _ = refs.pop(0), refs.pop(0)
        projected = dot(base[...], w_mesh[...]).astype(bf16)
    else:
        total_in = refs.pop(0)
        projected = base[...]
    payloads = refs[:steps]
    del refs[:steps]
    picks, slopes = refs[:steps], refs[steps : 2 * steps]
    del refs[: 2 * steps]
    total = None if first else total_in[...]
    nodes = projected.shape[0]
    for payload, pick, slope_out in zip(payloads, picks, slopes):
        grid = pick.shape[0]
        notes = payload[grid:, 0:grid].astype(f32)
        target = jnp.full((1, grid), -1.0, f32)
        for at in range(0, notes.shape[0] // 3 * 3, 3):
            named = notes[at : at + 1] == meta[1].astype(f32)
            target = jnp.where(named, notes[at + 1 : at + 2] + 256.0 * notes[at + 2 : at + 3], target)
        target = target.astype(i32)
        column = jnp.concatenate([upright(target[:, at : at + LANES]) for at in range(0, grid, LANES)], axis=0)
        picked = pick_rows(column, 0, nodes)
        pick[...] = picked
        pre = dot(payload[0:grid, :], w_grid[...]) + dot(picked, projected)
        act, slope = gated(pre)
        slope_out[...] = slope.astype(bf16)
        added = dot(pick_columns(target, 0, nodes), act.astype(bf16))
        total = added if total is None else total + added
    if first:
        refs.pop(0)[...] = projected
    if not last:
        refs[0][...] = total
        return
    keep, sends, whole = refs[0], refs[1:halves], refs[-1]
    whole[...] = total
    part = nodes // halves

    def half(shift):
        at = lax.rem(meta[0] + shift, halves)
        return whole[pl.ds(pl.multiple_of(at * part, part), part), :]

    keep[...] = half(0)
    for shift in range(1, halves):
        sends[shift - 1][...] = half(shift).astype(bf16)


def list_rows(list_here, projected, outs):
    listed = dot(list_here[...], projected).astype(bf16)
    at = 0
    for out in outs:
        out[...] = listed[at : at + out.shape[0]]
        at += out.shape[0]


def start_kernel(halves, shifts, *refs):
    meta = refs[0]
    parts = refs[1 : 1 + halves]
    mesh_init, w_enc_out, gain, w_send, list_here = refs[1 + halves : 6 + halves]
    hidden_out, enc_sum_out, sent = refs[6 + halves : 9 + halves]
    outs = refs[9 + halves : 9 + halves + shifts]
    whole = refs[-1]
    part = parts[0].shape[0]
    for shift in range(halves):
        at = lax.rem(meta[0] + shift, halves)
        whole[pl.ds(pl.multiple_of(at * part, part), part), :] = parts[shift][...]
    enc_sum = dot(whole[...], w_enc_out[...])
    enc_sum_out[...] = enc_sum
    hidden = (mesh_init[...].astype(f32) + enc_sum * norm_scale(enc_sum) * gain[...]).astype(bf16)
    hidden_out[...] = hidden
    projected = dot(hidden, w_send[0]).astype(bf16)
    sent[...] = projected
    list_rows(list_here, projected, outs)


def local_kernel(layer, hidden, sent, here, w_recv, pre, table):
    nodes = hidden.shape[0]
    table[0:nodes, :] = sent[...]
    table[nodes:, :] = dot(hidden[...], w_recv[layer]).astype(bf16)
    for at in range(0, pre.shape[0], BLOCK):
        pre[at : at + BLOCK, :] = dot(here[at : at + BLOCK, :], table[...])


def stack_halo(halos, halo):
    at = 0
    for block in halos:
        halo[at : at + block.shape[0], :] = block[...]
        at += block.shape[0]
    if at < halo.shape[0]:
        halo[at:, :] = jnp.zeros((halo.shape[0] - at, halo.shape[1]), bf16)


def node_sum(pre, halos, halo_here, there, slope_out, halo):
    nodes = there.shape[0] // 2
    stack_halo(halos, halo)
    table = halo[...]
    total = None
    for at in range(0, pre.shape[0], BLOCK):
        block = slice(at, at + BLOCK)
        act, slope = gated(pre[block, :] + dot(halo_here[block, :], table))
        slope_out[block, :] = slope.astype(bf16)
        added = dot(there[nodes:, block], act.astype(bf16))
        total = added if total is None else total + added
    return total


def layer_kernel(layer, shifts, *refs):
    hidden, pre = refs[:2]
    halos = refs[2 : 2 + shifts]
    halo_here, there, w_out, gain, w_send, list_here = refs[2 + shifts : 8 + shifts]
    hidden_out, agg_out, slope_out, sent_out = refs[8 + shifts : 12 + shifts]
    outs = refs[12 + shifts : 12 + 2 * shifts]
    total = node_sum(pre, halos, halo_here, there, slope_out, refs[-1])
    agg = dot(total.astype(bf16), w_out[layer])
    agg_out[...] = agg
    fresh = (hidden[...].astype(f32) + agg * norm_scale(agg) * gain[layer : layer + 1, :]).astype(bf16)
    hidden_out[...] = fresh
    projected = dot(fresh, w_send[layer + 1]).astype(bf16)
    sent_out[...] = projected
    list_rows(list_here, projected, outs)


def edge_grads(grad_agg, w_out, here, halo_there, slope, grad_pre, outs):
    nodes = grad_agg.shape[0]
    spread = dot_back(grad_agg.astype(bf16), w_out).astype(bf16)
    given = None
    for at in range(0, slope.shape[0], BLOCK):
        block = slice(at, at + BLOCK)
        grad = (dot(here[block, nodes:], spread) * slope[block, :].astype(f32)).astype(bf16)
        grad_pre[block, :] = grad
        added = dot(halo_there[:, block], grad)
        given = added if given is None else given + added
    given = given.astype(bf16)
    at = 0
    for out in outs:
        out[...] = given[at : at + out.shape[0]]
        at += out.shape[0]


def turn_kernel(layer, shifts, *refs):
    hidden, pre = refs[:2]
    halos = refs[2 : 2 + shifts]
    halo_here, there, w_out, gain, here, halo_there, cot = refs[2 + shifts : 9 + shifts]
    hidden_out, grad_pre = refs[9 + shifts : 11 + shifts]
    outs = refs[11 + shifts : 11 + 2 * shifts]
    slope, halo = refs[-2:]
    total = node_sum(pre, halos, halo_here, there, slope, halo)
    agg = dot(total.astype(bf16), w_out[layer])
    gain_row = gain[layer : layer + 1, :]
    hidden_out[...] = (hidden[...].astype(f32) + agg * norm_scale(agg) * gain_row).astype(bf16)
    edge_grads(norm_back(agg, gain_row, cot[...].astype(f32)), w_out[layer], here, halo_there, slope, grad_pre, outs)


def rest_kernel(layer, upstream, grad_pre, there, w_send, w_recv, rest):
    nodes = upstream.shape[0]
    sums = dot(there[...], grad_pre[...]).astype(bf16)
    rest[...] = (
        upstream[...].astype(f32)
        + dot_back(sums[0:nodes], w_send[layer])
        + dot_back(sums[nodes:], w_recv[layer])
    )


def arrived(rest, returned, list_there, w_send, halo):
    at = 0
    for block in returned:
        halo[at : at + block.shape[0], :] = block[...]
        at += block.shape[0]
    projected = dot_back(halo[...], w_send).astype(bf16)
    return rest[...] + dot(list_there[...], projected)


def back_kernel(layer, shifts, *refs):
    rest = refs[0]
    returned = refs[1 : 1 + shifts]
    list_there, w_send, agg, slope, gain, w_out, here, halo_there = refs[1 + shifts : 9 + shifts]
    upstream_out, grad_pre = refs[9 + shifts : 11 + shifts]
    outs = refs[11 + shifts : 11 + 2 * shifts]
    halo = refs[-1]
    upstream = arrived(rest, returned, list_there, w_send[layer + 1], halo)
    upstream_out[...] = upstream
    grad_agg = norm_back(agg[...], gain[layer : layer + 1, :], upstream)
    edge_grads(grad_agg, w_out[layer], here, halo_there, slope, grad_pre, outs)


def pair_grads(spread, pick, slope):
    return (dot(pick, spread) * slope.astype(f32)).astype(bf16)


def finish_kernel(shifts, *refs):
    rest = refs[0]
    returned = refs[1 : 1 + shifts]
    list_there, w_send, enc_sum, gain, w_enc_out, pick, slope = refs[1 + shifts : 8 + shifts]
    spread_out, outs, halo = refs[8 + shifts], refs[9 + shifts : -1], refs[-1]
    upstream = arrived(rest, returned, list_there, w_send[0], halo)
    spread = dot_back(norm_back(enc_sum[...], gain[...], upstream).astype(bf16), w_enc_out[...]).astype(bf16)
    spread_out[...] = spread
    at = 0
    for out in outs:
        piece = slice(at, at + out.shape[0])
        out[...] = pair_grads(spread, pick[piece, :], slope[piece, :])
        at += out.shape[0]


def others_kernel(count, *refs):
    spread = refs[0][...]
    picks, slopes, outs = refs[1 : 1 + count], refs[1 + count : 1 + 2 * count], refs[1 + 2 * count :]
    for pick, slope, out in zip(picks, slopes, outs):
        out[...] = pair_grads(spread, pick[...], slope[...])


def relay_kernel(first, count, own, passed, held, *refs):
    rows = passed.shape[0]
    refs[0][...] = (own[first : first + rows, :].astype(f32) + passed[...].astype(f32)).astype(bf16)
    if count > 1:
        refs[1][...] = held[...]


def grid_kernel(whole, *refs):
    blocks, pieces, w_grid, out = refs[:whole], refs[whole:-2], refs[-2], refs[-1]
    step = out.shape[0] // max(len(pieces), 1)
    for at in range(0, out.shape[0], step):
        total = pieces[at // step][...].astype(f32) if pieces else 0.0
        for block in blocks:
            total = total + block[at : at + step, :].astype(f32)
        out[at : at + step, :] = dot_back(total.astype(bf16), w_grid[...])


def shifted(value, axis, by):
    size = lax.axis_size(axis)
    return lax.ppermute(value, axis, [(at, (at + by) % size) for at in range(size)])


def partner(at, step, size):
    return at ^ step if size & (size - 1) == 0 else (at + step) % size


def sent_to(value, step):
    size = lax.axis_size("mesh")
    return lax.ppermute(value, "mesh", [(at, partner(at, step, size)) for at in range(size)])


def sent_back(value, step):
    size = lax.axis_size("mesh")
    return lax.ppermute(value, "mesh", [(partner(at, step, size), at) for at in range(size)])


def in_order(pieces, axis):
    return jnp.roll(jnp.stack(pieces)[::-1], lax.axis_index(axis) + 1, axis=0)


def on_device(
    grid_feats,
    g2m_shard,
    g2m_node,
    mesh_init,
    sender_slots,
    receivers,
    halo_index,
    w_enc_grid,
    w_enc_mesh,
    w_enc_out,
    enc_gain,
    w_send,
    w_recv,
    w_out,
    layer_gain,
    out_cot,
):
    shards = lax.axis_size("mesh")
    shard = lax.axis_index("mesh")
    halves = lax.axis_size("rep")
    feats = lax.axis_size("feat")
    nodes, width = mesh_init.shape
    grid, tops = g2m_shard.shape
    edges = sender_slots.shape[0]
    depth = halo_index.shape[2]
    shifts = shards - 1
    listed_rows = shifts * depth
    wide = -(-listed_rows // LANES) * LANES
    all_edges = edges * halves * feats
    enc_gain = enc_gain[None, :]

    (payload,) = call(
        note_kernel, [((grid + EXTRA, width), bf16)], [((tops, grid), i32), ((tops, grid), i32)], copied=True
    )(*(pltpu.with_memory_space_constraint(array, pltpu.HBM) for array in (grid_feats, g2m_shard.T, g2m_node.T)))
    if shards == 4:
        across = sent_to(payload, 2)
        payloads = [payload, sent_to(payload, 1), across]
    else:
        payloads = [payload] + [sent_to(payload, step) for step in range(1, shards)]

    place = sender_slots - nodes
    away = partner(shard, place // depth, shards)
    if shards & (shards - 1):
        away = lax.rem(shard - place // depth + shards, shards)
    slots = jnp.where(sender_slots < nodes, sender_slots, nodes + (away - 1) * depth + place % depth)
    both = jnp.stack([slots, receivers])
    both = in_order([both] + [shifted(both, "rep", step) for step in range(1, halves)], "rep")
    both = in_order([both] + [shifted(both, "feat", step) for step in range(1, feats)], "feat")
    both = both.reshape(feats * halves, 2, edges)
    readers = partner(shard, jnp.arange(1, shards, dtype=i32), shards)
    lists = jnp.take(halo_index[0], readers, axis=0).reshape(1, -1)
    here, there, halo_here, halo_there, list_here, list_there = call(
        place_kernel,
        [
            ((all_edges, 2 * nodes), bf16),
            ((2 * nodes, all_edges), bf16),
            ((all_edges, wide), bf16),
            ((wide, all_edges), bf16),
            ((listed_rows, nodes), bf16),
            ((nodes, listed_rows), bf16),
        ],
        products=[(all_edges, nodes, width), (all_edges, 2 * nodes, width)],
    )(both[:, 0].reshape(1, -1), both[:, 1].reshape(1, -1), lists)

    if shards == 4:
        across, list_here = lax.optimization_barrier((across, list_here))
        payloads.append(sent_to(across, 1))

    meta = jnp.stack([lax.axis_index("rep"), shard]).astype(i32)
    node_f32, node_bf16 = ((nodes, width), f32), ((nodes, width), bf16)
    row_shape, half = ((grid, width), bf16), nodes // halves
    square = (nodes, width, width)
    enc_picks, enc_slopes = [], []
    base, total = mesh_init, None
    groups = [payloads[:2]] + [payloads[at : at + 1] for at in range(2, shards)]
    for at, group in enumerate(groups):
        first, last = at == 0, at == len(groups) - 1
        count = len(group)
        outs = [((grid, nodes), bf16)] * count + [row_shape] * count
        outs += [node_bf16] if first else []
        outs += [((half, width), f32)] + [((half, width), bf16)] * (halves - 1) if last else [node_f32]
        got = list(
            call(
                functools.partial(encode_kernel, count, first, last, halves),
                outs,
                [node_f32] if last else [],
                [square] * first + [(grid, width, width), (grid, nodes, width), (nodes, grid, width)] * count,
            )(
                meta, base, w_enc_grid, *((w_enc_mesh, list_here) if first else (total,)), *group
            )
        )
        enc_picks += got[:count]
        enc_slopes += got[count : 2 * count]
        del got[: 2 * count]
        if first:
            base = got.pop(0)
        total = got[0]
    part = got[0]
    for step in range(1, halves):
        part = part + shifted(got[step], "rep", step).astype(f32)
    part = part.astype(bf16)
    pieces = [part] + [shifted(part, "feat", step) for step in range(1, feats)]
    if feats > 2:
        pieces = list(in_order(pieces, "feat"))
    part = sum(piece.astype(f32) for piece in pieces).astype(bf16)
    parts = [part] + [shifted(part, "rep", -step) for step in range(1, halves)]

    listed = [((depth, width), bf16)] * shifts
    hidden, enc_sum, sent, *outgoing = call(
        functools.partial(start_kernel, halves, shifts), [node_bf16, node_f32, node_bf16] + listed, [node_bf16],
        [square, square, (listed_rows, nodes, width)],
    )(meta, *parts, mesh_init, w_enc_out, enc_gain, w_send, list_here)

    edge_f32, edge_bf16 = ((all_edges, width), f32), ((all_edges, width), bf16)
    halo, back_halo = ((wide, width), bf16), ((listed_rows, width), bf16)

    forward_products = [(all_edges, wide, width), (nodes, all_edges, width), square]
    backward_products = [square, (all_edges, nodes, width), (wide, all_edges, width)]

    def local(layer):
        (pre,) = call(functools.partial(local_kernel, layer), [edge_f32], [((2 * nodes, width), bf16)], [square, (all_edges, 2 * nodes, width)])(
            hidden, sent, here, w_recv
        )
        return pre

    records = []
    for layer in range(LAYERS - 1):
        halos = [sent_to(block, step + 1) for step, block in enumerate(outgoing)]
        hidden, agg, slope, sent, *outgoing = call(
            functools.partial(layer_kernel, layer, shifts),
            [node_bf16, node_f32, edge_bf16, node_bf16] + listed,
            [halo],
            forward_products + [square, (listed_rows, nodes, width)],
        )(hidden, local(layer), *halos, halo_here, there, w_out, layer_gain, w_send, list_here)
        records.append((agg, slope))
    last = LAYERS - 1
    halos = [sent_to(block, step + 1) for step, block in enumerate(outgoing)]
    final_mesh, grad_pre, *outgoing = call(
        functools.partial(turn_kernel, last, shifts), [node_bf16, edge_bf16] + listed, [edge_bf16, halo],
        forward_products + backward_products,
    )(hidden, local(last), *halos, halo_here, there, w_out, layer_gain, here, halo_there, out_cot)
    upstream = out_cot
    for layer in reversed(range(LAYERS)):
        returned = [sent_back(block, step + 1) for step, block in enumerate(outgoing)]
        (rest,) = call(
            functools.partial(rest_kernel, layer), [node_f32], (), [(2 * nodes, all_edges, width), square, square]
        )(upstream, grad_pre, there, w_send, w_recv)
        if layer:
            agg, slope = records[layer - 1]
            upstream, grad_pre, *outgoing = call(
                functools.partial(back_kernel, layer - 1, shifts), [node_f32, edge_bf16] + listed, [back_halo],
                backward_products + [(listed_rows, width, width), (nodes, listed_rows, width)],
            )(rest, *returned, list_there, w_send, agg, slope, layer_gain, w_out, here, halo_there)
    relayed = shards == 4
    pieces = 2 if relayed else 1
    piece = ((grid // pieces, width), bf16)
    one = (grid, nodes, width)
    spread, *far = call(
        functools.partial(finish_kernel, shifts),
        [node_bf16] + [piece] * pieces,
        [back_halo],
        [square, (listed_rows, width, width), (nodes, listed_rows, width), one],
    )(rest, *returned, list_there, w_send, enc_sum, enc_gain, w_enc_out, enc_picks[-1], enc_slopes[-1])
    if relayed:
        passed = [sent_back(block, 1) for block in far]
    blocks = call(
        functools.partial(others_kernel, shards - 1), [row_shape] * (shards - 1), products=[one] * (shards - 1)
    )(spread, *enc_picks[:-1], *enc_slopes[:-1])
    if relayed:
        summed, near = [], blocks[1]
        for at, block in enumerate(passed):
            last = at == pieces - 1
            got = call(
                functools.partial(relay_kernel, at * piece[0][0], 1 + last), [piece] + [row_shape] * last
            )(blocks[2], block, blocks[1])
            summed.append(sent_back(got[0], 2))
        parts = [blocks[0], sent_back(got[1], 1)], summed
    else:
        blocks = [*blocks, far[0]]
        parts = [blocks[0]] + [sent_back(block, step) for step, block in enumerate(blocks) if step], []
    (grid_grad,) = call(
        functools.partial(grid_kernel, len(parts[0])), [((grid, width), f32)], products=[(grid, width, width)]
    )(*parts[0], *parts[1], w_enc_grid)
    return (final_mesh, grid_grad)


def solution(mesh):
    return jax.shard_map(
        on_device,
        mesh=mesh,
        in_specs=(
            P(("groups", "mesh", "feat", "rep"), None),
            P(("groups", "mesh", "feat", "rep"), None),
            P(("groups", "mesh", "feat", "rep"), None),
            P(("groups", "mesh"), None),
            P(("groups", "mesh", "feat", "rep")),
            P(("groups", "mesh", "feat", "rep")),
            P(("groups", "mesh"), None, None),
            P(),
            P(),
            P(),
            P(),
            P(),
            P(),
            P(),
            P(),
            P(("groups", "mesh"), None),
        ),
        out_specs=(P(("groups", "mesh"), None), P(("groups", "mesh", "feat", "rep"), None)),
        check_vma=False,
    )
```

```python
import functools
import math

import jax
import jax.numpy as jnp
from jax import lax
from jax.experimental import pallas as pl
from jax.experimental.pallas import tpu as pltpu
from jax.sharding import PartitionSpec as P

LAYERS = 3
LANES = 128
BLOCK = 512
EXTRA = 16
eps = 1e-05

f32 = jnp.float32
bf16 = jnp.bfloat16
i32 = jnp.int32


def norm_scale(totals):
    return lax.rsqrt(jnp.mean(totals * totals, axis=-1, keepdims=True) + eps)


def norm_back(totals, gain_row, upstream):
    scaled = norm_scale(totals)
    normed = totals * scaled
    slope = upstream * gain_row
    return scaled * (slope - normed * jnp.mean(slope * normed, axis=-1, keepdims=True))


def dot(left, right):
    return jnp.dot(left, right, preferred_element_type=f32)


def dot_back(left, right):
    return lax.dot_general(left, right, (((1,), (1,)), ((), ())), preferred_element_type=f32)


def gated(pre):
    sigma = 0.5 * jnp.tanh(0.5 * pre) + 0.5
    act = pre * sigma
    return act, sigma + act * (1.0 - sigma)


def as_mask(hit):
    return jnp.where(hit, 1.0, 0.0).astype(bf16)


def pick_columns(index, first, height):
    place = lax.broadcasted_iota(i32, (height, index.shape[1]), 0) + first
    return as_mask(place == index)


def upright(index):
    count = index.shape[1]
    if count < LANES:
        index = jnp.concatenate([index, jnp.full((1, LANES - count), -1, i32)], axis=1)
    return jnp.broadcast_to(index, (LANES, LANES)).T[:count]


def pick_rows(column, first, width):
    lane = lax.broadcasted_iota(i32, column.shape, 1) + first
    return jnp.concatenate([as_mask(column == lane + at) for at in range(0, width, LANES)], axis=1)


def call(body, outs, scratch=(), products=(), copied=False):
    def run(*args):
        def where(array):
            if copied:
                return pl.BlockSpec(memory_space=pltpu.HBM)
            return pl.BlockSpec(memory_space=pltpu.SMEM if array.dtype == i32 and array.ndim == 1 else pltpu.VMEM)

        def size(shape, dtype):
            return jnp.dtype(dtype).itemsize * math.prod(shape)

        own = sum(size(*held) for held in scratch) + (10 << 20)
        moved = sum(array.dtype.itemsize * array.size for array in args) + sum(size(*out) for out in outs)
        limit = own if own + moved < 40 << 20 else min(own + moved, 60 << 20)
        semaphores = [pltpu.SemaphoreType.DMA((len(args),))] if copied else []
        return pl.pallas_call(
            body,
            out_shape=tuple(jax.ShapeDtypeStruct(shape, dtype) for shape, dtype in outs),
            in_specs=[where(array) for array in args],
            out_specs=tuple(pl.BlockSpec(memory_space=pltpu.VMEM) for _ in outs),
            scratch_shapes=[pltpu.VMEM(shape, dtype) for shape, dtype in scratch] + semaphores,
            compiler_params=pltpu.CompilerParams(vmem_limit_bytes=limit),
            cost_estimate=pl.CostEstimate(
                flops=2 * sum(math.prod(product) for product in products), bytes_accessed=moved, transcendentals=0
            ),
        )(*args)

    return run


def place_kernel(slots, receivers, order, here, there, halo_here, halo_there, list_here, list_there):
    nodes = here.shape[1] // 2
    wide = halo_here.shape[1]

    def body(at):
        block = pl.ds(pl.multiple_of(at * LANES, LANES), LANES)
        slot, receiver = slots[:, block], receivers[:, block]
        slot_column, receiver_column = upright(slot), upright(receiver)
        here[block, 0:nodes] = pick_rows(slot_column, 0, nodes)
        here[block, nodes:] = pick_rows(receiver_column, 0, nodes)
        halo_here[block, :] = pick_rows(slot_column, nodes, wide)
        there[0:nodes, block] = pick_columns(slot, 0, nodes)
        there[nodes:, block] = pick_columns(receiver, 0, nodes)
        halo_there[:, block] = pick_columns(slot, nodes, wide)

    pl.loop(0, slots.shape[1] // LANES)(body)
    count = order.shape[1]
    for at in range(0, count, LANES):
        end = min(at + LANES, count)
        list_here[at:end, :] = pick_rows(upright(order[:, at:end]), 0, nodes)
    list_there[...] = pick_columns(order[...], 0, nodes)


def note_kernel(rows, shards, nodes, payload, shard_rows, node_rows, arrived):
    grid = rows.shape[0]
    copies = [
        pltpu.make_async_copy(rows, payload.at[0:grid], arrived.at[0]),
        pltpu.make_async_copy(shards, shard_rows, arrived.at[1]),
        pltpu.make_async_copy(nodes, node_rows, arrived.at[2]),
    ]
    for copy in copies:
        copy.start()
    copies[1].wait()
    copies[2].wait()
    row = lax.broadcasted_iota(i32, (EXTRA, grid), 0)
    notes = jnp.full((EXTRA, grid), -1, i32)
    for top in range(shards.shape[0]):
        node = node_rows[top : top + 1, :]
        for at, value in enumerate((shard_rows[top : top + 1, :], node & 255, node >> 8)):
            notes = jnp.where(row == 3 * top + at, value, notes)
    payload[grid:, 0:grid] = notes.astype(f32).astype(bf16)
    if grid < payload.shape[1]:
        payload[grid:, grid:] = jnp.zeros((EXTRA, payload.shape[1] - grid), bf16)
    copies[0].wait()


def encode_kernel(steps, first, last, halves, *refs):
    refs = list(refs)
    meta, base, w_grid = refs[:3]
    del refs[:3]
    if first:
        w_mesh, _ = refs.pop(0), refs.pop(0)
        projected = dot(base[...], w_mesh[...]).astype(bf16)
    else:
        total_in = refs.pop(0)
        projected = base[...]
    payloads = refs[:steps]
    del refs[:steps]
    picks, slopes = refs[:steps], refs[steps : 2 * steps]
    del refs[: 2 * steps]
    total = None if first else total_in[...]
    nodes = projected.shape[0]
    for payload, pick, slope_out in zip(payloads, picks, slopes):
        grid = pick.shape[0]
        notes = payload[grid:, 0:grid].astype(f32)
        target = jnp.full((1, grid), -1.0, f32)
        for at in range(0, notes.shape[0] // 3 * 3, 3):
            named = notes[at : at + 1] == meta[1].astype(f32)
            target = jnp.where(named, notes[at + 1 : at + 2] + 256.0 * notes[at + 2 : at + 3], target)
        target = target.astype(i32)
        column = jnp.concatenate([upright(target[:, at : at + LANES]) for at in range(0, grid, LANES)], axis=0)
        picked = pick_rows(column, 0, nodes)
        pick[...] = picked
        pre = dot(payload[0:grid, :], w_grid[...]) + dot(picked, projected)
        act, slope = gated(pre)
        slope_out[...] = slope.astype(bf16)
        added = dot(pick_columns(target, 0, nodes), act.astype(bf16))
        total = added if total is None else total + added
    if first:
        refs.pop(0)[...] = projected
    if not last:
        refs[0][...] = total
        return
    keep, sends, whole = refs[0], refs[1:halves], refs[-1]
    whole[...] = total
    part = nodes // halves

    def half(shift):
        at = lax.rem(meta[0] + shift, halves)
        return whole[pl.ds(pl.multiple_of(at * part, part), part), :]

    keep[...] = half(0)
    for shift in range(1, halves):
        sends[shift - 1][...] = half(shift).astype(bf16)


def hand_out(rows, outs, spots):
    rows = rows.astype(bf16)
    for out, spot in zip(outs, spots):
        out[...] = rows[spot : spot + out.shape[0]]


def start_kernel(halves, spots, *refs):
    meta = refs[0]
    parts = refs[1 : 1 + halves]
    mesh_init, w_enc_out, gain, w_send, list_here = refs[1 + halves : 6 + halves]
    hidden_out, enc_sum_out, sent = refs[6 + halves : 9 + halves]
    outs = refs[9 + halves : -1]
    whole = refs[-1]
    part = parts[0].shape[0]
    for shift in range(halves):
        at = lax.rem(meta[0] + shift, halves)
        whole[pl.ds(pl.multiple_of(at * part, part), part), :] = parts[shift][...]
    enc_sum = dot(whole[...], w_enc_out[...])
    enc_sum_out[...] = enc_sum
    hidden = (mesh_init[...].astype(f32) + enc_sum * norm_scale(enc_sum) * gain[...]).astype(bf16)
    hidden_out[...] = hidden
    projected = dot(hidden, w_send[0]).astype(bf16)
    sent[...] = projected
    hand_out(dot(list_here[...], projected), outs, spots)


def local_kernel(layer, hidden, sent, here, w_recv, pre, table):
    nodes = hidden.shape[0]
    table[0:nodes, :] = sent[...]
    table[nodes:, :] = dot(hidden[...], w_recv[layer]).astype(bf16)
    for at in range(0, pre.shape[0], BLOCK):
        pre[at : at + BLOCK, :] = dot(here[at : at + BLOCK, :], table[...])


def local_more_kernel(table, here, pre):
    skip = here.shape[0] - pre.shape[0]
    for at in range(0, pre.shape[0], BLOCK):
        pre[at : at + BLOCK, :] = dot(here[skip + at : skip + at + BLOCK, :], table[...])


def stack_halo(halos, halo):
    at = 0
    for blocks in halos:
        rows = blocks[0][...]
        if len(blocks) > 1:
            rows = (rows.astype(f32) + blocks[1][...].astype(f32)).astype(bf16)
        halo[at : at + rows.shape[0], :] = rows
        at += rows.shape[0]
    if at < halo.shape[0]:
        halo[at:, :] = jnp.zeros((halo.shape[0] - at, halo.shape[1]), bf16)


def node_sum(pres, halos, halo_here, there, slope_out, halo, act_out):
    nodes = there.shape[0] // 2
    stack_halo(halos, halo)
    half = pres[0].shape[0]
    for at in range(0, 2 * half, BLOCK):
        block = slice(at, at + BLOCK)
        pre = pres[at // half][at % half : at % half + BLOCK, :]
        act, slope = gated(pre + dot(halo_here[block, :], halo[...]))
        slope_out[block, :] = slope.astype(bf16)
        act_out[block, :] = act.astype(bf16)
    return dot(there[nodes:, :], act_out[...])


def split(refs, inward):
    groups = []
    for count in inward:
        groups.append(refs[:count])
        refs = refs[count:]
    return groups, refs


def layer_kernel(layer, inward, spots, *refs):
    hidden, pres = refs[0], refs[1:3]
    halos, refs = split(refs[3:], inward)
    halo_here, there, w_out, gain, w_send, list_here = refs[:6]
    hidden_out, agg_out, slope_out, sent_out = refs[6:10]
    outs = refs[10:-2]
    total = node_sum(pres, halos, halo_here, there, slope_out, *refs[-2:])
    agg = dot(total.astype(bf16), w_out[layer])
    agg_out[...] = agg
    fresh = (hidden[...].astype(f32) + agg * norm_scale(agg) * gain[layer : layer + 1, :]).astype(bf16)
    hidden_out[...] = fresh
    projected = dot(fresh, w_send[layer + 1]).astype(bf16)
    sent_out[...] = projected
    hand_out(dot(list_here[...], projected), outs, spots)


def edge_grads(grad_agg, w_out, here, halo_there, slope, grad_pre, outs, spots):
    nodes = grad_agg.shape[0]
    spread = dot_back(grad_agg.astype(bf16), w_out).astype(bf16)
    for at in range(0, slope.shape[0], BLOCK):
        block = slice(at, at + BLOCK)
        grad_act = dot(here[block, nodes:], spread)
        grad_pre[block, :] = (grad_act * slope[block, :].astype(f32)).astype(bf16)
    hand_out(dot(halo_there[...], grad_pre[...]), outs, spots)


def turn_kernel(layer, inward, spots, *refs):
    hidden, pres = refs[0], refs[1:3]
    halos, refs = split(refs[3:], inward)
    halo_here, there, w_out, gain, here, halo_there, cot = refs[:7]
    hidden_out, grad_pre = refs[7:9]
    outs = refs[9:-2]
    slope, halo = refs[-2:]
    total = node_sum(pres, halos, halo_here, there, slope, halo, grad_pre)
    agg = dot(total.astype(bf16), w_out[layer])
    gain_row = gain[layer : layer + 1, :]
    hidden_out[...] = (hidden[...].astype(f32) + agg * norm_scale(agg) * gain_row).astype(bf16)
    edge_grads(norm_back(agg, gain_row, cot[...].astype(f32)), w_out[layer], here, halo_there, slope, grad_pre, outs, spots)


def rest_kernel(layer, side, upstream, grad_pre, there, weights, rest):
    nodes = upstream.shape[0]
    sums = dot(there[side * nodes : (side + 1) * nodes, :], grad_pre[...]).astype(bf16)
    rest[...] = upstream[...].astype(f32) + dot_back(sums, weights[layer])


def arrived(rest, returned, list_there, w_send, halo):
    stack_halo(returned, halo)
    projected = dot_back(halo[...], w_send).astype(bf16)
    return rest[...] + dot(list_there[...], projected)


def back_kernel(layer, inward, spots, *refs):
    rest = refs[0]
    returned, refs = split(refs[1:], inward)
    list_there, w_send, agg, slope, gain, w_out, here, halo_there = refs[:8]
    upstream_out, grad_pre = refs[8:10]
    outs = refs[10:-1]
    halo = refs[-1]
    upstream = arrived(rest, returned, list_there, w_send[layer + 1], halo)
    upstream_out[...] = upstream
    grad_agg = norm_back(agg[...], gain[layer : layer + 1, :], upstream)
    edge_grads(grad_agg, w_out[layer], here, halo_there, slope, grad_pre, outs, spots)


def pair_grads(spread, pick, slope):
    return (dot(pick, spread) * slope.astype(f32)).astype(bf16)


def finish_kernel(inward, *refs):
    rest = refs[0]
    returned, refs = split(refs[1:], inward)
    list_there, w_send, enc_sum, gain, w_enc_out, pick, slope = refs[:7]
    spread_out, outs, halo = refs[7], refs[8:-1], refs[-1]
    upstream = arrived(rest, returned, list_there, w_send[0], halo)
    spread = dot_back(norm_back(enc_sum[...], gain[...], upstream).astype(bf16), w_enc_out[...]).astype(bf16)
    spread_out[...] = spread
    at = 0
    for out in outs:
        piece = slice(at, at + out.shape[0])
        out[...] = pair_grads(spread, pick[piece, :], slope[piece, :])
        at += out.shape[0]


def others_kernel(count, *refs):
    spread = refs[0][...]
    picks, slopes, outs = refs[1 : 1 + count], refs[1 + count : 1 + 2 * count], refs[1 + 2 * count :]
    for pick, slope, out in zip(picks, slopes, outs):
        out[...] = pair_grads(spread, pick[...], slope[...])


def relay_kernel(first, count, own, passed, held, *refs):
    rows = passed.shape[0]
    refs[0][...] = (own[first : first + rows, :].astype(f32) + passed[...].astype(f32)).astype(bf16)
    if count > 1:
        refs[1][...] = held[...]


def grid_kernel(whole, *refs):
    blocks, pieces, w_grid, out = refs[:whole], refs[whole:-2], refs[-2], refs[-1]
    step = out.shape[0] // max(len(pieces), 1)
    for at in range(0, out.shape[0], step):
        total = pieces[at // step][...].astype(f32) if pieces else 0.0
        for block in blocks:
            total = total + block[at : at + step, :].astype(f32)
        out[at : at + step, :] = dot_back(total.astype(bf16), w_grid[...])


def shifted(value, axis, by):
    size = lax.axis_size(axis)
    return lax.ppermute(value, axis, [(at, (at + by) % size) for at in range(size)])


def partner(at, step, size):
    return at ^ step if size & (size - 1) == 0 else (at + step) % size


def sent_to(value, step):
    size = lax.axis_size("mesh")
    return lax.ppermute(value, "mesh", [(at, partner(at, step, size)) for at in range(size)])


def sent_back(value, step):
    size = lax.axis_size("mesh")
    return lax.ppermute(value, "mesh", [(partner(at, step, size), at) for at in range(size)])


def in_order(pieces, axis):
    return jnp.roll(jnp.stack(pieces)[::-1], lax.axis_index(axis) + 1, axis=0)


def on_device(
    grid_feats,
    g2m_shard,
    g2m_node,
    mesh_init,
    sender_slots,
    receivers,
    halo_index,
    w_enc_grid,
    w_enc_mesh,
    w_enc_out,
    enc_gain,
    w_send,
    w_recv,
    w_out,
    layer_gain,
    out_cot,
):
    shards = lax.axis_size("mesh")
    shard = lax.axis_index("mesh")
    halves = lax.axis_size("rep")
    feats = lax.axis_size("feat")
    nodes, width = mesh_init.shape
    grid, tops = g2m_shard.shape
    edges = sender_slots.shape[0]
    depth = halo_index.shape[2]
    shifts = shards - 1
    listed_rows = shifts * depth
    wide = -(-listed_rows // LANES) * LANES
    all_edges = edges * halves * feats
    enc_gain = enc_gain[None, :]

    (payload,) = call(
        note_kernel, [((grid + EXTRA, width), bf16)], [((tops, grid), i32), ((tops, grid), i32)], copied=True
    )(*(pltpu.with_memory_space_constraint(array, pltpu.HBM) for array in (grid_feats, g2m_shard.T, g2m_node.T)))
    if shards == 4:
        across = sent_to(payload, 2)
        payloads = [payload, sent_to(payload, 1), across]
    else:
        payloads = [payload] + [sent_to(payload, step) for step in range(1, shards)]

    place = sender_slots - nodes
    away = partner(shard, place // depth, shards)
    if shards & (shards - 1):
        away = lax.rem(shard - place // depth + shards, shards)
    core = lax.axis_index("rep")
    shared = shards == 4 and halves == 2
    steps = jnp.arange(1, shards, dtype=i32)
    if shared:
        steps = jnp.where((core == 1) & (steps < 3), 3 - steps, steps)
    slots = jnp.where(sender_slots < nodes, sender_slots, nodes + (away - 1) * depth + place % depth)
    both = jnp.stack([slots, receivers])
    both = in_order([both] + [shifted(both, "rep", step) for step in range(1, halves)], "rep")
    both = in_order([both] + [shifted(both, "feat", step) for step in range(1, feats)], "feat")
    both = both.reshape(feats * halves, 2, edges)
    all_slots, all_receivers = both[:, 0].reshape(1, -1), both[:, 1].reshape(1, -1)
    if shared:
        entry = all_slots - nodes
        moved = jnp.where(entry < depth, depth, -depth)
        turned = (core == 1) & (entry >= 0) & (entry < 2 * depth)
        all_slots = all_slots + jnp.where(turned, moved, 0)
    readers = partner(shard, steps, shards)
    lists = jnp.take(halo_index[0], readers, axis=0).reshape(1, -1)
    here, there, halo_here, halo_there, list_here, list_there = call(
        place_kernel,
        [
            ((all_edges, 2 * nodes), bf16),
            ((2 * nodes, all_edges), bf16),
            ((all_edges, wide), bf16),
            ((wide, all_edges), bf16),
            ((listed_rows, nodes), bf16),
            ((nodes, listed_rows), bf16),
        ],
        products=[(all_edges, nodes, width), (all_edges, 2 * nodes, width)],
    )(all_slots, all_receivers, lists)

    if shards == 4:
        across, list_here = lax.optimization_barrier((across, list_here))
        payloads.append(sent_to(across, 1))

    meta = jnp.stack([lax.axis_index("rep"), shard]).astype(i32)
    node_f32, node_bf16 = ((nodes, width), f32), ((nodes, width), bf16)
    row_shape, half = ((grid, width), bf16), nodes // halves
    square = (nodes, width, width)
    enc_picks, enc_slopes = [], []
    base, total = mesh_init, None
    groups = [payloads[:2]] + [payloads[at : at + 1] for at in range(2, shards)]
    for at, group in enumerate(groups):
        first, last = at == 0, at == len(groups) - 1
        count = len(group)
        outs = [((grid, nodes), bf16)] * count + [row_shape] * count
        outs += [node_bf16] if first else []
        outs += [((half, width), f32)] + [((half, width), bf16)] * (halves - 1) if last else [node_f32]
        got = list(
            call(
                functools.partial(encode_kernel, count, first, last, halves),
                outs,
                [node_f32] if last else [],
                [square] * first + [(grid, width, width), (grid, nodes, width), (nodes, grid, width)] * count,
            )(
                meta, base, w_enc_grid, *((w_enc_mesh, list_here) if first else (total,)), *group
            )
        )
        enc_picks += got[:count]
        enc_slopes += got[count : 2 * count]
        del got[: 2 * count]
        if first:
            base = got.pop(0)
        total = got[0]
    part = got[0]
    for step in range(1, halves):
        part = part + shifted(got[step], "rep", step).astype(f32)
    part = part.astype(bf16)
    pieces = [part] + [shifted(part, "feat", step) for step in range(1, feats)]
    if feats > 2:
        pieces = list(in_order(pieces, "feat"))
    part = sum(piece.astype(f32) for piece in pieces).astype(bf16)
    parts = [part] + [shifted(part, "rep", -step) for step in range(1, halves)]

    spots = (0, 2 * depth) if shared else tuple(range(0, listed_rows, depth))
    inward = (1, 1, 2) if shared else (1,) * shifts
    listed = [((depth, width), bf16)] * len(spots)

    def exchange(blocks, send, early):
        if not shared:
            return [send(block, step + 1) for step, block in enumerate(blocks)], early
        first = lax.ppermute(
            blocks[0], ("mesh", "rep"), [(2 * at + side, 2 * (at ^ 1 + side) + side) for at in range(4) for side in range(2)]
        )
        third = lax.ppermute(blocks[1], ("mesh", "rep"), [(2 * at + 1, 2 * (at ^ 3) + 1) for at in range(4)])
        first, third, early = lax.optimization_barrier((first, third, early))
        return [
            first,
            lax.ppermute(first, "rep", [(0, 1), (1, 0)]),
            third,
            lax.ppermute(third, "rep", [(1, 0)]),
        ], early

    hidden, enc_sum, sent, *outgoing = call(
        functools.partial(start_kernel, halves, spots), [node_bf16, node_f32, node_bf16] + listed, [node_bf16],
        [square, square, (listed_rows, nodes, width)],
    )(meta, *parts, mesh_init, w_enc_out, enc_gain, w_send, list_here)

    half_f32, edge_bf16 = ((all_edges // 2, width), f32), ((all_edges, width), bf16)
    halo, back_halo = ((wide, width), bf16), ((listed_rows, width), bf16)
    forward_products = [(all_edges, wide, width), (nodes, all_edges, width), square]
    backward_products = [square, (all_edges, nodes, width), (wide, all_edges, width)]
    half_product = (all_edges // 2, 2 * nodes, width)

    def arriving(layer):
        early = call(
            functools.partial(local_kernel, layer), [half_f32, ((2 * nodes, width), bf16)], (), [square, half_product]
        )(hidden, sent, here, w_recv)
        halos, (pre, both_tables) = exchange(outgoing, sent_to, early)
        (more,) = call(local_more_kernel, [half_f32], (), [half_product])(both_tables, here)
        return hidden, pre, more, *halos

    records = []
    for layer in range(LAYERS - 1):
        hidden, agg, slope, sent, *outgoing = call(
            functools.partial(layer_kernel, layer, inward, spots),
            [node_bf16, node_f32, edge_bf16, node_bf16] + listed,
            [halo, edge_bf16],
            forward_products + [square, (listed_rows, nodes, width)],
        )(*arriving(layer), halo_here, there, w_out, layer_gain, w_send, list_here)
        records.append((agg, slope))
    last = LAYERS - 1
    final_mesh, grad_pre, *outgoing = call(
        functools.partial(turn_kernel, last, inward, spots), [node_bf16, edge_bf16] + listed, [edge_bf16, halo],
        forward_products + backward_products,
    )(*arriving(last), halo_here, there, w_out, layer_gain, here, halo_there, out_cot)
    upstream = out_cot
    for layer in reversed(range(LAYERS)):

        def rest_of(side, upstream, weights):
            (rest,) = call(
                functools.partial(rest_kernel, layer, side), [node_f32], (), [(nodes, all_edges, width), square]
            )(upstream, grad_pre, there, weights)
            return rest

        returned, early = exchange(outgoing, sent_back, rest_of(0, upstream, w_send))
        rest = rest_of(1, early, w_recv)
        if layer:
            agg, slope = records[layer - 1]
            upstream, grad_pre, *outgoing = call(
                functools.partial(back_kernel, layer - 1, inward, spots),
                [node_f32, edge_bf16] + listed,
                [back_halo],
                backward_products + [(listed_rows, width, width), (nodes, listed_rows, width)],
            )(rest, *returned, list_there, w_send, agg, slope, layer_gain, w_out, here, halo_there)
    relayed = shards == 4
    pieces = 2 if relayed else 1
    piece = ((grid // pieces, width), bf16)
    one = (grid, nodes, width)
    spread, *far = call(
        functools.partial(finish_kernel, inward),
        [node_bf16] + [piece] * pieces,
        [back_halo],
        [square, (listed_rows, width, width), (nodes, listed_rows, width), one],
    )(rest, *returned, list_there, w_send, enc_sum, enc_gain, w_enc_out, enc_picks[-1], enc_slopes[-1])
    if relayed:
        passed = [sent_back(block, 1) for block in far]
    blocks = call(
        functools.partial(others_kernel, shards - 1), [row_shape] * (shards - 1), products=[one] * (shards - 1)
    )(spread, *enc_picks[:-1], *enc_slopes[:-1])
    if relayed:
        summed, near = [], blocks[1]
        for at, block in enumerate(passed):
            last = at == pieces - 1
            got = call(
                functools.partial(relay_kernel, at * piece[0][0], 1 + last), [piece] + [row_shape] * last
            )(blocks[2], block, blocks[1])
            summed.append(sent_back(got[0], 2))
        parts = [blocks[0], sent_back(got[1], 1)], summed
    else:
        blocks = [*blocks, far[0]]
        parts = [blocks[0]] + [sent_back(block, step) for step, block in enumerate(blocks) if step], []
    (grid_grad,) = call(
        functools.partial(grid_kernel, len(parts[0])), [((grid, width), f32)], products=[(grid, width, width)]
    )(*parts[0], *parts[1], w_enc_grid)
    return (final_mesh, grid_grad)


def solution(mesh):
    return jax.shard_map(
        on_device,
        mesh=mesh,
        in_specs=(
            P(("groups", "mesh", "feat", "rep"), None),
            P(("groups", "mesh", "feat", "rep"), None),
            P(("groups", "mesh", "feat", "rep"), None),
            P(("groups", "mesh"), None),
            P(("groups", "mesh", "feat", "rep")),
            P(("groups", "mesh", "feat", "rep")),
            P(("groups", "mesh"), None, None),
            P(),
            P(),
            P(),
            P(),
            P(),
            P(),
            P(),
            P(),
            P(("groups", "mesh"), None),
        ),
        out_specs=(P(("groups", "mesh"), None), P(("groups", "mesh", "feat", "rep"), None)),
        check_vma=False,
    )
```

```python
import functools
import math

import jax
import jax.numpy as jnp
from jax import lax
from jax.experimental import pallas as pl
from jax.experimental.pallas import tpu as pltpu
from jax.sharding import PartitionSpec as P

LAYERS = 3
LANES = 128
BLOCK = 512
EXTRA = 16
eps = 1e-05

f32 = jnp.float32
bf16 = jnp.bfloat16
i32 = jnp.int32


def norm_scale(totals):
    return lax.rsqrt(jnp.mean(totals * totals, axis=-1, keepdims=True) + eps)


def norm_back(totals, gain_row, upstream):
    scaled = norm_scale(totals)
    normed = totals * scaled
    slope = upstream * gain_row
    return scaled * (slope - normed * jnp.mean(slope * normed, axis=-1, keepdims=True))


def dot(left, right):
    return jnp.dot(left, right, preferred_element_type=f32)


def dot_back(left, right):
    return lax.dot_general(left, right, (((1,), (1,)), ((), ())), preferred_element_type=f32)


def gated(pre):
    sigma = 0.5 * jnp.tanh(0.5 * pre) + 0.5
    act = pre * sigma
    return act, sigma + act * (1.0 - sigma)


def as_mask(hit):
    return jnp.where(hit, 1.0, 0.0).astype(bf16)


def pick_columns(index, first, height):
    place = lax.broadcasted_iota(i32, (height, index.shape[1]), 0) + first
    return as_mask(place == index)


def upright(index):
    count = index.shape[1]
    if count < LANES:
        index = jnp.concatenate([index, jnp.full((1, LANES - count), -1, i32)], axis=1)
    return jnp.broadcast_to(index, (LANES, LANES)).T[:count]


def pick_rows(column, first, width):
    lane = lax.broadcasted_iota(i32, column.shape, 1) + first
    return jnp.concatenate([as_mask(column == lane + at) for at in range(0, width, LANES)], axis=1)


def call(body, outs, scratch=(), products=(), copied=False):
    def run(*args):
        def where(array):
            if copied:
                return pl.BlockSpec(memory_space=pltpu.HBM)
            return pl.BlockSpec(memory_space=pltpu.SMEM if array.dtype == i32 and array.ndim == 1 else pltpu.VMEM)

        def size(shape, dtype):
            return jnp.dtype(dtype).itemsize * math.prod(shape)

        own = sum(size(*held) for held in scratch) + (10 << 20)
        moved = sum(array.dtype.itemsize * array.size for array in args) + sum(size(*out) for out in outs)
        limit = own if own + moved < 40 << 20 else min(own + moved, 60 << 20)
        semaphores = [pltpu.SemaphoreType.DMA((len(args),))] if copied else []
        return pl.pallas_call(
            body,
            out_shape=tuple(jax.ShapeDtypeStruct(shape, dtype) for shape, dtype in outs),
            in_specs=[where(array) for array in args],
            out_specs=tuple(pl.BlockSpec(memory_space=pltpu.VMEM) for _ in outs),
            scratch_shapes=[pltpu.VMEM(shape, dtype) for shape, dtype in scratch] + semaphores,
            compiler_params=pltpu.CompilerParams(vmem_limit_bytes=limit),
            cost_estimate=pl.CostEstimate(
                flops=2 * sum(math.prod(product) for product in products), bytes_accessed=moved, transcendentals=0
            ),
        )(*args)

    return run


def place_kernel(slots, receivers, order, here, there, halo_here, halo_there, list_here, list_there):
    nodes = here.shape[1] // 2
    wide = halo_here.shape[1]

    def body(at):
        block = pl.ds(pl.multiple_of(at * LANES, LANES), LANES)
        slot, receiver = slots[:, block], receivers[:, block]
        slot_column, receiver_column = upright(slot), upright(receiver)
        here[block, 0:nodes] = pick_rows(slot_column, 0, nodes)
        here[block, nodes:] = pick_rows(receiver_column, 0, nodes)
        halo_here[block, :] = pick_rows(slot_column, nodes, wide)
        there[0:nodes, block] = pick_columns(slot, 0, nodes)
        there[nodes:, block] = pick_columns(receiver, 0, nodes)
        halo_there[:, block] = pick_columns(slot, nodes, wide)

    pl.loop(0, slots.shape[1] // LANES)(body)
    count = order.shape[1]
    for at in range(0, count, LANES):
        end = min(at + LANES, count)
        list_here[at:end, :] = pick_rows(upright(order[:, at:end]), 0, nodes)
    list_there[...] = pick_columns(order[...], 0, nodes)


def note_kernel(rows, shards, nodes, payload, shard_rows, node_rows, arrived):
    grid = rows.shape[0]
    copies = [
        pltpu.make_async_copy(rows, payload.at[0:grid], arrived.at[0]),
        pltpu.make_async_copy(shards, shard_rows, arrived.at[1]),
        pltpu.make_async_copy(nodes, node_rows, arrived.at[2]),
    ]
    for copy in copies:
        copy.start()
    copies[1].wait()
    copies[2].wait()
    row = lax.broadcasted_iota(i32, (EXTRA, grid), 0)
    notes = jnp.full((EXTRA, grid), -1, i32)
    for top in range(shards.shape[0]):
        node = node_rows[top : top + 1, :]
        for at, value in enumerate((shard_rows[top : top + 1, :], node & 255, node >> 8)):
            notes = jnp.where(row == 3 * top + at, value, notes)
    payload[grid:, 0:grid] = notes.astype(f32).astype(bf16)
    if grid < payload.shape[1]:
        payload[grid:, grid:] = jnp.zeros((EXTRA, payload.shape[1] - grid), bf16)
    copies[0].wait()


def encode_kernel(steps, first, last, halves, *refs):
    refs = list(refs)
    meta, base, w_grid = refs[:3]
    del refs[:3]
    if first:
        w_mesh, _ = refs.pop(0), refs.pop(0)
        projected = dot(base[...], w_mesh[...]).astype(bf16)
    else:
        total_in = refs.pop(0)
        projected = base[...]
    payloads = refs[:steps]
    del refs[:steps]
    picks, slopes = refs[:steps], refs[steps : 2 * steps]
    del refs[: 2 * steps]
    total = None if first else total_in[...]
    nodes = projected.shape[0]
    for payload, pick, slope_out in zip(payloads, picks, slopes):
        grid = pick.shape[0]
        notes = payload[grid:, 0:grid].astype(f32)
        target = jnp.full((1, grid), -1.0, f32)
        for at in range(0, notes.shape[0] // 3 * 3, 3):
            named = notes[at : at + 1] == meta[1].astype(f32)
            target = jnp.where(named, notes[at + 1 : at + 2] + 256.0 * notes[at + 2 : at + 3], target)
        target = target.astype(i32)
        column = jnp.concatenate([upright(target[:, at : at + LANES]) for at in range(0, grid, LANES)], axis=0)
        picked = pick_rows(column, 0, nodes)
        pick[...] = picked
        pre = dot(payload[0:grid, :], w_grid[...]) + dot(picked, projected)
        act, slope = gated(pre)
        slope_out[...] = slope.astype(bf16)
        added = dot(pick_columns(target, 0, nodes), act.astype(bf16))
        total = added if total is None else total + added
    if first:
        refs.pop(0)[...] = projected
    if not last:
        refs[0][...] = total
        return
    keep, sends, whole = refs[0], refs[1:halves], refs[-1]
    whole[...] = total
    part = nodes // halves

    def half(shift):
        at = lax.rem(meta[0] + shift, halves)
        return whole[pl.ds(pl.multiple_of(at * part, part), part), :]

    keep[...] = half(0)
    for shift in range(1, halves):
        sends[shift - 1][...] = half(shift).astype(bf16)


def hand_out(rows, outs, spots):
    rows = rows.astype(bf16)
    for out, spot in zip(outs, spots):
        out[...] = rows[spot : spot + out.shape[0]]


def start_kernel(halves, spots, *refs):
    meta = refs[0]
    parts = refs[1 : 1 + halves]
    mesh_init, w_enc_out, gain, w_send, list_here = refs[1 + halves : 6 + halves]
    hidden_out, enc_sum_out, sent = refs[6 + halves : 9 + halves]
    outs = refs[9 + halves : -1]
    whole = refs[-1]
    part = parts[0].shape[0]
    for shift in range(halves):
        at = lax.rem(meta[0] + shift, halves)
        whole[pl.ds(pl.multiple_of(at * part, part), part), :] = parts[shift][...]
    enc_sum = dot(whole[...], w_enc_out[...])
    enc_sum_out[...] = enc_sum
    hidden = (mesh_init[...].astype(f32) + enc_sum * norm_scale(enc_sum) * gain[...]).astype(bf16)
    hidden_out[...] = hidden
    projected = dot(hidden, w_send[0]).astype(bf16)
    sent[...] = projected
    hand_out(dot(list_here[...], projected), outs, spots)


def local_kernel(layer, hidden, sent, here, w_recv, pre, table):
    nodes = hidden.shape[0]
    table[0:nodes, :] = sent[...]
    table[nodes:, :] = dot(hidden[...], w_recv[layer]).astype(bf16)
    for at in range(0, pre.shape[0], BLOCK):
        pre[at : at + BLOCK, :] = dot(here[at : at + BLOCK, :], table[...])


def local_more_kernel(table, here, pre):
    skip = here.shape[0] - pre.shape[0]
    for at in range(0, pre.shape[0], BLOCK):
        pre[at : at + BLOCK, :] = dot(here[skip + at : skip + at + BLOCK, :], table[...])


def stack_halo(meta, halos, halo):
    at = 0
    for blocks in halos:
        rows = blocks[0][...]
        if len(blocks) > 1:
            rows = jnp.where(meta[0] == 1, rows.astype(f32), blocks[1][...].astype(f32)).astype(bf16)
        halo[at : at + rows.shape[0], :] = rows
        at += rows.shape[0]
    if at < halo.shape[0]:
        halo[at:, :] = jnp.zeros((halo.shape[0] - at, halo.shape[1]), bf16)


def node_sum(meta, pres, halos, halo_here, there, slope_out, halo, act_out):
    nodes = there.shape[0] // 2
    stack_halo(meta, halos, halo)
    half = pres[0].shape[0]
    for at in range(0, 2 * half, BLOCK):
        block = slice(at, at + BLOCK)
        pre = pres[at // half][at % half : at % half + BLOCK, :]
        act, slope = gated(pre + dot(halo_here[block, :], halo[...]))
        slope_out[block, :] = slope.astype(bf16)
        act_out[block, :] = act.astype(bf16)
    return dot(there[nodes:, :], act_out[...])


def split(refs, inward):
    groups = []
    for count in inward:
        groups.append(refs[:count])
        refs = refs[count:]
    return groups, refs


def layer_kernel(layer, inward, spots, *refs):
    meta, hidden, pres = refs[0], refs[1], refs[2:4]
    halos, refs = split(refs[4:], inward)
    halo_here, there, w_out, gain, w_send, list_here = refs[:6]
    hidden_out, agg_out, slope_out, sent_out = refs[6:10]
    outs = refs[10:-2]
    total = node_sum(meta, pres, halos, halo_here, there, slope_out, *refs[-2:])
    agg = dot(total.astype(bf16), w_out[layer])
    agg_out[...] = agg
    fresh = (hidden[...].astype(f32) + agg * norm_scale(agg) * gain[layer : layer + 1, :]).astype(bf16)
    hidden_out[...] = fresh
    projected = dot(fresh, w_send[layer + 1]).astype(bf16)
    sent_out[...] = projected
    hand_out(dot(list_here[...], projected), outs, spots)


def edge_grads(grad_agg, w_out, here, halo_there, slope, grad_pre, outs, spots):
    nodes = grad_agg.shape[0]
    spread = dot_back(grad_agg.astype(bf16), w_out).astype(bf16)
    for at in range(0, slope.shape[0], BLOCK):
        block = slice(at, at + BLOCK)
        grad_act = dot(here[block, nodes:], spread)
        grad_pre[block, :] = (grad_act * slope[block, :].astype(f32)).astype(bf16)
    hand_out(dot(halo_there[...], grad_pre[...]), outs, spots)


def turn_kernel(layer, inward, spots, *refs):
    meta, hidden, pres = refs[0], refs[1], refs[2:4]
    halos, refs = split(refs[4:], inward)
    halo_here, there, w_out, gain, here, halo_there, cot = refs[:7]
    hidden_out, grad_pre = refs[7:9]
    outs = refs[9:-2]
    slope, halo = refs[-2:]
    total = node_sum(meta, pres, halos, halo_here, there, slope, halo, grad_pre)
    agg = dot(total.astype(bf16), w_out[layer])
    gain_row = gain[layer : layer + 1, :]
    hidden_out[...] = (hidden[...].astype(f32) + agg * norm_scale(agg) * gain_row).astype(bf16)
    edge_grads(norm_back(agg, gain_row, cot[...].astype(f32)), w_out[layer], here, halo_there, slope, grad_pre, outs, spots)


def rest_kernel(layer, side, upstream, grad_pre, there, weights, rest):
    nodes = upstream.shape[0]
    sums = dot(there[side * nodes : (side + 1) * nodes, :], grad_pre[...]).astype(bf16)
    rest[...] = upstream[...].astype(f32) + dot_back(sums, weights[layer])


def arrived(meta, rest, returned, list_there, w_send, halo):
    stack_halo(meta, returned, halo)
    projected = dot_back(halo[...], w_send).astype(bf16)
    return rest[...] + dot(list_there[...], projected)


def back_kernel(layer, inward, spots, *refs):
    meta, rest = refs[:2]
    returned, refs = split(refs[2:], inward)
    list_there, w_send, agg, slope, gain, w_out, here, halo_there = refs[:8]
    upstream_out, grad_pre = refs[8:10]
    outs = refs[10:-1]
    halo = refs[-1]
    upstream = arrived(meta, rest, returned, list_there, w_send[layer + 1], halo)
    upstream_out[...] = upstream
    grad_agg = norm_back(agg[...], gain[layer : layer + 1, :], upstream)
    edge_grads(grad_agg, w_out[layer], here, halo_there, slope, grad_pre, outs, spots)


def pair_grads(spread, pick, slope):
    return (dot(pick, spread) * slope.astype(f32)).astype(bf16)


def finish_kernel(inward, *refs):
    meta, rest = refs[:2]
    returned, refs = split(refs[2:], inward)
    list_there, w_send, enc_sum, gain, w_enc_out, pick, slope = refs[:7]
    spread_out, outs, halo = refs[7], refs[8:-1], refs[-1]
    upstream = arrived(meta, rest, returned, list_there, w_send[0], halo)
    spread = dot_back(norm_back(enc_sum[...], gain[...], upstream).astype(bf16), w_enc_out[...]).astype(bf16)
    spread_out[...] = spread
    at = 0
    for out in outs:
        piece = slice(at, at + out.shape[0])
        out[...] = pair_grads(spread, pick[piece, :], slope[piece, :])
        at += out.shape[0]


def others_kernel(count, *refs):
    spread = refs[0][...]
    picks, slopes, outs = refs[1 : 1 + count], refs[1 + count : 1 + 2 * count], refs[1 + 2 * count :]
    for pick, slope, out in zip(picks, slopes, outs):
        out[...] = pair_grads(spread, pick[...], slope[...])


def relay_kernel(first, count, own, passed, held, *refs):
    rows = passed.shape[0]
    refs[0][...] = (own[first : first + rows, :].astype(f32) + passed[...].astype(f32)).astype(bf16)
    if count > 1:
        refs[1][...] = held[...]


def grid_kernel(whole, *refs):
    blocks, pieces, w_grid, out = refs[:whole], refs[whole:-2], refs[-2], refs[-1]
    step = out.shape[0] // max(len(pieces), 1)
    for at in range(0, out.shape[0], step):
        total = pieces[at // step][...].astype(f32) if pieces else 0.0
        for block in blocks:
            total = total + block[at : at + step, :].astype(f32)
        out[at : at + step, :] = dot_back(total.astype(bf16), w_grid[...])


def shifted(value, axis, by):
    size = lax.axis_size(axis)
    return lax.ppermute(value, axis, [(at, (at + by) % size) for at in range(size)])


def partner(at, step, size):
    return at ^ step if size & (size - 1) == 0 else (at + step) % size


def sent_to(value, step):
    size = lax.axis_size("mesh")
    return lax.ppermute(value, "mesh", [(at, partner(at, step, size)) for at in range(size)])


def sent_back(value, step):
    size = lax.axis_size("mesh")
    return lax.ppermute(value, "mesh", [(partner(at, step, size), at) for at in range(size)])


def in_order(pieces, axis):
    return jnp.roll(jnp.stack(pieces)[::-1], lax.axis_index(axis) + 1, axis=0)


def on_device(
    grid_feats,
    g2m_shard,
    g2m_node,
    mesh_init,
    sender_slots,
    receivers,
    halo_index,
    w_enc_grid,
    w_enc_mesh,
    w_enc_out,
    enc_gain,
    w_send,
    w_recv,
    w_out,
    layer_gain,
    out_cot,
):
    shards = lax.axis_size("mesh")
    shard = lax.axis_index("mesh")
    halves = lax.axis_size("rep")
    feats = lax.axis_size("feat")
    nodes, width = mesh_init.shape
    grid, tops = g2m_shard.shape
    edges = sender_slots.shape[0]
    depth = halo_index.shape[2]
    shifts = shards - 1
    listed_rows = shifts * depth
    wide = -(-listed_rows // LANES) * LANES
    all_edges = edges * halves * feats
    enc_gain = enc_gain[None, :]

    (payload,) = call(
        note_kernel, [((grid + EXTRA, width), bf16)], [((tops, grid), i32), ((tops, grid), i32)], copied=True
    )(*(pltpu.with_memory_space_constraint(array, pltpu.HBM) for array in (grid_feats, g2m_shard.T, g2m_node.T)))
    if shards == 4:
        across = sent_to(payload, 2)
        payloads = [payload, sent_to(payload, 1), across]
    else:
        payloads = [payload] + [sent_to(payload, step) for step in range(1, shards)]

    place = sender_slots - nodes
    away = partner(shard, place // depth, shards)
    if shards & (shards - 1):
        away = lax.rem(shard - place // depth + shards, shards)
    core = lax.axis_index("rep")
    shared = shards == 4 and halves == 2
    steps = jnp.arange(1, shards, dtype=i32)
    if shared:
        steps = jnp.where((core == 1) & (steps < 3), 3 - steps, steps)
    slots = jnp.where(sender_slots < nodes, sender_slots, nodes + (away - 1) * depth + place % depth)
    both = jnp.stack([slots, receivers])
    both = in_order([both] + [shifted(both, "rep", step) for step in range(1, halves)], "rep")
    both = in_order([both] + [shifted(both, "feat", step) for step in range(1, feats)], "feat")
    both = both.reshape(feats * halves, 2, edges)
    all_slots, all_receivers = both[:, 0].reshape(1, -1), both[:, 1].reshape(1, -1)
    if shared:
        entry = all_slots - nodes
        moved = jnp.where(entry < depth, depth, -depth)
        turned = (core == 1) & (entry >= 0) & (entry < 2 * depth)
        all_slots = all_slots + jnp.where(turned, moved, 0)
    readers = partner(shard, steps, shards)
    lists = jnp.take(halo_index[0], readers, axis=0).reshape(1, -1)
    here, there, halo_here, halo_there, list_here, list_there = call(
        place_kernel,
        [
            ((all_edges, 2 * nodes), bf16),
            ((2 * nodes, all_edges), bf16),
            ((all_edges, wide), bf16),
            ((wide, all_edges), bf16),
            ((listed_rows, nodes), bf16),
            ((nodes, listed_rows), bf16),
        ],
        products=[(all_edges, nodes, width), (all_edges, 2 * nodes, width)],
    )(all_slots, all_receivers, lists)

    if shards == 4:
        across, list_here = lax.optimization_barrier((across, list_here))
        payloads.append(sent_to(across, 1))

    meta = jnp.stack([lax.axis_index("rep"), shard]).astype(i32)
    node_f32, node_bf16 = ((nodes, width), f32), ((nodes, width), bf16)
    row_shape, half = ((grid, width), bf16), nodes // halves
    square = (nodes, width, width)
    enc_picks, enc_slopes = [], []
    base, total = mesh_init, None
    groups = [payloads[:2]] + [payloads[at : at + 1] for at in range(2, shards)]
    for at, group in enumerate(groups):
        first, last = at == 0, at == len(groups) - 1
        count = len(group)
        outs = [((grid, nodes), bf16)] * count + [row_shape] * count
        outs += [node_bf16] if first else []
        outs += [((half, width), f32)] + [((half, width), bf16)] * (halves - 1) if last else [node_f32]
        got = list(
            call(
                functools.partial(encode_kernel, count, first, last, halves),
                outs,
                [node_f32] if last else [],
                [square] * first + [(grid, width, width), (grid, nodes, width), (nodes, grid, width)] * count,
            )(
                meta, base, w_enc_grid, *((w_enc_mesh, list_here) if first else (total,)), *group
            )
        )
        enc_picks += got[:count]
        enc_slopes += got[count : 2 * count]
        del got[: 2 * count]
        if first:
            base = got.pop(0)
        total = got[0]
    part = got[0]
    for step in range(1, halves):
        part = part + shifted(got[step], "rep", step).astype(f32)
    part = part.astype(bf16)
    pieces = [part] + [shifted(part, "feat", step) for step in range(1, feats)]
    if feats > 2:
        pieces = list(in_order(pieces, "feat"))
    part = sum(piece.astype(f32) for piece in pieces).astype(bf16)
    parts = [part] + [shifted(part, "rep", -step) for step in range(1, halves)]

    spots = (0, 2 * depth) if shared else tuple(range(0, listed_rows, depth))
    inward = (1, 1, 2) if shared else (1,) * shifts
    listed = [((depth, width), bf16)] * len(spots)

    def exchange(blocks, send, early):
        if not shared:
            return [send(block, step + 1) for step, block in enumerate(blocks)], early
        first = lax.ppermute(
            blocks[0], ("mesh", "rep"), [(2 * at + side, 2 * (at ^ 1 + side) + side) for at in range(4) for side in range(2)]
        )
        third = lax.ppermute(blocks[1], ("mesh", "rep"), [(2 * at + side, 2 * (at ^ 3 * side) + side) for at in range(4) for side in range(2)])
        first, third, early = lax.optimization_barrier((first, third, early))
        return [
            first,
            lax.ppermute(first, "rep", [(0, 1), (1, 0)]),
            third,
            lax.ppermute(third, "rep", [(0, 1), (1, 0)]),
        ], early

    hidden, enc_sum, sent, *outgoing = call(
        functools.partial(start_kernel, halves, spots), [node_bf16, node_f32, node_bf16] + listed, [node_bf16],
        [square, square, (listed_rows, nodes, width)],
    )(meta, *parts, mesh_init, w_enc_out, enc_gain, w_send, list_here)

    half_f32, edge_bf16 = ((all_edges // 2, width), f32), ((all_edges, width), bf16)
    halo, back_halo = ((wide, width), bf16), ((listed_rows, width), bf16)
    forward_products = [(all_edges, wide, width), (nodes, all_edges, width), square]
    backward_products = [square, (all_edges, nodes, width), (wide, all_edges, width)]
    half_product = (all_edges // 2, 2 * nodes, width)

    def arriving(layer):
        early = call(
            functools.partial(local_kernel, layer), [half_f32, ((2 * nodes, width), bf16)], (), [square, half_product]
        )(hidden, sent, here, w_recv)
        halos, (pre, both_tables) = exchange(outgoing, sent_to, early)
        (more,) = call(local_more_kernel, [half_f32], (), [half_product])(both_tables, here)
        return meta, hidden, pre, more, *halos

    records = []
    for layer in range(LAYERS - 1):
        hidden, agg, slope, sent, *outgoing = call(
            functools.partial(layer_kernel, layer, inward, spots),
            [node_bf16, node_f32, edge_bf16, node_bf16] + listed,
            [halo, edge_bf16],
            forward_products + [square, (listed_rows, nodes, width)],
        )(*arriving(layer), halo_here, there, w_out, layer_gain, w_send, list_here)
        records.append((agg, slope))
    last = LAYERS - 1
    final_mesh, grad_pre, *outgoing = call(
        functools.partial(turn_kernel, last, inward, spots), [node_bf16, edge_bf16] + listed, [edge_bf16, halo],
        forward_products + backward_products,
    )(*arriving(last), halo_here, there, w_out, layer_gain, here, halo_there, out_cot)
    upstream = out_cot
    for layer in reversed(range(LAYERS)):

        def rest_of(side, upstream, weights):
            (rest,) = call(
                functools.partial(rest_kernel, layer, side), [node_f32], (), [(nodes, all_edges, width), square]
            )(upstream, grad_pre, there, weights)
            return rest

        returned, early = exchange(outgoing, sent_back, rest_of(0, upstream, w_send))
        rest = rest_of(1, early, w_recv)
        if layer:
            agg, slope = records[layer - 1]
            upstream, grad_pre, *outgoing = call(
                functools.partial(back_kernel, layer - 1, inward, spots),
                [node_f32, edge_bf16] + listed,
                [back_halo],
                backward_products + [(listed_rows, width, width), (nodes, listed_rows, width)],
            )(meta, rest, *returned, list_there, w_send, agg, slope, layer_gain, w_out, here, halo_there)
    relayed = shards == 4
    pieces = 2 if relayed else 1
    piece = ((grid // pieces, width), bf16)
    one = (grid, nodes, width)
    spread, *far = call(
        functools.partial(finish_kernel, inward),
        [node_bf16] + [piece] * pieces,
        [back_halo],
        [square, (listed_rows, width, width), (nodes, listed_rows, width), one],
    )(meta, rest, *returned, list_there, w_send, enc_sum, enc_gain, w_enc_out, enc_picks[-1], enc_slopes[-1])
    if relayed:
        passed = [sent_back(block, 1) for block in far]
    blocks = call(
        functools.partial(others_kernel, shards - 1), [row_shape] * (shards - 1), products=[one] * (shards - 1)
    )(spread, *enc_picks[:-1], *enc_slopes[:-1])
    if relayed:
        summed, near = [], blocks[1]
        for at, block in enumerate(passed):
            last = at == pieces - 1
            got = call(
                functools.partial(relay_kernel, at * piece[0][0], 1 + last), [piece] + [row_shape] * last
            )(blocks[2], block, blocks[1])
            summed.append(sent_back(got[0], 2))
        parts = [blocks[0], sent_back(got[1], 1)], summed
    else:
        blocks = [*blocks, far[0]]
        parts = [blocks[0]] + [sent_back(block, step) for step, block in enumerate(blocks) if step], []
    (grid_grad,) = call(
        functools.partial(grid_kernel, len(parts[0])), [((grid, width), f32)], products=[(grid, width, width)]
    )(*parts[0], *parts[1], w_enc_grid)
    return (final_mesh, grid_grad)


def solution(mesh):
    return jax.shard_map(
        on_device,
        mesh=mesh,
        in_specs=(
            P(("groups", "mesh", "feat", "rep"), None),
            P(("groups", "mesh", "feat", "rep"), None),
            P(("groups", "mesh", "feat", "rep"), None),
            P(("groups", "mesh"), None),
            P(("groups", "mesh", "feat", "rep")),
            P(("groups", "mesh", "feat", "rep")),
            P(("groups", "mesh"), None, None),
            P(),
            P(),
            P(),
            P(),
            P(),
            P(),
            P(),
            P(),
            P(("groups", "mesh"), None),
        ),
        out_specs=(P(("groups", "mesh"), None), P(("groups", "mesh", "feat", "rep"), None)),
        check_vma=False,
    )
```

```python
import functools
import math

import jax
import jax.numpy as jnp
from jax import lax
from jax.experimental import pallas as pl
from jax.experimental.pallas import tpu as pltpu
from jax.sharding import PartitionSpec as P

LAYERS = 3
LANES = 128
BLOCK = 512
EXTRA = 16
eps = 1e-05

f32 = jnp.float32
bf16 = jnp.bfloat16
i32 = jnp.int32


def norm_scale(totals):
    return lax.rsqrt(jnp.mean(totals * totals, axis=-1, keepdims=True) + eps)


def norm_back(totals, gain_row, upstream):
    scaled = norm_scale(totals)
    normed = totals * scaled
    slope = upstream * gain_row
    return scaled * (slope - normed * jnp.mean(slope * normed, axis=-1, keepdims=True))


def dot(left, right):
    return jnp.dot(left, right, preferred_element_type=f32)


def dot_back(left, right):
    return lax.dot_general(left, right, (((1,), (1,)), ((), ())), preferred_element_type=f32)


def gated(pre):
    sigma = 0.5 * jnp.tanh(0.5 * pre) + 0.5
    act = pre * sigma
    return act, sigma + act * (1.0 - sigma)


def as_mask(hit):
    return jnp.where(hit, 1.0, 0.0).astype(bf16)


def pick_columns(index, first, height):
    place = lax.broadcasted_iota(i32, (height, index.shape[1]), 0) + first
    return as_mask(place == index)


def upright(index):
    count = index.shape[1]
    if count < LANES:
        index = jnp.concatenate([index, jnp.full((1, LANES - count), -1, i32)], axis=1)
    return jnp.broadcast_to(index, (LANES, LANES)).T[:count]


def pick_rows(column, first, width):
    lane = lax.broadcasted_iota(i32, column.shape, 1) + first
    return jnp.concatenate([as_mask(column == lane + at) for at in range(0, width, LANES)], axis=1)


def call(body, outs, scratch=(), products=(), copied=False):
    def run(*args):
        def where(array):
            if copied:
                return pl.BlockSpec(memory_space=pltpu.HBM)
            return pl.BlockSpec(memory_space=pltpu.SMEM if array.dtype == i32 and array.ndim == 1 else pltpu.VMEM)

        def size(shape, dtype):
            return jnp.dtype(dtype).itemsize * math.prod(shape)

        own = sum(size(*held) for held in scratch) + (10 << 20)
        moved = sum(array.dtype.itemsize * array.size for array in args) + sum(size(*out) for out in outs)
        limit = own if own + moved < 40 << 20 else min(own + moved, 60 << 20)
        semaphores = [pltpu.SemaphoreType.DMA((2 + len(outs),))] if copied else []
        return pl.pallas_call(
            body,
            out_shape=tuple(jax.ShapeDtypeStruct(shape, dtype) for shape, dtype in outs),
            in_specs=[where(array) for array in args],
            out_specs=tuple(pl.BlockSpec(memory_space=pltpu.VMEM) for _ in outs),
            scratch_shapes=[pltpu.VMEM(shape, dtype) for shape, dtype in scratch] + semaphores,
            compiler_params=pltpu.CompilerParams(vmem_limit_bytes=limit),
            cost_estimate=pl.CostEstimate(
                flops=2 * sum(math.prod(product) for product in products), bytes_accessed=moved, transcendentals=0
            ),
        )(*args)

    return run


def place_kernel(slots, receivers, order, here, there, halo_here, halo_there, list_here, list_there):
    nodes = here.shape[1] // 2
    wide = halo_here.shape[1]

    def body(at):
        block = pl.ds(pl.multiple_of(at * LANES, LANES), LANES)
        slot, receiver = slots[:, block], receivers[:, block]
        slot_column, receiver_column = upright(slot), upright(receiver)
        here[block, 0:nodes] = pick_rows(slot_column, 0, nodes)
        here[block, nodes:] = pick_rows(receiver_column, 0, nodes)
        halo_here[block, :] = pick_rows(slot_column, nodes, wide)
        there[0:nodes, block] = pick_columns(slot, 0, nodes)
        there[nodes:, block] = pick_columns(receiver, 0, nodes)
        halo_there[:, block] = pick_columns(slot, nodes, wide)

    pl.loop(0, slots.shape[1] // LANES)(body)
    count = order.shape[1]
    for at in range(0, count, LANES):
        end = min(at + LANES, count)
        list_here[at:end, :] = pick_rows(upright(order[:, at:end]), 0, nodes)
    list_there[...] = pick_columns(order[...], 0, nodes)


def note_kernel(rows, shards, nodes, payload, shard_rows, node_rows, arrived):
    grid = shards.shape[1]
    first = payload.shape[0] - EXTRA
    copies = [
        pltpu.make_async_copy(shards, shard_rows, arrived.at[0]),
        pltpu.make_async_copy(nodes, node_rows, arrived.at[1]),
        pltpu.make_async_copy(rows.at[0:first], payload.at[0:first], arrived.at[2]),
    ]
    for copy in copies:
        copy.start()
    for copy in copies[:2]:
        copy.wait()
    row = lax.broadcasted_iota(i32, (EXTRA, grid), 0)
    notes = jnp.full((EXTRA, grid), -1, i32)
    for top in range(shards.shape[0]):
        node = node_rows[top : top + 1, :]
        for at, value in enumerate((shard_rows[top : top + 1, :], node & 255, node >> 8)):
            notes = jnp.where(row == 3 * top + at, value, notes)
    payload[first:, 0:grid] = notes.astype(f32).astype(bf16)
    if grid < payload.shape[1]:
        payload[first:, grid:] = jnp.zeros((EXTRA, payload.shape[1] - grid), bf16)
    copies[2].wait()


def left_kernel(first, rows, notes, _, left, payload, arrived):
    grid = rows.shape[0]
    copies = [
        pltpu.make_async_copy(rows.at[first:], left, arrived.at[0]),
        pltpu.make_async_copy(rows, payload.at[0:grid], arrived.at[1]),
        pltpu.make_async_copy(notes.at[first:], payload.at[grid:], arrived.at[2]),
    ]
    for copy in copies:
        copy.start()
    for copy in copies:
        copy.wait()


def encode_kernel(counts, first, last, halves, *refs):
    refs = list(refs)
    meta, base, w_grid = refs[:3]
    del refs[:3]
    if first:
        w_mesh, _ = refs.pop(0), refs.pop(0)
        projected = dot(base[...], w_mesh[...]).astype(bf16)
    else:
        total_in = refs.pop(0)
        projected = base[...]
    payloads = []
    for count in counts:
        payloads.append(refs[:count])
        del refs[:count]
    steps = len(counts)
    picks, slopes = refs[:steps], refs[steps : 2 * steps]
    del refs[: 2 * steps]
    total = None if first else total_in[...]
    nodes = projected.shape[0]
    for payload, pick, slope_out in zip(payloads, picks, slopes):
        grid = pick.shape[0]
        rows = jnp.concatenate([piece[0 : grid // len(payload), :] for piece in payload], axis=0)
        notes = payload[0][grid // len(payload) :, 0:grid].astype(f32)
        target = jnp.full((1, grid), -1.0, f32)
        for at in range(0, notes.shape[0] // 3 * 3, 3):
            named = notes[at : at + 1] == meta[1:2, 0:grid].astype(f32)
            target = jnp.where(named, notes[at + 1 : at + 2] + 256.0 * notes[at + 2 : at + 3], target)
        target = target.astype(i32)
        column = jnp.concatenate([upright(target[:, at : at + LANES]) for at in range(0, grid, LANES)], axis=0)
        picked = pick_rows(column, 0, nodes)
        pick[...] = picked
        pre = dot(rows, w_grid[...]) + dot(picked, projected)
        act, slope = gated(pre)
        slope_out[...] = slope.astype(bf16)
        added = dot(pick_columns(target, 0, nodes), act.astype(bf16))
        total = added if total is None else total + added
    if first:
        refs.pop(0)[...] = projected
    if not last:
        refs[0][...] = total
        return
    keep, sends = refs[0], refs[1:halves]
    part = nodes // halves
    own = meta[0:1, :]

    def half(shift):
        rows = total[0:part]
        for at in range(1, halves):
            rows = jnp.where(own == (at - shift) % halves, total[at * part : (at + 1) * part], rows)
        return rows

    keep[...] = half(0)
    for shift in range(1, halves):
        sends[shift - 1][...] = half(shift).astype(bf16)


def hand_out(rows, outs, spots):
    rows = rows.astype(bf16)
    for out, spot in zip(outs, spots):
        out[...] = rows[spot : spot + out.shape[0]]


def start_kernel(halves, spots, *refs):
    meta = refs[0]
    parts = refs[1 : 1 + halves]
    mesh_init, w_enc_out, gain, w_send, list_here = refs[1 + halves : 6 + halves]
    hidden_out, enc_sum_out, sent = refs[6 + halves : 9 + halves]
    outs = refs[9 + halves : -1]
    whole = refs[-1]
    part = parts[0].shape[0]
    own = meta[0:1, :]
    for at in range(halves):
        rows = parts[0][...].astype(f32)
        for shift in range(1, halves):
            rows = jnp.where(own == (at - shift) % halves, parts[shift][...].astype(f32), rows)
        whole[at * part : (at + 1) * part, :] = rows.astype(bf16)
    enc_sum = dot(whole[...], w_enc_out[...])
    enc_sum_out[...] = enc_sum
    hidden = (mesh_init[...].astype(f32) + enc_sum * norm_scale(enc_sum) * gain[...]).astype(bf16)
    hidden_out[...] = hidden
    projected = dot(hidden, w_send[0]).astype(bf16)
    sent[...] = projected
    hand_out(dot(list_here[...], projected), outs, spots)


def local_kernel(layer, hidden, sent, here, w_recv, pre, table):
    nodes = hidden.shape[0]
    table[0:nodes, :] = sent[...]
    table[nodes:, :] = dot(hidden[...], w_recv[layer]).astype(bf16)
    for at in range(0, pre.shape[0], BLOCK):
        pre[at : at + BLOCK, :] = dot(here[at : at + BLOCK, :], table[...])


def local_more_kernel(table, here, pre):
    skip = here.shape[0] - pre.shape[0]
    for at in range(0, pre.shape[0], BLOCK):
        pre[at : at + BLOCK, :] = dot(here[skip + at : skip + at + BLOCK, :], table[...])


def stack_halo(halos, halo):
    at = 0
    for block in halos:
        halo[at : at + block.shape[0], :] = block[...]
        at += block.shape[0]
    if at < halo.shape[0]:
        halo[at:, :] = jnp.zeros((halo.shape[0] - at, halo.shape[1]), bf16)


def node_sum(pres, halos, halo_here, there, slope_out, halo, act_out):
    nodes = there.shape[0] // 2
    stack_halo(halos, halo)
    half = pres[0].shape[0]
    for at in range(0, 2 * half, BLOCK):
        block = slice(at, at + BLOCK)
        pre = pres[at // half][at % half : at % half + BLOCK, :]
        act, slope = gated(pre + dot(halo_here[block, :], halo[...]))
        slope_out[block, :] = slope.astype(bf16)
        act_out[block, :] = act.astype(bf16)
    return dot(there[nodes:, :], act_out[...])


def layer_kernel(layer, shifts, spots, *refs):
    hidden, pres = refs[0], refs[1:3]
    halos, refs = refs[3 : 3 + shifts], refs[3 + shifts :]
    halo_here, there, w_out, gain, w_send, list_here = refs[:6]
    hidden_out, agg_out, slope_out, sent_out = refs[6:10]
    outs = refs[10:-2]
    total = node_sum(pres, halos, halo_here, there, slope_out, *refs[-2:])
    agg = dot(total.astype(bf16), w_out[layer])
    agg_out[...] = agg
    fresh = (hidden[...].astype(f32) + agg * norm_scale(agg) * gain[layer : layer + 1, :]).astype(bf16)
    hidden_out[...] = fresh
    projected = dot(fresh, w_send[layer + 1]).astype(bf16)
    sent_out[...] = projected
    hand_out(dot(list_here[...], projected), outs, spots)


def edge_grads(grad_agg, w_out, here, halo_there, slope, grad_pre, outs, spots):
    nodes = grad_agg.shape[0]
    spread = dot_back(grad_agg.astype(bf16), w_out).astype(bf16)
    for at in range(0, slope.shape[0], BLOCK):
        block = slice(at, at + BLOCK)
        grad_act = dot(here[block, nodes:], spread)
        grad_pre[block, :] = (grad_act * slope[block, :].astype(f32)).astype(bf16)
    hand_out(dot(halo_there[...], grad_pre[...]), outs, spots)


def turn_kernel(layer, shifts, spots, *refs):
    hidden, pres = refs[0], refs[1:3]
    halos, refs = refs[3 : 3 + shifts], refs[3 + shifts :]
    halo_here, there, w_out, gain, here, halo_there, cot = refs[:7]
    hidden_out, grad_pre = refs[7:9]
    outs = refs[9:-2]
    slope, halo = refs[-2:]
    total = node_sum(pres, halos, halo_here, there, slope, halo, grad_pre)
    agg = dot(total.astype(bf16), w_out[layer])
    gain_row = gain[layer : layer + 1, :]
    hidden_out[...] = (hidden[...].astype(f32) + agg * norm_scale(agg) * gain_row).astype(bf16)
    edge_grads(norm_back(agg, gain_row, cot[...].astype(f32)), w_out[layer], here, halo_there, slope, grad_pre, outs, spots)


def rest_kernel(layer, side, upstream, grad_pre, there, weights, rest):
    nodes = upstream.shape[0]
    sums = dot(there[side * nodes : (side + 1) * nodes, :], grad_pre[...]).astype(bf16)
    rest[...] = upstream[...].astype(f32) + dot_back(sums, weights[layer])


def arrived(rest, returned, list_there, w_send, halo):
    stack_halo(returned, halo)
    projected = dot_back(halo[...], w_send).astype(bf16)
    return rest[...] + dot(list_there[...], projected)


def back_kernel(layer, shifts, spots, *refs):
    rest = refs[0]
    returned, refs = refs[1 : 1 + shifts], refs[1 + shifts :]
    list_there, w_send, agg, slope, gain, w_out, here, halo_there = refs[:8]
    upstream_out, grad_pre = refs[8:10]
    outs = refs[10:-1]
    halo = refs[-1]
    upstream = arrived(rest, returned, list_there, w_send[layer + 1], halo)
    upstream_out[...] = upstream
    grad_agg = norm_back(agg[...], gain[layer : layer + 1, :], upstream)
    edge_grads(grad_agg, w_out[layer], here, halo_there, slope, grad_pre, outs, spots)


def pair_grads(spread, pick, slope):
    return (dot(pick, spread) * slope.astype(f32)).astype(bf16)


def finish_kernel(shifts, *refs):
    rest = refs[0]
    returned, refs = refs[1 : 1 + shifts], refs[1 + shifts :]
    list_there, w_send, enc_sum, gain, w_enc_out, pick, slope, spread_out = refs[:8]
    outs, halo = refs[8:-1], refs[-1]
    upstream = arrived(rest, returned, list_there, w_send[0], halo)
    spread = dot_back(norm_back(enc_sum[...], gain[...], upstream).astype(bf16), w_enc_out[...]).astype(bf16)
    spread_out[...] = spread
    at = 0
    for out in outs:
        rows = slice(at, at + out.shape[0])
        out[...] = pair_grads(spread, pick[rows, :], slope[rows, :])
        at += out.shape[0]


def others_kernel(count, *refs):
    spread = refs[0][...]
    picks, slopes, outs = refs[1 : 1 + count], refs[1 + count : 1 + 2 * count], refs[1 + 2 * count :]
    for pick, slope, out in reversed(list(zip(picks, slopes, outs))):
        skip = pick.shape[0] - out.shape[0]
        out[...] = pair_grads(spread, pick[skip:, :], slope[skip:, :])


def relay_kernel(first, own, passed, *refs):
    rows = passed.shape[0]
    out = refs[0] if len(refs) == 1 else refs[-2]
    out[...] = (own[first : first + rows, :].astype(f32) + passed[...].astype(f32)).astype(bf16)
    if len(refs) > 1:
        refs[-1][...] = refs[0][...]


def sum_kernel(own, piece, total):
    total[...] = own[0 : piece.shape[0], :].astype(f32) + piece[...].astype(f32)


def grid_kernel(whole, *refs):
    blocks, pieces, (w_grid, out) = refs[:whole], refs[whole:-2], refs[-2:]
    if not pieces:
        total = blocks[0][...].astype(f32)
        for block in blocks[1:]:
            total = total + block[...].astype(f32)
        out[...] = dot_back(total.astype(bf16), w_grid[...])
        return
    (own, near), (summed, second) = blocks, pieces
    first = summed.shape[0]
    total = summed[...] + near[0:first, :].astype(f32)
    out[0:first, :] = dot_back(total.astype(bf16), w_grid[...])
    total = own[first:, :].astype(f32) + near[first:, :].astype(f32) + second[...].astype(f32)
    out[first:, :] = dot_back(total.astype(bf16), w_grid[...])


def shifted(value, axis, by):
    size = lax.axis_size(axis)
    return lax.ppermute(value, axis, [(at, (at + by) % size) for at in range(size)])


def partner(at, step, size):
    return at ^ step if size & (size - 1) == 0 else (at + step) % size


def sent_to(value, step):
    size = lax.axis_size("mesh")
    return lax.ppermute(value, "mesh", [(at, partner(at, step, size)) for at in range(size)])


def sent_back(value, step):
    size = lax.axis_size("mesh")
    return lax.ppermute(value, "mesh", [(partner(at, step, size), at) for at in range(size)])


def in_order(pieces, axis):
    return jnp.roll(jnp.stack(pieces)[::-1], lax.axis_index(axis) + 1, axis=0)


def on_device(
    grid_feats,
    g2m_shard,
    g2m_node,
    mesh_init,
    sender_slots,
    receivers,
    halo_index,
    w_enc_grid,
    w_enc_mesh,
    w_enc_out,
    enc_gain,
    w_send,
    w_recv,
    w_out,
    layer_gain,
    out_cot,
):
    shards = lax.axis_size("mesh")
    shard = lax.axis_index("mesh")
    halves = lax.axis_size("rep")
    feats = lax.axis_size("feat")
    nodes, width = mesh_init.shape
    grid, tops = g2m_shard.shape
    edges = sender_slots.shape[0]
    depth = halo_index.shape[2]
    shifts = shards - 1
    listed_rows = shifts * depth
    wide = -(-listed_rows // LANES) * LANES
    all_edges = edges * halves * feats
    enc_gain = enc_gain[None, :]

    relayed = shards == 4
    cuts = 2 if relayed else 1
    piece_rows = grid // cuts
    in_place = [pltpu.with_memory_space_constraint(array, pltpu.HBM) for array in (grid_feats, g2m_shard.T, g2m_node.T)]
    (payload,) = call(
        note_kernel,
        [((piece_rows + EXTRA, width), bf16)],
        [((tops, grid), i32), ((tops, grid), i32)],
        copied=True,
    )(*in_place)

    place = sender_slots - nodes
    away = partner(shard, place // depth, shards)
    if shards & (shards - 1):
        away = lax.rem(shard - place // depth + shards, shards)
    core = lax.axis_index("rep")
    shared = shards == 4 and halves == 2
    steps = jnp.arange(1, shards, dtype=i32)
    if shared:
        steps = jnp.where((core == 1) & (steps < 3), 3 - steps, steps)
    slots = jnp.where(sender_slots < nodes, sender_slots, nodes + (away - 1) * depth + place % depth)
    both = jnp.stack([slots, receivers])
    others = [shifted(both, "rep", step) for step in range(1, halves)]
    if relayed:
        left, whole = call(
            functools.partial(left_kernel, piece_rows),
            [((grid - piece_rows, width), bf16), ((grid + EXTRA, width), bf16)],
            copied=True,
        )(in_place[0], payload, others[0])
        across = [sent_to(payload, 2), sent_to(left, 2)]
        payloads = [[whole], [sent_to(whole, 1)], across, [sent_to(across[0], 1)]]
    else:
        payloads = [[payload]] + [[sent_to(payload, step)] for step in range(1, shards)]
    both = in_order([both] + others, "rep")
    both = in_order([both] + [shifted(both, "feat", step) for step in range(1, feats)], "feat")
    both = both.reshape(feats * halves, 2, edges)
    all_slots, all_receivers = both[:, 0].reshape(1, -1), both[:, 1].reshape(1, -1)
    if shared:
        entry = all_slots - nodes
        moved = jnp.where(entry < depth, depth, -depth)
        turned = (core == 1) & (entry >= 0) & (entry < 2 * depth)
        all_slots = all_slots + jnp.where(turned, moved, 0)
    readers = partner(shard, steps, shards)
    lists = jnp.take(halo_index[0], readers, axis=0).reshape(1, -1)
    here, there, halo_here, halo_there, list_here, list_there = call(
        place_kernel,
        [
            ((all_edges, 2 * nodes), bf16),
            ((2 * nodes, all_edges), bf16),
            ((all_edges, wide), bf16),
            ((wide, all_edges), bf16),
            ((listed_rows, nodes), bf16),
            ((nodes, listed_rows), bf16),
        ],
        products=[(all_edges, nodes, width), (all_edges, 2 * nodes, width)],
    )(all_slots, all_receivers, lists)

    if relayed:
        across[-1], list_here = lax.optimization_barrier((across[-1], list_here))
        payloads[-1].append(sent_to(across[-1], 1))

    meta = jnp.broadcast_to(jnp.stack([core, shard]).astype(i32)[:, None], (2, width))
    node_f32, node_bf16 = ((nodes, width), f32), ((nodes, width), bf16)
    row_shape, half = ((grid, width), bf16), nodes // halves
    square = (nodes, width, width)
    enc_picks, enc_slopes = [], []
    base, total = mesh_init, None
    groups = [payloads[:2]] + [payloads[at : at + 1] for at in range(2, shards)]
    for at, group in enumerate(groups):
        first, last = at == 0, at == len(groups) - 1
        count = len(group)
        outs = [((grid, nodes), bf16)] * count + [row_shape] * count
        outs += [node_bf16] if first else []
        outs += [((half, width), f32)] + [((half, width), bf16)] * (halves - 1) if last else [node_f32]
        got = list(
            call(
                functools.partial(encode_kernel, [len(block) for block in group], first, last, halves),
                outs,
                (),
                [square] * first + [(grid, width, width), (grid, nodes, width), (nodes, grid, width)] * count,
            )(
                meta, base, w_enc_grid, *((w_enc_mesh, list_here) if first else (total,)), *(piece for block in group for piece in block)
            )
        )
        enc_picks += got[:count]
        enc_slopes += got[count : 2 * count]
        del got[: 2 * count]
        if first:
            base = got.pop(0)
        total = got[0]
    part = got[0]
    for step in range(1, halves):
        part = part + shifted(got[step], "rep", step).astype(f32)
    part = part.astype(bf16)
    pieces = [part] + [shifted(part, "feat", step) for step in range(1, feats)]
    if feats > 2:
        pieces = list(in_order(pieces, "feat"))
    part = sum(piece.astype(f32) for piece in pieces).astype(bf16)
    parts = [part] + [shifted(part, "rep", -step) for step in range(1, halves)]

    spots = (0, 2 * depth) if shared else tuple(range(0, listed_rows, depth))
    listed = [((depth, width), bf16)] * len(spots)

    def exchange(blocks, send, early):
        if not shared:
            return [send(block, step + 1) for step, block in enumerate(blocks)], early
        first = lax.ppermute(
            blocks[0], ("mesh", "rep"), [(2 * at + side, 2 * (at ^ 1 + side) + side) for at in range(4) for side in range(2)]
        )
        third = send(blocks[1], 3)
        first, third, early = lax.optimization_barrier((first, third, early))
        return [first, shifted(first, "rep", 1), third], early

    hidden, enc_sum, sent, *outgoing = call(
        functools.partial(start_kernel, halves, spots), [node_bf16, node_f32, node_bf16] + listed, [node_bf16],
        [square, square, (listed_rows, nodes, width)],
    )(meta, *parts, mesh_init, w_enc_out, enc_gain, w_send, list_here)

    half_f32, edge_bf16 = ((all_edges // 2, width), f32), ((all_edges, width), bf16)
    halo, back_halo = ((wide, width), bf16), ((listed_rows, width), bf16)
    forward_products = [(all_edges, wide, width), (nodes, all_edges, width), square]
    backward_products = [square, (all_edges, nodes, width), (wide, all_edges, width)]
    half_product = (all_edges // 2, 2 * nodes, width)

    def arriving(layer):
        early = call(
            functools.partial(local_kernel, layer), [half_f32, ((2 * nodes, width), bf16)], (), [square, half_product]
        )(hidden, sent, here, w_recv)
        halos, (pre, both_tables) = exchange(outgoing, sent_to, early)
        (more,) = call(local_more_kernel, [half_f32], (), [half_product])(both_tables, here)
        return hidden, pre, more, *halos

    records = []
    for layer in range(LAYERS - 1):
        hidden, agg, slope, sent, *outgoing = call(
            functools.partial(layer_kernel, layer, shifts, spots),
            [node_bf16, node_f32, edge_bf16, node_bf16] + listed,
            [halo, edge_bf16],
            forward_products + [square, (listed_rows, nodes, width)],
        )(*arriving(layer), halo_here, there, w_out, layer_gain, w_send, list_here)
        records.append((agg, slope))
    last = LAYERS - 1
    final_mesh, grad_pre, *outgoing = call(
        functools.partial(turn_kernel, last, shifts, spots), [node_bf16, edge_bf16] + listed, [edge_bf16, halo],
        forward_products + backward_products,
    )(*arriving(last), halo_here, there, w_out, layer_gain, here, halo_there, out_cot)
    upstream = out_cot
    for layer in reversed(range(LAYERS)):

        def rest_of(side, upstream, weights):
            (rest,) = call(
                functools.partial(rest_kernel, layer, side), [node_f32], (), [(nodes, all_edges, width), square]
            )(upstream, grad_pre, there, weights)
            return rest

        returned, early = exchange(outgoing, sent_back, rest_of(0, upstream, w_send))
        rest = rest_of(1, early, w_recv)
        if layer:
            agg, slope = records[layer - 1]
            upstream, grad_pre, *outgoing = call(
                functools.partial(back_kernel, layer - 1, shifts, spots),
                [node_f32, edge_bf16] + listed,
                [back_halo],
                backward_products + [(listed_rows, width, width), (nodes, listed_rows, width)],
            )(rest, *returned, list_there, w_send, agg, slope, layer_gain, w_out, here, halo_there)
    piece = ((piece_rows, width), bf16)
    one = (grid, nodes, width)
    spread, *far = call(
        functools.partial(finish_kernel, shifts),
        [node_bf16] + [piece] * cuts,
        [back_halo],
        [square, (listed_rows, width, width), (nodes, listed_rows, width), one],
    )(rest, *returned, list_there, w_send, enc_sum, enc_gain, w_enc_out, enc_picks[-1], enc_slopes[-1])
    blocks = call(
        functools.partial(others_kernel, shards - 1), [row_shape] * (shards - 1), products=[one] * (shards - 1)
    )(spread, *enc_picks[:-1], *enc_slopes[:-1])
    if relayed:
        passed = [sent_back(block, 1) for block in far]
        first, near = call(functools.partial(relay_kernel, 0), [piece, row_shape])(blocks[2], passed[0], blocks[1])
        (second,) = call(functools.partial(relay_kernel, piece_rows), [piece])(blocks[2], passed[1])
        near = sent_back(near, 1)
        first, second = sent_back(first, 2), sent_back(second, 2)
        (summed,) = call(sum_kernel, [((piece_rows, width), f32)])(blocks[0], first)
        (grid_grad,) = call(
            functools.partial(grid_kernel, 2), [((grid, width), f32)], products=[(grid, width, width)]
        )(blocks[0], near, summed, second, w_enc_grid)
    else:
        blocks = [*blocks, *far]
        blocks = [blocks[0]] + [sent_back(block, step) for step, block in enumerate(blocks) if step]
        (grid_grad,) = call(
            functools.partial(grid_kernel, shards), [((grid, width), f32)], products=[(grid, width, width)]
        )(*blocks, w_enc_grid)
    return (final_mesh, grid_grad)


def solution(mesh):
    return jax.shard_map(
        on_device,
        mesh=mesh,
        in_specs=(
            P(("groups", "mesh", "feat", "rep"), None),
            P(("groups", "mesh", "feat", "rep"), None),
            P(("groups", "mesh", "feat", "rep"), None),
            P(("groups", "mesh"), None),
            P(("groups", "mesh", "feat", "rep")),
            P(("groups", "mesh", "feat", "rep")),
            P(("groups", "mesh"), None, None),
            P(),
            P(),
            P(),
            P(),
            P(),
            P(),
            P(),
            P(),
            P(("groups", "mesh"), None),
        ),
        out_specs=(P(("groups", "mesh"), None), P(("groups", "mesh", "feat", "rep"), None)),
        check_vma=False,
    )
```

```python
import functools
import math

import jax
import jax.numpy as jnp
from jax import lax
from jax.experimental import pallas as pl
from jax.experimental.pallas import tpu as pltpu
from jax.sharding import PartitionSpec as P

LAYERS = 3
LANES = 128
BLOCK = 512
EXTRA = 16
eps = 1e-05

f32 = jnp.float32
bf16 = jnp.bfloat16
i32 = jnp.int32


def norm_scale(totals):
    return lax.rsqrt(jnp.mean(totals * totals, axis=-1, keepdims=True) + eps)


def norm_back(totals, gain_row, upstream):
    scaled = norm_scale(totals)
    normed = totals * scaled
    slope = upstream * gain_row
    return scaled * (slope - normed * jnp.mean(slope * normed, axis=-1, keepdims=True))


def dot(left, right):
    return jnp.dot(left, right, preferred_element_type=f32)


def dot_back(left, right):
    return lax.dot_general(left, right, (((1,), (1,)), ((), ())), preferred_element_type=f32)


def gated(pre):
    sigma = 0.5 * jnp.tanh(0.5 * pre) + 0.5
    act = pre * sigma
    return act, sigma + act * (1.0 - sigma)


def as_mask(hit):
    return jnp.where(hit, 1.0, 0.0).astype(bf16)


def pick_columns(index, first, height):
    place = lax.broadcasted_iota(i32, (height, index.shape[1]), 0) + first
    return as_mask(place == index)


def upright(index):
    count = index.shape[1]
    if count < LANES:
        index = jnp.concatenate([index, jnp.full((1, LANES - count), -1, i32)], axis=1)
    return jnp.broadcast_to(index, (LANES, LANES)).T[:count]


def pick_rows(column, first, width):
    lane = lax.broadcasted_iota(i32, column.shape, 1) + first
    return jnp.concatenate([as_mask(column == lane + at) for at in range(0, width, LANES)], axis=1)


def call(body, outs, scratch=(), products=(), copied=False):
    def run(*args):
        def where(array):
            if copied:
                return pl.BlockSpec(memory_space=pltpu.HBM)
            return pl.BlockSpec(memory_space=pltpu.SMEM if array.dtype == i32 and array.ndim == 1 else pltpu.VMEM)

        def size(shape, dtype):
            return jnp.dtype(dtype).itemsize * math.prod(shape)

        own = sum(size(*held) for held in scratch) + (10 << 20)
        moved = sum(array.dtype.itemsize * array.size for array in args) + sum(size(*out) for out in outs)
        limit = own if own + moved < 40 << 20 else min(own + moved, 60 << 20)
        semaphores = [pltpu.SemaphoreType.DMA((2 + len(outs),))] if copied else []
        return pl.pallas_call(
            body,
            out_shape=tuple(jax.ShapeDtypeStruct(shape, dtype) for shape, dtype in outs),
            in_specs=[where(array) for array in args],
            out_specs=tuple(pl.BlockSpec(memory_space=pltpu.VMEM) for _ in outs),
            scratch_shapes=[pltpu.VMEM(shape, dtype) for shape, dtype in scratch] + semaphores,
            compiler_params=pltpu.CompilerParams(vmem_limit_bytes=limit),
            cost_estimate=pl.CostEstimate(
                flops=2 * sum(math.prod(product) for product in products), bytes_accessed=moved, transcendentals=0
            ),
        )(*args)

    return run


def place_kernel(slots, receivers, order, here, there, halo_here, halo_there, list_here, list_there):
    nodes = here.shape[1] // 2
    wide = halo_here.shape[1]

    def body(at):
        block = pl.ds(pl.multiple_of(at * LANES, LANES), LANES)
        slot, receiver = slots[:, block], receivers[:, block]
        slot_column, receiver_column = upright(slot), upright(receiver)
        here[block, 0:nodes] = pick_rows(slot_column, 0, nodes)
        here[block, nodes:] = pick_rows(receiver_column, 0, nodes)
        halo_here[block, :] = pick_rows(slot_column, nodes, wide)
        there[0:nodes, block] = pick_columns(slot, 0, nodes)
        there[nodes:, block] = pick_columns(receiver, 0, nodes)
        halo_there[:, block] = pick_columns(slot, nodes, wide)

    pl.loop(0, slots.shape[1] // LANES)(body)
    count = order.shape[1]
    for at in range(0, count, LANES):
        end = min(at + LANES, count)
        list_here[at:end, :] = pick_rows(upright(order[:, at:end]), 0, nodes)
    list_there[...] = pick_columns(order[...], 0, nodes)


def note_kernel(rows, shards, nodes, payload, shard_rows, node_rows, arrived):
    grid = shards.shape[1]
    first = payload.shape[0] - EXTRA
    copies = [
        pltpu.make_async_copy(shards, shard_rows, arrived.at[0]),
        pltpu.make_async_copy(nodes, node_rows, arrived.at[1]),
        pltpu.make_async_copy(rows.at[0:first], payload.at[0:first], arrived.at[2]),
    ]
    for copy in copies:
        copy.start()
    for copy in copies[:2]:
        copy.wait()
    row = lax.broadcasted_iota(i32, (EXTRA, grid), 0)
    notes = jnp.full((EXTRA, grid), -1, i32)
    for top in range(shards.shape[0]):
        node = node_rows[top : top + 1, :]
        for at, value in enumerate((shard_rows[top : top + 1, :], node & 255, node >> 8)):
            notes = jnp.where(row == 3 * top + at, value, notes)
    payload[first:, 0:grid] = notes.astype(f32).astype(bf16)
    if grid < payload.shape[1]:
        payload[first:, grid:] = jnp.zeros((EXTRA, payload.shape[1] - grid), bf16)
    copies[2].wait()


def again_kernel(payload, _, out, arrived):
    copy = pltpu.make_async_copy(payload, out, arrived.at[0])
    copy.start()
    copy.wait()


def encode_kernel(steps, first, last, halves, *refs):
    refs = list(refs)
    meta, base, w_grid = refs[:3]
    del refs[:3]
    if first:
        w_mesh, _ = refs.pop(0), refs.pop(0)
        projected = dot(base[...], w_mesh[...]).astype(bf16)
    else:
        total_in = refs.pop(0)
        projected = base[...]
    payloads = refs[:steps]
    del refs[:steps]
    picks, slopes = refs[:steps], refs[steps : 2 * steps]
    del refs[: 2 * steps]
    total = None if first else total_in[...]
    nodes = projected.shape[0]
    for payload, pick, slope_out in zip(payloads, picks, slopes):
        grid = pick.shape[0]
        notes = payload[grid:, 0:grid].astype(f32)
        target = jnp.full((1, grid), -1.0, f32)
        for at in range(0, notes.shape[0] // 3 * 3, 3):
            named = notes[at : at + 1] == meta[1:2, 0:grid].astype(f32)
            target = jnp.where(named, notes[at + 1 : at + 2] + 256.0 * notes[at + 2 : at + 3], target)
        target = target.astype(i32)
        column = jnp.concatenate([upright(target[:, at : at + LANES]) for at in range(0, grid, LANES)], axis=0)
        picked = pick_rows(column, 0, nodes)
        pick[...] = picked
        pre = dot(payload[0:grid, :], w_grid[...]) + dot(picked, projected)
        act, slope = gated(pre)
        slope_out[...] = slope.astype(bf16)
        added = dot(pick_columns(target, 0, nodes), act.astype(bf16))
        total = added if total is None else total + added
    if first:
        refs.pop(0)[...] = projected
    if not last:
        refs[0][...] = total
        return
    keep, sends = refs[0], refs[1:halves]
    part = nodes // halves
    own = meta[0:1, :]

    def half(shift):
        rows = total[0:part]
        for at in range(1, halves):
            rows = jnp.where(own == (at - shift) % halves, total[at * part : (at + 1) * part], rows)
        return rows

    keep[...] = half(0)
    for shift in range(1, halves):
        sends[shift - 1][...] = half(shift).astype(bf16)


def hand_out(rows, outs, spots):
    rows = rows.astype(bf16)
    for out, (first, count) in zip(outs, spots):
        out[...] = rows[first : first + count]


def start_kernel(halves, spots, *refs):
    meta = refs[0]
    parts = refs[1 : 1 + halves]
    mesh_init, w_enc_out, gain, w_send, list_here = refs[1 + halves : 6 + halves]
    hidden_out, enc_sum_out, sent = refs[6 + halves : 9 + halves]
    outs = refs[9 + halves : -1]
    whole = refs[-1]
    part = parts[0].shape[0]
    own = meta[0:1, :]
    for at in range(halves):
        rows = parts[0][...].astype(f32)
        for shift in range(1, halves):
            rows = jnp.where(own == (at - shift) % halves, parts[shift][...].astype(f32), rows)
        whole[at * part : (at + 1) * part, :] = rows.astype(bf16)
    enc_sum = dot(whole[...], w_enc_out[...])
    enc_sum_out[...] = enc_sum
    hidden = (mesh_init[...].astype(f32) + enc_sum * norm_scale(enc_sum) * gain[...]).astype(bf16)
    hidden_out[...] = hidden
    projected = dot(hidden, w_send[0]).astype(bf16)
    sent[...] = projected
    hand_out(dot(list_here[...], projected), outs, spots)


def local_kernel(layer, hidden, sent, here, w_recv, pre, table):
    nodes = hidden.shape[0]
    table[0:nodes, :] = sent[...]
    table[nodes:, :] = dot(hidden[...], w_recv[layer]).astype(bf16)
    for at in range(0, pre.shape[0], BLOCK):
        pre[at : at + BLOCK, :] = dot(here[at : at + BLOCK, :], table[...])


def local_more_kernel(table, here, pre):
    skip = here.shape[0] - pre.shape[0]
    for at in range(0, pre.shape[0], BLOCK):
        pre[at : at + BLOCK, :] = dot(here[skip + at : skip + at + BLOCK, :], table[...])


def pass_kernel(own, got, out):
    rows = own.shape[0]
    out[0:rows, :] = own[...]
    out[rows:, :] = got[rows:, :]


def stack_halo(inward, halos, halo):
    at = 0
    for rows, block in zip(inward, halos):
        halo[at : at + rows, :] = block[0:rows, :]
        at += rows
    if at < halo.shape[0]:
        halo[at:, :] = jnp.zeros((halo.shape[0] - at, halo.shape[1]), bf16)


def node_sum(inward, pres, halos, halo_here, there, slope_out, halo, act_out):
    nodes = there.shape[0] // 2
    stack_halo(inward, halos, halo)
    half = pres[0].shape[0]
    for at in range(0, 2 * half, BLOCK):
        block = slice(at, at + BLOCK)
        pre = pres[at // half][at % half : at % half + BLOCK, :]
        act, slope = gated(pre + dot(halo_here[block, :], halo[...]))
        slope_out[block, :] = slope.astype(bf16)
        act_out[block, :] = act.astype(bf16)
    return dot(there[nodes:, :], act_out[...])


def layer_kernel(layer, inward, spots, *refs):
    hidden, pres = refs[0], refs[1:3]
    halos, refs = refs[3 : 3 + len(inward)], refs[3 + len(inward) :]
    halo_here, there, w_out, gain, w_send, list_here = refs[:6]
    hidden_out, agg_out, slope_out, sent_out = refs[6:10]
    outs = refs[10:-2]
    total = node_sum(inward, pres, halos, halo_here, there, slope_out, *refs[-2:])
    agg = dot(total.astype(bf16), w_out[layer])
    agg_out[...] = agg
    fresh = (hidden[...].astype(f32) + agg * norm_scale(agg) * gain[layer : layer + 1, :]).astype(bf16)
    hidden_out[...] = fresh
    projected = dot(fresh, w_send[layer + 1]).astype(bf16)
    sent_out[...] = projected
    hand_out(dot(list_here[...], projected), outs, spots)


def edge_grads(grad_agg, w_out, here, halo_there, slope, grad_pre, outs, spots):
    nodes = grad_agg.shape[0]
    spread = dot_back(grad_agg.astype(bf16), w_out).astype(bf16)
    for at in range(0, slope.shape[0], BLOCK):
        block = slice(at, at + BLOCK)
        grad_act = dot(here[block, nodes:], spread)
        grad_pre[block, :] = (grad_act * slope[block, :].astype(f32)).astype(bf16)
    hand_out(dot(halo_there[...], grad_pre[...]), outs, spots)


def turn_kernel(layer, inward, spots, *refs):
    hidden, pres = refs[0], refs[1:3]
    halos, refs = refs[3 : 3 + len(inward)], refs[3 + len(inward) :]
    halo_here, there, w_out, gain, here, halo_there, cot = refs[:7]
    hidden_out, grad_pre = refs[7:9]
    outs = refs[9:-2]
    slope, halo = refs[-2:]
    total = node_sum(inward, pres, halos, halo_here, there, slope, halo, grad_pre)
    agg = dot(total.astype(bf16), w_out[layer])
    gain_row = gain[layer : layer + 1, :]
    hidden_out[...] = (hidden[...].astype(f32) + agg * norm_scale(agg) * gain_row).astype(bf16)
    edge_grads(norm_back(agg, gain_row, cot[...].astype(f32)), w_out[layer], here, halo_there, slope, grad_pre, outs, spots)


def rest_kernel(layer, side, upstream, grad_pre, there, weights, rest):
    nodes = upstream.shape[0]
    sums = dot(there[side * nodes : (side + 1) * nodes, :], grad_pre[...]).astype(bf16)
    rest[...] = upstream[...].astype(f32) + dot_back(sums, weights[layer])


def arrived(inward, rest, returned, list_there, w_send, halo):
    stack_halo(inward, returned, halo)
    projected = dot_back(halo[...], w_send).astype(bf16)
    return rest[...] + dot(list_there[...], projected)


def back_kernel(layer, inward, spots, *refs):
    rest = refs[0]
    returned, refs = refs[1 : 1 + len(inward)], refs[1 + len(inward) :]
    list_there, w_send, agg, slope, gain, w_out, here, halo_there = refs[:8]
    upstream_out, grad_pre = refs[8:10]
    outs = refs[10:-1]
    halo = refs[-1]
    upstream = arrived(inward, rest, returned, list_there, w_send[layer + 1], halo)
    upstream_out[...] = upstream
    grad_agg = norm_back(agg[...], gain[layer : layer + 1, :], upstream)
    edge_grads(grad_agg, w_out[layer], here, halo_there, slope, grad_pre, outs, spots)


def pair_grads(spread, pick, slope):
    return (dot(pick, spread) * slope.astype(f32)).astype(bf16)


def finish_kernel(inward, *refs):
    rest = refs[0]
    returned, refs = refs[1 : 1 + len(inward)], refs[1 + len(inward) :]
    list_there, w_send, enc_sum, gain, w_enc_out, pick, slope, spread_out = refs[:8]
    outs, halo = refs[8:-1], refs[-1]
    upstream = arrived(inward, rest, returned, list_there, w_send[0], halo)
    spread = dot_back(norm_back(enc_sum[...], gain[...], upstream).astype(bf16), w_enc_out[...]).astype(bf16)
    spread_out[...] = spread
    at = 0
    for out in outs:
        rows = slice(at, at + out.shape[0])
        out[...] = pair_grads(spread, pick[rows, :], slope[rows, :])
        at += out.shape[0]


def others_kernel(count, *refs):
    spread = refs[0][...]
    picks, slopes, outs = refs[1 : 1 + count], refs[1 + count : 1 + 2 * count], refs[1 + 2 * count :]
    for pick, slope, out in reversed(list(zip(picks, slopes, outs))):
        skip = pick.shape[0] - out.shape[0]
        out[...] = pair_grads(spread, pick[skip:, :], slope[skip:, :])


def relay_kernel(first, own, passed, *refs):
    rows = passed.shape[0]
    out = refs[0] if len(refs) == 1 else refs[-2]
    out[...] = (own[first : first + rows, :].astype(f32) + passed[...].astype(f32)).astype(bf16)
    if len(refs) > 1:
        refs[-1][...] = refs[0][...]


def sum_kernel(own, piece, total):
    total[...] = own[0 : piece.shape[0], :].astype(f32) + piece[...].astype(f32)


def grid_kernel(whole, *refs):
    blocks, pieces, (w_grid, out) = refs[:whole], refs[whole:-2], refs[-2:]
    if not pieces:
        total = blocks[0][...].astype(f32)
        for block in blocks[1:]:
            total = total + block[...].astype(f32)
        out[...] = dot_back(total.astype(bf16), w_grid[...])
        return
    (own, near), (summed, second) = blocks, pieces
    first = summed.shape[0]
    total = summed[...] + near[0:first, :].astype(f32)
    out[0:first, :] = dot_back(total.astype(bf16), w_grid[...])
    total = own[first:, :].astype(f32) + near[first:, :].astype(f32) + second[...].astype(f32)
    out[first:, :] = dot_back(total.astype(bf16), w_grid[...])


def shifted(value, axis, by):
    size = lax.axis_size(axis)
    return lax.ppermute(value, axis, [(at, (at + by) % size) for at in range(size)])


def partner(at, step, size):
    return at ^ step if size & (size - 1) == 0 else (at + step) % size


def sent_to(value, step):
    size = lax.axis_size("mesh")
    return lax.ppermute(value, "mesh", [(at, partner(at, step, size)) for at in range(size)])


def sent_back(value, step):
    size = lax.axis_size("mesh")
    return lax.ppermute(value, "mesh", [(partner(at, step, size), at) for at in range(size)])


def in_order(pieces, axis):
    return jnp.roll(jnp.stack(pieces)[::-1], lax.axis_index(axis) + 1, axis=0)


def on_device(
    grid_feats,
    g2m_shard,
    g2m_node,
    mesh_init,
    sender_slots,
    receivers,
    halo_index,
    w_enc_grid,
    w_enc_mesh,
    w_enc_out,
    enc_gain,
    w_send,
    w_recv,
    w_out,
    layer_gain,
    out_cot,
):
    shards = lax.axis_size("mesh")
    shard = lax.axis_index("mesh")
    halves = lax.axis_size("rep")
    feats = lax.axis_size("feat")
    nodes, width = mesh_init.shape
    grid, tops = g2m_shard.shape
    edges = sender_slots.shape[0]
    depth = halo_index.shape[2]
    shifts = shards - 1
    listed_rows = shifts * depth
    wide = -(-listed_rows // LANES) * LANES
    all_edges = edges * halves * feats
    enc_gain = enc_gain[None, :]

    relayed = shards == 4
    cuts = 2 if relayed else 1
    piece_rows = grid // cuts
    in_place = [pltpu.with_memory_space_constraint(array, pltpu.HBM) for array in (grid_feats, g2m_shard.T, g2m_node.T)]
    (payload,) = call(
        note_kernel,
        [((grid + EXTRA, width), bf16)],
        [((tops, grid), i32), ((tops, grid), i32)],
        copied=True,
    )(*in_place)

    payload, sender_slots = lax.optimization_barrier((payload, sender_slots))
    place = sender_slots - nodes
    away = partner(shard, place // depth, shards)
    if shards & (shards - 1):
        away = lax.rem(shard - place // depth + shards, shards)
    if relayed:
        away = jnp.where(away < 3, 3 - away, away)
    slots = jnp.where(sender_slots < nodes, sender_slots, nodes + (away - 1) * depth + place % depth)
    both = jnp.stack([slots, receivers])
    others = [shifted(both, "rep", step) for step in range(1, halves)]
    if relayed:
        across = sent_to(payload, 2)
        (again,) = call(again_kernel, [((grid + EXTRA, width), bf16)], copied=True)(payload, others[0])
        payloads = [again, sent_to(again, 1), across]
    else:
        payloads = [payload] + [sent_to(payload, step) for step in range(1, shards)]
    both = in_order([both] + others, "rep")
    both = in_order([both] + [shifted(both, "feat", step) for step in range(1, feats)], "feat")
    both = both.reshape(feats * halves, 2, edges)
    all_slots, all_receivers = both[:, 0].reshape(1, -1), both[:, 1].reshape(1, -1)
    readers = partner(shard, jnp.arange(1, shards, dtype=i32), shards)
    lists = jnp.take(halo_index[0], readers, axis=0).reshape(1, -1)
    here, there, halo_here, halo_there, list_here, list_there = call(
        place_kernel,
        [
            ((all_edges, 2 * nodes), bf16),
            ((2 * nodes, all_edges), bf16),
            ((all_edges, wide), bf16),
            ((wide, all_edges), bf16),
            ((listed_rows, nodes), bf16),
            ((nodes, listed_rows), bf16),
        ],
        products=[(all_edges, nodes, width), (all_edges, 2 * nodes, width)],
    )(all_slots, all_receivers, lists)

    if relayed:
        across, list_here = lax.optimization_barrier((across, list_here))
        payloads.append(sent_to(across, 1))

    meta = jnp.broadcast_to(jnp.stack([lax.axis_index("rep"), shard]).astype(i32)[:, None], (2, width))
    node_f32, node_bf16 = ((nodes, width), f32), ((nodes, width), bf16)
    row_shape, half = ((grid, width), bf16), nodes // halves
    square = (nodes, width, width)
    enc_picks, enc_slopes = [], []
    base, total = mesh_init, None
    groups = [payloads[:2]] + [payloads[at : at + 1] for at in range(2, shards)]
    for at, group in enumerate(groups):
        first, last = at == 0, at == len(groups) - 1
        count = len(group)
        outs = [((grid, nodes), bf16)] * count + [row_shape] * count
        outs += [node_bf16] if first else []
        outs += [((half, width), f32)] + [((half, width), bf16)] * (halves - 1) if last else [node_f32]
        got = list(
            call(
                functools.partial(encode_kernel, count, first, last, halves),
                outs,
                (),
                [square] * first + [(grid, width, width), (grid, nodes, width), (nodes, grid, width)] * count,
            )(
                meta, base, w_enc_grid, *((w_enc_mesh, list_here) if first else (total,)), *group
            )
        )
        enc_picks += got[:count]
        enc_slopes += got[count : 2 * count]
        del got[: 2 * count]
        if first:
            base = got.pop(0)
        total = got[0]
    part = got[0]
    for step in range(1, halves):
        part = part + shifted(got[step], "rep", step).astype(f32)
    part = part.astype(bf16)
    pieces = [part] + [shifted(part, "feat", step) for step in range(1, feats)]
    if feats > 2:
        pieces = list(in_order(pieces, "feat"))
    part = sum(piece.astype(f32) for piece in pieces).astype(bf16)
    parts = [part] + [shifted(part, "rep", -step) for step in range(1, halves)]

    spots = [(depth, 2 * depth), (0, depth)] if relayed else [(at, depth) for at in range(0, listed_rows, depth)]
    inward = [depth, 2 * depth] if relayed else [depth] * shifts
    listed = [((rows, width), bf16) for _, rows in spots]

    def exchange(blocks, send, early, stages):
        if not relayed:
            return [send(block, step + 1) for step, block in enumerate(blocks)], early
        got = send(blocks[0], stages[0])
        got, early = lax.optimization_barrier((got, early))
        (both_blocks,) = call(pass_kernel, [((2 * depth, width), bf16)])(blocks[1], got)
        return [got, send(both_blocks, stages[1])], early

    hidden, enc_sum, sent, *outgoing = call(
        functools.partial(start_kernel, halves, spots), [node_bf16, node_f32, node_bf16] + listed, [node_bf16],
        [square, square, (listed_rows, nodes, width)],
    )(meta, *parts, mesh_init, w_enc_out, enc_gain, w_send, list_here)

    half_f32, edge_bf16 = ((all_edges // 2, width), f32), ((all_edges, width), bf16)
    halo, back_halo = ((wide, width), bf16), ((listed_rows, width), bf16)
    forward_products = [(all_edges, wide, width), (nodes, all_edges, width), square]
    backward_products = [square, (all_edges, nodes, width), (wide, all_edges, width)]
    half_product = (all_edges // 2, 2 * nodes, width)

    def arriving(layer):
        early = call(
            functools.partial(local_kernel, layer), [half_f32, ((2 * nodes, width), bf16)], (), [square, half_product]
        )(hidden, sent, here, w_recv)
        halos, (pre, both_tables) = exchange(outgoing, sent_to, early, (2, 1))
        (more,) = call(local_more_kernel, [half_f32], (), [half_product])(both_tables, here)
        return hidden, pre, more, *halos

    records = []
    for layer in range(LAYERS - 1):
        hidden, agg, slope, sent, *outgoing = call(
            functools.partial(layer_kernel, layer, inward, spots),
            [node_bf16, node_f32, edge_bf16, node_bf16] + listed,
            [halo, edge_bf16],
            forward_products + [square, (listed_rows, nodes, width)],
        )(*arriving(layer), halo_here, there, w_out, layer_gain, w_send, list_here)
        records.append((agg, slope))
    last = LAYERS - 1
    final_mesh, grad_pre, *outgoing = call(
        functools.partial(turn_kernel, last, inward, spots), [node_bf16, edge_bf16] + listed, [edge_bf16, halo],
        forward_products + backward_products,
    )(*arriving(last), halo_here, there, w_out, layer_gain, here, halo_there, out_cot)
    upstream = out_cot
    for layer in reversed(range(LAYERS)):

        def rest_of(side, upstream, weights):
            (rest,) = call(
                functools.partial(rest_kernel, layer, side), [node_f32], (), [(nodes, all_edges, width), square]
            )(upstream, grad_pre, there, weights)
            return rest

        returned, early = exchange(outgoing, sent_back, rest_of(0, upstream, w_send), (1, 2))
        rest = rest_of(1, early, w_recv)
        if layer:
            agg, slope = records[layer - 1]
            upstream, grad_pre, *outgoing = call(
                functools.partial(back_kernel, layer - 1, inward, spots),
                [node_f32, edge_bf16] + listed,
                [back_halo],
                backward_products + [(listed_rows, width, width), (nodes, listed_rows, width)],
            )(rest, *returned, list_there, w_send, agg, slope, layer_gain, w_out, here, halo_there)
    piece = ((piece_rows, width), bf16)
    one = (grid, nodes, width)
    spread, *far = call(
        functools.partial(finish_kernel, inward),
        [node_bf16] + [piece] * cuts,
        [back_halo],
        [square, (listed_rows, width, width), (nodes, listed_rows, width), one],
    )(rest, *returned, list_there, w_send, enc_sum, enc_gain, w_enc_out, enc_picks[-1], enc_slopes[-1])
    blocks = call(
        functools.partial(others_kernel, shards - 1), [row_shape] * (shards - 1), products=[one] * (shards - 1)
    )(spread, *enc_picks[:-1], *enc_slopes[:-1])
    if relayed:
        passed = [sent_back(block, 1) for block in far]
        first, near = call(functools.partial(relay_kernel, 0), [piece, row_shape])(blocks[2], passed[0], blocks[1])
        (second,) = call(functools.partial(relay_kernel, piece_rows), [piece])(blocks[2], passed[1])
        near = sent_back(near, 1)
        first, second = sent_back(first, 2), sent_back(second, 2)
        (summed,) = call(sum_kernel, [((piece_rows, width), f32)])(blocks[0], first)
        (grid_grad,) = call(
            functools.partial(grid_kernel, 2), [((grid, width), f32)], products=[(grid, width, width)]
        )(blocks[0], near, summed, second, w_enc_grid)
    else:
        blocks = [*blocks, *far]
        blocks = [blocks[0]] + [sent_back(block, step) for step, block in enumerate(blocks) if step]
        (grid_grad,) = call(
            functools.partial(grid_kernel, shards), [((grid, width), f32)], products=[(grid, width, width)]
        )(*blocks, w_enc_grid)
    return (final_mesh, grid_grad)


def solution(mesh):
    return jax.shard_map(
        on_device,
        mesh=mesh,
        in_specs=(
            P(("groups", "mesh", "feat", "rep"), None),
            P(("groups", "mesh", "feat", "rep"), None),
            P(("groups", "mesh", "feat", "rep"), None),
            P(("groups", "mesh"), None),
            P(("groups", "mesh", "feat", "rep")),
            P(("groups", "mesh", "feat", "rep")),
            P(("groups", "mesh"), None, None),
            P(),
            P(),
            P(),
            P(),
            P(),
            P(),
            P(),
            P(),
            P(("groups", "mesh"), None),
        ),
        out_specs=(P(("groups", "mesh"), None), P(("groups", "mesh", "feat", "rep"), None)),
        check_vma=False,
    )
```

```python
import functools
import math

import jax
import jax.numpy as jnp
from jax import lax
from jax.experimental import pallas as pl
from jax.experimental.pallas import tpu as pltpu
from jax.sharding import PartitionSpec as P

LAYERS = 3
LANES = 128
BLOCK = 512
EXTRA = 16
eps = 1e-05

f32 = jnp.float32
bf16 = jnp.bfloat16
i32 = jnp.int32


def norm_scale(totals):
    return lax.rsqrt(jnp.mean(totals * totals, axis=-1, keepdims=True) + eps)


def norm_back(totals, gain_row, upstream):
    scaled = norm_scale(totals)
    normed = totals * scaled
    slope = upstream * gain_row
    return scaled * (slope - normed * jnp.mean(slope * normed, axis=-1, keepdims=True))


def dot(left, right):
    return jnp.dot(left, right, preferred_element_type=f32)


def dot_back(left, right):
    return lax.dot_general(left, right, (((1,), (1,)), ((), ())), preferred_element_type=f32)


def gated(pre):
    sigma = 0.5 * jnp.tanh(0.5 * pre) + 0.5
    act = pre * sigma
    return act, sigma + act * (1.0 - sigma)


def as_mask(hit):
    return jnp.where(hit, 1.0, 0.0).astype(bf16)


def pick_columns(index, first, height):
    place = lax.broadcasted_iota(i32, (height, index.shape[1]), 0) + first
    return as_mask(place == index)


def upright(index):
    count = index.shape[1]
    if count < LANES:
        index = jnp.concatenate([index, jnp.full((1, LANES - count), -1, i32)], axis=1)
    return jnp.broadcast_to(index, (LANES, LANES)).T[:count]


def pick_rows(column, first, width):
    lane = lax.broadcasted_iota(i32, column.shape, 1) + first
    return jnp.concatenate([as_mask(column == lane + at) for at in range(0, width, LANES)], axis=1)


def call(body, outs, scratch=(), products=(), copied=False):
    def run(*args):
        def where(array):
            if copied:
                return pl.BlockSpec(memory_space=pltpu.HBM)
            return pl.BlockSpec(memory_space=pltpu.SMEM if array.dtype == i32 and array.ndim == 1 else pltpu.VMEM)

        def size(shape, dtype):
            return jnp.dtype(dtype).itemsize * math.prod(shape)

        own = sum(size(*held) for held in scratch) + (10 << 20)
        moved = sum(array.dtype.itemsize * array.size for array in args) + sum(size(*out) for out in outs)
        limit = own if own + moved < 40 << 20 else min(own + moved, 60 << 20)
        semaphores = [pltpu.SemaphoreType.DMA((2 + len(outs),))] if copied else []
        return pl.pallas_call(
            body,
            out_shape=tuple(jax.ShapeDtypeStruct(shape, dtype) for shape, dtype in outs),
            in_specs=[where(array) for array in args],
            out_specs=tuple(pl.BlockSpec(memory_space=pltpu.VMEM) for _ in outs),
            scratch_shapes=[pltpu.VMEM(shape, dtype) for shape, dtype in scratch] + semaphores,
            compiler_params=pltpu.CompilerParams(vmem_limit_bytes=limit),
            cost_estimate=pl.CostEstimate(
                flops=2 * sum(math.prod(product) for product in products), bytes_accessed=moved, transcendentals=0
            ),
        )(*args)

    return run


def place_kernel(slots, receivers, order, here, there, halo_here, halo_there, list_here, list_there):
    nodes = here.shape[1] // 2
    wide = halo_here.shape[1]

    def body(at):
        block = pl.ds(pl.multiple_of(at * LANES, LANES), LANES)
        slot, receiver = slots[:, block], receivers[:, block]
        slot_column, receiver_column = upright(slot), upright(receiver)
        here[block, 0:nodes] = pick_rows(slot_column, 0, nodes)
        here[block, nodes:] = pick_rows(receiver_column, 0, nodes)
        halo_here[block, :] = pick_rows(slot_column, nodes, wide)
        there[0:nodes, block] = pick_columns(slot, 0, nodes)
        there[nodes:, block] = pick_columns(receiver, 0, nodes)
        halo_there[:, block] = pick_columns(slot, nodes, wide)

    pl.loop(0, slots.shape[1] // LANES)(body)
    count = order.shape[1]
    for at in range(0, count, LANES):
        end = min(at + LANES, count)
        list_here[at:end, :] = pick_rows(upright(order[:, at:end]), 0, nodes)
    list_there[...] = pick_columns(order[...], 0, nodes)


def note_kernel(rows, shards, nodes, payload, shard_rows, node_rows, arrived):
    grid = shards.shape[1]
    first = payload.shape[0] - EXTRA
    copies = [
        pltpu.make_async_copy(shards, shard_rows, arrived.at[0]),
        pltpu.make_async_copy(nodes, node_rows, arrived.at[1]),
        pltpu.make_async_copy(rows.at[0:first], payload.at[0:first], arrived.at[2]),
    ]
    for copy in copies:
        copy.start()
    for copy in copies[:2]:
        copy.wait()
    row = lax.broadcasted_iota(i32, (EXTRA, grid), 0)
    notes = jnp.full((EXTRA, grid), -1, i32)
    for top in range(shards.shape[0]):
        node = node_rows[top : top + 1, :]
        for at, value in enumerate((shard_rows[top : top + 1, :], node & 255, node >> 8)):
            notes = jnp.where(row == 3 * top + at, value, notes)
    payload[first:, 0:grid] = notes.astype(f32).astype(bf16)
    if grid < payload.shape[1]:
        payload[first:, grid:] = jnp.zeros((EXTRA, payload.shape[1] - grid), bf16)
    copies[2].wait()


def encode_kernel(steps, first, last, halves, *refs):
    refs = list(refs)
    meta, base, w_grid = refs[:3]
    del refs[:3]
    if first:
        w_mesh, _ = refs.pop(0), refs.pop(0)
        projected = dot(base[...], w_mesh[...]).astype(bf16)
    else:
        total_in = refs.pop(0)
        projected = base[...]
    payloads = refs[:steps]
    del refs[:steps]
    picks, slopes = refs[:steps], refs[steps : 2 * steps]
    del refs[: 2 * steps]
    total = None if first else total_in[...]
    nodes = projected.shape[0]
    for payload, pick, slope_out in zip(payloads, picks, slopes):
        grid = pick.shape[0]
        notes = payload[grid:, 0:grid].astype(f32)
        target = jnp.full((1, grid), -1.0, f32)
        for at in range(0, notes.shape[0] // 3 * 3, 3):
            named = notes[at : at + 1] == meta[1:2, 0:grid].astype(f32)
            target = jnp.where(named, notes[at + 1 : at + 2] + 256.0 * notes[at + 2 : at + 3], target)
        target = target.astype(i32)
        column = jnp.concatenate([upright(target[:, at : at + LANES]) for at in range(0, grid, LANES)], axis=0)
        picked = pick_rows(column, 0, nodes)
        pick[...] = picked
        pre = dot(payload[0:grid, :], w_grid[...]) + dot(picked, projected)
        act, slope = gated(pre)
        slope_out[...] = slope.astype(bf16)
        added = dot(pick_columns(target, 0, nodes), act.astype(bf16))
        total = added if total is None else total + added
    if first:
        refs.pop(0)[...] = projected
    if not last:
        refs[0][...] = total
        return
    keep, sends = refs[0], refs[1:halves]
    part = nodes // halves
    own = meta[0:1, :]

    def half(shift):
        rows = total[0:part]
        for at in range(1, halves):
            rows = jnp.where(own == (at - shift) % halves, total[at * part : (at + 1) * part], rows)
        return rows

    keep[...] = half(0)
    for shift in range(1, halves):
        sends[shift - 1][...] = half(shift).astype(bf16)


def hand_out(rows, outs):
    rows = rows.astype(bf16)
    at = 0
    for out in outs:
        out[...] = rows[at : at + out.shape[0]]
        at += out.shape[0]


def start_kernel(halves, *refs):
    meta = refs[0]
    parts = refs[1 : 1 + halves]
    mesh_init, w_enc_out, gain, w_send, list_here = refs[1 + halves : 6 + halves]
    hidden_out, enc_sum_out, sent = refs[6 + halves : 9 + halves]
    outs = refs[9 + halves : -1]
    whole = refs[-1]
    part = parts[0].shape[0]
    own = meta[0:1, :]
    for at in range(halves):
        rows = parts[0][...].astype(f32)
        for shift in range(1, halves):
            rows = jnp.where(own == (at - shift) % halves, parts[shift][...].astype(f32), rows)
        whole[at * part : (at + 1) * part, :] = rows.astype(bf16)
    enc_sum = dot(whole[...], w_enc_out[...])
    enc_sum_out[...] = enc_sum
    hidden = (mesh_init[...].astype(f32) + enc_sum * norm_scale(enc_sum) * gain[...]).astype(bf16)
    hidden_out[...] = hidden
    projected = dot(hidden, w_send[0]).astype(bf16)
    sent[...] = projected
    hand_out(dot(list_here[...], projected), outs)


def local_kernel(layer, hidden, sent, here, w_recv, pre, table):
    nodes = hidden.shape[0]
    table[0:nodes, :] = sent[...]
    table[nodes:, :] = dot(hidden[...], w_recv[layer]).astype(bf16)
    for at in range(0, pre.shape[0], BLOCK):
        pre[at : at + BLOCK, :] = dot(here[at : at + BLOCK, :], table[...])


def stack_halo(halos, halo):
    at = 0
    for block in halos:
        halo[at : at + block.shape[0], :] = block[...]
        at += block.shape[0]
    if at < halo.shape[0]:
        halo[at:, :] = jnp.zeros((halo.shape[0] - at, halo.shape[1]), bf16)


def node_sum(pre, halos, halo_here, there, slope_out, halo, act_out):
    nodes = there.shape[0] // 2
    stack_halo(halos, halo)
    for at in range(0, pre.shape[0], BLOCK):
        block = slice(at, at + BLOCK)
        act, slope = gated(pre[block, :] + dot(halo_here[block, :], halo[...]))
        slope_out[block, :] = slope.astype(bf16)
        act_out[block, :] = act.astype(bf16)
    return dot(there[nodes:, :], act_out[...])


def layer_kernel(layer, shifts, *refs):
    hidden, pre = refs[:2]
    halos, refs = refs[2 : 2 + shifts], refs[2 + shifts :]
    halo_here, there, w_out, gain, w_send, list_here = refs[:6]
    hidden_out, agg_out, slope_out, sent_out = refs[6:10]
    outs = refs[10:-2]
    total = node_sum(pre, halos, halo_here, there, slope_out, *refs[-2:])
    agg = dot(total.astype(bf16), w_out[layer])
    agg_out[...] = agg
    fresh = (hidden[...].astype(f32) + agg * norm_scale(agg) * gain[layer : layer + 1, :]).astype(bf16)
    hidden_out[...] = fresh
    projected = dot(fresh, w_send[layer + 1]).astype(bf16)
    sent_out[...] = projected
    hand_out(dot(list_here[...], projected), outs)


def edge_grads(grad_agg, w_out, here, halo_there, slope, grad_pre, outs):
    nodes = grad_agg.shape[0]
    spread = dot_back(grad_agg.astype(bf16), w_out).astype(bf16)
    for at in range(0, slope.shape[0], BLOCK):
        block = slice(at, at + BLOCK)
        grad_act = dot(here[block, nodes:], spread)
        grad_pre[block, :] = (grad_act * slope[block, :].astype(f32)).astype(bf16)
    hand_out(dot(halo_there[...], grad_pre[...]), outs)


def turn_kernel(layer, shifts, *refs):
    hidden, pre = refs[:2]
    halos, refs = refs[2 : 2 + shifts], refs[2 + shifts :]
    halo_here, there, w_out, gain, here, halo_there, cot = refs[:7]
    hidden_out, grad_pre = refs[7:9]
    outs = refs[9:-2]
    slope, halo = refs[-2:]
    total = node_sum(pre, halos, halo_here, there, slope, halo, grad_pre)
    agg = dot(total.astype(bf16), w_out[layer])
    gain_row = gain[layer : layer + 1, :]
    hidden_out[...] = (hidden[...].astype(f32) + agg * norm_scale(agg) * gain_row).astype(bf16)
    edge_grads(norm_back(agg, gain_row, cot[...].astype(f32)), w_out[layer], here, halo_there, slope, grad_pre, outs)


def rest_kernel(layer, upstream, grad_pre, there, w_send, w_recv, rest):
    nodes = upstream.shape[0]
    sums = dot(there[...], grad_pre[...]).astype(bf16)
    rest[...] = (
        upstream[...].astype(f32)
        + dot_back(sums[0:nodes], w_send[layer])
        + dot_back(sums[nodes:], w_recv[layer])
    )


def arrived(rest, returned, list_there, w_send, halo):
    stack_halo(returned, halo)
    projected = dot_back(halo[...], w_send).astype(bf16)
    return rest[...] + dot(list_there[...], projected)


def back_kernel(layer, shifts, *refs):
    rest = refs[0]
    returned, refs = refs[1 : 1 + shifts], refs[1 + shifts :]
    list_there, w_send, agg, slope, gain, w_out, here, halo_there = refs[:8]
    upstream_out, grad_pre = refs[8:10]
    outs = refs[10:-1]
    halo = refs[-1]
    upstream = arrived(rest, returned, list_there, w_send[layer + 1], halo)
    upstream_out[...] = upstream
    grad_agg = norm_back(agg[...], gain[layer : layer + 1, :], upstream)
    edge_grads(grad_agg, w_out[layer], here, halo_there, slope, grad_pre, outs)


def pair_grads(spread, pick, slope):
    return (dot(pick, spread) * slope.astype(f32)).astype(bf16)


def finish_kernel(shifts, *refs):
    rest = refs[0]
    returned, refs = refs[1 : 1 + shifts], refs[1 + shifts :]
    list_there, w_send, enc_sum, gain, w_enc_out, pick, slope, spread_out = refs[:8]
    outs, halo = refs[8:-1], refs[-1]
    upstream = arrived(rest, returned, list_there, w_send[0], halo)
    spread = dot_back(norm_back(enc_sum[...], gain[...], upstream).astype(bf16), w_enc_out[...]).astype(bf16)
    spread_out[...] = spread
    at = 0
    for out in outs:
        rows = slice(at, at + out.shape[0])
        out[...] = pair_grads(spread, pick[rows, :], slope[rows, :])
        at += out.shape[0]


def others_kernel(count, *refs):
    spread = refs[0][...]
    picks, slopes, outs = refs[1 : 1 + count], refs[1 + count : 1 + 2 * count], refs[1 + 2 * count :]
    for pick, slope, out in reversed(list(zip(picks, slopes, outs))):
        skip = pick.shape[0] - out.shape[0]
        out[...] = pair_grads(spread, pick[skip:, :], slope[skip:, :])


def relay_kernel(first, own, passed, *refs):
    rows = passed.shape[0]
    out = refs[0] if len(refs) == 1 else refs[-2]
    out[...] = (own[first : first + rows, :].astype(f32) + passed[...].astype(f32)).astype(bf16)
    if len(refs) > 1:
        refs[-1][...] = refs[0][...]


def sum_kernel(own, piece, total):
    total[...] = own[0 : piece.shape[0], :].astype(f32) + piece[...].astype(f32)


def grid_kernel(whole, *refs):
    blocks, pieces, (w_grid, out) = refs[:whole], refs[whole:-2], refs[-2:]
    if not pieces:
        total = blocks[0][...].astype(f32)
        for block in blocks[1:]:
            total = total + block[...].astype(f32)
        out[...] = dot_back(total.astype(bf16), w_grid[...])
        return
    (own, near), (summed, second) = blocks, pieces
    first = summed.shape[0]
    total = summed[...] + near[0:first, :].astype(f32)
    out[0:first, :] = dot_back(total.astype(bf16), w_grid[...])
    total = own[first:, :].astype(f32) + near[first:, :].astype(f32) + second[...].astype(f32)
    out[first:, :] = dot_back(total.astype(bf16), w_grid[...])


def shifted(value, axis, by):
    size = lax.axis_size(axis)
    return lax.ppermute(value, axis, [(at, (at + by) % size) for at in range(size)])


def partner(at, step, size):
    return at ^ step if size & (size - 1) == 0 else (at + step) % size


def sent_to(value, step):
    size = lax.axis_size("mesh")
    return lax.ppermute(value, "mesh", [(at, partner(at, step, size)) for at in range(size)])


def sent_back(value, step):
    size = lax.axis_size("mesh")
    return lax.ppermute(value, "mesh", [(partner(at, step, size), at) for at in range(size)])


def in_order(pieces, axis):
    return jnp.roll(jnp.stack(pieces)[::-1], lax.axis_index(axis) + 1, axis=0)


def on_device(
    grid_feats,
    g2m_shard,
    g2m_node,
    mesh_init,
    sender_slots,
    receivers,
    halo_index,
    w_enc_grid,
    w_enc_mesh,
    w_enc_out,
    enc_gain,
    w_send,
    w_recv,
    w_out,
    layer_gain,
    out_cot,
):
    shards = lax.axis_size("mesh")
    shard = lax.axis_index("mesh")
    halves = lax.axis_size("rep")
    feats = lax.axis_size("feat")
    nodes, width = mesh_init.shape
    grid, tops = g2m_shard.shape
    edges = sender_slots.shape[0]
    depth = halo_index.shape[2]
    shifts = shards - 1
    listed_rows = shifts * depth
    wide = -(-listed_rows // LANES) * LANES
    all_edges = edges * halves * feats
    enc_gain = enc_gain[None, :]

    relayed = shards == 4
    cuts = 2 if relayed else 1
    piece_rows = grid // cuts
    in_place = [pltpu.with_memory_space_constraint(array, pltpu.HBM) for array in (grid_feats, g2m_shard.T, g2m_node.T)]
    (payload,) = call(
        note_kernel,
        [((grid + EXTRA, width), bf16)],
        [((tops, grid), i32), ((tops, grid), i32)],
        copied=True,
    )(*in_place)

    place = sender_slots - nodes
    away = partner(shard, place // depth, shards)
    if shards & (shards - 1):
        away = lax.rem(shard - place // depth + shards, shards)
    slots = jnp.where(sender_slots < nodes, sender_slots, nodes + (shifts - away) * depth + place % depth)
    both = jnp.stack([slots, receivers])
    others = [shifted(both, "rep", step) for step in range(1, halves)]
    if relayed:
        across = sent_to(payload, 2)
        payloads = [payload, sent_to(payload, 1), across]
    else:
        payloads = [payload] + [sent_to(payload, step) for step in range(1, shards)]
    both = in_order([both] + others, "rep")
    both = in_order([both] + [shifted(both, "feat", step) for step in range(1, feats)], "feat")
    both = both.reshape(feats * halves, 2, edges)
    all_slots, all_receivers = both[:, 0].reshape(1, -1), both[:, 1].reshape(1, -1)
    readers = partner(shard, shards - jnp.arange(1, shards, dtype=i32), shards)
    lists = jnp.take(halo_index[0], readers, axis=0).reshape(1, -1)
    here, there, halo_here, halo_there, list_here, list_there = call(
        place_kernel,
        [
            ((all_edges, 2 * nodes), bf16),
            ((2 * nodes, all_edges), bf16),
            ((all_edges, wide), bf16),
            ((wide, all_edges), bf16),
            ((listed_rows, nodes), bf16),
            ((nodes, listed_rows), bf16),
        ],
        products=[(all_edges, nodes, width), (all_edges, 2 * nodes, width)],
    )(all_slots, all_receivers, lists)

    if relayed:
        across, list_here = lax.optimization_barrier((across, list_here))
        payloads.append(sent_to(across, 1))

    meta = jnp.broadcast_to(jnp.stack([lax.axis_index("rep"), shard]).astype(i32)[:, None], (2, width))
    node_f32, node_bf16 = ((nodes, width), f32), ((nodes, width), bf16)
    row_shape, half = ((grid, width), bf16), nodes // halves
    square = (nodes, width, width)
    enc_picks, enc_slopes = [], []
    base, total = mesh_init, None
    groups = [payloads[:2]] + [payloads[at : at + 1] for at in range(2, shards)]
    for at, group in enumerate(groups):
        first, last = at == 0, at == len(groups) - 1
        count = len(group)
        outs = [((grid, nodes), bf16)] * count + [row_shape] * count
        outs += [node_bf16] if first else []
        outs += [((half, width), f32)] + [((half, width), bf16)] * (halves - 1) if last else [node_f32]
        got = list(
            call(
                functools.partial(encode_kernel, count, first, last, halves),
                outs,
                (),
                [square] * first + [(grid, width, width), (grid, nodes, width), (nodes, grid, width)] * count,
            )(
                meta, base, w_enc_grid, *((w_enc_mesh, list_here) if first else (total,)), *group
            )
        )
        enc_picks += got[:count]
        enc_slopes += got[count : 2 * count]
        del got[: 2 * count]
        if first:
            base = got.pop(0)
        total = got[0]
    part = got[0]
    for step in range(1, halves):
        part = part + shifted(got[step], "rep", step).astype(f32)
    part = part.astype(bf16)
    pieces = [part] + [shifted(part, "feat", step) for step in range(1, feats)]
    if feats > 2:
        pieces = list(in_order(pieces, "feat"))
    part = sum(piece.astype(f32) for piece in pieces).astype(bf16)
    parts = [part] + [shifted(part, "rep", -step) for step in range(1, halves)]

    listed = [((depth, width), bf16)] * shifts

    def exchange(blocks, send):
        return [send(block, shifts - at) for at, block in enumerate(blocks)]

    hidden, enc_sum, sent, *outgoing = call(
        functools.partial(start_kernel, halves), [node_bf16, node_f32, node_bf16] + listed, [node_bf16],
        [square, square, (listed_rows, nodes, width)],
    )(meta, *parts, mesh_init, w_enc_out, enc_gain, w_send, list_here)

    edge_f32, edge_bf16 = ((all_edges, width), f32), ((all_edges, width), bf16)
    halo, back_halo = ((wide, width), bf16), ((listed_rows, width), bf16)
    forward_products = [(all_edges, wide, width), (nodes, all_edges, width), square]
    backward_products = [square, (all_edges, nodes, width), (wide, all_edges, width)]

    def arriving(layer):
        (pre,) = call(
            functools.partial(local_kernel, layer),
            [edge_f32],
            [((2 * nodes, width), bf16)],
            [square, (all_edges, 2 * nodes, width)],
        )(hidden, sent, here, w_recv)
        return hidden, pre, *exchange(outgoing, sent_to)

    records = []
    for layer in range(LAYERS - 1):
        hidden, agg, slope, sent, *outgoing = call(
            functools.partial(layer_kernel, layer, shifts),
            [node_bf16, node_f32, edge_bf16, node_bf16] + listed,
            [halo, edge_bf16],
            forward_products + [square, (listed_rows, nodes, width)],
        )(*arriving(layer), halo_here, there, w_out, layer_gain, w_send, list_here)
        records.append((agg, slope))
    last = LAYERS - 1
    final_mesh, grad_pre, *outgoing = call(
        functools.partial(turn_kernel, last, shifts), [node_bf16, edge_bf16] + listed, [edge_bf16, halo],
        forward_products + backward_products,
    )(*arriving(last), halo_here, there, w_out, layer_gain, here, halo_there, out_cot)
    upstream = out_cot
    for layer in reversed(range(LAYERS)):
        returned = exchange(outgoing, sent_back)
        (rest,) = call(
            functools.partial(rest_kernel, layer), [node_f32], (), [(2 * nodes, all_edges, width), square, square]
        )(upstream, grad_pre, there, w_send, w_recv)
        if layer:
            agg, slope = records[layer - 1]
            upstream, grad_pre, *outgoing = call(
                functools.partial(back_kernel, layer - 1, shifts),
                [node_f32, edge_bf16] + listed,
                [back_halo],
                backward_products + [(listed_rows, width, width), (nodes, listed_rows, width)],
            )(rest, *returned, list_there, w_send, agg, slope, layer_gain, w_out, here, halo_there)
    piece = ((piece_rows, width), bf16)
    one = (grid, nodes, width)
    spread, *far = call(
        functools.partial(finish_kernel, shifts),
        [node_bf16] + [piece] * cuts,
        [back_halo],
        [square, (listed_rows, width, width), (nodes, listed_rows, width), one],
    )(rest, *returned, list_there, w_send, enc_sum, enc_gain, w_enc_out, enc_picks[-1], enc_slopes[-1])
    blocks = call(
        functools.partial(others_kernel, shards - 1), [row_shape] * (shards - 1), products=[one] * (shards - 1)
    )(spread, *enc_picks[:-1], *enc_slopes[:-1])
    if relayed:
        passed = [sent_back(block, 1) for block in far]
        first, near = call(functools.partial(relay_kernel, 0), [piece, row_shape])(blocks[2], passed[0], blocks[1])
        (second,) = call(functools.partial(relay_kernel, piece_rows), [piece])(blocks[2], passed[1])
        near = sent_back(near, 1)
        first, second = sent_back(first, 2), sent_back(second, 2)
        (summed,) = call(sum_kernel, [((piece_rows, width), f32)])(blocks[0], first)
        (grid_grad,) = call(
            functools.partial(grid_kernel, 2), [((grid, width), f32)], products=[(grid, width, width)]
        )(blocks[0], near, summed, second, w_enc_grid)
    else:
        blocks = [*blocks, *far]
        blocks = [blocks[0]] + [sent_back(block, step) for step, block in enumerate(blocks) if step]
        (grid_grad,) = call(
            functools.partial(grid_kernel, shards), [((grid, width), f32)], products=[(grid, width, width)]
        )(*blocks, w_enc_grid)
    return (final_mesh, grid_grad)


def solution(mesh):
    return jax.shard_map(
        on_device,
        mesh=mesh,
        in_specs=(
            P(("groups", "mesh", "feat", "rep"), None),
            P(("groups", "mesh", "feat", "rep"), None),
            P(("groups", "mesh", "feat", "rep"), None),
            P(("groups", "mesh"), None),
            P(("groups", "mesh", "feat", "rep")),
            P(("groups", "mesh", "feat", "rep")),
            P(("groups", "mesh"), None, None),
            P(),
            P(),
            P(),
            P(),
            P(),
            P(),
            P(),
            P(),
            P(("groups", "mesh"), None),
        ),
        out_specs=(P(("groups", "mesh"), None), P(("groups", "mesh", "feat", "rep"), None)),
        check_vma=False,
    )
```

```python
import functools
import math

import jax
import jax.numpy as jnp
from jax import lax
from jax.experimental import pallas as pl
from jax.experimental.pallas import tpu as pltpu
from jax.sharding import PartitionSpec as P

LAYERS = 3
LANES = 128
BLOCK = 512
EXTRA = 16
eps = 1e-05

f32 = jnp.float32
bf16 = jnp.bfloat16
i32 = jnp.int32


def norm_scale(totals):
    return lax.rsqrt(jnp.mean(totals * totals, axis=-1, keepdims=True) + eps)


def norm_back(totals, gain_row, upstream):
    scaled = norm_scale(totals)
    normed = totals * scaled
    slope = upstream * gain_row
    return scaled * (slope - normed * jnp.mean(slope * normed, axis=-1, keepdims=True))


def dot(left, right):
    return jnp.dot(left, right, preferred_element_type=f32)


def dot_back(left, right):
    return lax.dot_general(left, right, (((1,), (1,)), ((), ())), preferred_element_type=f32)


def gated(pre):
    sigma = 0.5 * jnp.tanh(0.5 * pre) + 0.5
    act = pre * sigma
    return act, sigma + act * (1.0 - sigma)


def as_mask(hit):
    return jnp.where(hit, 1.0, 0.0).astype(bf16)


def pick_columns(index, first, height):
    place = lax.broadcasted_iota(i32, (height, index.shape[1]), 0) + first
    return as_mask(place == index)


def upright(index):
    count = index.shape[1]
    if count < LANES:
        index = jnp.concatenate([index, jnp.full((1, LANES - count), -1, i32)], axis=1)
    return jnp.broadcast_to(index, (LANES, LANES)).T[:count]


def pick_rows(column, first, width):
    lane = lax.broadcasted_iota(i32, column.shape, 1) + first
    return jnp.concatenate([as_mask(column == lane + at) for at in range(0, width, LANES)], axis=1)


def call(body, outs, scratch=(), products=(), copied=False):
    def run(*args):
        def where(array):
            if copied:
                return pl.BlockSpec(memory_space=pltpu.HBM)
            return pl.BlockSpec(memory_space=pltpu.SMEM if array.dtype == i32 and array.ndim == 1 else pltpu.VMEM)

        def size(shape, dtype):
            return jnp.dtype(dtype).itemsize * math.prod(shape)

        own = sum(size(*held) for held in scratch) + (10 << 20)
        moved = sum(array.dtype.itemsize * array.size for array in args) + sum(size(*out) for out in outs)
        limit = own if own + moved < 40 << 20 else min(own + moved, 60 << 20)
        semaphores = [pltpu.SemaphoreType.DMA((2 + len(outs),))] if copied else []
        return pl.pallas_call(
            body,
            out_shape=tuple(jax.ShapeDtypeStruct(shape, dtype) for shape, dtype in outs),
            in_specs=[where(array) for array in args],
            out_specs=tuple(pl.BlockSpec(memory_space=pltpu.VMEM) for _ in outs),
            scratch_shapes=[pltpu.VMEM(shape, dtype) for shape, dtype in scratch] + semaphores,
            compiler_params=pltpu.CompilerParams(vmem_limit_bytes=limit),
            cost_estimate=pl.CostEstimate(
                flops=2 * sum(math.prod(product) for product in products), bytes_accessed=moved, transcendentals=0
            ),
        )(*args)

    return run


def place_kernel(slots, receivers, order, here, there, halo_here, halo_there, list_here, list_there):
    nodes = here.shape[1] // 2
    wide = halo_here.shape[1]

    def body(at):
        block = pl.ds(pl.multiple_of(at * LANES, LANES), LANES)
        slot, receiver = slots[:, block], receivers[:, block]
        slot_column, receiver_column = upright(slot), upright(receiver)
        here[block, 0:nodes] = pick_rows(slot_column, 0, nodes)
        here[block, nodes:] = pick_rows(receiver_column, 0, nodes)
        halo_here[block, :] = pick_rows(slot_column, nodes, wide)
        there[0:nodes, block] = pick_columns(slot, 0, nodes)
        there[nodes:, block] = pick_columns(receiver, 0, nodes)
        halo_there[:, block] = pick_columns(slot, nodes, wide)

    pl.loop(0, slots.shape[1] // LANES)(body)
    count = order.shape[1]
    for at in range(0, count, LANES):
        end = min(at + LANES, count)
        list_here[at:end, :] = pick_rows(upright(order[:, at:end]), 0, nodes)
    list_there[...] = pick_columns(order[...], 0, nodes)


def note_kernel(rows, shards, nodes, payload, shard_rows, node_rows, arrived):
    grid = shards.shape[1]
    first = payload.shape[0] - EXTRA
    copies = [
        pltpu.make_async_copy(shards, shard_rows, arrived.at[0]),
        pltpu.make_async_copy(nodes, node_rows, arrived.at[1]),
        pltpu.make_async_copy(rows.at[0:first], payload.at[0:first], arrived.at[2]),
    ]
    for copy in copies:
        copy.start()
    for copy in copies[:2]:
        copy.wait()
    row = lax.broadcasted_iota(i32, (EXTRA, grid), 0)
    notes = jnp.full((EXTRA, grid), -1, i32)
    for top in range(shards.shape[0]):
        node = node_rows[top : top + 1, :]
        for at, value in enumerate((shard_rows[top : top + 1, :], node & 255, node >> 8)):
            notes = jnp.where(row == 3 * top + at, value, notes)
    payload[first:, 0:grid] = notes.astype(f32).astype(bf16)
    if grid < payload.shape[1]:
        payload[first:, grid:] = jnp.zeros((EXTRA, payload.shape[1] - grid), bf16)
    copies[2].wait()


def encode_kernel(steps, first, last, halves, *refs):
    refs = list(refs)
    meta, base, w_grid = refs[:3]
    del refs[:3]
    if first:
        w_mesh, _ = refs.pop(0), refs.pop(0)
        projected = dot(base[...], w_mesh[...]).astype(bf16)
    else:
        total_in = refs.pop(0)
        projected = base[...]
    payloads = refs[:steps]
    del refs[:steps]
    picks, slopes = refs[:steps], refs[steps : 2 * steps]
    del refs[: 2 * steps]
    total = None if first else total_in[...]
    nodes = projected.shape[0]
    for payload, pick, slope_out in zip(payloads, picks, slopes):
        grid = pick.shape[0]
        notes = payload[grid:, 0:grid].astype(f32)
        target = jnp.full((1, grid), -1.0, f32)
        for at in range(0, notes.shape[0] // 3 * 3, 3):
            named = notes[at : at + 1] == meta[1:2, 0:grid].astype(f32)
            target = jnp.where(named, notes[at + 1 : at + 2] + 256.0 * notes[at + 2 : at + 3], target)
        target = target.astype(i32)
        column = jnp.concatenate([upright(target[:, at : at + LANES]) for at in range(0, grid, LANES)], axis=0)
        picked = pick_rows(column, 0, nodes)
        pick[...] = picked
        pre = dot(payload[0:grid, :], w_grid[...]) + dot(picked, projected)
        act, slope = gated(pre)
        slope_out[...] = slope.astype(bf16)
        added = dot(pick_columns(target, 0, nodes), act.astype(bf16))
        total = added if total is None else total + added
    if first:
        refs.pop(0)[...] = projected
    if not last:
        refs[0][...] = total
        return
    keep, sends = refs[0], refs[1:halves]
    part = nodes // halves
    own = meta[0:1, :]

    def half(shift):
        rows = total[0:part]
        for at in range(1, halves):
            rows = jnp.where(own == (at - shift) % halves, total[at * part : (at + 1) * part], rows)
        return rows

    keep[...] = half(0)
    for shift in range(1, halves):
        sends[shift - 1][...] = half(shift).astype(bf16)


def hand_out(rows, outs):
    rows = rows.astype(bf16)
    depth = outs[0].shape[0]
    count = rows.shape[0] // depth
    for at, out in enumerate(outs):
        first = 0 if at == 0 else (count - len(outs) + at) * depth
        out[...] = rows[first : first + depth]


def start_kernel(halves, *refs):
    meta = refs[0]
    parts = refs[1 : 1 + halves]
    mesh_init, w_enc_out, gain, w_send, list_here = refs[1 + halves : 6 + halves]
    hidden_out, enc_sum_out, sent = refs[6 + halves : 9 + halves]
    outs = refs[9 + halves : -1]
    whole = refs[-1]
    part = parts[0].shape[0]
    own = meta[0:1, :]
    for at in range(halves):
        rows = parts[0][...].astype(f32)
        for shift in range(1, halves):
            rows = jnp.where(own == (at - shift) % halves, parts[shift][...].astype(f32), rows)
        whole[at * part : (at + 1) * part, :] = rows.astype(bf16)
    enc_sum = dot(whole[...], w_enc_out[...])
    enc_sum_out[...] = enc_sum
    hidden = (mesh_init[...].astype(f32) + enc_sum * norm_scale(enc_sum) * gain[...]).astype(bf16)
    hidden_out[...] = hidden
    projected = dot(hidden, w_send[0]).astype(bf16)
    sent[...] = projected
    hand_out(dot(list_here[...], projected), outs)


def local_kernel(layer, hidden, sent, here, w_recv, pre, table):
    nodes = hidden.shape[0]
    table[0:nodes, :] = sent[...]
    table[nodes:, :] = dot(hidden[...], w_recv[layer]).astype(bf16)
    for at in range(0, pre.shape[0], BLOCK):
        pre[at : at + BLOCK, :] = dot(here[at : at + BLOCK, :], table[...])


def local_more_kernel(table, here, pre):
    skip = here.shape[0] - pre.shape[0]
    for at in range(0, pre.shape[0], BLOCK):
        pre[at : at + BLOCK, :] = dot(here[skip + at : skip + at + BLOCK, :], table[...])


def stack_halo(halos, halo):
    at = 0
    for block in halos:
        halo[at : at + block.shape[0], :] = block[...]
        at += block.shape[0]
    if at < halo.shape[0]:
        halo[at:, :] = jnp.zeros((halo.shape[0] - at, halo.shape[1]), bf16)


def node_sum(pres, halos, halo_here, there, slope_out, halo, act_out):
    nodes = there.shape[0] // 2
    stack_halo(halos, halo)
    half = pres[0].shape[0]
    for at in range(0, 2 * half, BLOCK):
        block = slice(at, at + BLOCK)
        pre = pres[at // half][at % half : at % half + BLOCK, :]
        act, slope = gated(pre + dot(halo_here[block, :], halo[...]))
        slope_out[block, :] = slope.astype(bf16)
        act_out[block, :] = act.astype(bf16)
    return dot(there[nodes:, :], act_out[...])


def layer_kernel(layer, shifts, *refs):
    hidden, pres = refs[0], refs[1:3]
    halos, refs = refs[3 : 3 + shifts], refs[3 + shifts :]
    halo_here, there, w_out, gain, w_send, list_here = refs[:6]
    hidden_out, agg_out, slope_out, sent_out = refs[6:10]
    outs = refs[10:-2]
    total = node_sum(pres, halos, halo_here, there, slope_out, *refs[-2:])
    agg = dot(total.astype(bf16), w_out[layer])
    agg_out[...] = agg
    fresh = (hidden[...].astype(f32) + agg * norm_scale(agg) * gain[layer : layer + 1, :]).astype(bf16)
    hidden_out[...] = fresh
    projected = dot(fresh, w_send[layer + 1]).astype(bf16)
    sent_out[...] = projected
    hand_out(dot(list_here[...], projected), outs)


def edge_grads(listed, grad_agg, w_out, here, halo_there, slope, grad_pre, outs):
    nodes = grad_agg.shape[0]
    spread = dot_back(grad_agg.astype(bf16), w_out).astype(bf16)
    for at in range(0, slope.shape[0], BLOCK):
        block = slice(at, at + BLOCK)
        grad_act = dot(here[block, nodes:], spread)
        grad_pre[block, :] = (grad_act * slope[block, :].astype(f32)).astype(bf16)
    hand_out(dot(halo_there[...], grad_pre[...])[0:listed], outs)


def turn_kernel(layer, shifts, *refs):
    hidden, pres = refs[0], refs[1:3]
    halos, refs = refs[3 : 3 + shifts], refs[3 + shifts :]
    halo_here, there, w_out, gain, here, halo_there, cot = refs[:7]
    hidden_out, grad_pre = refs[7:9]
    outs = refs[9:-2]
    slope, halo = refs[-2:]
    total = node_sum(pres, halos, halo_here, there, slope, halo, grad_pre)
    agg = dot(total.astype(bf16), w_out[layer])
    gain_row = gain[layer : layer + 1, :]
    hidden_out[...] = (hidden[...].astype(f32) + agg * norm_scale(agg) * gain_row).astype(bf16)
    edge_grads(shifts * outs[0].shape[0], norm_back(agg, gain_row, cot[...].astype(f32)), w_out[layer], here, halo_there, slope, grad_pre, outs)


def rest_kernel(layer, side, upstream, grad_pre, there, weights, rest):
    nodes = upstream.shape[0]
    sums = dot(there[side * nodes : (side + 1) * nodes, :], grad_pre[...]).astype(bf16)
    rest[...] = upstream[...].astype(f32) + dot_back(sums, weights[layer])


def arrived(rest, returned, list_there, w_send, halo):
    stack_halo(returned, halo)
    projected = dot_back(halo[...], w_send).astype(bf16)
    return rest[...] + dot(list_there[...], projected)


def back_kernel(layer, shifts, *refs):
    rest = refs[0]
    returned, refs = refs[1 : 1 + shifts], refs[1 + shifts :]
    list_there, w_send, agg, slope, gain, w_out, here, halo_there = refs[:8]
    upstream_out, grad_pre = refs[8:10]
    outs = refs[10:-1]
    halo = refs[-1]
    upstream = arrived(rest, returned, list_there, w_send[layer + 1], halo)
    upstream_out[...] = upstream
    grad_agg = norm_back(agg[...], gain[layer : layer + 1, :], upstream)
    edge_grads(shifts * outs[0].shape[0], grad_agg, w_out[layer], here, halo_there, slope, grad_pre, outs)


def pair_grads(spread, pick, slope):
    return (dot(pick, spread) * slope.astype(f32)).astype(bf16)


def finish_kernel(shifts, *refs):
    rest = refs[0]
    returned, refs = refs[1 : 1 + shifts], refs[1 + shifts :]
    list_there, w_send, enc_sum, gain, w_enc_out, pick, slope, spread_out = refs[:8]
    outs, halo = refs[8:-1], refs[-1]
    upstream = arrived(rest, returned, list_there, w_send[0], halo)
    spread = dot_back(norm_back(enc_sum[...], gain[...], upstream).astype(bf16), w_enc_out[...]).astype(bf16)
    spread_out[...] = spread
    at = 0
    for out in outs:
        rows = slice(at, at + out.shape[0])
        out[...] = pair_grads(spread, pick[rows, :], slope[rows, :])
        at += out.shape[0]


def others_kernel(count, *refs):
    spread = refs[0][...]
    picks, slopes, outs = refs[1 : 1 + count], refs[1 + count : 1 + 2 * count], refs[1 + 2 * count :]
    for pick, slope, out in reversed(list(zip(picks, slopes, outs))):
        skip = pick.shape[0] - out.shape[0]
        out[...] = pair_grads(spread, pick[skip:, :], slope[skip:, :])


def relay_kernel(first, own, passed, *refs):
    rows = passed.shape[0]
    out = refs[0] if len(refs) == 1 else refs[-2]
    out[...] = (own[first : first + rows, :].astype(f32) + passed[...].astype(f32)).astype(bf16)
    if len(refs) > 1:
        refs[-1][...] = refs[0][...]


def sum_kernel(own, piece, total):
    total[...] = own[0 : piece.shape[0], :].astype(f32) + piece[...].astype(f32)


def grid_kernel(whole, *refs):
    blocks, pieces, (w_grid, out) = refs[:whole], refs[whole:-2], refs[-2:]
    if not pieces:
        total = blocks[0][...].astype(f32)
        for block in blocks[1:]:
            total = total + block[...].astype(f32)
        out[...] = dot_back(total.astype(bf16), w_grid[...])
        return
    (own, near), (summed, second) = blocks, pieces
    first = summed.shape[0]
    total = summed[...] + near[0:first, :].astype(f32)
    out[0:first, :] = dot_back(total.astype(bf16), w_grid[...])
    total = own[first:, :].astype(f32) + near[first:, :].astype(f32) + second[...].astype(f32)
    out[first:, :] = dot_back(total.astype(bf16), w_grid[...])


def shifted(value, axis, by):
    size = lax.axis_size(axis)
    return lax.ppermute(value, axis, [(at, (at + by) % size) for at in range(size)])


def partner(at, step, size):
    return at ^ step if size & (size - 1) == 0 else (at + step) % size


def sent_to(value, step):
    size = lax.axis_size("mesh")
    return lax.ppermute(value, "mesh", [(at, partner(at, step, size)) for at in range(size)])


def sent_back(value, step):
    size = lax.axis_size("mesh")
    return lax.ppermute(value, "mesh", [(partner(at, step, size), at) for at in range(size)])


def in_order(pieces, axis):
    return jnp.roll(jnp.stack(pieces)[::-1], lax.axis_index(axis) + 1, axis=0)


def on_device(
    grid_feats,
    g2m_shard,
    g2m_node,
    mesh_init,
    sender_slots,
    receivers,
    halo_index,
    w_enc_grid,
    w_enc_mesh,
    w_enc_out,
    enc_gain,
    w_send,
    w_recv,
    w_out,
    layer_gain,
    out_cot,
):
    shards = lax.axis_size("mesh")
    shard = lax.axis_index("mesh")
    halves = lax.axis_size("rep")
    feats = lax.axis_size("feat")
    nodes, width = mesh_init.shape
    grid, tops = g2m_shard.shape
    edges = sender_slots.shape[0]
    depth = halo_index.shape[2]
    shifts = shards - 1
    listed_rows = shifts * depth
    wide = -(-listed_rows // LANES) * LANES
    all_edges = edges * halves * feats
    enc_gain = enc_gain[None, :]

    relayed = shards == 4
    cuts = 2 if relayed else 1
    shared = relayed and halves == 2
    piece_rows = grid // cuts
    in_place = [pltpu.with_memory_space_constraint(array, pltpu.HBM) for array in (grid_feats, g2m_shard.T, g2m_node.T)]
    (payload,) = call(
        note_kernel,
        [((grid + EXTRA, width), bf16)],
        [((tops, grid), i32), ((tops, grid), i32)],
        copied=True,
    )(*in_place)

    place = sender_slots - nodes
    away = partner(shard, place // depth, shards)
    if shards & (shards - 1):
        away = lax.rem(shard - place // depth + shards, shards)
    slots = jnp.where(sender_slots < nodes, sender_slots, nodes + (shifts - away) * depth + place % depth)
    both = jnp.stack([slots, receivers])
    others = [shifted(both, "rep", step) for step in range(1, halves)]
    if relayed:
        across = sent_to(payload, 2)
        payloads = [payload, sent_to(payload, 1), across]
    else:
        payloads = [payload] + [sent_to(payload, step) for step in range(1, shards)]
    both = in_order([both] + others, "rep")
    both = in_order([both] + [shifted(both, "feat", step) for step in range(1, feats)], "feat")
    both = both.reshape(feats * halves, 2, edges)
    all_slots, all_receivers = both[:, 0].reshape(1, -1), both[:, 1].reshape(1, -1)
    steps = shards - jnp.arange(1, shards, dtype=i32)
    if shared:
        core = lax.axis_index("rep")
        steps = jnp.where((core == 0) & (steps > 1), 5 - steps, steps)
        entry = all_slots - nodes
        turned = (core == 0) & (entry >= 0) & (entry < 2 * depth)
        all_slots = all_slots + jnp.where(turned, jnp.where(entry < depth, depth, -depth), 0)
    readers = partner(shard, steps, shards)
    lists = jnp.take(halo_index[0], readers, axis=0).reshape(1, -1)
    here, there, halo_here, halo_there, list_here, list_there = call(
        place_kernel,
        [
            ((all_edges, 2 * nodes), bf16),
            ((2 * nodes, all_edges), bf16),
            ((all_edges, wide), bf16),
            ((wide, all_edges), bf16),
            ((listed_rows, nodes), bf16),
            ((nodes, listed_rows), bf16),
        ],
        products=[(all_edges, nodes, width), (all_edges, 2 * nodes, width)],
    )(all_slots, all_receivers, lists)

    if relayed:
        across, list_here = lax.optimization_barrier((across, list_here))
        payloads.append(sent_to(across, 1))

    meta = jnp.broadcast_to(jnp.stack([lax.axis_index("rep"), shard]).astype(i32)[:, None], (2, width))
    node_f32, node_bf16 = ((nodes, width), f32), ((nodes, width), bf16)
    row_shape, half = ((grid, width), bf16), nodes // halves
    square = (nodes, width, width)
    enc_picks, enc_slopes = [], []
    base, total = mesh_init, None
    groups = [payloads[:2]] + [payloads[at : at + 1] for at in range(2, shards)]
    for at, group in enumerate(groups):
        first, last = at == 0, at == len(groups) - 1
        count = len(group)
        outs = [((grid, nodes), bf16)] * count + [row_shape] * count
        outs += [node_bf16] if first else []
        outs += [((half, width), f32)] + [((half, width), bf16)] * (halves - 1) if last else [node_f32]
        got = list(
            call(
                functools.partial(encode_kernel, count, first, last, halves),
                outs,
                (),
                [square] * first + [(grid, width, width), (grid, nodes, width), (nodes, grid, width)] * count,
            )(
                meta, base, w_enc_grid, *((w_enc_mesh, list_here) if first else (total,)), *group
            )
        )
        enc_picks += got[:count]
        enc_slopes += got[count : 2 * count]
        del got[: 2 * count]
        if first:
            base = got.pop(0)
        total = got[0]
    part = got[0]
    for step in range(1, halves):
        part = part + shifted(got[step], "rep", step).astype(f32)
    part = part.astype(bf16)
    pieces = [part] + [shifted(part, "feat", step) for step in range(1, feats)]
    if feats > 2:
        pieces = list(in_order(pieces, "feat"))
    part = sum(piece.astype(f32) for piece in pieces).astype(bf16)
    parts = [part] + [shifted(part, "rep", -step) for step in range(1, halves)]

    listed = [((depth, width), bf16)] * (2 if shared else shifts)

    def exchange(blocks, send, early):
        if not shared:
            return [send(block, shifts - at) for at, block in enumerate(blocks)], early
        far = lax.ppermute(
            blocks[0], ("mesh", "rep"), [(2 * at + side, 2 * (at ^ (2 + side)) + side) for at in range(4) for side in range(2)]
        )
        near = send(blocks[1], 1)
        far, early = lax.optimization_barrier((far, early))
        return [far, shifted(far, "rep", 1), near], early

    hidden, enc_sum, sent, *outgoing = call(
        functools.partial(start_kernel, halves), [node_bf16, node_f32, node_bf16] + listed, [node_bf16],
        [square, square, (listed_rows, nodes, width)],
    )(meta, *parts, mesh_init, w_enc_out, enc_gain, w_send, list_here)

    half_f32, edge_bf16 = ((all_edges // 2, width), f32), ((all_edges, width), bf16)
    halo, back_halo = ((wide, width), bf16), ((listed_rows, width), bf16)
    forward_products = [(all_edges, wide, width), (nodes, all_edges, width), square]
    backward_products = [square, (all_edges, nodes, width), (wide, all_edges, width)]
    half_product = (all_edges // 2, 2 * nodes, width)

    def arriving(layer):
        early = call(
            functools.partial(local_kernel, layer), [half_f32, ((2 * nodes, width), bf16)], (), [square, half_product]
        )(hidden, sent, here, w_recv)
        halos, (pre, both_tables) = exchange(outgoing, sent_to, early)
        (more,) = call(local_more_kernel, [half_f32], (), [half_product])(both_tables, here)
        return hidden, pre, more, *halos

    records = []
    for layer in range(LAYERS - 1):
        hidden, agg, slope, sent, *outgoing = call(
            functools.partial(layer_kernel, layer, shifts),
            [node_bf16, node_f32, edge_bf16, node_bf16] + listed,
            [halo, edge_bf16],
            forward_products + [square, (listed_rows, nodes, width)],
        )(*arriving(layer), halo_here, there, w_out, layer_gain, w_send, list_here)
        records.append((agg, slope))
    last = LAYERS - 1
    final_mesh, grad_pre, *outgoing = call(
        functools.partial(turn_kernel, last, shifts), [node_bf16, edge_bf16] + listed, [edge_bf16, halo],
        forward_products + backward_products,
    )(*arriving(last), halo_here, there, w_out, layer_gain, here, halo_there, out_cot)
    upstream = out_cot
    for layer in reversed(range(LAYERS)):

        def rest_of(side, upstream, weights):
            (rest,) = call(
                functools.partial(rest_kernel, layer, side), [node_f32], (), [(nodes, all_edges, width), square]
            )(upstream, grad_pre, there, weights)
            return rest

        returned, early = exchange(outgoing, sent_back, rest_of(0, upstream, w_send))
        rest = rest_of(1, early, w_recv)
        if layer:
            agg, slope = records[layer - 1]
            upstream, grad_pre, *outgoing = call(
                functools.partial(back_kernel, layer - 1, shifts),
                [node_f32, edge_bf16] + listed,
                [back_halo],
                backward_products + [(listed_rows, width, width), (nodes, listed_rows, width)],
            )(rest, *returned, list_there, w_send, agg, slope, layer_gain, w_out, here, halo_there)
    piece = ((piece_rows, width), bf16)
    one = (grid, nodes, width)
    spread, *far = call(
        functools.partial(finish_kernel, shifts),
        [node_bf16] + [piece] * cuts,
        [back_halo],
        [square, (listed_rows, width, width), (nodes, listed_rows, width), one],
    )(rest, *returned, list_there, w_send, enc_sum, enc_gain, w_enc_out, enc_picks[-1], enc_slopes[-1])
    blocks = call(
        functools.partial(others_kernel, shards - 1), [row_shape] * (shards - 1), products=[one] * (shards - 1)
    )(spread, *enc_picks[:-1], *enc_slopes[:-1])
    if relayed:
        passed = [sent_back(block, 1) for block in far]
        first, near = call(functools.partial(relay_kernel, 0), [piece, row_shape])(blocks[2], passed[0], blocks[1])
        (second,) = call(functools.partial(relay_kernel, piece_rows), [piece])(blocks[2], passed[1])
        near = sent_back(near, 1)
        first, second = sent_back(first, 2), sent_back(second, 2)
        (summed,) = call(sum_kernel, [((piece_rows, width), f32)])(blocks[0], first)
        (grid_grad,) = call(
            functools.partial(grid_kernel, 2), [((grid, width), f32)], products=[(grid, width, width)]
        )(blocks[0], near, summed, second, w_enc_grid)
    else:
        blocks = [*blocks, *far]
        blocks = [blocks[0]] + [sent_back(block, step) for step, block in enumerate(blocks) if step]
        (grid_grad,) = call(
            functools.partial(grid_kernel, shards), [((grid, width), f32)], products=[(grid, width, width)]
        )(*blocks, w_enc_grid)
    return (final_mesh, grid_grad)


def solution(mesh):
    return jax.shard_map(
        on_device,
        mesh=mesh,
        in_specs=(
            P(("groups", "mesh", "feat", "rep"), None),
            P(("groups", "mesh", "feat", "rep"), None),
            P(("groups", "mesh", "feat", "rep"), None),
            P(("groups", "mesh"), None),
            P(("groups", "mesh", "feat", "rep")),
            P(("groups", "mesh", "feat", "rep")),
            P(("groups", "mesh"), None, None),
            P(),
            P(),
            P(),
            P(),
            P(),
            P(),
            P(),
            P(),
            P(("groups", "mesh"), None),
        ),
        out_specs=(P(("groups", "mesh"), None), P(("groups", "mesh", "feat", "rep"), None)),
        check_vma=False,
    )
```

```python
import functools
import math

import jax
import jax.numpy as jnp
from jax import lax
from jax.experimental import pallas as pl
from jax.experimental.pallas import tpu as pltpu
from jax.sharding import PartitionSpec as P

LAYERS = 3
LANES = 128
BLOCK = 512
EXTRA = 16
eps = 1e-05

f32 = jnp.float32
bf16 = jnp.bfloat16
i32 = jnp.int32


def norm_scale(totals):
    return lax.rsqrt(jnp.mean(totals * totals, axis=-1, keepdims=True) + eps)


def norm_back(totals, gain_row, upstream):
    scaled = norm_scale(totals)
    normed = totals * scaled
    slope = upstream * gain_row
    return scaled * (slope - normed * jnp.mean(slope * normed, axis=-1, keepdims=True))


def dot(left, right):
    return jnp.dot(left, right, preferred_element_type=f32)


def dot_back(left, right):
    return lax.dot_general(left, right, (((1,), (1,)), ((), ())), preferred_element_type=f32)


def gated(half):
    half = half.astype(bf16)
    bend = jnp.tanh(half)
    act = half + half * bend
    return act, (1.0 + act) + bend * (1.0 - act)


def as_mask(hit):
    return jnp.where(hit, 1.0, 0.0).astype(bf16)


def pick_columns(index, first, height):
    place = lax.broadcasted_iota(i32, (height, index.shape[1]), 0) + first
    return as_mask(place == index)


def upright(index):
    count = index.shape[1]
    if count < LANES:
        index = jnp.concatenate([index, jnp.full((1, LANES - count), -1, i32)], axis=1)
    return jnp.broadcast_to(index, (LANES, LANES)).T[:count]


def pick_rows(column, first, width):
    lane = lax.broadcasted_iota(i32, column.shape, 1) + first
    return jnp.concatenate([as_mask(column == lane + at) for at in range(0, width, LANES)], axis=1)


def call(body, outs, scratch=(), products=(), copied=False):
    def run(*args):
        def where(array):
            if copied:
                return pl.BlockSpec(memory_space=pltpu.HBM)
            return pl.BlockSpec(memory_space=pltpu.SMEM if array.dtype == i32 and array.ndim == 1 else pltpu.VMEM)

        def size(shape, dtype):
            return jnp.dtype(dtype).itemsize * math.prod(shape)

        own = sum(size(*held) for held in scratch) + (10 << 20)
        moved = sum(array.dtype.itemsize * array.size for array in args) + sum(size(*out) for out in outs)
        limit = own if own + moved < 40 << 20 else min(own + moved, 60 << 20)
        semaphores = [pltpu.SemaphoreType.DMA((2 + len(outs),))] if copied else []
        return pl.pallas_call(
            body,
            out_shape=tuple(jax.ShapeDtypeStruct(shape, dtype) for shape, dtype in outs),
            in_specs=[where(array) for array in args],
            out_specs=tuple(pl.BlockSpec(memory_space=pltpu.VMEM) for _ in outs),
            scratch_shapes=[pltpu.VMEM(shape, dtype) for shape, dtype in scratch] + semaphores,
            compiler_params=pltpu.CompilerParams(vmem_limit_bytes=limit),
            cost_estimate=pl.CostEstimate(
                flops=2 * sum(math.prod(product) for product in products), bytes_accessed=moved, transcendentals=0
            ),
        )(*args)

    return run


def place_kernel(slots, receivers, order, here, there, halo_here, halo_there, list_here, list_there):
    nodes = here.shape[1] // 2
    wide = halo_here.shape[1]

    def body(at):
        block = pl.ds(pl.multiple_of(at * LANES, LANES), LANES)
        slot, receiver = slots[:, block], receivers[:, block]
        slot_column, receiver_column = upright(slot), upright(receiver)
        here[block, 0:nodes] = pick_rows(slot_column, 0, nodes)
        here[block, nodes:] = pick_rows(receiver_column, 0, nodes)
        halo_here[block, :] = pick_rows(slot_column, nodes, wide)
        there[0:nodes, block] = pick_columns(slot, 0, nodes)
        there[nodes:, block] = pick_columns(receiver, 0, nodes)
        halo_there[:, block] = pick_columns(slot, nodes, wide)

    pl.loop(0, slots.shape[1] // LANES)(body)
    count = order.shape[1]
    for at in range(0, count, LANES):
        end = min(at + LANES, count)
        list_here[at:end, :] = pick_rows(upright(order[:, at:end]), 0, nodes)
    list_there[...] = pick_columns(order[...], 0, nodes)


def note_kernel(rows, shards, nodes, payload, shard_rows, node_rows, arrived):
    grid = shards.shape[1]
    first = payload.shape[0] - EXTRA
    copies = [
        pltpu.make_async_copy(shards, shard_rows, arrived.at[0]),
        pltpu.make_async_copy(nodes, node_rows, arrived.at[1]),
        pltpu.make_async_copy(rows.at[0:first], payload.at[0:first], arrived.at[2]),
    ]
    for copy in copies:
        copy.start()
    for copy in copies[:2]:
        copy.wait()
    row = lax.broadcasted_iota(i32, (EXTRA, grid), 0)
    notes = jnp.full((EXTRA, grid), -1, i32)
    for top in range(shards.shape[0]):
        node = node_rows[top : top + 1, :]
        for at, value in enumerate((shard_rows[top : top + 1, :], node & 255, node >> 8)):
            notes = jnp.where(row == 3 * top + at, value, notes)
    payload[first:, 0:grid] = notes.astype(f32).astype(bf16)
    if grid < payload.shape[1]:
        payload[first:, grid:] = jnp.zeros((EXTRA, payload.shape[1] - grid), bf16)
    copies[2].wait()


def encode_kernel(steps, first, last, halves, *refs):
    refs = list(refs)
    meta, base, w_grid = refs[:3]
    del refs[:3]
    if first:
        w_mesh, _ = refs.pop(0), refs.pop(0)
        projected = dot(base[...], w_mesh[...]).astype(bf16)
    else:
        total_in = refs.pop(0)
        projected = base[...]
    payloads = refs[:steps]
    del refs[:steps]
    picks, slopes = refs[:steps], refs[steps : 2 * steps]
    del refs[: 2 * steps]
    total = None if first else total_in[...]
    nodes = projected.shape[0]
    for payload, pick, slope_out in zip(payloads, picks, slopes):
        grid = pick.shape[0]
        notes = payload[grid:, 0:grid].astype(f32)
        target = jnp.full((1, grid), -1.0, f32)
        for at in range(0, notes.shape[0] // 3 * 3, 3):
            named = notes[at : at + 1] == meta[1:2, 0:grid].astype(f32)
            target = jnp.where(named, notes[at + 1 : at + 2] + 256.0 * notes[at + 2 : at + 3], target)
        target = target.astype(i32)
        column = jnp.concatenate([upright(target[:, at : at + LANES]) for at in range(0, grid, LANES)], axis=0)
        picked = pick_rows(column, 0, nodes)
        pick[...] = picked
        pre = dot(payload[0:grid, :], w_grid[...]) + dot(picked, projected)
        act, slope = gated(0.5 * pre)
        slope_out[...] = slope.astype(bf16)
        added = dot(pick_columns(target, 0, nodes), act.astype(bf16))
        total = added if total is None else total + added
    if first:
        refs.pop(0)[...] = projected
    if not last:
        refs[0][...] = total
        return
    keep, sends = refs[0], refs[1:halves]
    part = nodes // halves
    own = meta[0:1, :]

    def half(shift):
        rows = total[0:part]
        for at in range(1, halves):
            rows = jnp.where(own == (at - shift) % halves, total[at * part : (at + 1) * part], rows)
        return rows

    keep[...] = half(0)
    for shift in range(1, halves):
        sends[shift - 1][...] = half(shift).astype(bf16)


def hand_out(rows, outs):
    rows = rows.astype(bf16)
    depth = outs[0].shape[0]
    count = rows.shape[0] // depth
    for at, out in enumerate(outs):
        first = 0 if at == 0 else (count - len(outs) + at) * depth
        out[...] = rows[first : first + depth]


def start_kernel(halves, *refs):
    meta = refs[0]
    parts = refs[1 : 1 + halves]
    mesh_init, w_enc_out, gain, w_send, list_here = refs[1 + halves : 6 + halves]
    hidden_out, enc_sum_out, sent = refs[6 + halves : 9 + halves]
    outs = refs[9 + halves : -1]
    whole = refs[-1]
    part = parts[0].shape[0]
    own = meta[0:1, :]
    for at in range(halves):
        rows = parts[0][...].astype(f32)
        for shift in range(1, halves):
            rows = jnp.where(own == (at - shift) % halves, parts[shift][...].astype(f32), rows)
        whole[at * part : (at + 1) * part, :] = rows.astype(bf16)
    enc_sum = dot(whole[...], w_enc_out[...])
    enc_sum_out[...] = enc_sum
    hidden = (mesh_init[...].astype(f32) + enc_sum * norm_scale(enc_sum) * gain[...]).astype(bf16)
    hidden_out[...] = hidden
    projected = (0.5 * dot(hidden, w_send[0])).astype(bf16)
    sent[...] = projected
    hand_out(dot(list_here[...], projected), outs)


def local_kernel(layer, hidden, sent, here, w_recv, pre, table):
    nodes = hidden.shape[0]
    table[0:nodes, :] = sent[...]
    table[nodes:, :] = (0.5 * dot(hidden[...], w_recv[layer])).astype(bf16)
    for at in range(0, pre.shape[0], BLOCK):
        pre[at : at + BLOCK, :] = dot(here[at : at + BLOCK, :], table[...])


def local_more_kernel(table, here, pre):
    skip = here.shape[0] - pre.shape[0]
    for at in range(0, pre.shape[0], BLOCK):
        pre[at : at + BLOCK, :] = dot(here[skip + at : skip + at + BLOCK, :], table[...])


def stack_halo(halos, halo):
    at = 0
    for block in halos:
        halo[at : at + block.shape[0], :] = block[...]
        at += block.shape[0]
    if at < halo.shape[0]:
        halo[at:, :] = jnp.zeros((halo.shape[0] - at, halo.shape[1]), bf16)


def node_sum(pres, halos, halo_here, there, slope_out, halo, act_out):
    nodes = there.shape[0] // 2
    stack_halo(halos, halo)
    half = pres[0].shape[0]
    for at in range(0, 2 * half, BLOCK):
        block = slice(at, at + BLOCK)
        pre = pres[at // half][at % half : at % half + BLOCK, :]
        act, slope = gated(pre + dot(halo_here[block, :], halo[...]))
        slope_out[block, :] = slope.astype(bf16)
        act_out[block, :] = act.astype(bf16)
    return dot(there[nodes:, :], act_out[...])


def layer_kernel(layer, shifts, *refs):
    hidden, pres = refs[0], refs[1:3]
    halos, refs = refs[3 : 3 + shifts], refs[3 + shifts :]
    halo_here, there, w_out, gain, w_send, list_here = refs[:6]
    hidden_out, agg_out, slope_out, sent_out = refs[6:10]
    outs = refs[10:-2]
    total = node_sum(pres, halos, halo_here, there, slope_out, *refs[-2:])
    agg = dot(total.astype(bf16), w_out[layer])
    agg_out[...] = agg
    fresh = (hidden[...].astype(f32) + agg * norm_scale(agg) * gain[layer : layer + 1, :]).astype(bf16)
    hidden_out[...] = fresh
    projected = (0.5 * dot(fresh, w_send[layer + 1])).astype(bf16)
    sent_out[...] = projected
    hand_out(dot(list_here[...], projected), outs)


def edge_grads(listed, grad_agg, w_out, here, halo_there, slope, grad_pre, outs):
    nodes = grad_agg.shape[0]
    spread = (0.5 * dot_back(grad_agg.astype(bf16), w_out)).astype(bf16)
    for at in range(0, slope.shape[0], BLOCK):
        block = slice(at, at + BLOCK)
        grad_act = dot(here[block, nodes:], spread)
        grad_pre[block, :] = (grad_act * slope[block, :].astype(f32)).astype(bf16)
    hand_out(dot(halo_there[...], grad_pre[...])[0:listed], outs)


def turn_kernel(layer, shifts, *refs):
    hidden, pres = refs[0], refs[1:3]
    halos, refs = refs[3 : 3 + shifts], refs[3 + shifts :]
    halo_here, there, w_out, gain, here, halo_there, cot = refs[:7]
    hidden_out, grad_pre = refs[7:9]
    outs = refs[9:-2]
    slope, halo = refs[-2:]
    total = node_sum(pres, halos, halo_here, there, slope, halo, grad_pre)
    agg = dot(total.astype(bf16), w_out[layer])
    gain_row = gain[layer : layer + 1, :]
    hidden_out[...] = (hidden[...].astype(f32) + agg * norm_scale(agg) * gain_row).astype(bf16)
    edge_grads(shifts * outs[0].shape[0], norm_back(agg, gain_row, cot[...].astype(f32)), w_out[layer], here, halo_there, slope, grad_pre, outs)


def rest_kernel(layer, side, upstream, grad_pre, there, weights, rest):
    nodes = upstream.shape[0]
    sums = dot(there[side * nodes : (side + 1) * nodes, :], grad_pre[...]).astype(bf16)
    rest[...] = upstream[...].astype(f32) + dot_back(sums, weights[layer])


def arrived(rest, returned, list_there, w_send, halo):
    stack_halo(returned, halo)
    projected = dot_back(halo[...], w_send).astype(bf16)
    return rest[...] + dot(list_there[...], projected)


def back_kernel(layer, shifts, *refs):
    rest = refs[0]
    returned, refs = refs[1 : 1 + shifts], refs[1 + shifts :]
    list_there, w_send, agg, slope, gain, w_out, here, halo_there = refs[:8]
    upstream_out, grad_pre = refs[8:10]
    outs = refs[10:-1]
    halo = refs[-1]
    upstream = arrived(rest, returned, list_there, w_send[layer + 1], halo)
    upstream_out[...] = upstream
    grad_agg = norm_back(agg[...], gain[layer : layer + 1, :], upstream)
    edge_grads(shifts * outs[0].shape[0], grad_agg, w_out[layer], here, halo_there, slope, grad_pre, outs)


def pair_grads(spread, pick, slope):
    return (dot(pick, spread) * slope.astype(f32)).astype(bf16)


def finish_kernel(shifts, *refs):
    rest = refs[0]
    returned, refs = refs[1 : 1 + shifts], refs[1 + shifts :]
    list_there, w_send, enc_sum, gain, w_enc_out, pick, slope, spread_out = refs[:8]
    outs, halo = refs[8:-1], refs[-1]
    upstream = arrived(rest, returned, list_there, w_send[0], halo)
    spread = (0.5 * dot_back(norm_back(enc_sum[...], gain[...], upstream).astype(bf16), w_enc_out[...])).astype(bf16)
    spread_out[...] = spread
    at = 0
    for out in outs:
        rows = slice(at, at + out.shape[0])
        out[...] = pair_grads(spread, pick[rows, :], slope[rows, :])
        at += out.shape[0]


def others_kernel(count, *refs):
    spread = refs[0][...]
    picks, slopes, outs = refs[1 : 1 + count], refs[1 + count : 1 + 2 * count], refs[1 + 2 * count :]
    for pick, slope, out in reversed(list(zip(picks, slopes, outs))):
        skip = pick.shape[0] - out.shape[0]
        out[...] = pair_grads(spread, pick[skip:, :], slope[skip:, :])


def relay_kernel(first, own, passed, *refs):
    rows = passed.shape[0]
    out = refs[0] if len(refs) == 1 else refs[-2]
    out[...] = (own[first : first + rows, :].astype(f32) + passed[...].astype(f32)).astype(bf16)
    if len(refs) > 1:
        refs[-1][...] = refs[0][...]


def sum_kernel(own, piece, total):
    total[...] = own[0 : piece.shape[0], :].astype(f32) + piece[...].astype(f32)


def grid_kernel(whole, *refs):
    blocks, pieces, (w_grid, out) = refs[:whole], refs[whole:-2], refs[-2:]
    if not pieces:
        total = blocks[0][...].astype(f32)
        for block in blocks[1:]:
            total = total + block[...].astype(f32)
        out[...] = dot_back(total.astype(bf16), w_grid[...])
        return
    (own, near), (summed, second) = blocks, pieces
    first = summed.shape[0]
    total = summed[...] + near[0:first, :].astype(f32)
    out[0:first, :] = dot_back(total.astype(bf16), w_grid[...])
    total = own[first:, :].astype(f32) + near[first:, :].astype(f32) + second[...].astype(f32)
    out[first:, :] = dot_back(total.astype(bf16), w_grid[...])


def shifted(value, axis, by):
    size = lax.axis_size(axis)
    return lax.ppermute(value, axis, [(at, (at + by) % size) for at in range(size)])


def partner(at, step, size):
    return at ^ step if size & (size - 1) == 0 else (at + step) % size


def sent_to(value, step):
    size = lax.axis_size("mesh")
    return lax.ppermute(value, "mesh", [(at, partner(at, step, size)) for at in range(size)])


def sent_back(value, step):
    size = lax.axis_size("mesh")
    return lax.ppermute(value, "mesh", [(partner(at, step, size), at) for at in range(size)])


def in_order(pieces, axis):
    return jnp.roll(jnp.stack(pieces)[::-1], lax.axis_index(axis) + 1, axis=0)


def on_device(
    grid_feats,
    g2m_shard,
    g2m_node,
    mesh_init,
    sender_slots,
    receivers,
    halo_index,
    w_enc_grid,
    w_enc_mesh,
    w_enc_out,
    enc_gain,
    w_send,
    w_recv,
    w_out,
    layer_gain,
    out_cot,
):
    shards = lax.axis_size("mesh")
    shard = lax.axis_index("mesh")
    halves = lax.axis_size("rep")
    feats = lax.axis_size("feat")
    nodes, width = mesh_init.shape
    grid, tops = g2m_shard.shape
    edges = sender_slots.shape[0]
    depth = halo_index.shape[2]
    shifts = shards - 1
    listed_rows = shifts * depth
    wide = -(-listed_rows // LANES) * LANES
    all_edges = edges * halves * feats
    enc_gain = enc_gain[None, :]

    relayed = shards == 4
    cuts = 2 if relayed else 1
    shared = relayed and halves == 2
    piece_rows = grid // cuts
    in_place = [pltpu.with_memory_space_constraint(array, pltpu.HBM) for array in (grid_feats, g2m_shard.T, g2m_node.T)]
    (payload,) = call(
        note_kernel,
        [((grid + EXTRA, width), bf16)],
        [((tops, grid), i32), ((tops, grid), i32)],
        copied=True,
    )(*in_place)

    place = sender_slots - nodes
    away = partner(shard, place // depth, shards)
    if shards & (shards - 1):
        away = lax.rem(shard - place // depth + shards, shards)
    slots = jnp.where(sender_slots < nodes, sender_slots, nodes + (shifts - away) * depth + place % depth)
    both = jnp.stack([slots, receivers])
    others = [shifted(both, "rep", step) for step in range(1, halves)]
    if relayed:
        across = sent_to(payload, 2)
        payloads = [payload, sent_to(payload, 1), across]
    else:
        payloads = [payload] + [sent_to(payload, step) for step in range(1, shards)]
    both = in_order([both] + others, "rep")
    both = in_order([both] + [shifted(both, "feat", step) for step in range(1, feats)], "feat")
    both = both.reshape(feats * halves, 2, edges)
    all_slots, all_receivers = both[:, 0].reshape(1, -1), both[:, 1].reshape(1, -1)
    steps = shards - jnp.arange(1, shards, dtype=i32)
    if shared:
        core = lax.axis_index("rep")
        steps = jnp.where((core == 0) & (steps > 1), 5 - steps, steps)
        entry = all_slots - nodes
        turned = (core == 0) & (entry >= 0) & (entry < 2 * depth)
        all_slots = all_slots + jnp.where(turned, jnp.where(entry < depth, depth, -depth), 0)
    readers = partner(shard, steps, shards)
    lists = jnp.take(halo_index[0], readers, axis=0).reshape(1, -1)
    here, there, halo_here, halo_there, list_here, list_there = call(
        place_kernel,
        [
            ((all_edges, 2 * nodes), bf16),
            ((2 * nodes, all_edges), bf16),
            ((all_edges, wide), bf16),
            ((wide, all_edges), bf16),
            ((listed_rows, nodes), bf16),
            ((nodes, listed_rows), bf16),
        ],
        products=[(all_edges, nodes, width), (all_edges, 2 * nodes, width)],
    )(all_slots, all_receivers, lists)

    if relayed:
        across, list_here = lax.optimization_barrier((across, list_here))
        payloads.append(sent_to(across, 1))

    meta = jnp.broadcast_to(jnp.stack([lax.axis_index("rep"), shard]).astype(i32)[:, None], (2, width))
    node_f32, node_bf16 = ((nodes, width), f32), ((nodes, width), bf16)
    row_shape, half = ((grid, width), bf16), nodes // halves
    square = (nodes, width, width)
    enc_picks, enc_slopes = [], []
    base, total = mesh_init, None
    groups = [payloads[:2]] + [payloads[at : at + 1] for at in range(2, shards)]
    for at, group in enumerate(groups):
        first, last = at == 0, at == len(groups) - 1
        count = len(group)
        outs = [((grid, nodes), bf16)] * count + [row_shape] * count
        outs += [node_bf16] if first else []
        outs += [((half, width), f32)] + [((half, width), bf16)] * (halves - 1) if last else [node_f32]
        got = list(
            call(
                functools.partial(encode_kernel, count, first, last, halves),
                outs,
                (),
                [square] * first + [(grid, width, width), (grid, nodes, width), (nodes, grid, width)] * count,
            )(
                meta, base, w_enc_grid, *((w_enc_mesh, list_here) if first else (total,)), *group
            )
        )
        enc_picks += got[:count]
        enc_slopes += got[count : 2 * count]
        del got[: 2 * count]
        if first:
            base = got.pop(0)
        total = got[0]
    part = got[0]
    for step in range(1, halves):
        part = part + shifted(got[step], "rep", step).astype(f32)
    part = part.astype(bf16)
    pieces = [part] + [shifted(part, "feat", step) for step in range(1, feats)]
    if feats > 2:
        pieces = list(in_order(pieces, "feat"))
    part = sum(piece.astype(f32) for piece in pieces).astype(bf16)
    parts = [part] + [shifted(part, "rep", -step) for step in range(1, halves)]

    listed = [((depth, width), bf16)] * (2 if shared else shifts)

    def exchange(blocks, send, early):
        if not shared:
            return [send(block, shifts - at) for at, block in enumerate(blocks)], early
        far = lax.ppermute(
            blocks[0], ("mesh", "rep"), [(2 * at + side, 2 * (at ^ (2 + side)) + side) for at in range(4) for side in range(2)]
        )
        near = send(blocks[1], 1)
        far, early = lax.optimization_barrier((far, early))
        return [far, shifted(far, "rep", 1), near], early

    hidden, enc_sum, sent, *outgoing = call(
        functools.partial(start_kernel, halves), [node_bf16, node_f32, node_bf16] + listed, [node_bf16],
        [square, square, (listed_rows, nodes, width)],
    )(meta, *parts, mesh_init, w_enc_out, enc_gain, w_send, list_here)

    half_f32, edge_bf16 = ((all_edges // 2, width), f32), ((all_edges, width), bf16)
    halo, back_halo = ((wide, width), bf16), ((listed_rows, width), bf16)
    forward_products = [(all_edges, wide, width), (nodes, all_edges, width), square]
    backward_products = [square, (all_edges, nodes, width), (wide, all_edges, width)]
    half_product = (all_edges // 2, 2 * nodes, width)

    def arriving(layer):
        early = call(
            functools.partial(local_kernel, layer), [half_f32, ((2 * nodes, width), bf16)], (), [square, half_product]
        )(hidden, sent, here, w_recv)
        halos, (pre, both_tables) = exchange(outgoing, sent_to, early)
        (more,) = call(local_more_kernel, [half_f32], (), [half_product])(both_tables, here)
        return hidden, pre, more, *halos

    records = []
    for layer in range(LAYERS - 1):
        hidden, agg, slope, sent, *outgoing = call(
            functools.partial(layer_kernel, layer, shifts),
            [node_bf16, node_f32, edge_bf16, node_bf16] + listed,
            [halo, edge_bf16],
            forward_products + [square, (listed_rows, nodes, width)],
        )(*arriving(layer), halo_here, there, w_out, layer_gain, w_send, list_here)
        records.append((agg, slope))
    last = LAYERS - 1
    final_mesh, grad_pre, *outgoing = call(
        functools.partial(turn_kernel, last, shifts), [node_bf16, edge_bf16] + listed, [edge_bf16, halo],
        forward_products + backward_products,
    )(*arriving(last), halo_here, there, w_out, layer_gain, here, halo_there, out_cot)
    upstream = out_cot
    for layer in reversed(range(LAYERS)):

        def rest_of(side, upstream, weights):
            (rest,) = call(
                functools.partial(rest_kernel, layer, side), [node_f32], (), [(nodes, all_edges, width), square]
            )(upstream, grad_pre, there, weights)
            return rest

        returned, early = exchange(outgoing, sent_back, rest_of(0, upstream, w_send))
        rest = rest_of(1, early, w_recv)
        if layer:
            agg, slope = records[layer - 1]
            upstream, grad_pre, *outgoing = call(
                functools.partial(back_kernel, layer - 1, shifts),
                [node_f32, edge_bf16] + listed,
                [back_halo],
                backward_products + [(listed_rows, width, width), (nodes, listed_rows, width)],
            )(rest, *returned, list_there, w_send, agg, slope, layer_gain, w_out, here, halo_there)
    piece = ((piece_rows, width), bf16)
    one = (grid, nodes, width)
    spread, *far = call(
        functools.partial(finish_kernel, shifts),
        [node_bf16] + [piece] * cuts,
        [back_halo],
        [square, (listed_rows, width, width), (nodes, listed_rows, width), one],
    )(rest, *returned, list_there, w_send, enc_sum, enc_gain, w_enc_out, enc_picks[-1], enc_slopes[-1])
    blocks = call(
        functools.partial(others_kernel, shards - 1), [row_shape] * (shards - 1), products=[one] * (shards - 1)
    )(spread, *enc_picks[:-1], *enc_slopes[:-1])
    if relayed:
        passed = [sent_back(block, 1) for block in far]
        first, near = call(functools.partial(relay_kernel, 0), [piece, row_shape])(blocks[2], passed[0], blocks[1])
        (second,) = call(functools.partial(relay_kernel, piece_rows), [piece])(blocks[2], passed[1])
        near = sent_back(near, 1)
        first, second = sent_back(first, 2), sent_back(second, 2)
        (summed,) = call(sum_kernel, [((piece_rows, width), f32)])(blocks[0], first)
        (grid_grad,) = call(
            functools.partial(grid_kernel, 2), [((grid, width), f32)], products=[(grid, width, width)]
        )(blocks[0], near, summed, second, w_enc_grid)
    else:
        blocks = [*blocks, *far]
        blocks = [blocks[0]] + [sent_back(block, step) for step, block in enumerate(blocks) if step]
        (grid_grad,) = call(
            functools.partial(grid_kernel, shards), [((grid, width), f32)], products=[(grid, width, width)]
        )(*blocks, w_enc_grid)
    return (final_mesh, grid_grad)


def solution(mesh):
    return jax.shard_map(
        on_device,
        mesh=mesh,
        in_specs=(
            P(("groups", "mesh", "feat", "rep"), None),
            P(("groups", "mesh", "feat", "rep"), None),
            P(("groups", "mesh", "feat", "rep"), None),
            P(("groups", "mesh"), None),
            P(("groups", "mesh", "feat", "rep")),
            P(("groups", "mesh", "feat", "rep")),
            P(("groups", "mesh"), None, None),
            P(),
            P(),
            P(),
            P(),
            P(),
            P(),
            P(),
            P(),
            P(("groups", "mesh"), None),
        ),
        out_specs=(P(("groups", "mesh"), None), P(("groups", "mesh", "feat", "rep"), None)),
        check_vma=False,
    )
```

```python
import functools
import math

import jax
import jax.numpy as jnp
from jax import lax
from jax.experimental import pallas as pl
from jax.experimental.pallas import tpu as pltpu
from jax.sharding import PartitionSpec as P

LAYERS = 3
LANES = 128
BLOCK = 512
EXTRA = 16
eps = 1e-05

f32 = jnp.float32
bf16 = jnp.bfloat16
i32 = jnp.int32


def norm_scale(totals):
    return lax.rsqrt(jnp.mean(totals * totals, axis=-1, keepdims=True) + eps)


def norm_back(totals, gain_row, upstream):
    scaled = norm_scale(totals)
    normed = totals * scaled
    slope = upstream * gain_row
    return scaled * (slope - normed * jnp.mean(slope * normed, axis=-1, keepdims=True))


def dot(left, right):
    return jnp.dot(left, right, preferred_element_type=f32)


def dot_back(left, right):
    return lax.dot_general(left, right, (((1,), (1,)), ((), ())), preferred_element_type=f32)


def gated(half):
    half = half.astype(bf16)
    bend = jnp.tanh(half)
    act = half + half * bend
    return act, (1.0 + act) + bend * (1.0 - act)


def as_mask(hit):
    return jnp.where(hit, 1.0, 0.0).astype(bf16)


def pick_columns(index, first, height):
    place = lax.broadcasted_iota(i32, (height, index.shape[1]), 0) + first
    return as_mask(place == index)


def upright(index):
    count = index.shape[1]
    if count < LANES:
        index = jnp.concatenate([index, jnp.full((1, LANES - count), -1, i32)], axis=1)
    return jnp.broadcast_to(index, (LANES, LANES)).T[:count]


def pick_rows(column, first, width):
    lane = lax.broadcasted_iota(i32, column.shape, 1) + first
    return jnp.concatenate([as_mask(column == lane + at) for at in range(0, width, LANES)], axis=1)


def call(body, outs, scratch=(), products=(), copied=False):
    def run(*args):
        def where(array):
            if copied:
                return pl.BlockSpec(memory_space=pltpu.HBM)
            return pl.BlockSpec(memory_space=pltpu.SMEM if array.dtype == i32 and array.ndim == 1 else pltpu.VMEM)

        def size(shape, dtype):
            return jnp.dtype(dtype).itemsize * math.prod(shape)

        own = sum(size(*held) for held in scratch) + (10 << 20)
        moved = sum(array.dtype.itemsize * array.size for array in args) + sum(size(*out) for out in outs)
        limit = own if own + moved < 40 << 20 else min(own + moved, 60 << 20)
        semaphores = [pltpu.SemaphoreType.DMA((2 + len(outs),))] if copied else []
        return pl.pallas_call(
            body,
            out_shape=tuple(jax.ShapeDtypeStruct(shape, dtype) for shape, dtype in outs),
            in_specs=[where(array) for array in args],
            out_specs=tuple(pl.BlockSpec(memory_space=pltpu.VMEM) for _ in outs),
            scratch_shapes=[pltpu.VMEM(shape, dtype) for shape, dtype in scratch] + semaphores,
            compiler_params=pltpu.CompilerParams(vmem_limit_bytes=limit),
            cost_estimate=pl.CostEstimate(
                flops=2 * sum(math.prod(product) for product in products), bytes_accessed=moved, transcendentals=0
            ),
        )(*args)

    return run


def place_kernel(slots, receivers, order, here, there, halo_here, halo_there, list_here, list_there):
    nodes = here.shape[1] // 2
    wide = halo_here.shape[1]

    def body(at):
        block = pl.ds(pl.multiple_of(at * LANES, LANES), LANES)
        slot, receiver = slots[:, block], receivers[:, block]
        slot_column, receiver_column = upright(slot), upright(receiver)
        here[block, 0:nodes] = pick_rows(slot_column, 0, nodes)
        here[block, nodes:] = pick_rows(receiver_column, 0, nodes)
        halo_here[block, :] = pick_rows(slot_column, nodes, wide)
        there[0:nodes, block] = pick_columns(slot, 0, nodes)
        there[nodes:, block] = pick_columns(receiver, 0, nodes)
        halo_there[:, block] = pick_columns(slot, nodes, wide)

    pl.loop(0, slots.shape[1] // LANES)(body)
    count = order.shape[1]
    for at in range(0, count, LANES):
        end = min(at + LANES, count)
        list_here[at:end, :] = pick_rows(upright(order[:, at:end]), 0, nodes)
    list_there[...] = pick_columns(order[...], 0, nodes)


def note_kernel(rows, shards, nodes, payload, shard_rows, node_rows, arrived):
    grid = shards.shape[1]
    first = payload.shape[0] - EXTRA
    copies = [
        pltpu.make_async_copy(shards, shard_rows, arrived.at[0]),
        pltpu.make_async_copy(nodes, node_rows, arrived.at[1]),
        pltpu.make_async_copy(rows.at[0:first], payload.at[0:first], arrived.at[2]),
    ]
    for copy in copies:
        copy.start()
    for copy in copies[:2]:
        copy.wait()
    row = lax.broadcasted_iota(i32, (EXTRA, grid), 0)
    notes = jnp.full((EXTRA, grid), -1, i32)
    for top in range(shards.shape[0]):
        node = node_rows[top : top + 1, :]
        for at, value in enumerate((shard_rows[top : top + 1, :], node & 255, node >> 8)):
            notes = jnp.where(row == 3 * top + at, value, notes)
    payload[first:, 0:grid] = notes.astype(f32).astype(bf16)
    if grid < payload.shape[1]:
        payload[first:, grid:] = jnp.zeros((EXTRA, payload.shape[1] - grid), bf16)
    copies[2].wait()


def encode_kernel(steps, first, last, halves, *refs):
    refs = list(refs)
    meta, base, w_grid = refs[:3]
    del refs[:3]
    if first:
        w_mesh, _ = refs.pop(0), refs.pop(0)
        projected = dot(base[...], w_mesh[...]).astype(bf16)
    else:
        total_in = refs.pop(0)
        projected = base[...]
    payloads = refs[:steps]
    del refs[:steps]
    picks, slopes = refs[:steps], refs[steps : 2 * steps]
    del refs[: 2 * steps]
    total = None if first else total_in[...]
    nodes = projected.shape[0]
    for payload, pick, slope_out in zip(payloads, picks, slopes):
        grid = pick.shape[0]
        notes = payload[grid:, 0:grid].astype(f32)
        target = jnp.full((1, grid), -1.0, f32)
        for at in range(0, notes.shape[0] // 3 * 3, 3):
            named = notes[at : at + 1] == meta[1:2, 0:grid].astype(f32)
            target = jnp.where(named, notes[at + 1 : at + 2] + 256.0 * notes[at + 2 : at + 3], target)
        target = target.astype(i32)
        column = jnp.concatenate([upright(target[:, at : at + LANES]) for at in range(0, grid, LANES)], axis=0)
        picked = pick_rows(column, 0, nodes)
        pick[...] = picked
        pre = dot(payload[0:grid, :], w_grid[...]) + dot(picked, projected)
        act, slope = gated(0.5 * pre)
        slope_out[...] = slope.astype(bf16)
        added = dot(pick_columns(target, 0, nodes), act.astype(bf16))
        total = added if total is None else total + added
    if first:
        refs.pop(0)[...] = projected
    if not last:
        refs[0][...] = total
        return
    keep, sends = refs[0], refs[1:halves]
    part = nodes // halves
    own = meta[0:1, :]

    def half(shift):
        rows = total[0:part]
        for at in range(1, halves):
            rows = jnp.where(own == (at - shift) % halves, total[at * part : (at + 1) * part], rows)
        return rows

    keep[...] = half(0)
    for shift in range(1, halves):
        sends[shift - 1][...] = half(shift).astype(bf16)


def hand_out(rows, outs):
    rows = rows.astype(bf16)
    depth = outs[0].shape[0]
    count = rows.shape[0] // depth
    for at, out in enumerate(outs):
        first = 0 if at == 0 else (count - len(outs) + at) * depth
        out[...] = rows[first : first + depth]


def start_kernel(halves, *refs):
    meta = refs[0]
    parts = refs[1 : 1 + halves]
    mesh_init, w_enc_out, gain, w_send, list_here = refs[1 + halves : 6 + halves]
    hidden_out, enc_sum_out, sent = refs[6 + halves : 9 + halves]
    outs = refs[9 + halves : -1]
    whole = refs[-1]
    part = parts[0].shape[0]
    own = meta[0:1, :]
    for at in range(halves):
        rows = parts[0][...].astype(f32)
        for shift in range(1, halves):
            rows = jnp.where(own == (at - shift) % halves, parts[shift][...].astype(f32), rows)
        whole[at * part : (at + 1) * part, :] = rows.astype(bf16)
    enc_sum = dot(whole[...], w_enc_out[...])
    enc_sum_out[...] = enc_sum
    hidden = (mesh_init[...].astype(f32) + enc_sum * norm_scale(enc_sum) * gain[...]).astype(bf16)
    hidden_out[...] = hidden
    projected = (0.5 * dot(hidden, w_send[0])).astype(bf16)
    sent[...] = projected
    hand_out(dot(list_here[...], projected), outs)


def local_kernel(layer, hidden, sent, here, w_recv, pre, table):
    nodes = hidden.shape[0]
    table[0:nodes, :] = sent[...]
    table[nodes:, :] = (0.5 * dot(hidden[...], w_recv[layer])).astype(bf16)
    for at in range(0, pre.shape[0], BLOCK):
        pre[at : at + BLOCK, :] = dot(here[at : at + BLOCK, :], table[...])


def local_more_kernel(table, here, pre):
    skip = here.shape[0] - pre.shape[0]
    for at in range(0, pre.shape[0], BLOCK):
        pre[at : at + BLOCK, :] = dot(here[skip + at : skip + at + BLOCK, :], table[...])


def stack_halo(halos, halo):
    at = 0
    for block in halos:
        halo[at : at + block.shape[0], :] = block[...]
        at += block.shape[0]
    if at < halo.shape[0]:
        halo[at:, :] = jnp.zeros((halo.shape[0] - at, halo.shape[1]), bf16)


def node_sum(pres, halos, halo_here, there, slope_out, halo, act_out):
    nodes = there.shape[0] // 2
    stack_halo(halos, halo)
    half = pres[0].shape[0]
    for at in range(0, 2 * half, BLOCK):
        block = slice(at, at + BLOCK)
        pre = pres[at // half][at % half : at % half + BLOCK, :]
        act, slope = gated(pre + dot(halo_here[block, :], halo[...]))
        slope_out[block, :] = slope.astype(bf16)
        act_out[block, :] = act.astype(bf16)
    return dot(there[nodes:, :], act_out[...])


def layer_kernel(layer, shifts, *refs):
    hidden, pres = refs[0], refs[1:3]
    halos, refs = refs[3 : 3 + shifts], refs[3 + shifts :]
    halo_here, there, w_out, gain, w_send, list_here = refs[:6]
    hidden_out, agg_out, slope_out, sent_out = refs[6:10]
    outs = refs[10:-2]
    total = node_sum(pres, halos, halo_here, there, slope_out, *refs[-2:])
    agg = dot(total.astype(bf16), w_out[layer])
    agg_out[...] = agg
    fresh = (hidden[...].astype(f32) + agg * norm_scale(agg) * gain[layer : layer + 1, :]).astype(bf16)
    hidden_out[...] = fresh
    projected = (0.5 * dot(fresh, w_send[layer + 1])).astype(bf16)
    sent_out[...] = projected
    hand_out(dot(list_here[...], projected), outs)


def edge_grads(listed, grad_agg, w_out, here, halo_there, slope, grad_pre, outs):
    nodes = grad_agg.shape[0]
    spread = (0.5 * dot_back(grad_agg.astype(bf16), w_out)).astype(bf16)
    for at in range(0, slope.shape[0], BLOCK):
        block = slice(at, at + BLOCK)
        grad_act = dot(here[block, nodes:], spread)
        grad_pre[block, :] = grad_act.astype(bf16) * slope[block, :]
    hand_out(dot(halo_there[...], grad_pre[...])[0:listed], outs)


def turn_kernel(layer, shifts, *refs):
    hidden, pres = refs[0], refs[1:3]
    halos, refs = refs[3 : 3 + shifts], refs[3 + shifts :]
    halo_here, there, w_out, gain, here, halo_there, cot = refs[:7]
    hidden_out, grad_pre = refs[7:9]
    outs = refs[9:-2]
    slope, halo = refs[-2:]
    total = node_sum(pres, halos, halo_here, there, slope, halo, grad_pre)
    agg = dot(total.astype(bf16), w_out[layer])
    gain_row = gain[layer : layer + 1, :]
    hidden_out[...] = (hidden[...].astype(f32) + agg * norm_scale(agg) * gain_row).astype(bf16)
    edge_grads(shifts * outs[0].shape[0], norm_back(agg, gain_row, cot[...].astype(f32)), w_out[layer], here, halo_there, slope, grad_pre, outs)


def rest_kernel(layer, side, upstream, grad_pre, there, weights, rest):
    nodes = upstream.shape[0]
    sums = dot(there[side * nodes : (side + 1) * nodes, :], grad_pre[...]).astype(bf16)
    rest[...] = upstream[...].astype(f32) + dot_back(sums, weights[layer])


def arrived(rest, returned, list_there, w_send, halo):
    stack_halo(returned, halo)
    projected = dot_back(halo[...], w_send).astype(bf16)
    return rest[...] + dot(list_there[...], projected)


def back_kernel(layer, shifts, *refs):
    rest = refs[0]
    returned, refs = refs[1 : 1 + shifts], refs[1 + shifts :]
    list_there, w_send, agg, slope, gain, w_out, here, halo_there = refs[:8]
    upstream_out, grad_pre = refs[8:10]
    outs = refs[10:-1]
    halo = refs[-1]
    upstream = arrived(rest, returned, list_there, w_send[layer + 1], halo)
    upstream_out[...] = upstream
    grad_agg = norm_back(agg[...], gain[layer : layer + 1, :], upstream)
    edge_grads(shifts * outs[0].shape[0], grad_agg, w_out[layer], here, halo_there, slope, grad_pre, outs)


def pair_grads(spread, pick, slope):
    return dot(pick, spread).astype(bf16) * slope


def finish_kernel(shifts, *refs):
    rest = refs[0]
    returned, refs = refs[1 : 1 + shifts], refs[1 + shifts :]
    list_there, w_send, enc_sum, gain, w_enc_out, pick, slope, spread_out = refs[:8]
    outs, halo = refs[8:-1], refs[-1]
    upstream = arrived(rest, returned, list_there, w_send[0], halo)
    spread = (0.5 * dot_back(norm_back(enc_sum[...], gain[...], upstream).astype(bf16), w_enc_out[...])).astype(bf16)
    spread_out[...] = spread
    at = 0
    for out in outs:
        rows = slice(at, at + out.shape[0])
        out[...] = pair_grads(spread, pick[rows, :], slope[rows, :])
        at += out.shape[0]


def others_kernel(count, *refs):
    spread = refs[0][...]
    picks, slopes, outs = refs[1 : 1 + count], refs[1 + count : 1 + 2 * count], refs[1 + 2 * count :]
    for pick, slope, out in reversed(list(zip(picks, slopes, outs))):
        skip = pick.shape[0] - out.shape[0]
        out[...] = pair_grads(spread, pick[skip:, :], slope[skip:, :])


def relay_kernel(first, own, passed, *refs):
    rows = passed.shape[0]
    out = refs[0] if len(refs) == 1 else refs[-2]
    out[...] = (own[first : first + rows, :].astype(f32) + passed[...].astype(f32)).astype(bf16)
    if len(refs) > 1:
        refs[-1][...] = refs[0][...]


def sum_kernel(own, piece, total):
    total[...] = own[0 : piece.shape[0], :].astype(f32) + piece[...].astype(f32)


def grid_kernel(whole, *refs):
    blocks, pieces, (w_grid, out) = refs[:whole], refs[whole:-2], refs[-2:]
    if not pieces:
        total = blocks[0][...].astype(f32)
        for block in blocks[1:]:
            total = total + block[...].astype(f32)
        out[...] = dot_back(total.astype(bf16), w_grid[...])
        return
    (own, near), (summed, second) = blocks, pieces
    first = summed.shape[0]
    total = summed[...] + near[0:first, :].astype(f32)
    out[0:first, :] = dot_back(total.astype(bf16), w_grid[...])
    total = own[first:, :].astype(f32) + near[first:, :].astype(f32) + second[...].astype(f32)
    out[first:, :] = dot_back(total.astype(bf16), w_grid[...])


def shifted(value, axis, by):
    size = lax.axis_size(axis)
    return lax.ppermute(value, axis, [(at, (at + by) % size) for at in range(size)])


def partner(at, step, size):
    return at ^ step if size & (size - 1) == 0 else (at + step) % size


def sent_to(value, step):
    size = lax.axis_size("mesh")
    return lax.ppermute(value, "mesh", [(at, partner(at, step, size)) for at in range(size)])


def sent_back(value, step):
    size = lax.axis_size("mesh")
    return lax.ppermute(value, "mesh", [(partner(at, step, size), at) for at in range(size)])


def in_order(pieces, axis):
    return jnp.roll(jnp.stack(pieces)[::-1], lax.axis_index(axis) + 1, axis=0)


def on_device(
    grid_feats,
    g2m_shard,
    g2m_node,
    mesh_init,
    sender_slots,
    receivers,
    halo_index,
    w_enc_grid,
    w_enc_mesh,
    w_enc_out,
    enc_gain,
    w_send,
    w_recv,
    w_out,
    layer_gain,
    out_cot,
):
    shards = lax.axis_size("mesh")
    shard = lax.axis_index("mesh")
    halves = lax.axis_size("rep")
    feats = lax.axis_size("feat")
    nodes, width = mesh_init.shape
    grid, tops = g2m_shard.shape
    edges = sender_slots.shape[0]
    depth = halo_index.shape[2]
    shifts = shards - 1
    listed_rows = shifts * depth
    wide = -(-listed_rows // LANES) * LANES
    all_edges = edges * halves * feats
    enc_gain = enc_gain[None, :]

    relayed = shards == 4
    cuts = 2 if relayed else 1
    shared = relayed and halves == 2
    piece_rows = grid // cuts
    in_place = [pltpu.with_memory_space_constraint(array, pltpu.HBM) for array in (grid_feats, g2m_shard.T, g2m_node.T)]
    (payload,) = call(
        note_kernel,
        [((grid + EXTRA, width), bf16)],
        [((tops, grid), i32), ((tops, grid), i32)],
        copied=True,
    )(*in_place)

    place = sender_slots - nodes
    away = partner(shard, place // depth, shards)
    if shards & (shards - 1):
        away = lax.rem(shard - place // depth + shards, shards)
    slots = jnp.where(sender_slots < nodes, sender_slots, nodes + (shifts - away) * depth + place % depth)
    both = jnp.stack([slots, receivers])
    others = [shifted(both, "rep", step) for step in range(1, halves)]
    if relayed:
        across = sent_to(payload, 2)
        payloads = [payload, sent_to(payload, 1), across]
    else:
        payloads = [payload] + [sent_to(payload, step) for step in range(1, shards)]
    both = in_order([both] + others, "rep")
    both = in_order([both] + [shifted(both, "feat", step) for step in range(1, feats)], "feat")
    both = both.reshape(feats * halves, 2, edges)
    all_slots, all_receivers = both[:, 0].reshape(1, -1), both[:, 1].reshape(1, -1)
    steps = shards - jnp.arange(1, shards, dtype=i32)
    if shared:
        core = lax.axis_index("rep")
        steps = jnp.where((core == 0) & (steps > 1), 5 - steps, steps)
        entry = all_slots - nodes
        turned = (core == 0) & (entry >= 0) & (entry < 2 * depth)
        all_slots = all_slots + jnp.where(turned, jnp.where(entry < depth, depth, -depth), 0)
    readers = partner(shard, steps, shards)
    lists = jnp.take(halo_index[0], readers, axis=0).reshape(1, -1)
    here, there, halo_here, halo_there, list_here, list_there = call(
        place_kernel,
        [
            ((all_edges, 2 * nodes), bf16),
            ((2 * nodes, all_edges), bf16),
            ((all_edges, wide), bf16),
            ((wide, all_edges), bf16),
            ((listed_rows, nodes), bf16),
            ((nodes, listed_rows), bf16),
        ],
        products=[(all_edges, nodes, width), (all_edges, 2 * nodes, width)],
    )(all_slots, all_receivers, lists)

    if relayed:
        across, list_here = lax.optimization_barrier((across, list_here))
        payloads.append(sent_to(across, 1))

    meta = jnp.broadcast_to(jnp.stack([lax.axis_index("rep"), shard]).astype(i32)[:, None], (2, width))
    node_f32, node_bf16 = ((nodes, width), f32), ((nodes, width), bf16)
    row_shape, half = ((grid, width), bf16), nodes // halves
    square = (nodes, width, width)
    enc_picks, enc_slopes = [], []
    base, total = mesh_init, None
    groups = [payloads[:2]] + [payloads[at : at + 1] for at in range(2, shards)]
    for at, group in enumerate(groups):
        first, last = at == 0, at == len(groups) - 1
        count = len(group)
        outs = [((grid, nodes), bf16)] * count + [row_shape] * count
        outs += [node_bf16] if first else []
        outs += [((half, width), f32)] + [((half, width), bf16)] * (halves - 1) if last else [node_f32]
        got = list(
            call(
                functools.partial(encode_kernel, count, first, last, halves),
                outs,
                (),
                [square] * first + [(grid, width, width), (grid, nodes, width), (nodes, grid, width)] * count,
            )(
                meta, base, w_enc_grid, *((w_enc_mesh, list_here) if first else (total,)), *group
            )
        )
        enc_picks += got[:count]
        enc_slopes += got[count : 2 * count]
        del got[: 2 * count]
        if first:
            base = got.pop(0)
        total = got[0]
    part = got[0]
    for step in range(1, halves):
        part = part + shifted(got[step], "rep", step).astype(f32)
    part = part.astype(bf16)
    pieces = [part] + [shifted(part, "feat", step) for step in range(1, feats)]
    if feats > 2:
        pieces = list(in_order(pieces, "feat"))
    part = sum(piece.astype(f32) for piece in pieces).astype(bf16)
    parts = [part] + [shifted(part, "rep", -step) for step in range(1, halves)]

    listed = [((depth, width), bf16)] * (2 if shared else shifts)

    def exchange(blocks, send, early):
        if not shared:
            return [send(block, shifts - at) for at, block in enumerate(blocks)], early
        far = lax.ppermute(
            blocks[0], ("mesh", "rep"), [(2 * at + side, 2 * (at ^ (2 + side)) + side) for at in range(4) for side in range(2)]
        )
        block, early = lax.optimization_barrier((blocks[1], early))
        near = send(block, 1)
        far, early = lax.optimization_barrier((far, early))
        return [far, shifted(far, "rep", 1), near], early

    hidden, enc_sum, sent, *outgoing = call(
        functools.partial(start_kernel, halves), [node_bf16, node_f32, node_bf16] + listed, [node_bf16],
        [square, square, (listed_rows, nodes, width)],
    )(meta, *parts, mesh_init, w_enc_out, enc_gain, w_send, list_here)

    half_f32, edge_bf16 = ((all_edges // 2, width), f32), ((all_edges, width), bf16)
    halo, back_halo = ((wide, width), bf16), ((listed_rows, width), bf16)
    forward_products = [(all_edges, wide, width), (nodes, all_edges, width), square]
    backward_products = [square, (all_edges, nodes, width), (wide, all_edges, width)]
    half_product = (all_edges // 2, 2 * nodes, width)

    def arriving(layer):
        early = call(
            functools.partial(local_kernel, layer), [half_f32, ((2 * nodes, width), bf16)], (), [square, half_product]
        )(hidden, sent, here, w_recv)
        halos, (pre, both_tables) = exchange(outgoing, sent_to, early)
        (more,) = call(local_more_kernel, [half_f32], (), [half_product])(both_tables, here)
        return hidden, pre, more, *halos

    records = []
    for layer in range(LAYERS - 1):
        hidden, agg, slope, sent, *outgoing = call(
            functools.partial(layer_kernel, layer, shifts),
            [node_bf16, node_f32, edge_bf16, node_bf16] + listed,
            [halo, edge_bf16],
            forward_products + [square, (listed_rows, nodes, width)],
        )(*arriving(layer), halo_here, there, w_out, layer_gain, w_send, list_here)
        records.append((agg, slope))
    last = LAYERS - 1
    final_mesh, grad_pre, *outgoing = call(
        functools.partial(turn_kernel, last, shifts), [node_bf16, edge_bf16] + listed, [edge_bf16, halo],
        forward_products + backward_products,
    )(*arriving(last), halo_here, there, w_out, layer_gain, here, halo_there, out_cot)
    upstream = out_cot
    for layer in reversed(range(LAYERS)):

        def rest_of(side, upstream, weights):
            (rest,) = call(
                functools.partial(rest_kernel, layer, side), [node_f32], (), [(nodes, all_edges, width), square]
            )(upstream, grad_pre, there, weights)
            return rest

        returned, early = exchange(outgoing, sent_back, rest_of(0, upstream, w_send))
        rest = rest_of(1, early, w_recv)
        if layer:
            agg, slope = records[layer - 1]
            upstream, grad_pre, *outgoing = call(
                functools.partial(back_kernel, layer - 1, shifts),
                [node_f32, edge_bf16] + listed,
                [back_halo],
                backward_products + [(listed_rows, width, width), (nodes, listed_rows, width)],
            )(rest, *returned, list_there, w_send, agg, slope, layer_gain, w_out, here, halo_there)
    piece = ((piece_rows, width), bf16)
    one = (grid, nodes, width)
    spread, *far = call(
        functools.partial(finish_kernel, shifts),
        [node_bf16] + [piece] * cuts,
        [back_halo],
        [square, (listed_rows, width, width), (nodes, listed_rows, width), one],
    )(rest, *returned, list_there, w_send, enc_sum, enc_gain, w_enc_out, enc_picks[-1], enc_slopes[-1])
    blocks = call(
        functools.partial(others_kernel, shards - 1), [row_shape] * (shards - 1), products=[one] * (shards - 1)
    )(spread, *enc_picks[:-1], *enc_slopes[:-1])
    if relayed:
        passed = [sent_back(block, 1) for block in far]
        first, near = call(functools.partial(relay_kernel, 0), [piece, row_shape])(blocks[2], passed[0], blocks[1])
        (second,) = call(functools.partial(relay_kernel, piece_rows), [piece])(blocks[2], passed[1])
        near = sent_back(near, 1)
        first, second = sent_back(first, 2), sent_back(second, 2)
        (summed,) = call(sum_kernel, [((piece_rows, width), f32)])(blocks[0], first)
        (grid_grad,) = call(
            functools.partial(grid_kernel, 2), [((grid, width), f32)], products=[(grid, width, width)]
        )(blocks[0], near, summed, second, w_enc_grid)
    else:
        blocks = [*blocks, *far]
        blocks = [blocks[0]] + [sent_back(block, step) for step, block in enumerate(blocks) if step]
        (grid_grad,) = call(
            functools.partial(grid_kernel, shards), [((grid, width), f32)], products=[(grid, width, width)]
        )(*blocks, w_enc_grid)
    return (final_mesh, grid_grad)


def solution(mesh):
    return jax.shard_map(
        on_device,
        mesh=mesh,
        in_specs=(
            P(("groups", "mesh", "feat", "rep"), None),
            P(("groups", "mesh", "feat", "rep"), None),
            P(("groups", "mesh", "feat", "rep"), None),
            P(("groups", "mesh"), None),
            P(("groups", "mesh", "feat", "rep")),
            P(("groups", "mesh", "feat", "rep")),
            P(("groups", "mesh"), None, None),
            P(),
            P(),
            P(),
            P(),
            P(),
            P(),
            P(),
            P(),
            P(("groups", "mesh"), None),
        ),
        out_specs=(P(("groups", "mesh"), None), P(("groups", "mesh", "feat", "rep"), None)),
        check_vma=False,
    )
```

```python
import functools
import math

import jax
import jax.numpy as jnp
from jax import lax
from jax.experimental import pallas as pl
from jax.experimental.pallas import tpu as pltpu
from jax.sharding import PartitionSpec as P

LAYERS = 3
LANES = 128
BLOCK = 512
EXTRA = 16
eps = 1e-05

f32 = jnp.float32
bf16 = jnp.bfloat16
i32 = jnp.int32


def norm_scale(totals):
    return lax.rsqrt(jnp.mean(totals * totals, axis=-1, keepdims=True) + eps)


def norm_back(totals, gain_row, upstream):
    scaled = norm_scale(totals)
    normed = totals * scaled
    slope = upstream * gain_row
    return scaled * (slope - normed * jnp.mean(slope * normed, axis=-1, keepdims=True))


def dot(left, right):
    return jnp.dot(left, right, preferred_element_type=f32)


def dot_back(left, right):
    return lax.dot_general(left, right, (((1,), (1,)), ((), ())), preferred_element_type=f32)


def gated(half):
    half = half.astype(bf16)
    bend = jnp.tanh(half)
    act = half + half * bend
    return act, (1.0 + act) + bend * (1.0 - act)


def as_mask(hit):
    return jnp.where(hit, 1.0, 0.0).astype(bf16)


def pick_columns(index, first, height):
    place = lax.broadcasted_iota(i32, (height, index.shape[1]), 0) + first
    return as_mask(place == index)


def upright(index):
    count = index.shape[1]
    if count < LANES:
        index = jnp.concatenate([index, jnp.full((1, LANES - count), -1, i32)], axis=1)
    return jnp.broadcast_to(index, (LANES, LANES)).T[:count]


def pick_rows(column, first, width):
    lane = lax.broadcasted_iota(i32, column.shape, 1) + first
    return jnp.concatenate([as_mask(column == lane + at) for at in range(0, width, LANES)], axis=1)


def call(body, outs, scratch=(), products=(), copied=False):
    def run(*args):
        def where(array):
            if copied:
                return pl.BlockSpec(memory_space=pltpu.HBM)
            return pl.BlockSpec(memory_space=pltpu.SMEM if array.dtype == i32 and array.ndim == 1 else pltpu.VMEM)

        def size(shape, dtype):
            return jnp.dtype(dtype).itemsize * math.prod(shape)

        own = sum(size(*held) for held in scratch) + (10 << 20)
        moved = sum(array.dtype.itemsize * array.size for array in args) + sum(size(*out) for out in outs)
        limit = own if own + moved < 40 << 20 else min(own + moved, 60 << 20)
        semaphores = [pltpu.SemaphoreType.DMA((2 + len(outs),))] if copied else []
        return pl.pallas_call(
            body,
            out_shape=tuple(jax.ShapeDtypeStruct(shape, dtype) for shape, dtype in outs),
            in_specs=[where(array) for array in args],
            out_specs=tuple(pl.BlockSpec(memory_space=pltpu.VMEM) for _ in outs),
            scratch_shapes=[pltpu.VMEM(shape, dtype) for shape, dtype in scratch] + semaphores,
            compiler_params=pltpu.CompilerParams(vmem_limit_bytes=limit),
            cost_estimate=pl.CostEstimate(
                flops=2 * sum(math.prod(product) for product in products), bytes_accessed=moved, transcendentals=0
            ),
        )(*args)

    return run


def place_kernel(slots, receivers, order, here, there, halo_here, halo_there, list_here, list_there):
    nodes = here.shape[1] // 2
    wide = halo_here.shape[1]

    def body(at):
        block = pl.ds(pl.multiple_of(at * LANES, LANES), LANES)
        slot, receiver = slots[:, block], receivers[:, block]
        slot_column, receiver_column = upright(slot), upright(receiver)
        here[block, 0:nodes] = pick_rows(slot_column, 0, nodes)
        here[block, nodes:] = pick_rows(receiver_column, 0, nodes)
        halo_here[block, :] = pick_rows(slot_column, nodes, wide)
        there[0:nodes, block] = pick_columns(slot, 0, nodes)
        there[nodes:, block] = pick_columns(receiver, 0, nodes)
        halo_there[:, block] = pick_columns(slot, nodes, wide)

    pl.loop(0, slots.shape[1] // LANES)(body)
    count = order.shape[1]
    for at in range(0, count, LANES):
        end = min(at + LANES, count)
        list_here[at:end, :] = pick_rows(upright(order[:, at:end]), 0, nodes)
    list_there[...] = pick_columns(order[...], 0, nodes)


def note_kernel(rows, shards, nodes, payload, shard_rows, node_rows, arrived):
    grid = shards.shape[1]
    first = payload.shape[0] - EXTRA
    copies = [
        pltpu.make_async_copy(shards, shard_rows, arrived.at[0]),
        pltpu.make_async_copy(nodes, node_rows, arrived.at[1]),
        pltpu.make_async_copy(rows.at[0:first], payload.at[0:first], arrived.at[2]),
    ]
    for copy in copies:
        copy.start()
    for copy in copies[:2]:
        copy.wait()
    row = lax.broadcasted_iota(i32, (EXTRA, grid), 0)
    notes = jnp.full((EXTRA, grid), -1, i32)
    for top in range(shards.shape[0]):
        node = node_rows[top : top + 1, :]
        for at, value in enumerate((shard_rows[top : top + 1, :], node & 255, node >> 8)):
            notes = jnp.where(row == 3 * top + at, value, notes)
    payload[first:, 0:grid] = notes.astype(f32).astype(bf16)
    if grid < payload.shape[1]:
        payload[first:, grid:] = jnp.zeros((EXTRA, payload.shape[1] - grid), bf16)
    copies[2].wait()


def encode_kernel(steps, first, last, halves, *refs):
    refs = list(refs)
    meta, base, w_grid = refs[:3]
    del refs[:3]
    if first:
        w_mesh, _ = refs.pop(0), refs.pop(0)
        projected = dot(base[...], w_mesh[...]).astype(bf16)
    else:
        total_in = refs.pop(0)
        projected = base[...]
    payloads = refs[:steps]
    del refs[:steps]
    picks, slopes = refs[:steps], refs[steps : 2 * steps]
    del refs[: 2 * steps]
    total = None if first else total_in[...]
    nodes = projected.shape[0]
    for payload, pick, slope_out in zip(payloads, picks, slopes):
        grid = pick.shape[0]
        notes = payload[grid:, 0:grid].astype(f32)
        target = jnp.full((1, grid), -1.0, f32)
        for at in range(0, notes.shape[0] // 3 * 3, 3):
            named = notes[at : at + 1] == meta[1:2, 0:grid].astype(f32)
            target = jnp.where(named, notes[at + 1 : at + 2] + 256.0 * notes[at + 2 : at + 3], target)
        target = target.astype(i32)
        column = jnp.concatenate([upright(target[:, at : at + LANES]) for at in range(0, grid, LANES)], axis=0)
        picked = pick_rows(column, 0, nodes)
        pick[...] = picked
        pre = dot(payload[0:grid, :], w_grid[...]) + dot(picked, projected)
        act, slope = gated(0.5 * pre)
        slope_out[...] = slope.astype(bf16)
        added = dot(pick_columns(target, 0, nodes), act.astype(bf16))
        total = added if total is None else total + added
    if first:
        refs.pop(0)[...] = projected
    if not last:
        refs[0][...] = total
        return
    keep, sends = refs[0], refs[1:halves]
    part = nodes // halves
    own = meta[0:1, :]

    def half(shift):
        rows = total[0:part]
        for at in range(1, halves):
            rows = jnp.where(own == (at - shift) % halves, total[at * part : (at + 1) * part], rows)
        return rows

    keep[...] = half(0)
    for shift in range(1, halves):
        sends[shift - 1][...] = half(shift).astype(bf16)


def hand_out(rows, outs):
    rows = rows.astype(bf16)
    depth = outs[0].shape[0]
    count = rows.shape[0] // depth
    for at, out in enumerate(outs):
        first = 0 if at == 0 else (count - len(outs) + at) * depth
        out[...] = rows[first : first + depth]


def updated(hidden, total, w_out, gain_row):
    agg = dot(total, w_out)
    return (hidden.astype(f32) + agg * norm_scale(agg) * gain_row).astype(bf16), agg


def listed_update(list_here, total, hidden, w_out, gain_row, w_send):
    picks = list_here[...]
    rows, kept = dot(picks, total).astype(bf16), dot(picks, hidden)
    return 0.5 * dot(updated(kept, rows, w_out, gain_row)[0], w_send)


def start_kernel(halves, *refs):
    meta = refs[0]
    parts = refs[1 : 1 + halves]
    mesh_init, w_enc_out, gain, w_send, list_here, whole = refs[1 + halves : 7 + halves]
    part = parts[0].shape[0]
    own = meta[0:1, :]
    for at in range(halves):
        rows = parts[0][...].astype(f32)
        for shift in range(1, halves):
            rows = jnp.where(own == (at - shift) % halves, parts[shift][...].astype(f32), rows)
        whole[at * part : (at + 1) * part, :] = rows.astype(bf16)
    hand_out(
        listed_update(list_here, whole[...], mesh_init[...], w_enc_out[...], gain[...], w_send[0]), refs[7 + halves :]
    )


def local_kernel(layer, total, hidden, w_out, gain, w_send, w_recv, here, hidden_out, agg_out, pre, table):
    nodes = hidden.shape[0]
    if layer:
        fresh, agg = updated(hidden[...], total[...], w_out[layer - 1], gain[layer - 1 : layer, :])
    else:
        fresh, agg = updated(hidden[...], total[...], w_out[...], gain[...])
    hidden_out[...] = fresh
    agg_out[...] = agg
    table[0:nodes, :] = (0.5 * dot(fresh, w_send[layer])).astype(bf16)
    table[nodes:, :] = (0.5 * dot(fresh, w_recv[layer])).astype(bf16)
    for at in range(0, pre.shape[0], BLOCK):
        pre[at : at + BLOCK, :] = dot(here[at : at + BLOCK, :], table[...])


def local_more_kernel(table, here, pre):
    skip = here.shape[0] - pre.shape[0]
    for at in range(0, pre.shape[0], BLOCK):
        pre[at : at + BLOCK, :] = dot(here[skip + at : skip + at + BLOCK, :], table[...])


def stack_halo(halos, halo):
    at = 0
    for block in halos:
        halo[at : at + block.shape[0], :] = block[...]
        at += block.shape[0]
    if at < halo.shape[0]:
        halo[at:, :] = jnp.zeros((halo.shape[0] - at, halo.shape[1]), bf16)


def node_sum(pres, halos, halo_here, there, slope_out, halo, act_out):
    nodes = there.shape[0] // 2
    stack_halo(halos, halo)
    half = pres[0].shape[0]
    for at in range(0, 2 * half, BLOCK):
        block = slice(at, at + BLOCK)
        pre = pres[at // half][at % half : at % half + BLOCK, :]
        act, slope = gated(pre + dot(halo_here[block, :], halo[...]))
        slope_out[block, :] = slope.astype(bf16)
        act_out[block, :] = act.astype(bf16)
    return dot(there[nodes:, :], act_out[...])


def layer_kernel(layer, shifts, *refs):
    hidden, pres = refs[0], refs[1:3]
    halos, refs = refs[3 : 3 + shifts], refs[3 + shifts :]
    halo_here, there, w_out, gain, w_send, list_here = refs[:6]
    total_out, slope_out = refs[6:8]
    outs = refs[8:-2]
    total = node_sum(pres, halos, halo_here, there, slope_out, *refs[-2:]).astype(bf16)
    total_out[...] = total
    gain_row = gain[layer : layer + 1, :]
    hand_out(listed_update(list_here, total, hidden[...], w_out[layer], gain_row, w_send[layer + 1]), outs)


def edge_grads(listed, grad_agg, w_out, here, halo_there, slope, grad_pre, outs):
    nodes = grad_agg.shape[0]
    spread = (0.5 * dot_back(grad_agg.astype(bf16), w_out)).astype(bf16)
    for at in range(0, slope.shape[0], BLOCK):
        block = slice(at, at + BLOCK)
        grad_act = dot(here[block, nodes:], spread)
        grad_pre[block, :] = grad_act.astype(bf16) * slope[block, :]
    hand_out(dot(halo_there[...], grad_pre[...])[0:listed], outs)


def turn_kernel(layer, shifts, *refs):
    hidden, pres = refs[0], refs[1:3]
    halos, refs = refs[3 : 3 + shifts], refs[3 + shifts :]
    halo_here, there, w_out, gain, here, halo_there, cot = refs[:7]
    hidden_out, grad_pre = refs[7:9]
    outs = refs[9:-2]
    slope, halo = refs[-2:]
    total = node_sum(pres, halos, halo_here, there, slope, halo, grad_pre)
    gain_row = gain[layer : layer + 1, :]
    fresh, agg = updated(hidden[...], total.astype(bf16), w_out[layer], gain_row)
    hidden_out[...] = fresh
    edge_grads(shifts * outs[0].shape[0], norm_back(agg, gain_row, cot[...].astype(f32)), w_out[layer], here, halo_there, slope, grad_pre, outs)


def rest_kernel(layer, side, upstream, grad_pre, there, weights, rest):
    nodes = upstream.shape[0]
    sums = dot(there[side * nodes : (side + 1) * nodes, :], grad_pre[...]).astype(bf16)
    rest[...] = upstream[...].astype(f32) + dot_back(sums, weights[layer])


def arrived(rest, returned, list_there, w_send, halo):
    stack_halo(returned, halo)
    projected = dot_back(halo[...], w_send).astype(bf16)
    return rest[...] + dot(list_there[...], projected)


def back_kernel(layer, shifts, *refs):
    rest = refs[0]
    returned, refs = refs[1 : 1 + shifts], refs[1 + shifts :]
    list_there, w_send, agg, slope, gain, w_out, here, halo_there = refs[:8]
    upstream_out, grad_pre = refs[8:10]
    outs = refs[10:-1]
    halo = refs[-1]
    upstream = arrived(rest, returned, list_there, w_send[layer + 1], halo)
    upstream_out[...] = upstream
    grad_agg = norm_back(agg[...], gain[layer : layer + 1, :], upstream)
    edge_grads(shifts * outs[0].shape[0], grad_agg, w_out[layer], here, halo_there, slope, grad_pre, outs)


def pair_grads(spread, pick, slope):
    return dot(pick, spread).astype(bf16) * slope


def finish_kernel(shifts, *refs):
    rest = refs[0]
    returned, refs = refs[1 : 1 + shifts], refs[1 + shifts :]
    list_there, w_send, enc_sum, gain, w_enc_out, pick, slope, spread_out = refs[:8]
    outs, halo = refs[8:-1], refs[-1]
    upstream = arrived(rest, returned, list_there, w_send[0], halo)
    spread = (0.5 * dot_back(norm_back(enc_sum[...], gain[...], upstream).astype(bf16), w_enc_out[...])).astype(bf16)
    spread_out[...] = spread
    at = 0
    for out in outs:
        rows = slice(at, at + out.shape[0])
        out[...] = pair_grads(spread, pick[rows, :], slope[rows, :])
        at += out.shape[0]


def others_kernel(count, *refs):
    spread = refs[0][...]
    picks, slopes, outs = refs[1 : 1 + count], refs[1 + count : 1 + 2 * count], refs[1 + 2 * count :]
    for pick, slope, out in reversed(list(zip(picks, slopes, outs))):
        skip = pick.shape[0] - out.shape[0]
        out[...] = pair_grads(spread, pick[skip:, :], slope[skip:, :])


def relay_kernel(first, own, passed, *refs):
    rows = passed.shape[0]
    out = refs[0] if len(refs) == 1 else refs[-2]
    out[...] = (own[first : first + rows, :].astype(f32) + passed[...].astype(f32)).astype(bf16)
    if len(refs) > 1:
        refs[-1][...] = refs[0][...]


def sum_kernel(own, piece, total):
    total[...] = own[0 : piece.shape[0], :].astype(f32) + piece[...].astype(f32)


def grid_kernel(whole, *refs):
    blocks, pieces, (w_grid, out) = refs[:whole], refs[whole:-2], refs[-2:]
    if not pieces:
        total = blocks[0][...].astype(f32)
        for block in blocks[1:]:
            total = total + block[...].astype(f32)
        out[...] = dot_back(total.astype(bf16), w_grid[...])
        return
    (own, near), (summed, second) = blocks, pieces
    first = summed.shape[0]
    total = summed[...] + near[0:first, :].astype(f32)
    out[0:first, :] = dot_back(total.astype(bf16), w_grid[...])
    total = own[first:, :].astype(f32) + near[first:, :].astype(f32) + second[...].astype(f32)
    out[first:, :] = dot_back(total.astype(bf16), w_grid[...])


def shifted(value, axis, by):
    size = lax.axis_size(axis)
    return lax.ppermute(value, axis, [(at, (at + by) % size) for at in range(size)])


def partner(at, step, size):
    return at ^ step if size & (size - 1) == 0 else (at + step) % size


def sent_to(value, step):
    size = lax.axis_size("mesh")
    return lax.ppermute(value, "mesh", [(at, partner(at, step, size)) for at in range(size)])


def sent_back(value, step):
    size = lax.axis_size("mesh")
    return lax.ppermute(value, "mesh", [(partner(at, step, size), at) for at in range(size)])


def in_order(pieces, axis):
    return jnp.roll(jnp.stack(pieces)[::-1], lax.axis_index(axis) + 1, axis=0)


def on_device(
    grid_feats,
    g2m_shard,
    g2m_node,
    mesh_init,
    sender_slots,
    receivers,
    halo_index,
    w_enc_grid,
    w_enc_mesh,
    w_enc_out,
    enc_gain,
    w_send,
    w_recv,
    w_out,
    layer_gain,
    out_cot,
):
    shards = lax.axis_size("mesh")
    shard = lax.axis_index("mesh")
    halves = lax.axis_size("rep")
    feats = lax.axis_size("feat")
    nodes, width = mesh_init.shape
    grid, tops = g2m_shard.shape
    edges = sender_slots.shape[0]
    depth = halo_index.shape[2]
    shifts = shards - 1
    listed_rows = shifts * depth
    wide = -(-listed_rows // LANES) * LANES
    all_edges = edges * halves * feats
    enc_gain = enc_gain[None, :]

    relayed = shards == 4
    cuts = 2 if relayed else 1
    shared = relayed and halves == 2
    piece_rows = grid // cuts
    in_place = [pltpu.with_memory_space_constraint(array, pltpu.HBM) for array in (grid_feats, g2m_shard.T, g2m_node.T)]
    (payload,) = call(
        note_kernel,
        [((grid + EXTRA, width), bf16)],
        [((tops, grid), i32), ((tops, grid), i32)],
        copied=True,
    )(*in_place)

    place = sender_slots - nodes
    away = partner(shard, place // depth, shards)
    if shards & (shards - 1):
        away = lax.rem(shard - place // depth + shards, shards)
    slots = jnp.where(sender_slots < nodes, sender_slots, nodes + (shifts - away) * depth + place % depth)
    both = jnp.stack([slots, receivers])
    others = [shifted(both, "rep", step) for step in range(1, halves)]
    if relayed:
        across = sent_to(payload, 2)
        payloads = [payload, sent_to(payload, 1), across]
    else:
        payloads = [payload] + [sent_to(payload, step) for step in range(1, shards)]
    both = in_order([both] + others, "rep")
    both = in_order([both] + [shifted(both, "feat", step) for step in range(1, feats)], "feat")
    both = both.reshape(feats * halves, 2, edges)
    all_slots, all_receivers = both[:, 0].reshape(1, -1), both[:, 1].reshape(1, -1)
    steps = shards - jnp.arange(1, shards, dtype=i32)
    if shared:
        core = lax.axis_index("rep")
        steps = jnp.where((core == 0) & (steps > 1), 5 - steps, steps)
        entry = all_slots - nodes
        turned = (core == 0) & (entry >= 0) & (entry < 2 * depth)
        all_slots = all_slots + jnp.where(turned, jnp.where(entry < depth, depth, -depth), 0)
    readers = partner(shard, steps, shards)
    lists = jnp.take(halo_index[0], readers, axis=0).reshape(1, -1)
    here, there, halo_here, halo_there, list_here, list_there = call(
        place_kernel,
        [
            ((all_edges, 2 * nodes), bf16),
            ((2 * nodes, all_edges), bf16),
            ((all_edges, wide), bf16),
            ((wide, all_edges), bf16),
            ((listed_rows, nodes), bf16),
            ((nodes, listed_rows), bf16),
        ],
        products=[(all_edges, nodes, width), (all_edges, 2 * nodes, width)],
    )(all_slots, all_receivers, lists)

    if relayed:
        across, list_here = lax.optimization_barrier((across, list_here))
        payloads.append(sent_to(across, 1))

    meta = jnp.broadcast_to(jnp.stack([lax.axis_index("rep"), shard]).astype(i32)[:, None], (2, width))
    node_f32, node_bf16 = ((nodes, width), f32), ((nodes, width), bf16)
    row_shape, half = ((grid, width), bf16), nodes // halves
    square = (nodes, width, width)
    enc_picks, enc_slopes = [], []
    base, total = mesh_init, None
    groups = [payloads[:2]] + [payloads[at : at + 1] for at in range(2, shards)]
    for at, group in enumerate(groups):
        first, last = at == 0, at == len(groups) - 1
        count = len(group)
        outs = [((grid, nodes), bf16)] * count + [row_shape] * count
        outs += [node_bf16] if first else []
        outs += [((half, width), f32)] + [((half, width), bf16)] * (halves - 1) if last else [node_f32]
        got = list(
            call(
                functools.partial(encode_kernel, count, first, last, halves),
                outs,
                (),
                [square] * first + [(grid, width, width), (grid, nodes, width), (nodes, grid, width)] * count,
            )(
                meta, base, w_enc_grid, *((w_enc_mesh, list_here) if first else (total,)), *group
            )
        )
        enc_picks += got[:count]
        enc_slopes += got[count : 2 * count]
        del got[: 2 * count]
        if first:
            base = got.pop(0)
        total = got[0]
    part = got[0]
    for step in range(1, halves):
        part = part + shifted(got[step], "rep", step).astype(f32)
    part = part.astype(bf16)
    pieces = [part] + [shifted(part, "feat", step) for step in range(1, feats)]
    if feats > 2:
        pieces = list(in_order(pieces, "feat"))
    part = sum(piece.astype(f32) for piece in pieces).astype(bf16)
    parts = [part] + [shifted(part, "rep", -step) for step in range(1, halves)]

    listed = [((depth, width), bf16)] * (2 if shared else shifts)

    def exchange(blocks, send, early):
        if not shared:
            return [send(block, shifts - at) for at, block in enumerate(blocks)], early
        far = lax.ppermute(
            blocks[0], ("mesh", "rep"), [(2 * at + side, 2 * (at ^ (2 + side)) + side) for at in range(4) for side in range(2)]
        )
        near = send(blocks[1], 1)
        far, early = lax.optimization_barrier((far, early))
        return [far, shifted(far, "rep", 1), near], early

    listed_products = [(listed_rows, width, width)] * 2 + [(listed_rows, nodes, width)] * 2
    total, *outgoing = call(functools.partial(start_kernel, halves), [node_bf16] + listed, (), listed_products)(
        meta, *parts, mesh_init, w_enc_out, enc_gain, w_send, list_here
    )

    half_f32, edge_bf16 = ((all_edges // 2, width), f32), ((all_edges, width), bf16)
    halo, back_halo = ((wide, width), bf16), ((listed_rows, width), bf16)
    forward_products = [(all_edges, wide, width), (nodes, all_edges, width), square]
    backward_products = [square, (all_edges, nodes, width), (wide, all_edges, width)]
    half_product = (all_edges // 2, 2 * nodes, width)

    hidden, sums, slopes = mesh_init, [], []
    for layer in range(LAYERS):
        weights = (w_out, layer_gain) if layer else (w_enc_out, enc_gain)
        early = call(
            functools.partial(local_kernel, layer),
            [node_bf16, node_f32, half_f32, ((2 * nodes, width), bf16)],
            (),
            [square, square, square, half_product],
        )(total, hidden, *weights, w_send, w_recv, here)
        halos, (hidden, agg, pre, both_tables) = exchange(outgoing, sent_to, early)
        (more,) = call(local_more_kernel, [half_f32], (), [half_product])(both_tables, here)
        sums.append(agg)
        if layer == LAYERS - 1:
            break
        total, slope, *outgoing = call(
            functools.partial(layer_kernel, layer, shifts),
            [node_bf16, edge_bf16] + listed,
            [halo, edge_bf16],
            forward_products[:2] + listed_products,
        )(hidden, pre, more, *halos, halo_here, there, w_out, layer_gain, w_send, list_here)
        slopes.append(slope)
    enc_sum, records = sums[0], list(zip(sums[1:], slopes))
    final_mesh, grad_pre, *outgoing = call(
        functools.partial(turn_kernel, layer, shifts), [node_bf16, edge_bf16] + listed, [edge_bf16, halo],
        forward_products + backward_products,
    )(hidden, pre, more, *halos, halo_here, there, w_out, layer_gain, here, halo_there, out_cot)
    upstream = out_cot
    for layer in reversed(range(LAYERS)):

        def rest_of(side, upstream, weights):
            (rest,) = call(
                functools.partial(rest_kernel, layer, side), [node_f32], (), [(nodes, all_edges, width), square]
            )(upstream, grad_pre, there, weights)
            return rest

        returned, early = exchange(outgoing, sent_back, rest_of(0, upstream, w_send))
        rest = rest_of(1, early, w_recv)
        if layer:
            agg, slope = records[layer - 1]
            upstream, grad_pre, *outgoing = call(
                functools.partial(back_kernel, layer - 1, shifts),
                [node_f32, edge_bf16] + listed,
                [back_halo],
                backward_products + [(listed_rows, width, width), (nodes, listed_rows, width)],
            )(rest, *returned, list_there, w_send, agg, slope, layer_gain, w_out, here, halo_there)
    piece = ((piece_rows, width), bf16)
    one = (grid, nodes, width)
    spread, *far = call(
        functools.partial(finish_kernel, shifts),
        [node_bf16] + [piece] * cuts,
        [back_halo],
        [square, (listed_rows, width, width), (nodes, listed_rows, width), one],
    )(rest, *returned, list_there, w_send, enc_sum, enc_gain, w_enc_out, enc_picks[-1], enc_slopes[-1])
    blocks = call(
        functools.partial(others_kernel, shards - 1), [row_shape] * (shards - 1), products=[one] * (shards - 1)
    )(spread, *enc_picks[:-1], *enc_slopes[:-1])
    if relayed:
        passed = [sent_back(block, 1) for block in far]
        first, near = call(functools.partial(relay_kernel, 0), [piece, row_shape])(blocks[2], passed[0], blocks[1])
        (second,) = call(functools.partial(relay_kernel, piece_rows), [piece])(blocks[2], passed[1])
        near = sent_back(near, 1)
        first, second = sent_back(first, 2), sent_back(second, 2)
        (summed,) = call(sum_kernel, [((piece_rows, width), f32)])(blocks[0], first)
        (grid_grad,) = call(
            functools.partial(grid_kernel, 2), [((grid, width), f32)], products=[(grid, width, width)]
        )(blocks[0], near, summed, second, w_enc_grid)
    else:
        blocks = [*blocks, *far]
        blocks = [blocks[0]] + [sent_back(block, step) for step, block in enumerate(blocks) if step]
        (grid_grad,) = call(
            functools.partial(grid_kernel, shards), [((grid, width), f32)], products=[(grid, width, width)]
        )(*blocks, w_enc_grid)
    return (final_mesh, grid_grad)


def solution(mesh):
    return jax.shard_map(
        on_device,
        mesh=mesh,
        in_specs=(
            P(("groups", "mesh", "feat", "rep"), None),
            P(("groups", "mesh", "feat", "rep"), None),
            P(("groups", "mesh", "feat", "rep"), None),
            P(("groups", "mesh"), None),
            P(("groups", "mesh", "feat", "rep")),
            P(("groups", "mesh", "feat", "rep")),
            P(("groups", "mesh"), None, None),
            P(),
            P(),
            P(),
            P(),
            P(),
            P(),
            P(),
            P(),
            P(("groups", "mesh"), None),
        ),
        out_specs=(P(("groups", "mesh"), None), P(("groups", "mesh", "feat", "rep"), None)),
        check_vma=False,
    )
```

```python
import functools
import math

import jax
import jax.numpy as jnp
from jax import lax
from jax.experimental import pallas as pl
from jax.experimental.pallas import tpu as pltpu
from jax.sharding import PartitionSpec as P

LAYERS = 3
LANES = 128
BLOCK = 512
EXTRA = 16
eps = 1e-05

f32 = jnp.float32
bf16 = jnp.bfloat16
i32 = jnp.int32


def norm_scale(totals):
    return lax.rsqrt(jnp.mean(totals * totals, axis=-1, keepdims=True) + eps)


def norm_back(totals, gain_row, upstream):
    scaled = norm_scale(totals)
    normed = totals * scaled
    slope = upstream * gain_row
    return scaled * (slope - normed * jnp.mean(slope * normed, axis=-1, keepdims=True))


def dot(left, right):
    return jnp.dot(left, right, preferred_element_type=f32)


def dot_back(left, right):
    return lax.dot_general(left, right, (((1,), (1,)), ((), ())), preferred_element_type=f32)


def gated(half):
    half = half.astype(bf16)
    bend = jnp.tanh(half)
    act = half + half * bend
    return act, (1.0 + act) + bend * (1.0 - act)


def as_mask(hit):
    return jnp.where(hit, 1.0, 0.0).astype(bf16)


def pick_columns(index, first, height):
    place = lax.broadcasted_iota(i32, (height, index.shape[1]), 0) + first
    return as_mask(place == index)


def upright(index):
    count = index.shape[1]
    if count < LANES:
        index = jnp.concatenate([index, jnp.full((1, LANES - count), -1, i32)], axis=1)
    return jnp.broadcast_to(index, (LANES, LANES)).T[:count]


def pick_rows(column, first, width):
    lane = lax.broadcasted_iota(i32, column.shape, 1) + first
    return jnp.concatenate([as_mask(column == lane + at) for at in range(0, width, LANES)], axis=1)


def call(body, outs, scratch=(), products=(), copied=False):
    def run(*args):
        def where(array):
            if copied:
                return pl.BlockSpec(memory_space=pltpu.HBM)
            return pl.BlockSpec(memory_space=pltpu.SMEM if array.dtype == i32 and array.ndim == 1 else pltpu.VMEM)

        def size(shape, dtype):
            return jnp.dtype(dtype).itemsize * math.prod(shape)

        own = sum(size(*held) for held in scratch) + (10 << 20)
        moved = sum(array.dtype.itemsize * array.size for array in args) + sum(size(*out) for out in outs)
        limit = own if own + moved < 40 << 20 else min(own + moved, 60 << 20)
        semaphores = [pltpu.SemaphoreType.DMA((2 + len(outs),))] if copied else []
        return pl.pallas_call(
            body,
            out_shape=tuple(jax.ShapeDtypeStruct(shape, dtype) for shape, dtype in outs),
            in_specs=[where(array) for array in args],
            out_specs=tuple(pl.BlockSpec(memory_space=pltpu.VMEM) for _ in outs),
            scratch_shapes=[pltpu.VMEM(shape, dtype) for shape, dtype in scratch] + semaphores,
            compiler_params=pltpu.CompilerParams(vmem_limit_bytes=limit),
            cost_estimate=pl.CostEstimate(
                flops=2 * sum(math.prod(product) for product in products), bytes_accessed=moved, transcendentals=0
            ),
        )(*args)

    return run


def place_kernel(
    slots, receivers, order, latents, here, there, halo_here, halo_there, list_here, list_there, kept
):
    nodes = here.shape[1] // 2
    wide = halo_here.shape[1]

    def body(at):
        block = pl.ds(pl.multiple_of(at * LANES, LANES), LANES)
        slot, receiver = slots[:, block], receivers[:, block]
        slot_column, receiver_column = upright(slot), upright(receiver)
        here[block, 0:nodes] = pick_rows(slot_column, 0, nodes)
        here[block, nodes:] = pick_rows(receiver_column, 0, nodes)
        halo_here[block, :] = pick_rows(slot_column, nodes, wide)
        there[0:nodes, block] = pick_columns(slot, 0, nodes)
        there[nodes:, block] = pick_columns(receiver, 0, nodes)
        halo_there[:, block] = pick_columns(slot, nodes, wide)

    pl.loop(0, slots.shape[1] // LANES)(body)
    count = order.shape[1]
    for at in range(0, count, LANES):
        end = min(at + LANES, count)
        list_here[at:end, :] = pick_rows(upright(order[:, at:end]), 0, nodes)
    list_there[...] = pick_columns(order[...], 0, nodes)
    kept[...] = dot(list_here[...], latents[...]).astype(bf16)


def note_kernel(rows, shards, nodes, payload, shard_rows, node_rows, arrived):
    grid = shards.shape[1]
    first = payload.shape[0] - EXTRA
    copies = [
        pltpu.make_async_copy(shards, shard_rows, arrived.at[0]),
        pltpu.make_async_copy(nodes, node_rows, arrived.at[1]),
        pltpu.make_async_copy(rows.at[0:first], payload.at[0:first], arrived.at[2]),
    ]
    for copy in copies:
        copy.start()
    for copy in copies[:2]:
        copy.wait()
    row = lax.broadcasted_iota(i32, (EXTRA, grid), 0)
    notes = jnp.full((EXTRA, grid), -1, i32)
    for top in range(shards.shape[0]):
        node = node_rows[top : top + 1, :]
        for at, value in enumerate((shard_rows[top : top + 1, :], node & 255, node >> 8)):
            notes = jnp.where(row == 3 * top + at, value, notes)
    payload[first:, 0:grid] = notes.astype(f32).astype(bf16)
    if grid < payload.shape[1]:
        payload[first:, grid:] = jnp.zeros((EXTRA, payload.shape[1] - grid), bf16)
    copies[2].wait()


def encode_kernel(steps, first, last, halves, *refs):
    refs = list(refs)
    meta, base, w_grid = refs[:3]
    del refs[:3]
    if first:
        w_mesh, _ = refs.pop(0), refs.pop(0)
        projected = dot(base[...], w_mesh[...]).astype(bf16)
    else:
        total_in = refs.pop(0)
        projected = base[...]
    payloads = refs[:steps]
    del refs[:steps]
    picks, slopes = refs[:steps], refs[steps : 2 * steps]
    del refs[: 2 * steps]
    total = None if first else total_in[...]
    nodes = projected.shape[0]
    for payload, pick, slope_out in zip(payloads, picks, slopes):
        grid = pick.shape[0]
        notes = payload[grid:, 0:grid].astype(f32)
        target = jnp.full((1, grid), -1.0, f32)
        for at in range(0, notes.shape[0] // 3 * 3, 3):
            named = notes[at : at + 1] == meta[1:2, 0:grid].astype(f32)
            target = jnp.where(named, notes[at + 1 : at + 2] + 256.0 * notes[at + 2 : at + 3], target)
        target = target.astype(i32)
        column = jnp.concatenate([upright(target[:, at : at + LANES]) for at in range(0, grid, LANES)], axis=0)
        picked = pick_rows(column, 0, nodes)
        pick[...] = picked
        pre = dot(payload[0:grid, :], w_grid[...]) + dot(picked, projected)
        act, slope = gated(0.5 * pre)
        slope_out[...] = slope.astype(bf16)
        added = dot(pick_columns(target, 0, nodes), act.astype(bf16))
        total = added if total is None else total + added
    if first:
        refs.pop(0)[...] = projected
    if not last:
        refs[0][...] = total
        return
    keep, sends = refs[0], refs[1:halves]
    part = nodes // halves
    own = meta[0:1, :]

    def half(shift):
        rows = total[0:part]
        for at in range(1, halves):
            rows = jnp.where(own == (at - shift) % halves, total[at * part : (at + 1) * part], rows)
        return rows

    keep[...] = half(0)
    for shift in range(1, halves):
        sends[shift - 1][...] = half(shift).astype(bf16)


def hand_out(rows, outs):
    rows = rows.astype(bf16)
    depth = outs[0].shape[0]
    count = rows.shape[0] // depth
    for at, out in enumerate(outs):
        first = 0 if at == 0 else (count - len(outs) + at) * depth
        out[...] = rows[first : first + depth]


def updated(hidden, total, w_out, gain_row):
    agg = dot(total, w_out)
    return (hidden.astype(f32) + agg * norm_scale(agg) * gain_row).astype(bf16), agg


def listed_update(list_here, total, kept, w_out, gain_row, w_send):
    rows = dot(list_here[...], total).astype(bf16)
    return 0.5 * dot(updated(kept, rows, w_out, gain_row)[0], w_send)


def start_kernel(halves, *refs):
    meta = refs[0]
    parts = refs[1 : 1 + halves]
    kept, w_enc_out, gain, w_send, list_here, whole = refs[1 + halves : 7 + halves]
    part = parts[0].shape[0]
    own = meta[0:1, :]
    for at in range(halves):
        rows = parts[0][...].astype(f32)
        for shift in range(1, halves):
            rows = jnp.where(own == (at - shift) % halves, parts[shift][...].astype(f32), rows)
        whole[at * part : (at + 1) * part, :] = rows.astype(bf16)
    hand_out(
        listed_update(list_here, whole[...], kept[...], w_enc_out[...], gain[...], w_send[0]), refs[7 + halves :]
    )


def local_kernel(
    layer, total, hidden, w_out, gain, w_send, w_recv, here, list_here, hidden_out, agg_out, pre, table, kept_out
):
    nodes = hidden.shape[0]
    if layer:
        fresh, agg = updated(hidden[...], total[...], w_out[layer - 1], gain[layer - 1 : layer, :])
    else:
        fresh, agg = updated(hidden[...], total[...], w_out[...], gain[...])
    hidden_out[...] = fresh
    agg_out[...] = agg
    kept_out[...] = dot(list_here[...], fresh).astype(bf16)
    table[0:nodes, :] = (0.5 * dot(fresh, w_send[layer])).astype(bf16)
    table[nodes:, :] = (0.5 * dot(fresh, w_recv[layer])).astype(bf16)
    for at in range(0, pre.shape[0], BLOCK):
        pre[at : at + BLOCK, :] = dot(here[at : at + BLOCK, :], table[...])


def local_more_kernel(table, here, pre):
    skip = here.shape[0] - pre.shape[0]
    for at in range(0, pre.shape[0], BLOCK):
        pre[at : at + BLOCK, :] = dot(here[skip + at : skip + at + BLOCK, :], table[...])


def stack_halo(halos, halo):
    at = 0
    for block in halos:
        halo[at : at + block.shape[0], :] = block[...]
        at += block.shape[0]
    if at < halo.shape[0]:
        halo[at:, :] = jnp.zeros((halo.shape[0] - at, halo.shape[1]), bf16)


def node_sum(pres, halos, halo_here, there, slope_out, halo, act_out):
    nodes = there.shape[0] // 2
    stack_halo(halos, halo)
    half = pres[0].shape[0]
    for at in range(0, 2 * half, BLOCK):
        block = slice(at, at + BLOCK)
        pre = pres[at // half][at % half : at % half + BLOCK, :]
        act, slope = gated(pre + dot(halo_here[block, :], halo[...]))
        slope_out[block, :] = slope.astype(bf16)
        act_out[block, :] = act.astype(bf16)
    return dot(there[nodes:, :], act_out[...])


def layer_kernel(layer, shifts, *refs):
    kept, pres = refs[0], refs[1:3]
    halos, refs = refs[3 : 3 + shifts], refs[3 + shifts :]
    halo_here, there, w_out, gain, w_send, list_here = refs[:6]
    total_out, slope_out = refs[6:8]
    outs = refs[8:-2]
    total = node_sum(pres, halos, halo_here, there, slope_out, *refs[-2:]).astype(bf16)
    total_out[...] = total
    gain_row = gain[layer : layer + 1, :]
    hand_out(listed_update(list_here, total, kept[...], w_out[layer], gain_row, w_send[layer + 1]), outs)


def edge_grads(listed, grad_agg, w_out, here, halo_there, slope, grad_pre, outs):
    nodes = grad_agg.shape[0]
    spread = (0.5 * dot_back(grad_agg.astype(bf16), w_out)).astype(bf16)
    for at in range(0, slope.shape[0], BLOCK):
        block = slice(at, at + BLOCK)
        grad_act = dot(here[block, nodes:], spread)
        grad_pre[block, :] = grad_act.astype(bf16) * slope[block, :]
    hand_out(dot(halo_there[...], grad_pre[...])[0:listed], outs)


def turn_kernel(layer, shifts, *refs):
    hidden, pres = refs[0], refs[1:3]
    halos, refs = refs[3 : 3 + shifts], refs[3 + shifts :]
    halo_here, there, w_out, gain, here, halo_there, cot = refs[:7]
    hidden_out, grad_pre = refs[7:9]
    outs = refs[9:-2]
    slope, halo = refs[-2:]
    total = node_sum(pres, halos, halo_here, there, slope, halo, grad_pre)
    gain_row = gain[layer : layer + 1, :]
    fresh, agg = updated(hidden[...], total.astype(bf16), w_out[layer], gain_row)
    hidden_out[...] = fresh
    edge_grads(shifts * outs[0].shape[0], norm_back(agg, gain_row, cot[...].astype(f32)), w_out[layer], here, halo_there, slope, grad_pre, outs)


def rest_kernel(layer, side, upstream, grad_pre, there, weights, rest):
    nodes = upstream.shape[0]
    sums = dot(there[side * nodes : (side + 1) * nodes, :], grad_pre[...]).astype(bf16)
    rest[...] = upstream[...].astype(f32) + dot_back(sums, weights[layer])


def arrived(rest, returned, list_there, w_send, halo):
    stack_halo(returned, halo)
    projected = dot_back(halo[...], w_send).astype(bf16)
    return rest[...] + dot(list_there[...], projected)


def back_kernel(layer, shifts, *refs):
    rest = refs[0]
    returned, refs = refs[1 : 1 + shifts], refs[1 + shifts :]
    list_there, w_send, agg, slope, gain, w_out, here, halo_there = refs[:8]
    upstream_out, grad_pre = refs[8:10]
    outs = refs[10:-1]
    halo = refs[-1]
    upstream = arrived(rest, returned, list_there, w_send[layer + 1], halo)
    upstream_out[...] = upstream
    grad_agg = norm_back(agg[...], gain[layer : layer + 1, :], upstream)
    edge_grads(shifts * outs[0].shape[0], grad_agg, w_out[layer], here, halo_there, slope, grad_pre, outs)


def pair_grads(spread, pick, slope):
    return dot(pick, spread).astype(bf16) * slope


def finish_kernel(shifts, *refs):
    rest = refs[0]
    returned, refs = refs[1 : 1 + shifts], refs[1 + shifts :]
    list_there, w_send, enc_sum, gain, w_enc_out, pick, slope, spread_out = refs[:8]
    outs, halo = refs[8:-1], refs[-1]
    upstream = arrived(rest, returned, list_there, w_send[0], halo)
    spread = (0.5 * dot_back(norm_back(enc_sum[...], gain[...], upstream).astype(bf16), w_enc_out[...])).astype(bf16)
    spread_out[...] = spread
    at = 0
    for out in outs:
        rows = slice(at, at + out.shape[0])
        out[...] = pair_grads(spread, pick[rows, :], slope[rows, :])
        at += out.shape[0]


def others_kernel(count, *refs):
    spread = refs[0][...]
    picks, slopes, outs = refs[1 : 1 + count], refs[1 + count : 1 + 2 * count], refs[1 + 2 * count :]
    for pick, slope, out in reversed(list(zip(picks, slopes, outs))):
        skip = pick.shape[0] - out.shape[0]
        out[...] = pair_grads(spread, pick[skip:, :], slope[skip:, :])


def relay_kernel(first, own, passed, *refs):
    rows = passed.shape[0]
    out = refs[0] if len(refs) == 1 else refs[-2]
    out[...] = (own[first : first + rows, :].astype(f32) + passed[...].astype(f32)).astype(bf16)
    if len(refs) > 1:
        refs[-1][...] = refs[0][...]


def sum_kernel(own, piece, total):
    total[...] = own[0 : piece.shape[0], :].astype(f32) + piece[...].astype(f32)


def grid_kernel(whole, *refs):
    blocks, pieces, (w_grid, out) = refs[:whole], refs[whole:-2], refs[-2:]
    if not pieces:
        total = blocks[0][...].astype(f32)
        for block in blocks[1:]:
            total = total + block[...].astype(f32)
        out[...] = dot_back(total.astype(bf16), w_grid[...])
        return
    (own, near), (summed, second) = blocks, pieces
    first = summed.shape[0]
    total = summed[...] + near[0:first, :].astype(f32)
    out[0:first, :] = dot_back(total.astype(bf16), w_grid[...])
    total = own[first:, :].astype(f32) + near[first:, :].astype(f32) + second[...].astype(f32)
    out[first:, :] = dot_back(total.astype(bf16), w_grid[...])


def shifted(value, axis, by):
    size = lax.axis_size(axis)
    return lax.ppermute(value, axis, [(at, (at + by) % size) for at in range(size)])


def partner(at, step, size):
    return at ^ step if size & (size - 1) == 0 else (at + step) % size


def sent_to(value, step):
    size = lax.axis_size("mesh")
    return lax.ppermute(value, "mesh", [(at, partner(at, step, size)) for at in range(size)])


def sent_back(value, step):
    size = lax.axis_size("mesh")
    return lax.ppermute(value, "mesh", [(partner(at, step, size), at) for at in range(size)])


def in_order(pieces, axis):
    return jnp.roll(jnp.stack(pieces)[::-1], lax.axis_index(axis) + 1, axis=0)


def on_device(
    grid_feats,
    g2m_shard,
    g2m_node,
    mesh_init,
    sender_slots,
    receivers,
    halo_index,
    w_enc_grid,
    w_enc_mesh,
    w_enc_out,
    enc_gain,
    w_send,
    w_recv,
    w_out,
    layer_gain,
    out_cot,
):
    shards = lax.axis_size("mesh")
    shard = lax.axis_index("mesh")
    halves = lax.axis_size("rep")
    feats = lax.axis_size("feat")
    nodes, width = mesh_init.shape
    grid, tops = g2m_shard.shape
    edges = sender_slots.shape[0]
    depth = halo_index.shape[2]
    shifts = shards - 1
    listed_rows = shifts * depth
    wide = -(-listed_rows // LANES) * LANES
    all_edges = edges * halves * feats
    enc_gain = enc_gain[None, :]

    relayed = shards == 4
    cuts = 2 if relayed else 1
    shared = relayed and halves == 2
    piece_rows = grid // cuts
    in_place = [pltpu.with_memory_space_constraint(array, pltpu.HBM) for array in (grid_feats, g2m_shard.T, g2m_node.T)]
    (payload,) = call(
        note_kernel,
        [((grid + EXTRA, width), bf16)],
        [((tops, grid), i32), ((tops, grid), i32)],
        copied=True,
    )(*in_place)

    place = sender_slots - nodes
    away = partner(shard, place // depth, shards)
    if shards & (shards - 1):
        away = lax.rem(shard - place // depth + shards, shards)
    slots = jnp.where(sender_slots < nodes, sender_slots, nodes + (shifts - away) * depth + place % depth)
    both = jnp.stack([slots, receivers])
    others = [shifted(both, "rep", step) for step in range(1, halves)]
    if relayed:
        across = sent_to(payload, 2)
        payloads = [payload, sent_to(payload, 1), across]
    else:
        payloads = [payload] + [sent_to(payload, step) for step in range(1, shards)]
    both = in_order([both] + others, "rep")
    both = in_order([both] + [shifted(both, "feat", step) for step in range(1, feats)], "feat")
    both = both.reshape(feats * halves, 2, edges)
    all_slots, all_receivers = both[:, 0].reshape(1, -1), both[:, 1].reshape(1, -1)
    steps = shards - jnp.arange(1, shards, dtype=i32)
    if shared:
        core = lax.axis_index("rep")
        steps = jnp.where((core == 0) & (steps > 1), 5 - steps, steps)
        entry = all_slots - nodes
        turned = (core == 0) & (entry >= 0) & (entry < 2 * depth)
        all_slots = all_slots + jnp.where(turned, jnp.where(entry < depth, depth, -depth), 0)
    readers = partner(shard, steps, shards)
    lists = jnp.take(halo_index[0], readers, axis=0).reshape(1, -1)
    here, there, halo_here, halo_there, list_here, list_there, kept = call(
        place_kernel,
        [
            ((all_edges, 2 * nodes), bf16),
            ((2 * nodes, all_edges), bf16),
            ((all_edges, wide), bf16),
            ((wide, all_edges), bf16),
            ((listed_rows, nodes), bf16),
            ((nodes, listed_rows), bf16),
            ((listed_rows, width), bf16),
        ],
        products=[(all_edges, nodes, width), (all_edges, 2 * nodes, width)],
    )(all_slots, all_receivers, lists, mesh_init)

    if relayed:
        across, list_here = lax.optimization_barrier((across, list_here))
        payloads.append(sent_to(across, 1))

    meta = jnp.broadcast_to(jnp.stack([lax.axis_index("rep"), shard]).astype(i32)[:, None], (2, width))
    node_f32, node_bf16 = ((nodes, width), f32), ((nodes, width), bf16)
    row_shape, half = ((grid, width), bf16), nodes // halves
    square = (nodes, width, width)
    enc_picks, enc_slopes = [], []
    base, total = mesh_init, None
    groups = [payloads[:2]] + [payloads[at : at + 1] for at in range(2, shards)]
    for at, group in enumerate(groups):
        first, last = at == 0, at == len(groups) - 1
        count = len(group)
        outs = [((grid, nodes), bf16)] * count + [row_shape] * count
        outs += [node_bf16] if first else []
        outs += [((half, width), f32)] + [((half, width), bf16)] * (halves - 1) if last else [node_f32]
        got = list(
            call(
                functools.partial(encode_kernel, count, first, last, halves),
                outs,
                (),
                [square] * first + [(grid, width, width), (grid, nodes, width), (nodes, grid, width)] * count,
            )(
                meta, base, w_enc_grid, *((w_enc_mesh, list_here) if first else (total,)), *group
            )
        )
        enc_picks += got[:count]
        enc_slopes += got[count : 2 * count]
        del got[: 2 * count]
        if first:
            base = got.pop(0)
        total = got[0]
    part = got[0]
    for step in range(1, halves):
        part = part + shifted(got[step], "rep", step).astype(f32)
    part = part.astype(bf16)
    pieces = [part] + [shifted(part, "feat", step) for step in range(1, feats)]
    if feats > 2:
        pieces = list(in_order(pieces, "feat"))
    part = sum(piece.astype(f32) for piece in pieces).astype(bf16)
    parts = [part] + [shifted(part, "rep", -step) for step in range(1, halves)]

    listed = [((depth, width), bf16)] * (2 if shared else shifts)

    def exchange(blocks, send, early):
        if not shared:
            return [send(block, shifts - at) for at, block in enumerate(blocks)], early
        far = lax.ppermute(
            blocks[0], ("mesh", "rep"), [(2 * at + side, 2 * (at ^ (2 + side)) + side) for at in range(4) for side in range(2)]
        )
        near = send(blocks[1], 1)
        far, early = lax.optimization_barrier((far, early))
        return [far, shifted(far, "rep", 1), near], early

    listed_products = [(listed_rows, width, width)] * 2 + [(listed_rows, nodes, width)] * 2
    total, *outgoing = call(functools.partial(start_kernel, halves), [node_bf16] + listed, (), listed_products)(
        meta, *parts, kept, w_enc_out, enc_gain, w_send, list_here
    )

    half_f32, edge_bf16 = ((all_edges // 2, width), f32), ((all_edges, width), bf16)
    halo, back_halo = ((wide, width), bf16), ((listed_rows, width), bf16)
    forward_products = [(all_edges, wide, width), (nodes, all_edges, width), square]
    backward_products = [square, (all_edges, nodes, width), (wide, all_edges, width)]
    half_product = (all_edges // 2, 2 * nodes, width)

    hidden, sums, slopes = mesh_init, [], []
    for layer in range(LAYERS):
        weights = (w_out, layer_gain) if layer else (w_enc_out, enc_gain)
        early = call(
            functools.partial(local_kernel, layer),
            [node_bf16, node_f32, half_f32, ((2 * nodes, width), bf16), back_halo],
            (),
            [square, square, square, half_product],
        )(total, hidden, *weights, w_send, w_recv, here, list_here)
        halos, (hidden, agg, pre, both_tables, kept) = exchange(outgoing, sent_to, early)
        (more,) = call(local_more_kernel, [half_f32], (), [half_product])(both_tables, here)
        sums.append(agg)
        if layer == LAYERS - 1:
            break
        total, slope, *outgoing = call(
            functools.partial(layer_kernel, layer, shifts),
            [node_bf16, edge_bf16] + listed,
            [halo, edge_bf16],
            forward_products[:2] + listed_products,
        )(kept, pre, more, *halos, halo_here, there, w_out, layer_gain, w_send, list_here)
        slopes.append(slope)
    enc_sum, records = sums[0], list(zip(sums[1:], slopes))
    final_mesh, grad_pre, *outgoing = call(
        functools.partial(turn_kernel, layer, shifts), [node_bf16, edge_bf16] + listed, [edge_bf16, halo],
        forward_products + backward_products,
    )(hidden, pre, more, *halos, halo_here, there, w_out, layer_gain, here, halo_there, out_cot)
    upstream = out_cot
    for layer in reversed(range(LAYERS)):

        def rest_of(side, upstream, weights):
            (rest,) = call(
                functools.partial(rest_kernel, layer, side), [node_f32], (), [(nodes, all_edges, width), square]
            )(upstream, grad_pre, there, weights)
            return rest

        returned, early = exchange(outgoing, sent_back, rest_of(0, upstream, w_send))
        rest = rest_of(1, early, w_recv)
        if layer:
            agg, slope = records[layer - 1]
            upstream, grad_pre, *outgoing = call(
                functools.partial(back_kernel, layer - 1, shifts),
                [node_f32, edge_bf16] + listed,
                [back_halo],
                backward_products + [(listed_rows, width, width), (nodes, listed_rows, width)],
            )(rest, *returned, list_there, w_send, agg, slope, layer_gain, w_out, here, halo_there)
    piece = ((piece_rows, width), bf16)
    one = (grid, nodes, width)
    spread, *far = call(
        functools.partial(finish_kernel, shifts),
        [node_bf16] + [piece] * cuts,
        [back_halo],
        [square, (listed_rows, width, width), (nodes, listed_rows, width), one],
    )(rest, *returned, list_there, w_send, enc_sum, enc_gain, w_enc_out, enc_picks[-1], enc_slopes[-1])
    blocks = call(
        functools.partial(others_kernel, shards - 1), [row_shape] * (shards - 1), products=[one] * (shards - 1)
    )(spread, *enc_picks[:-1], *enc_slopes[:-1])
    if relayed:
        passed = [sent_back(block, 1) for block in far]
        first, near = call(functools.partial(relay_kernel, 0), [piece, row_shape])(blocks[2], passed[0], blocks[1])
        (second,) = call(functools.partial(relay_kernel, piece_rows), [piece])(blocks[2], passed[1])
        near = sent_back(near, 1)
        first, second = sent_back(first, 2), sent_back(second, 2)
        (summed,) = call(sum_kernel, [((piece_rows, width), f32)])(blocks[0], first)
        (grid_grad,) = call(
            functools.partial(grid_kernel, 2), [((grid, width), f32)], products=[(grid, width, width)]
        )(blocks[0], near, summed, second, w_enc_grid)
    else:
        blocks = [*blocks, *far]
        blocks = [blocks[0]] + [sent_back(block, step) for step, block in enumerate(blocks) if step]
        (grid_grad,) = call(
            functools.partial(grid_kernel, shards), [((grid, width), f32)], products=[(grid, width, width)]
        )(*blocks, w_enc_grid)
    return (final_mesh, grid_grad)


def solution(mesh):
    return jax.shard_map(
        on_device,
        mesh=mesh,
        in_specs=(
            P(("groups", "mesh", "feat", "rep"), None),
            P(("groups", "mesh", "feat", "rep"), None),
            P(("groups", "mesh", "feat", "rep"), None),
            P(("groups", "mesh"), None),
            P(("groups", "mesh", "feat", "rep")),
            P(("groups", "mesh", "feat", "rep")),
            P(("groups", "mesh"), None, None),
            P(),
            P(),
            P(),
            P(),
            P(),
            P(),
            P(),
            P(),
            P(("groups", "mesh"), None),
        ),
        out_specs=(P(("groups", "mesh"), None), P(("groups", "mesh", "feat", "rep"), None)),
        check_vma=False,
    )
```

```python
import functools
import math

import jax
import jax.numpy as jnp
from jax import lax
from jax.experimental import pallas as pl
from jax.experimental.pallas import tpu as pltpu
from jax.sharding import PartitionSpec as P

LAYERS = 3
LANES = 128
BLOCK = 1024
EXTRA = 16
eps = 1e-05

f32 = jnp.float32
bf16 = jnp.bfloat16
i32 = jnp.int32


def norm_scale(totals):
    return lax.rsqrt(jnp.mean(totals * totals, axis=-1, keepdims=True) + eps)


def norm_back(totals, gain_row, upstream):
    scaled = norm_scale(totals)
    normed = totals * scaled
    slope = upstream * gain_row
    return scaled * (slope - normed * jnp.mean(slope * normed, axis=-1, keepdims=True))


def dot(left, right):
    return jnp.dot(left, right, preferred_element_type=f32)


def dot_back(left, right):
    return lax.dot_general(left, right, (((1,), (1,)), ((), ())), preferred_element_type=f32)


def gated(half):
    half = half.astype(bf16)
    bend = jnp.tanh(half)
    act = half + half * bend
    return act, (1.0 + act) + bend * (1.0 - act)


def as_mask(hit):
    return jnp.where(hit, 1.0, 0.0).astype(bf16)


def pick_columns(index, first, height):
    place = lax.broadcasted_iota(i32, (height, index.shape[1]), 0) + first
    return as_mask(place == index)


def upright(index):
    count = index.shape[1]
    if count < LANES:
        index = jnp.concatenate([index, jnp.full((1, LANES - count), -1, i32)], axis=1)
    return jnp.broadcast_to(index, (LANES, LANES)).T[:count]


def pick_rows(column, first, width):
    lane = lax.broadcasted_iota(i32, column.shape, 1) + first
    return jnp.concatenate([as_mask(column == lane + at) for at in range(0, width, LANES)], axis=1)


def call(body, outs, scratch=(), products=(), copied=False):
    def run(*args):
        def where(array):
            if copied:
                return pl.BlockSpec(memory_space=pltpu.HBM)
            return pl.BlockSpec(memory_space=pltpu.SMEM if array.dtype == i32 and array.ndim == 1 else pltpu.VMEM)

        def size(shape, dtype):
            return jnp.dtype(dtype).itemsize * math.prod(shape)

        own = sum(size(*held) for held in scratch) + (10 << 20)
        moved = sum(array.dtype.itemsize * array.size for array in args) + sum(size(*out) for out in outs)
        limit = own if own + moved < 40 << 20 else min(own + moved, 60 << 20)
        semaphores = [pltpu.SemaphoreType.DMA((2 + len(outs),))] if copied else []
        return pl.pallas_call(
            body,
            out_shape=tuple(jax.ShapeDtypeStruct(shape, dtype) for shape, dtype in outs),
            in_specs=[where(array) for array in args],
            out_specs=tuple(pl.BlockSpec(memory_space=pltpu.VMEM) for _ in outs),
            scratch_shapes=[pltpu.VMEM(shape, dtype) for shape, dtype in scratch] + semaphores,
            compiler_params=pltpu.CompilerParams(vmem_limit_bytes=limit),
            cost_estimate=pl.CostEstimate(
                flops=2 * sum(math.prod(product) for product in products), bytes_accessed=moved, transcendentals=0
            ),
        )(*args)

    return run


def place_kernel(slots, receivers, order, here, there, halo_here, halo_there, list_here, list_there):
    nodes = here.shape[1] // 2
    wide = halo_here.shape[1]

    def body(at):
        block = pl.ds(pl.multiple_of(at * LANES, LANES), LANES)
        slot, receiver = slots[:, block], receivers[:, block]
        slot_column, receiver_column = upright(slot), upright(receiver)
        here[block, 0:nodes] = pick_rows(slot_column, 0, nodes)
        here[block, nodes:] = pick_rows(receiver_column, 0, nodes)
        halo_here[block, :] = pick_rows(slot_column, nodes, wide)
        there[0:nodes, block] = pick_columns(slot, 0, nodes)
        there[nodes:, block] = pick_columns(receiver, 0, nodes)
        halo_there[:, block] = pick_columns(slot, nodes, wide)

    pl.loop(0, slots.shape[1] // LANES)(body)
    count = order.shape[1]
    for at in range(0, count, LANES):
        end = min(at + LANES, count)
        list_here[at:end, :] = pick_rows(upright(order[:, at:end]), 0, nodes)
    list_there[...] = pick_columns(order[...], 0, nodes)


def note_kernel(rows, shards, nodes, payload, shard_rows, node_rows, arrived):
    grid = shards.shape[1]
    first = payload.shape[0] - EXTRA
    copies = [
        pltpu.make_async_copy(shards, shard_rows, arrived.at[0]),
        pltpu.make_async_copy(nodes, node_rows, arrived.at[1]),
        pltpu.make_async_copy(rows.at[0:first], payload.at[0:first], arrived.at[2]),
    ]
    for copy in copies:
        copy.start()
    for copy in copies[:2]:
        copy.wait()
    row = lax.broadcasted_iota(i32, (EXTRA, grid), 0)
    notes = jnp.full((EXTRA, grid), -1, i32)
    for top in range(shards.shape[0]):
        node = node_rows[top : top + 1, :]
        for at, value in enumerate((shard_rows[top : top + 1, :], node & 255, node >> 8)):
            notes = jnp.where(row == 3 * top + at, value, notes)
    payload[first:, 0:grid] = notes.astype(f32).astype(bf16)
    if grid < payload.shape[1]:
        payload[first:, grid:] = jnp.zeros((EXTRA, payload.shape[1] - grid), bf16)
    copies[2].wait()


def encode_kernel(steps, first, last, halves, *refs):
    refs = list(refs)
    meta, base, w_grid = refs[:3]
    del refs[:3]
    if first:
        w_mesh, _ = refs.pop(0), refs.pop(0)
        projected = dot(base[...], w_mesh[...]).astype(bf16)
    else:
        total_in = refs.pop(0)
        projected = base[...]
    payloads = refs[:steps]
    del refs[:steps]
    picks, slopes = refs[:steps], refs[steps : 2 * steps]
    del refs[: 2 * steps]
    total = None if first else total_in[...]
    nodes = projected.shape[0]
    for payload, pick, slope_out in zip(payloads, picks, slopes):
        grid = pick.shape[0]
        notes = payload[grid:, 0:grid].astype(f32)
        target = jnp.full((1, grid), -1.0, f32)
        for at in range(0, notes.shape[0] // 3 * 3, 3):
            named = notes[at : at + 1] == meta[1:2, 0:grid].astype(f32)
            target = jnp.where(named, notes[at + 1 : at + 2] + 256.0 * notes[at + 2 : at + 3], target)
        target = target.astype(i32)
        column = jnp.concatenate([upright(target[:, at : at + LANES]) for at in range(0, grid, LANES)], axis=0)
        picked = pick_rows(column, 0, nodes)
        pick[...] = picked
        pre = dot(payload[0:grid, :], w_grid[...]) + dot(picked, projected)
        act, slope = gated(0.5 * pre)
        slope_out[...] = slope.astype(bf16)
        added = dot(pick_columns(target, 0, nodes), act.astype(bf16))
        total = added if total is None else total + added
    if first:
        refs.pop(0)[...] = projected
    if not last:
        refs[0][...] = total
        return
    keep, sends = refs[0], refs[1:halves]
    part = nodes // halves
    own = meta[0:1, :]

    def half(shift):
        rows = total[0:part]
        for at in range(1, halves):
            rows = jnp.where(own == (at - shift) % halves, total[at * part : (at + 1) * part], rows)
        return rows

    keep[...] = half(0)
    for shift in range(1, halves):
        sends[shift - 1][...] = half(shift).astype(bf16)


def hand_out(rows, outs):
    rows = rows.astype(bf16)
    depth = outs[0].shape[0]
    count = rows.shape[0] // depth
    for at, out in enumerate(outs):
        first = 0 if at == 0 else (count - len(outs) + at) * depth
        out[...] = rows[first : first + depth]


def updated(hidden, total, w_out, gain_row):
    agg = dot(total, w_out)
    return (hidden.astype(f32) + agg * norm_scale(agg) * gain_row).astype(bf16), agg


def listed_update(list_here, total, hidden, w_out, gain_row, w_send):
    picks = list_here[...]
    rows, kept = dot(picks, total).astype(bf16), dot(picks, hidden)
    return 0.5 * dot(updated(kept, rows, w_out, gain_row)[0], w_send)


def start_kernel(halves, *refs):
    meta = refs[0]
    parts = refs[1 : 1 + halves]
    mesh_init, w_enc_out, gain, w_send, list_here, whole = refs[1 + halves : 7 + halves]
    part = parts[0].shape[0]
    own = meta[0:1, :]
    for at in range(halves):
        rows = parts[0][...].astype(f32)
        for shift in range(1, halves):
            rows = jnp.where(own == (at - shift) % halves, parts[shift][...].astype(f32), rows)
        whole[at * part : (at + 1) * part, :] = rows.astype(bf16)
    hand_out(
        listed_update(list_here, whole[...], mesh_init[...], w_enc_out[...], gain[...], w_send[0]), refs[7 + halves :]
    )


def local_kernel(layer, total, hidden, w_out, gain, w_send, w_recv, here, hidden_out, agg_out, pre, table):
    nodes = hidden.shape[0]
    if layer:
        fresh, agg = updated(hidden[...], total[...], w_out[layer - 1], gain[layer - 1 : layer, :])
    else:
        fresh, agg = updated(hidden[...], total[...], w_out[...], gain[...])
    hidden_out[...] = fresh
    agg_out[...] = agg
    table[0:nodes, :] = (0.5 * dot(fresh, w_send[layer])).astype(bf16)
    table[nodes:, :] = (0.5 * dot(fresh, w_recv[layer])).astype(bf16)
    for at in range(0, pre.shape[0], BLOCK):
        pre[at : at + BLOCK, :] = dot(here[at : at + BLOCK, :], table[...])


def local_more_kernel(table, here, pre):
    skip = here.shape[0] - pre.shape[0]
    for at in range(0, pre.shape[0], BLOCK):
        pre[at : at + BLOCK, :] = dot(here[skip + at : skip + at + BLOCK, :], table[...])


def stack_halo(halos, halo):
    at = 0
    for block in halos:
        halo[at : at + block.shape[0], :] = block[...]
        at += block.shape[0]
    if at < halo.shape[0]:
        halo[at:, :] = jnp.zeros((halo.shape[0] - at, halo.shape[1]), bf16)


def node_sum(pres, halos, halo_here, there, slope_out, halo, act_out):
    nodes = there.shape[0] // 2
    stack_halo(halos, halo)
    half = pres[0].shape[0]
    for at in range(0, 2 * half, BLOCK):
        block = slice(at, at + BLOCK)
        pre = pres[at // half][at % half : at % half + BLOCK, :]
        act, slope = gated(pre + dot(halo_here[block, :], halo[...]))
        slope_out[block, :] = slope.astype(bf16)
        act_out[block, :] = act.astype(bf16)
    return dot(there[nodes:, :], act_out[...])


def layer_kernel(layer, shifts, *refs):
    hidden, pres = refs[0], refs[1:3]
    halos, refs = refs[3 : 3 + shifts], refs[3 + shifts :]
    halo_here, there, w_out, gain, w_send, list_here = refs[:6]
    total_out, slope_out = refs[6:8]
    outs = refs[8:-2]
    total = node_sum(pres, halos, halo_here, there, slope_out, *refs[-2:]).astype(bf16)
    total_out[...] = total
    gain_row = gain[layer : layer + 1, :]
    hand_out(listed_update(list_here, total, hidden[...], w_out[layer], gain_row, w_send[layer + 1]), outs)


def edge_grads(listed, grad_agg, w_out, here, halo_there, slope, grad_pre, outs):
    nodes = grad_agg.shape[0]
    spread = (0.5 * dot_back(grad_agg.astype(bf16), w_out)).astype(bf16)
    for at in range(0, slope.shape[0], BLOCK):
        block = slice(at, at + BLOCK)
        grad_act = dot(here[block, nodes:], spread)
        grad_pre[block, :] = grad_act.astype(bf16) * slope[block, :]
    hand_out(dot(halo_there[...], grad_pre[...])[0:listed], outs)


def turn_kernel(layer, shifts, *refs):
    hidden, pres = refs[0], refs[1:3]
    halos, refs = refs[3 : 3 + shifts], refs[3 + shifts :]
    halo_here, there, w_out, gain, here, halo_there, cot = refs[:7]
    hidden_out, grad_pre = refs[7:9]
    outs = refs[9:-2]
    slope, halo = refs[-2:]
    total = node_sum(pres, halos, halo_here, there, slope, halo, grad_pre)
    gain_row = gain[layer : layer + 1, :]
    fresh, agg = updated(hidden[...], total.astype(bf16), w_out[layer], gain_row)
    hidden_out[...] = fresh
    edge_grads(shifts * outs[0].shape[0], norm_back(agg, gain_row, cot[...].astype(f32)), w_out[layer], here, halo_there, slope, grad_pre, outs)


def rest_kernel(layer, side, upstream, grad_pre, there, weights, rest):
    nodes = upstream.shape[0]
    sums = dot(there[side * nodes : (side + 1) * nodes, :], grad_pre[...]).astype(bf16)
    rest[...] = upstream[...].astype(f32) + dot_back(sums, weights[layer])


def arrived(rest, returned, list_there, w_send, halo):
    stack_halo(returned, halo)
    projected = dot_back(halo[...], w_send).astype(bf16)
    return rest[...] + dot(list_there[...], projected)


def back_kernel(layer, shifts, *refs):
    rest = refs[0]
    returned, refs = refs[1 : 1 + shifts], refs[1 + shifts :]
    list_there, w_send, agg, slope, gain, w_out, here, halo_there = refs[:8]
    upstream_out, grad_pre = refs[8:10]
    outs = refs[10:-1]
    halo = refs[-1]
    upstream = arrived(rest, returned, list_there, w_send[layer + 1], halo)
    upstream_out[...] = upstream
    grad_agg = norm_back(agg[...], gain[layer : layer + 1, :], upstream)
    edge_grads(shifts * outs[0].shape[0], grad_agg, w_out[layer], here, halo_there, slope, grad_pre, outs)


def pair_grads(spread, pick, slope):
    return dot(pick, spread).astype(bf16) * slope


def finish_kernel(shifts, *refs):
    rest = refs[0]
    returned, refs = refs[1 : 1 + shifts], refs[1 + shifts :]
    list_there, w_send, enc_sum, gain, w_enc_out, pick, slope, spread_out = refs[:8]
    outs, halo = refs[8:-1], refs[-1]
    upstream = arrived(rest, returned, list_there, w_send[0], halo)
    spread = (0.5 * dot_back(norm_back(enc_sum[...], gain[...], upstream).astype(bf16), w_enc_out[...])).astype(bf16)
    spread_out[...] = spread
    at = 0
    for out in outs:
        rows = slice(at, at + out.shape[0])
        out[...] = pair_grads(spread, pick[rows, :], slope[rows, :])
        at += out.shape[0]


def others_kernel(count, *refs):
    spread = refs[0][...]
    picks, slopes, outs = refs[1 : 1 + count], refs[1 + count : 1 + 2 * count], refs[1 + 2 * count :]
    for pick, slope, out in reversed(list(zip(picks, slopes, outs))):
        skip = pick.shape[0] - out.shape[0]
        out[...] = pair_grads(spread, pick[skip:, :], slope[skip:, :])


def relay_kernel(first, own, passed, *refs):
    rows = passed.shape[0]
    out = refs[0] if len(refs) == 1 else refs[-2]
    out[...] = (own[first : first + rows, :].astype(f32) + passed[...].astype(f32)).astype(bf16)
    if len(refs) > 1:
        refs[-1][...] = refs[0][...]


def sum_kernel(own, piece, total):
    total[...] = own[0 : piece.shape[0], :].astype(f32) + piece[...].astype(f32)


def grid_kernel(whole, *refs):
    blocks, pieces, (w_grid, out) = refs[:whole], refs[whole:-2], refs[-2:]
    if not pieces:
        total = blocks[0][...].astype(f32)
        for block in blocks[1:]:
            total = total + block[...].astype(f32)
        out[...] = dot_back(total.astype(bf16), w_grid[...])
        return
    (own, near), (summed, second) = blocks, pieces
    first = summed.shape[0]
    total = summed[...] + near[0:first, :].astype(f32)
    out[0:first, :] = dot_back(total.astype(bf16), w_grid[...])
    total = own[first:, :].astype(f32) + near[first:, :].astype(f32) + second[...].astype(f32)
    out[first:, :] = dot_back(total.astype(bf16), w_grid[...])


def shifted(value, axis, by):
    size = lax.axis_size(axis)
    return lax.ppermute(value, axis, [(at, (at + by) % size) for at in range(size)])


def partner(at, step, size):
    return at ^ step if size & (size - 1) == 0 else (at + step) % size


def sent_to(value, step):
    size = lax.axis_size("mesh")
    return lax.ppermute(value, "mesh", [(at, partner(at, step, size)) for at in range(size)])


def sent_back(value, step):
    size = lax.axis_size("mesh")
    return lax.ppermute(value, "mesh", [(partner(at, step, size), at) for at in range(size)])


def in_order(pieces, axis):
    return jnp.roll(jnp.stack(pieces)[::-1], lax.axis_index(axis) + 1, axis=0)


def on_device(
    grid_feats,
    g2m_shard,
    g2m_node,
    mesh_init,
    sender_slots,
    receivers,
    halo_index,
    w_enc_grid,
    w_enc_mesh,
    w_enc_out,
    enc_gain,
    w_send,
    w_recv,
    w_out,
    layer_gain,
    out_cot,
):
    shards = lax.axis_size("mesh")
    shard = lax.axis_index("mesh")
    halves = lax.axis_size("rep")
    feats = lax.axis_size("feat")
    nodes, width = mesh_init.shape
    grid, tops = g2m_shard.shape
    edges = sender_slots.shape[0]
    depth = halo_index.shape[2]
    shifts = shards - 1
    listed_rows = shifts * depth
    wide = -(-listed_rows // LANES) * LANES
    all_edges = edges * halves * feats
    enc_gain = enc_gain[None, :]

    relayed = shards == 4
    cuts = 2 if relayed else 1
    shared = relayed and halves == 2
    piece_rows = grid // cuts
    in_place = [pltpu.with_memory_space_constraint(array, pltpu.HBM) for array in (grid_feats, g2m_shard.T, g2m_node.T)]
    (payload,) = call(
        note_kernel,
        [((grid + EXTRA, width), bf16)],
        [((tops, grid), i32), ((tops, grid), i32)],
        copied=True,
    )(*in_place)

    place = sender_slots - nodes
    away = partner(shard, place // depth, shards)
    if shards & (shards - 1):
        away = lax.rem(shard - place // depth + shards, shards)
    slots = jnp.where(sender_slots < nodes, sender_slots, nodes + (shifts - away) * depth + place % depth)
    both = jnp.stack([slots, receivers])
    others = [shifted(both, "rep", step) for step in range(1, halves)]
    if relayed:
        across = sent_to(payload, 2)
        payloads = [payload, sent_to(payload, 1), across]
    else:
        payloads = [payload] + [sent_to(payload, step) for step in range(1, shards)]
    both = in_order([both] + others, "rep")
    both = in_order([both] + [shifted(both, "feat", step) for step in range(1, feats)], "feat")
    both = both.reshape(feats * halves, 2, edges)
    all_slots, all_receivers = both[:, 0].reshape(1, -1), both[:, 1].reshape(1, -1)
    steps = shards - jnp.arange(1, shards, dtype=i32)
    if shared:
        core = lax.axis_index("rep")
        steps = jnp.where((core == 0) & (steps > 1), 5 - steps, steps)
        entry = all_slots - nodes
        turned = (core == 0) & (entry >= 0) & (entry < 2 * depth)
        all_slots = all_slots + jnp.where(turned, jnp.where(entry < depth, depth, -depth), 0)
    readers = partner(shard, steps, shards)
    lists = jnp.take(halo_index[0], readers, axis=0).reshape(1, -1)
    here, there, halo_here, halo_there, list_here, list_there = call(
        place_kernel,
        [
            ((all_edges, 2 * nodes), bf16),
            ((2 * nodes, all_edges), bf16),
            ((all_edges, wide), bf16),
            ((wide, all_edges), bf16),
            ((listed_rows, nodes), bf16),
            ((nodes, listed_rows), bf16),
        ],
        products=[(all_edges, nodes, width), (all_edges, 2 * nodes, width)],
    )(all_slots, all_receivers, lists)

    if relayed:
        across, list_here = lax.optimization_barrier((across, list_here))
        payloads.append(sent_to(across, 1))

    meta = jnp.broadcast_to(jnp.stack([lax.axis_index("rep"), shard]).astype(i32)[:, None], (2, width))
    node_f32, node_bf16 = ((nodes, width), f32), ((nodes, width), bf16)
    row_shape, half = ((grid, width), bf16), nodes // halves
    square = (nodes, width, width)
    enc_picks, enc_slopes = [], []
    base, total = mesh_init, None
    groups = [payloads[:2]] + [payloads[at : at + 1] for at in range(2, shards)]
    for at, group in enumerate(groups):
        first, last = at == 0, at == len(groups) - 1
        count = len(group)
        outs = [((grid, nodes), bf16)] * count + [row_shape] * count
        outs += [node_bf16] if first else []
        outs += [((half, width), f32)] + [((half, width), bf16)] * (halves - 1) if last else [node_f32]
        got = list(
            call(
                functools.partial(encode_kernel, count, first, last, halves),
                outs,
                (),
                [square] * first + [(grid, width, width), (grid, nodes, width), (nodes, grid, width)] * count,
            )(
                meta, base, w_enc_grid, *((w_enc_mesh, list_here) if first else (total,)), *group
            )
        )
        enc_picks += got[:count]
        enc_slopes += got[count : 2 * count]
        del got[: 2 * count]
        if first:
            base = got.pop(0)
        total = got[0]
    part = got[0]
    for step in range(1, halves):
        part = part + shifted(got[step], "rep", step).astype(f32)
    part = part.astype(bf16)
    pieces = [part] + [shifted(part, "feat", step) for step in range(1, feats)]
    if feats > 2:
        pieces = list(in_order(pieces, "feat"))
    part = sum(piece.astype(f32) for piece in pieces).astype(bf16)
    parts = [part] + [shifted(part, "rep", -step) for step in range(1, halves)]

    listed = [((depth, width), bf16)] * (2 if shared else shifts)

    def exchange(blocks, send, early):
        if not shared:
            return [send(block, shifts - at) for at, block in enumerate(blocks)], early
        far = lax.ppermute(
            blocks[0], ("mesh", "rep"), [(2 * at + side, 2 * (at ^ (2 + side)) + side) for at in range(4) for side in range(2)]
        )
        near = send(blocks[1], 1)
        far, early = lax.optimization_barrier((far, early))
        return [far, shifted(far, "rep", 1), near], early

    listed_products = [(listed_rows, width, width)] * 2 + [(listed_rows, nodes, width)] * 2
    total, *outgoing = call(functools.partial(start_kernel, halves), [node_bf16] + listed, (), listed_products)(
        meta, *parts, mesh_init, w_enc_out, enc_gain, w_send, list_here
    )

    half_f32, edge_bf16 = ((all_edges // 2, width), f32), ((all_edges, width), bf16)
    halo, back_halo = ((wide, width), bf16), ((listed_rows, width), bf16)
    forward_products = [(all_edges, wide, width), (nodes, all_edges, width), square]
    backward_products = [square, (all_edges, nodes, width), (wide, all_edges, width)]
    half_product = (all_edges // 2, 2 * nodes, width)

    hidden, sums, slopes = mesh_init, [], []
    for layer in range(LAYERS):
        weights = (w_out, layer_gain) if layer else (w_enc_out, enc_gain)
        early = call(
            functools.partial(local_kernel, layer),
            [node_bf16, node_f32, half_f32, ((2 * nodes, width), bf16)],
            (),
            [square, square, square, half_product],
        )(total, hidden, *weights, w_send, w_recv, here)
        halos, (hidden, agg, pre, both_tables) = exchange(outgoing, sent_to, early)
        (more,) = call(local_more_kernel, [half_f32], (), [half_product])(both_tables, here)
        sums.append(agg)
        if layer == LAYERS - 1:
            break
        total, slope, *outgoing = call(
            functools.partial(layer_kernel, layer, shifts),
            [node_bf16, edge_bf16] + listed,
            [halo, edge_bf16],
            forward_products[:2] + listed_products,
        )(hidden, pre, more, *halos, halo_here, there, w_out, layer_gain, w_send, list_here)
        slopes.append(slope)
    enc_sum, records = sums[0], list(zip(sums[1:], slopes))
    final_mesh, grad_pre, *outgoing = call(
        functools.partial(turn_kernel, layer, shifts), [node_bf16, edge_bf16] + listed, [edge_bf16, halo],
        forward_products + backward_products,
    )(hidden, pre, more, *halos, halo_here, there, w_out, layer_gain, here, halo_there, out_cot)
    upstream = out_cot
    for layer in reversed(range(LAYERS)):

        def rest_of(side, upstream, weights):
            (rest,) = call(
                functools.partial(rest_kernel, layer, side), [node_f32], (), [(nodes, all_edges, width), square]
            )(upstream, grad_pre, there, weights)
            return rest

        returned, early = exchange(outgoing, sent_back, rest_of(0, upstream, w_send))
        rest = rest_of(1, early, w_recv)
        if layer:
            agg, slope = records[layer - 1]
            upstream, grad_pre, *outgoing = call(
                functools.partial(back_kernel, layer - 1, shifts),
                [node_f32, edge_bf16] + listed,
                [back_halo],
                backward_products + [(listed_rows, width, width), (nodes, listed_rows, width)],
            )(rest, *returned, list_there, w_send, agg, slope, layer_gain, w_out, here, halo_there)
    piece = ((piece_rows, width), bf16)
    one = (grid, nodes, width)
    spread, *far = call(
        functools.partial(finish_kernel, shifts),
        [node_bf16] + [piece] * cuts,
        [back_halo],
        [square, (listed_rows, width, width), (nodes, listed_rows, width), one],
    )(rest, *returned, list_there, w_send, enc_sum, enc_gain, w_enc_out, enc_picks[-1], enc_slopes[-1])
    blocks = call(
        functools.partial(others_kernel, shards - 1), [row_shape] * (shards - 1), products=[one] * (shards - 1)
    )(spread, *enc_picks[:-1], *enc_slopes[:-1])
    if relayed:
        passed = [sent_back(block, 1) for block in far]
        first, near = call(functools.partial(relay_kernel, 0), [piece, row_shape])(blocks[2], passed[0], blocks[1])
        (second,) = call(functools.partial(relay_kernel, piece_rows), [piece])(blocks[2], passed[1])
        near = sent_back(near, 1)
        first, second = sent_back(first, 2), sent_back(second, 2)
        (summed,) = call(sum_kernel, [((piece_rows, width), f32)])(blocks[0], first)
        (grid_grad,) = call(
            functools.partial(grid_kernel, 2), [((grid, width), f32)], products=[(grid, width, width)]
        )(blocks[0], near, summed, second, w_enc_grid)
    else:
        blocks = [*blocks, *far]
        blocks = [blocks[0]] + [sent_back(block, step) for step, block in enumerate(blocks) if step]
        (grid_grad,) = call(
            functools.partial(grid_kernel, shards), [((grid, width), f32)], products=[(grid, width, width)]
        )(*blocks, w_enc_grid)
    return (final_mesh, grid_grad)


def solution(mesh):
    return jax.shard_map(
        on_device,
        mesh=mesh,
        in_specs=(
            P(("groups", "mesh", "feat", "rep"), None),
            P(("groups", "mesh", "feat", "rep"), None),
            P(("groups", "mesh", "feat", "rep"), None),
            P(("groups", "mesh"), None),
            P(("groups", "mesh", "feat", "rep")),
            P(("groups", "mesh", "feat", "rep")),
            P(("groups", "mesh"), None, None),
            P(),
            P(),
            P(),
            P(),
            P(),
            P(),
            P(),
            P(),
            P(("groups", "mesh"), None),
        ),
        out_specs=(P(("groups", "mesh"), None), P(("groups", "mesh", "feat", "rep"), None)),
        check_vma=False,
    )
```

```python
import functools
import math

import jax
import jax.numpy as jnp
from jax import lax
from jax.experimental import pallas as pl
from jax.experimental.pallas import tpu as pltpu
from jax.sharding import PartitionSpec as P

LAYERS = 3
LANES = 128
BLOCK = 512
EXTRA = 16
eps = 1e-05

f32 = jnp.float32
bf16 = jnp.bfloat16
i32 = jnp.int32


def norm_scale(totals):
    return lax.rsqrt(jnp.mean(totals * totals, axis=-1, keepdims=True) + eps)


def norm_back(totals, gain_row, upstream):
    scaled = norm_scale(totals)
    normed = totals * scaled
    slope = upstream * gain_row
    return scaled * (slope - normed * jnp.mean(slope * normed, axis=-1, keepdims=True))


def dot(left, right):
    return jnp.dot(left, right, preferred_element_type=f32)


def dot_back(left, right):
    return lax.dot_general(left, right, (((1,), (1,)), ((), ())), preferred_element_type=f32)


def gated(half):
    half = half.astype(bf16)
    bend = jnp.tanh(half)
    act = half + half * bend
    return act, (1.0 + act) + bend * (1.0 - act)


def as_mask(hit):
    return jnp.where(hit, 1.0, 0.0).astype(bf16)


def pick_columns(index, first, height):
    place = lax.broadcasted_iota(i32, (height, index.shape[1]), 0) + first
    return as_mask(place == index)


def upright(index):
    count = index.shape[1]
    if count < LANES:
        index = jnp.concatenate([index, jnp.full((1, LANES - count), -1, i32)], axis=1)
    return jnp.broadcast_to(index, (LANES, LANES)).T[:count]


def pick_rows(column, first, width):
    lane = lax.broadcasted_iota(i32, column.shape, 1) + first
    return jnp.concatenate([as_mask(column == lane + at) for at in range(0, width, LANES)], axis=1)


def call(body, outs, scratch=(), products=(), copied=False):
    def run(*args):
        def where(array):
            if copied:
                return pl.BlockSpec(memory_space=pltpu.HBM)
            return pl.BlockSpec(memory_space=pltpu.SMEM if array.dtype == i32 and array.ndim == 1 else pltpu.VMEM)

        def size(shape, dtype):
            return jnp.dtype(dtype).itemsize * math.prod(shape)

        own = sum(size(*held) for held in scratch) + (10 << 20)
        moved = sum(array.dtype.itemsize * array.size for array in args) + sum(size(*out) for out in outs)
        limit = own if own + moved < 40 << 20 else min(own + moved, 60 << 20)
        semaphores = [pltpu.SemaphoreType.DMA((2 + len(outs),))] if copied else []
        return pl.pallas_call(
            body,
            out_shape=tuple(jax.ShapeDtypeStruct(shape, dtype) for shape, dtype in outs),
            in_specs=[where(array) for array in args],
            out_specs=tuple(pl.BlockSpec(memory_space=pltpu.VMEM) for _ in outs),
            scratch_shapes=[pltpu.VMEM(shape, dtype) for shape, dtype in scratch] + semaphores,
            compiler_params=pltpu.CompilerParams(vmem_limit_bytes=limit),
            cost_estimate=pl.CostEstimate(
                flops=2 * sum(math.prod(product) for product in products), bytes_accessed=moved, transcendentals=0
            ),
        )(*args)

    return run


def place_kernel(slots, receivers, order, here, there, halo_here, halo_there, list_here, list_there):
    nodes = here.shape[1] // 2
    wide = halo_here.shape[1]

    def body(at):
        block = pl.ds(pl.multiple_of(at * LANES, LANES), LANES)
        slot, receiver = slots[:, block], receivers[:, block]
        slot_column, receiver_column = upright(slot), upright(receiver)
        here[block, 0:nodes] = pick_rows(slot_column, 0, nodes)
        here[block, nodes:] = pick_rows(receiver_column, 0, nodes)
        halo_here[block, :] = pick_rows(slot_column, nodes, wide)
        there[0:nodes, block] = pick_columns(slot, 0, nodes)
        there[nodes:, block] = pick_columns(receiver, 0, nodes)
        halo_there[:, block] = pick_columns(slot, nodes, wide)

    pl.loop(0, slots.shape[1] // LANES)(body)
    count = order.shape[1]
    for at in range(0, count, LANES):
        end = min(at + LANES, count)
        list_here[at:end, :] = pick_rows(upright(order[:, at:end]), 0, nodes)
    list_there[...] = pick_columns(order[...], 0, nodes)


def note_kernel(rows, shards, nodes, payload, shard_rows, node_rows, arrived):
    grid = shards.shape[1]
    first = payload.shape[0] - EXTRA
    copies = [
        pltpu.make_async_copy(shards, shard_rows, arrived.at[0]),
        pltpu.make_async_copy(nodes, node_rows, arrived.at[1]),
        pltpu.make_async_copy(rows.at[0:first], payload.at[0:first], arrived.at[2]),
    ]
    for copy in copies:
        copy.start()
    for copy in copies[:2]:
        copy.wait()
    row = lax.broadcasted_iota(i32, (EXTRA, grid), 0)
    notes = jnp.full((EXTRA, grid), -1, i32)
    for top in range(shards.shape[0]):
        node = node_rows[top : top + 1, :]
        for at, value in enumerate((shard_rows[top : top + 1, :], node & 255, node >> 8)):
            notes = jnp.where(row == 3 * top + at, value, notes)
    payload[first:, 0:grid] = notes.astype(f32).astype(bf16)
    if grid < payload.shape[1]:
        payload[first:, grid:] = jnp.zeros((EXTRA, payload.shape[1] - grid), bf16)
    copies[2].wait()


def encode_kernel(steps, first, last, halves, *refs):
    refs = list(refs)
    meta, base, w_grid = refs[:3]
    del refs[:3]
    if first:
        w_mesh, _ = refs.pop(0), refs.pop(0)
        projected = dot(base[...], w_mesh[...]).astype(bf16)
    else:
        total_in = refs.pop(0)
        projected = base[...]
    payloads = refs[:steps]
    del refs[:steps]
    picks, slopes = refs[:steps], refs[steps : 2 * steps]
    del refs[: 2 * steps]
    total = None if first else total_in[...]
    nodes = projected.shape[0]
    for payload, pick, slope_out in zip(payloads, picks, slopes):
        grid = pick.shape[0]
        notes = payload[grid:, 0:grid].astype(f32)
        target = jnp.full((1, grid), -1.0, f32)
        for at in range(0, notes.shape[0] // 3 * 3, 3):
            named = notes[at : at + 1] == meta[1:2, 0:grid].astype(f32)
            target = jnp.where(named, notes[at + 1 : at + 2] + 256.0 * notes[at + 2 : at + 3], target)
        target = target.astype(i32)
        column = jnp.concatenate([upright(target[:, at : at + LANES]) for at in range(0, grid, LANES)], axis=0)
        picked = pick_rows(column, 0, nodes)
        pick[...] = picked
        pre = dot(payload[0:grid, :], w_grid[...]) + dot(picked, projected)
        act, slope = gated(0.5 * pre)
        slope_out[...] = slope.astype(bf16)
        added = dot(pick_columns(target, 0, nodes), act.astype(bf16))
        total = added if total is None else total + added
    if first:
        refs.pop(0)[...] = projected
    if not last:
        refs[0][...] = total
        return
    keep, sends = refs[0], refs[1:halves]
    part = nodes // halves
    own = meta[0:1, :]

    def half(shift):
        rows = total[0:part]
        for at in range(1, halves):
            rows = jnp.where(own == (at - shift) % halves, total[at * part : (at + 1) * part], rows)
        return rows

    keep[...] = half(0)
    for shift in range(1, halves):
        sends[shift - 1][...] = half(shift).astype(bf16)


def hand_out(rows, outs):
    rows = rows.astype(bf16)
    depth = outs[0].shape[0]
    count = rows.shape[0] // depth
    for at, out in enumerate(outs):
        first = 0 if at == 0 else (count - len(outs) + at) * depth
        out[...] = rows[first : first + depth]


def updated(hidden, total, w_out, gain_row):
    agg = dot(total, w_out)
    return (hidden.astype(f32) + agg * norm_scale(agg) * gain_row).astype(bf16), agg


def listed_update(list_here, total, hidden, w_out, gain_row, w_send):
    picks = list_here[...]
    rows, kept = dot(picks, total).astype(bf16), dot(picks, hidden)
    return 0.5 * dot(updated(kept, rows, w_out, gain_row)[0], w_send)


def start_kernel(halves, *refs):
    meta = refs[0]
    parts = refs[1 : 1 + halves]
    mesh_init, w_enc_out, gain, w_send, list_here, whole = refs[1 + halves : 7 + halves]
    part = parts[0].shape[0]
    own = meta[0:1, :]
    for at in range(halves):
        rows = parts[0][...].astype(f32)
        for shift in range(1, halves):
            rows = jnp.where(own == (at - shift) % halves, parts[shift][...].astype(f32), rows)
        whole[at * part : (at + 1) * part, :] = rows.astype(bf16)
    hand_out(
        listed_update(list_here, whole[...], mesh_init[...], w_enc_out[...], gain[...], w_send[0]), refs[7 + halves :]
    )


def local_kernel(layer, total, hidden, w_out, gain, w_send, w_recv, here, hidden_out, agg_out, pre, table):
    nodes = hidden.shape[0]
    if layer:
        fresh, agg = updated(hidden[...], total[...], w_out[layer - 1], gain[layer - 1 : layer, :])
    else:
        fresh, agg = updated(hidden[...], total[...], w_out[...], gain[...])
    hidden_out[...] = fresh
    agg_out[...] = agg
    table[0:nodes, :] = (0.5 * dot(fresh, w_send[layer])).astype(bf16)
    table[nodes:, :] = (0.5 * dot(fresh, w_recv[layer])).astype(bf16)
    for at in range(0, pre.shape[0], BLOCK):
        pre[at : at + BLOCK, :] = dot(here[at : at + BLOCK, :], table[...])


def local_more_kernel(table, here, pre):
    skip = here.shape[0] - pre.shape[0]
    for at in range(0, pre.shape[0], BLOCK):
        pre[at : at + BLOCK, :] = dot(here[skip + at : skip + at + BLOCK, :], table[...])


def stack_halo(halos, halo):
    at = 0
    for block in halos:
        halo[at : at + block.shape[0], :] = block[...]
        at += block.shape[0]
    if at < halo.shape[0]:
        halo[at:, :] = jnp.zeros((halo.shape[0] - at, halo.shape[1]), bf16)


def node_sum(pres, halos, halo_here, there, slope_out, halo, act_out):
    nodes = there.shape[0] // 2
    stack_halo(halos, halo)
    half = pres[0].shape[0]
    for at in range(0, 2 * half, BLOCK):
        block = slice(at, at + BLOCK)
        pre = pres[at // half][at % half : at % half + BLOCK, :]
        act, slope = gated(pre + dot(halo_here[block, :], halo[...]))
        slope_out[block, :] = slope.astype(bf16)
        act_out[block, :] = act.astype(bf16)
    return dot(there[nodes:, :], act_out[...])


def layer_kernel(layer, shifts, *refs):
    hidden, pres = refs[0], refs[1:3]
    halos, refs = refs[3 : 3 + shifts], refs[3 + shifts :]
    halo_here, there, w_out, gain, w_send, list_here = refs[:6]
    total_out, slope_out = refs[6:8]
    outs = refs[8:-2]
    total = node_sum(pres, halos, halo_here, there, slope_out, *refs[-2:]).astype(bf16)
    total_out[...] = total
    gain_row = gain[layer : layer + 1, :]
    hand_out(listed_update(list_here, total, hidden[...], w_out[layer], gain_row, w_send[layer + 1]), outs)


def edge_grads(listed, grad_agg, w_out, here, halo_there, slope, grad_pre, outs):
    nodes = grad_agg.shape[0]
    spread = (0.5 * dot_back(grad_agg.astype(bf16), w_out)).astype(bf16)
    for at in range(0, slope.shape[0], BLOCK):
        block = slice(at, at + BLOCK)
        grad_act = dot(here[block, nodes:], spread)
        grad_pre[block, :] = grad_act.astype(bf16) * slope[block, :]
    hand_out(dot(halo_there[...], grad_pre[...])[0:listed], outs)


def turn_kernel(layer, shifts, *refs):
    hidden, pres = refs[0], refs[1:3]
    halos, refs = refs[3 : 3 + shifts], refs[3 + shifts :]
    halo_here, there, w_out, gain, here, halo_there, cot = refs[:7]
    hidden_out, grad_pre = refs[7:9]
    outs = refs[9:-2]
    slope, halo = refs[-2:]
    total = node_sum(pres, halos, halo_here, there, slope, halo, grad_pre)
    gain_row = gain[layer : layer + 1, :]
    fresh, agg = updated(hidden[...], total.astype(bf16), w_out[layer], gain_row)
    hidden_out[...] = fresh
    edge_grads(shifts * outs[0].shape[0], norm_back(agg, gain_row, cot[...].astype(f32)), w_out[layer], here, halo_there, slope, grad_pre, outs)


def rest_kernel(layer, side, upstream, grad_pre, there, weights, rest):
    nodes = upstream.shape[0]
    sums = dot(there[side * nodes : (side + 1) * nodes, :], grad_pre[...]).astype(bf16)
    rest[...] = upstream[...].astype(f32) + dot_back(sums, weights[layer])


def arrived(rest, returned, list_there, w_send, halo):
    stack_halo(returned, halo)
    projected = dot_back(halo[...], w_send).astype(bf16)
    return rest[...] + dot(list_there[...], projected)


def back_kernel(layer, shifts, *refs):
    rest = refs[0]
    returned, refs = refs[1 : 1 + shifts], refs[1 + shifts :]
    list_there, w_send, agg, slope, gain, w_out, here, halo_there = refs[:8]
    upstream_out, grad_pre = refs[8:10]
    outs = refs[10:-1]
    halo = refs[-1]
    upstream = arrived(rest, returned, list_there, w_send[layer + 1], halo)
    upstream_out[...] = upstream
    grad_agg = norm_back(agg[...], gain[layer : layer + 1, :], upstream)
    edge_grads(shifts * outs[0].shape[0], grad_agg, w_out[layer], here, halo_there, slope, grad_pre, outs)


def pair_grads(spread, pick, slope):
    return dot(pick, spread).astype(bf16) * slope


def finish_kernel(shifts, *refs):
    rest = refs[0]
    returned, refs = refs[1 : 1 + shifts], refs[1 + shifts :]
    list_there, w_send, enc_sum, gain, w_enc_out, pick, slope, spread_out = refs[:8]
    outs, halo = refs[8:-1], refs[-1]
    upstream = arrived(rest, returned, list_there, w_send[0], halo)
    spread = (0.5 * dot_back(norm_back(enc_sum[...], gain[...], upstream).astype(bf16), w_enc_out[...])).astype(bf16)
    spread_out[...] = spread
    at = 0
    for out in outs:
        rows = slice(at, at + out.shape[0])
        out[...] = pair_grads(spread, pick[rows, :], slope[rows, :])
        at += out.shape[0]


def others_kernel(count, *refs):
    spread = refs[0][...]
    picks, slopes, outs = refs[1 : 1 + count], refs[1 + count : 1 + 2 * count], refs[1 + 2 * count :]
    for pick, slope, out in reversed(list(zip(picks, slopes, outs))):
        skip = pick.shape[0] - out.shape[0]
        out[...] = pair_grads(spread, pick[skip:, :], slope[skip:, :])


def relay_kernel(first, own, passed, out):
    rows = passed.shape[0]
    out[...] = (own[first : first + rows, :].astype(f32) + passed[...].astype(f32)).astype(bf16)


def sum_kernel(own, piece, total):
    total[...] = own[0 : piece.shape[0], :].astype(f32) + piece[...].astype(f32)


def grid_kernel(whole, *refs):
    blocks, pieces, (w_grid, out) = refs[:whole], refs[whole:-2], refs[-2:]
    if not pieces:
        total = blocks[0][...].astype(f32)
        for block in blocks[1:]:
            total = total + block[...].astype(f32)
        out[...] = dot_back(total.astype(bf16), w_grid[...])
        return
    (own, near), (summed, second) = blocks, pieces
    first = summed.shape[0]
    total = summed[...] + near[0:first, :].astype(f32)
    out[0:first, :] = dot_back(total.astype(bf16), w_grid[...])
    total = own[first:, :].astype(f32) + near[first:, :].astype(f32) + second[...].astype(f32)
    out[first:, :] = dot_back(total.astype(bf16), w_grid[...])


def shifted(value, axis, by):
    size = lax.axis_size(axis)
    return lax.ppermute(value, axis, [(at, (at + by) % size) for at in range(size)])


def partner(at, step, size):
    return at ^ step if size & (size - 1) == 0 else (at + step) % size


def sent_to(value, step):
    size = lax.axis_size("mesh")
    return lax.ppermute(value, "mesh", [(at, partner(at, step, size)) for at in range(size)])


def sent_back(value, step):
    size = lax.axis_size("mesh")
    return lax.ppermute(value, "mesh", [(partner(at, step, size), at) for at in range(size)])


def in_order(pieces, axis):
    return jnp.roll(jnp.stack(pieces)[::-1], lax.axis_index(axis) + 1, axis=0)


def on_device(
    grid_feats,
    g2m_shard,
    g2m_node,
    mesh_init,
    sender_slots,
    receivers,
    halo_index,
    w_enc_grid,
    w_enc_mesh,
    w_enc_out,
    enc_gain,
    w_send,
    w_recv,
    w_out,
    layer_gain,
    out_cot,
):
    shards = lax.axis_size("mesh")
    shard = lax.axis_index("mesh")
    halves = lax.axis_size("rep")
    feats = lax.axis_size("feat")
    nodes, width = mesh_init.shape
    grid, tops = g2m_shard.shape
    edges = sender_slots.shape[0]
    depth = halo_index.shape[2]
    shifts = shards - 1
    listed_rows = shifts * depth
    wide = -(-listed_rows // LANES) * LANES
    all_edges = edges * halves * feats
    enc_gain = enc_gain[None, :]

    relayed = shards == 4
    cuts = 2 if relayed else 1
    shared = relayed and halves == 2
    piece_rows = grid // cuts
    in_place = [pltpu.with_memory_space_constraint(array, pltpu.HBM) for array in (grid_feats, g2m_shard.T, g2m_node.T)]
    (payload,) = call(
        note_kernel,
        [((grid + EXTRA, width), bf16)],
        [((tops, grid), i32), ((tops, grid), i32)],
        copied=True,
    )(*in_place)

    place = sender_slots - nodes
    away = partner(shard, place // depth, shards)
    if shards & (shards - 1):
        away = lax.rem(shard - place // depth + shards, shards)
    slots = jnp.where(sender_slots < nodes, sender_slots, nodes + (shifts - away) * depth + place % depth)
    both = jnp.stack([slots, receivers])
    others = [shifted(both, "rep", step) for step in range(1, halves)]
    if relayed:
        across = sent_to(payload, 2)
        payloads = [payload, sent_to(payload, 1), across]
    else:
        payloads = [payload] + [sent_to(payload, step) for step in range(1, shards)]
    both = in_order([both] + others, "rep")
    both = in_order([both] + [shifted(both, "feat", step) for step in range(1, feats)], "feat")
    both = both.reshape(feats * halves, 2, edges)
    all_slots, all_receivers = both[:, 0].reshape(1, -1), both[:, 1].reshape(1, -1)
    steps = shards - jnp.arange(1, shards, dtype=i32)
    if shared:
        core = lax.axis_index("rep")
        steps = jnp.where((core == 0) & (steps > 1), 5 - steps, steps)
        entry = all_slots - nodes
        turned = (core == 0) & (entry >= 0) & (entry < 2 * depth)
        all_slots = all_slots + jnp.where(turned, jnp.where(entry < depth, depth, -depth), 0)
    readers = partner(shard, steps, shards)
    lists = jnp.take(halo_index[0], readers, axis=0).reshape(1, -1)
    here, there, halo_here, halo_there, list_here, list_there = call(
        place_kernel,
        [
            ((all_edges, 2 * nodes), bf16),
            ((2 * nodes, all_edges), bf16),
            ((all_edges, wide), bf16),
            ((wide, all_edges), bf16),
            ((listed_rows, nodes), bf16),
            ((nodes, listed_rows), bf16),
        ],
        products=[(all_edges, nodes, width), (all_edges, 2 * nodes, width)],
    )(all_slots, all_receivers, lists)

    if relayed:
        across, list_here = lax.optimization_barrier((across, list_here))
        payloads.append(sent_to(across, 1))

    meta = jnp.broadcast_to(jnp.stack([lax.axis_index("rep"), shard]).astype(i32)[:, None], (2, width))
    node_f32, node_bf16 = ((nodes, width), f32), ((nodes, width), bf16)
    row_shape, half = ((grid, width), bf16), nodes // halves
    square = (nodes, width, width)
    enc_picks, enc_slopes = [], []
    base, total = mesh_init, None
    groups = [payloads[:2]] + [payloads[at : at + 1] for at in range(2, shards)]
    for at, group in enumerate(groups):
        first, last = at == 0, at == len(groups) - 1
        count = len(group)
        outs = [((grid, nodes), bf16)] * count + [row_shape] * count
        outs += [node_bf16] if first else []
        outs += [((half, width), f32)] + [((half, width), bf16)] * (halves - 1) if last else [node_f32]
        got = list(
            call(
                functools.partial(encode_kernel, count, first, last, halves),
                outs,
                (),
                [square] * first + [(grid, width, width), (grid, nodes, width), (nodes, grid, width)] * count,
            )(
                meta, base, w_enc_grid, *((w_enc_mesh, list_here) if first else (total,)), *group
            )
        )
        enc_picks += got[:count]
        enc_slopes += got[count : 2 * count]
        del got[: 2 * count]
        if first:
            base = got.pop(0)
        total = got[0]
    part = got[0]
    for step in range(1, halves):
        part = part + shifted(got[step], "rep", step).astype(f32)
    part = part.astype(bf16)
    pieces = [part] + [shifted(part, "feat", step) for step in range(1, feats)]
    if feats > 2:
        pieces = list(in_order(pieces, "feat"))
    part = sum(piece.astype(f32) for piece in pieces).astype(bf16)
    parts = [part] + [shifted(part, "rep", -step) for step in range(1, halves)]

    listed = [((depth, width), bf16)] * (2 if shared else shifts)

    def exchange(blocks, send, early):
        if not shared:
            return [send(block, shifts - at) for at, block in enumerate(blocks)], early
        far = lax.ppermute(
            blocks[0], ("mesh", "rep"), [(2 * at + side, 2 * (at ^ (2 + side)) + side) for at in range(4) for side in range(2)]
        )
        near = send(blocks[1], 1)
        far, early = lax.optimization_barrier((far, early))
        return [far, shifted(far, "rep", 1), near], early

    listed_products = [(listed_rows, width, width)] * 2 + [(listed_rows, nodes, width)] * 2
    total, *outgoing = call(functools.partial(start_kernel, halves), [node_bf16] + listed, (), listed_products)(
        meta, *parts, mesh_init, w_enc_out, enc_gain, w_send, list_here
    )

    half_f32, edge_bf16 = ((all_edges // 2, width), f32), ((all_edges, width), bf16)
    halo, back_halo = ((wide, width), bf16), ((listed_rows, width), bf16)
    forward_products = [(all_edges, wide, width), (nodes, all_edges, width), square]
    backward_products = [square, (all_edges, nodes, width), (wide, all_edges, width)]
    half_product = (all_edges // 2, 2 * nodes, width)

    hidden, sums, slopes = mesh_init, [], []
    for layer in range(LAYERS):
        weights = (w_out, layer_gain) if layer else (w_enc_out, enc_gain)
        early = call(
            functools.partial(local_kernel, layer),
            [node_bf16, node_f32, half_f32, ((2 * nodes, width), bf16)],
            (),
            [square, square, square, half_product],
        )(total, hidden, *weights, w_send, w_recv, here)
        halos, (hidden, agg, pre, both_tables) = exchange(outgoing, sent_to, early)
        (more,) = call(local_more_kernel, [half_f32], (), [half_product])(both_tables, here)
        sums.append(agg)
        if layer == LAYERS - 1:
            break
        total, slope, *outgoing = call(
            functools.partial(layer_kernel, layer, shifts),
            [node_bf16, edge_bf16] + listed,
            [halo, edge_bf16],
            forward_products[:2] + listed_products,
        )(hidden, pre, more, *halos, halo_here, there, w_out, layer_gain, w_send, list_here)
        slopes.append(slope)
    enc_sum, records = sums[0], list(zip(sums[1:], slopes))
    final_mesh, grad_pre, *outgoing = call(
        functools.partial(turn_kernel, layer, shifts), [node_bf16, edge_bf16] + listed, [edge_bf16, halo],
        forward_products + backward_products,
    )(hidden, pre, more, *halos, halo_here, there, w_out, layer_gain, here, halo_there, out_cot)
    upstream = out_cot
    for layer in reversed(range(LAYERS)):

        def rest_of(side, upstream, weights):
            (rest,) = call(
                functools.partial(rest_kernel, layer, side), [node_f32], (), [(nodes, all_edges, width), square]
            )(upstream, grad_pre, there, weights)
            return rest

        returned, early = exchange(outgoing, sent_back, rest_of(0, upstream, w_send))
        rest = rest_of(1, early, w_recv)
        if layer:
            agg, slope = records[layer - 1]
            upstream, grad_pre, *outgoing = call(
                functools.partial(back_kernel, layer - 1, shifts),
                [node_f32, edge_bf16] + listed,
                [back_halo],
                backward_products + [(listed_rows, width, width), (nodes, listed_rows, width)],
            )(rest, *returned, list_there, w_send, agg, slope, layer_gain, w_out, here, halo_there)
    piece = ((piece_rows, width), bf16)
    one = (grid, nodes, width)
    spread, *far = call(
        functools.partial(finish_kernel, shifts),
        [node_bf16] + [piece] * cuts,
        [back_halo],
        [square, (listed_rows, width, width), (nodes, listed_rows, width), one],
    )(rest, *returned, list_there, w_send, enc_sum, enc_gain, w_enc_out, enc_picks[-1], enc_slopes[-1])
    blocks = call(
        functools.partial(others_kernel, shards - 1), [row_shape] * (shards - 1), products=[one] * (shards - 1)
    )(spread, *enc_picks[:-1], *enc_slopes[:-1])
    if relayed:
        passed = [sent_back(block, 1) for block in far]
        (first,) = call(functools.partial(relay_kernel, 0), [piece])(blocks[2], passed[0])
        (second,) = call(functools.partial(relay_kernel, piece_rows), [piece])(blocks[2], passed[1])
        near = sent_back(blocks[1], 1)
        first, second = sent_back(first, 2), sent_back(second, 2)
        (summed,) = call(sum_kernel, [((piece_rows, width), f32)])(blocks[0], first)
        (grid_grad,) = call(
            functools.partial(grid_kernel, 2), [((grid, width), f32)], products=[(grid, width, width)]
        )(blocks[0], near, summed, second, w_enc_grid)
    else:
        blocks = [*blocks, *far]
        blocks = [blocks[0]] + [sent_back(block, step) for step, block in enumerate(blocks) if step]
        (grid_grad,) = call(
            functools.partial(grid_kernel, shards), [((grid, width), f32)], products=[(grid, width, width)]
        )(*blocks, w_enc_grid)
    return (final_mesh, grid_grad)


def solution(mesh):
    return jax.shard_map(
        on_device,
        mesh=mesh,
        in_specs=(
            P(("groups", "mesh", "feat", "rep"), None),
            P(("groups", "mesh", "feat", "rep"), None),
            P(("groups", "mesh", "feat", "rep"), None),
            P(("groups", "mesh"), None),
            P(("groups", "mesh", "feat", "rep")),
            P(("groups", "mesh", "feat", "rep")),
            P(("groups", "mesh"), None, None),
            P(),
            P(),
            P(),
            P(),
            P(),
            P(),
            P(),
            P(),
            P(("groups", "mesh"), None),
        ),
        out_specs=(P(("groups", "mesh"), None), P(("groups", "mesh", "feat", "rep"), None)),
        check_vma=False,
    )
```
